32 devices in a mesh: dp: 4 (over y, x), gx: 2 (over core), yz: 4 (over z).
Axes of the slice: x: 2, y: 2, z: 4, core: 2. Of those that a mesh axis runs over, the one named last changes fastest.
Arguments:
- volumes: bfloat16 [4, 4, 2, 4, 16384], P('dp', None, 'gx', 'yz'), may hold values from -6 to 6
- first_kernel: bfloat16 [32, 4, 3, 3, 3], replicated, may hold values from -0.625 to 0.625
- second_kernel: bfloat16 [64, 32, 3, 3, 3], replicated, may hold values from -0.21875 to 0.21875
- cotangent: bfloat16 [4, 64, 2, 4, 256], P('dp', None, 'gx', 'yz'), may hold values from -6 to 6
Outputs:
- features: bfloat16 [4, 64, 2, 4, 256], P('dp', None, 'gx', 'yz')
- act_grad: float32 [4, 32, 2, 4, 2048], P('dp', None, 'gx', 'yz')
- first_grad: float32 [32, 4, 3, 3, 3], replicated
- second_grad: float32 [64, 32, 3, 3, 3], replicated
The draws below stay inside these ranges and needn't reach their ends.
All inputs are finite; a program needn't handle non-finite values.
Results may differ from the reference program's by a relative error of at most 0.019.
The reference program's roundings to bfloat16 on the way count: a program that leaves them out, or rounds other values in their place, can miss the bound.
Values may be sent and summed in bfloat16 or wider, within the bound.
No kernel may reach another device: no remote copies, remote signals or barrier semaphores. Data moves between devices by JAX's collectives and lax.ppermute only.
A program may use at most 128 MiB of HBM per device.

```python
import jax
import jax.numpy as jnp
from jax import lax

IN_CH = 4
C1 = 32
C2 = 64
CX = 32
CY = 32
CZ = 16
PX = 2
PY = 4
PZ = 1
BLOCKS = 4
VOLS = 4
N_GX = 2


def block_scale(rng, shape, shards, smallest, largest):
    def one(axis_at, parts):
        steps = jax.random.uniform(jax.random.fold_in(jax.random.fold_in(rng, 6), axis_at), (parts,), jnp.float32, smallest / len(shards), largest / len(shards))
        return jnp.repeat(jnp.exp(steps), shape[axis_at] // parts).reshape((-1,) + (1,) * (len(shape) - axis_at - 1))

    loudness = one(*shards[0])
    for cut in shards[1:]:
        loudness = loudness * one(*cut)
    return loudness


def normal_values(rng, extent, scale, reach, cuts=(), held_as=jnp.bfloat16):
    drawn = scale * jax.random.normal(rng, extent, jnp.float32)
    if cuts:
        drawn = drawn * block_scale(rng, extent, cuts, -0.22, 0.18)
    return jnp.clip(drawn, -reach, reach).astype(held_as)


def setup_inputs(seed: int = 0) -> dict:
    key_of = jax.random.split(jax.random.key(seed), 5)
    return {
        "volumes": normal_values(key_of[0], (VOLS, IN_CH, PX, BLOCKS, CX * CY * CZ), 1.0, 6.0, ((0, 4), (2, 2), (3, 4))),
        "first_kernel": normal_values(key_of[1], (C1, IN_CH, 3, 3, 3), (27 * IN_CH) ** -0.5, 0.625),
        "second_kernel": normal_values(key_of[2], (C2, C1, 3, 3, 3), (27 * C1) ** -0.5, 0.21875),
        "cotangent": normal_values(key_of[3], (VOLS, C2, PX, BLOCKS, CX * CY * CZ // 64), 1.0, 6.0, ((0, 4), (2, 2), (3, 4))),
    }


SLOPE = 0.3

def convolve_same(values, kernel):
    return lax.conv_general_dilated(values, kernel, (1, 1, 1), 'SAME', dimension_numbers=('NCDHW', 'OIDHW', 'NCDHW'), preferred_element_type=jnp.float32)

def kernel_grad(padded, grad):
    result = lax.conv_general_dilated(padded, grad, (1, 1, 1), 'VALID', dimension_numbers=('CNDHW', 'IODHW', 'NCDHW'), preferred_element_type=jnp.float32)
    return result.transpose(1, 0, 2, 3, 4)

def leaky(values):
    return jnp.where(values > 0, values, SLOPE * values)

def leaky_slope(values):
    return jnp.where(values > 0, jnp.float32(1.0), jnp.float32(SLOPE))

def average_pool(values):
    bat, chan, xs, ys, zs = values.shape
    return values.reshape(bat, chan, xs // 2, 2, ys // 2, 2, zs // 2, 2).mean(axis=(3, 5, 7))

def spread_back(values):
    bat, chan, xs, ys, zs = values.shape
    grown = jnp.broadcast_to(values[:, :, :, None, :, None, :, None], (bat, chan, xs, 2, ys, 2, zs, 2))
    return grown.reshape(bat, chan, 2 * xs, 2 * ys, 2 * zs) * 0.125

def pad_all(values):
    return jnp.pad(values, ((0, 0), (0, 0), (1, 1), (1, 1), (1, 1)))

def to_space(values, factor):
    bat, chan = (values.shape[0], values.shape[1])
    xs, ys, zs = (CX // factor, CY // factor, CZ // factor)
    grid = values.reshape(bat, chan, N_GX, PY, PZ, xs, ys, zs).transpose(0, 1, 2, 5, 3, 6, 4, 7)
    return grid.reshape(bat, chan, N_GX * xs, PY * ys, PZ * zs)

def to_blocks(values):
    bat, chan, xs, ys, zs = values.shape
    lx, ly, lz = (xs // N_GX, ys // PY, zs // PZ)
    grid = values.reshape(bat, chan, N_GX, lx, PY, ly, PZ, lz).transpose(0, 1, 2, 4, 6, 3, 5, 7)
    return grid.reshape(bat, chan, N_GX, PY * PZ, lx * ly * lz)

def reference(volumes, first_kernel, second_kernel, cotangent):
    flipped = jnp.flip(second_kernel, (2, 3, 4)).transpose(1, 0, 2, 3, 4)
    spatial_in = to_space(volumes, 1)
    spatial_up = to_space(cotangent, 4)

    def one_volume(pair):
        single = pair[0][None]
        upstream = pair[1][None]
        pre_first = convolve_same(single, first_kernel)
        act_first = average_pool(leaky(pre_first)).astype(jnp.bfloat16)
        pre_second = convolve_same(act_first, second_kernel)
        feature_out = average_pool(leaky(pre_second)).astype(jnp.bfloat16)
        grad_second = (spread_back(upstream.astype(jnp.float32)) * leaky_slope(pre_second)).astype(jnp.bfloat16)
        act_grad = convolve_same(grad_second, flipped)
        grad_first = (spread_back(act_grad) * leaky_slope(pre_first)).astype(jnp.bfloat16)
        second_part = kernel_grad(pad_all(act_first), grad_second)
        first_part = kernel_grad(pad_all(single), grad_first)
        return (feature_out[0], act_grad[0], first_part, second_part)
    feature_all, grad_all, first_parts, second_parts = lax.map(one_volume, (spatial_in, spatial_up))
    return (to_blocks(feature_all), to_blocks(grad_all), lax.optimization_barrier(jnp.sum(first_parts, axis=0)), lax.optimization_barrier(jnp.sum(second_parts, axis=0)))
```

```python
import functools

import jax
import jax.numpy as jnp
import numpy as np
from jax import lax
from jax.experimental import pallas as pl
from jax.experimental.pallas import tpu as pltpu
from jax.sharding import PartitionSpec as P

CX = 32
CY = 32
CZ = 16
SLOPE = 0.3
F32 = jnp.float32
BF16 = jnp.bfloat16
VMEM_LIMIT = 56 * 1024 * 1024


def leaky(values):
    return jnp.where(values > 0, values, SLOPE * values)


def leaky_slope(values):
    return jnp.where(values > 0, jnp.float32(1.0), jnp.float32(SLOPE))


def convolve_valid(padded, kernel):
    return lax.conv_general_dilated(
        padded,
        kernel,
        (1, 1, 1),
        "VALID",
        dimension_numbers=("NCDHW", "OIDHW", "NCDHW"),
        preferred_element_type=F32,
    )


def kernel_grad(padded, grad):
    result = lax.conv_general_dilated(
        padded,
        grad,
        (1, 1, 1),
        "VALID",
        dimension_numbers=("CNDHW", "IODHW", "NCDHW"),
        preferred_element_type=F32,
    )
    return result.transpose(1, 0, 2, 3, 4)


def average_pool(values):
    bat, chan, xs, ys, zs = values.shape
    return values.reshape(bat, chan, xs // 2, 2, ys // 2, 2, zs // 2, 2).mean(axis=(3, 5, 7))


def spread_back(values):
    bat, chan, xs, ys, zs = values.shape
    grown = jnp.broadcast_to(
        values[:, :, :, None, :, None, :, None], (bat, chan, xs, 2, ys, 2, zs, 2)
    )
    return grown.reshape(bat, chan, 2 * xs, 2 * ys, 2 * zs) * 0.125


def unflatten(values, factor):
    return values[:, :, 0, 0].reshape(
        values.shape[0], values.shape[1], CX // factor, CY // factor, CZ // factor
    )


def flatten(values):
    return values.reshape(values.shape[0], values.shape[1], 1, 1, -1)


def extend_along(values, dim, axis, routes):
    size = values.shape[dim]
    first = lax.slice_in_dim(values, 0, 1, axis=dim)
    last = lax.slice_in_dim(values, size - 1, size, axis=dim)
    before = lax.ppermute(last, axis, routes)
    after = lax.ppermute(first, axis, [(b, a) for a, b in routes])
    return jnp.concatenate([before, values, after], axis=dim)


def extend(values, rows_y, rows_z):
    planes = lax.axis_size("gx")
    count = rows_y * rows_z
    values = extend_along(values, 2, "gx", [(i, i + 1) for i in range(planes - 1)])
    values = extend_along(values, 3, "yz", [(i, i + rows_z) for i in range(count - rows_z)])
    return extend_along(
        values, 4, "yz", [(i, i + 1) for i in range(count - 1) if (i + 1) % rows_z]
    )


def on_device_plain(rows_y, rows_z, volumes, first_kernel, second_kernel, cotangent):
    upstream = unflatten(cotangent, 4)
    padded_in = extend(unflatten(volumes, 1), rows_y, rows_z)
    pre_first = convolve_valid(padded_in, first_kernel)
    act_first = average_pool(leaky(pre_first)).astype(BF16)
    padded_mid = extend(act_first, rows_y, rows_z)
    pre_second = convolve_valid(padded_mid, second_kernel)
    features = average_pool(leaky(pre_second)).astype(BF16)
    grad_second = (spread_back(upstream.astype(F32)) * leaky_slope(pre_second)).astype(BF16)
    flipped = jnp.flip(second_kernel, (2, 3, 4)).transpose(1, 0, 2, 3, 4)
    act_grad = convolve_valid(extend(grad_second, rows_y, rows_z), flipped)
    grad_first = (spread_back(act_grad) * leaky_slope(pre_first)).astype(BF16)
    first_grad, second_grad = lax.psum(
        (kernel_grad(padded_in, grad_first), kernel_grad(padded_mid, grad_second)),
        ("dp", "gx", "yz"),
    )
    return (flatten(features), flatten(act_grad), first_grad, second_grad)


FINE = 48 * CZ
KEPT = 40 * CZ
OWN = CY * CZ
COARSE = 256
MID = (CY // 2) * (CZ // 2)
NF = 18
NS = 17


def constants():
    kept = np.arange(KEPT)
    row = np.where(kept < OWN + 64, kept // CZ, kept // CZ - 40)
    lane = ((row // 2) * 8 + (kept % CZ) // 2) % COARSE
    pool_first = (lane[:, None] == np.arange(COARSE)[None]) * 0.125
    spread_first = pool_first[:OWN, :MID].T
    mid = np.arange(8 * MID)
    plane, y, z = mid // MID, (mid // 8) % 16, mid % 8
    pooled = plane * 32 + (y // 2) * 4 + z // 2
    pool_second = (pooled[:, None] == np.arange(256)[None]) * 0.125
    spread_own = pool_second.T
    spread_rim = np.zeros((256, 8, 128))
    spread_end = np.zeros((384, 256))
    for z in range(8):
        for p in range(8):
            spread_rim[p * 4 + z // 2, p, z] = 0.125
            spread_rim[128 + p * 4 + z // 2, p, 120 + z] = 0.125
        for y in range(16):
            spread_end[(y // 2) * 4 + z // 2, y * 8 + z] = 0.125
        spread_end[128 + z // 2, 128 + z] = 0.125
        spread_end[256 + z // 2, 248 + z] = 0.125
    rim = np.zeros((256, 256))
    for x in range(8):
        for z in range(4):
            rim[x * 32 + z, x * 4 + z] = 1
            rim[x * 32 + 28 + z, 128 + x * 4 + z] = 1
    made = (
        rim,
        pool_first,
        spread_first,
        pool_second,
        spread_own,
        spread_rim.reshape(256, 1024),
        spread_end,
    )
    return [jnp.asarray(a, BF16) for a in made]


def dot(a, b):
    return jnp.dot(a, b, preferred_element_type=F32)


def dot_lanes(a, b):
    return lax.dot_general(a, b, (((1,), (1,)), ((), ())), preferred_element_type=F32)


def pack_kernel(vol_ref, cot_ref, rim_ref, own_ref, x_ref, low_ref, high_ref, xlow_ref, xhigh_ref):
    gx = lax.axis_index("gx")
    own_ref[0:8, :] = jnp.zeros((8, OWN), F32)
    own_ref[128:136, :] = jnp.zeros((8, OWN), F32)
    for x in range(CX):
        own_ref[4 + 4 * x : 8 + 4 * x, :] = vol_ref[:, x * OWN : (x + 1) * OWN].astype(F32)
    low_ref[0:128, :] = own_ref[0:128, 0:128].astype(BF16)
    high_ref[0:128, :] = own_ref[0:128, OWN - 128 : OWN].astype(BF16)
    blank = jnp.zeros((8, 128), F32)
    low_ref[128:144, :] = jnp.concatenate([own_ref[128:136, 0:128], blank]).astype(BF16)
    high_ref[128:144, :] = jnp.concatenate([own_ref[128:136, OWN - 128 : OWN], blank]).astype(BF16)
    start = pl.multiple_of(112 * (1 - gx), 8)
    face = own_ref[pl.ds(start, 24), :]
    face = jnp.concatenate([face, jnp.zeros((8, OWN), F32)]).astype(BF16)
    x_ref[0:32, :] = face
    xlow_ref[0:32, :] = face[:, 0:128]
    xhigh_ref[0:32, :] = face[:, OWN - 128 : OWN]
    cot = cot_ref[...]
    rims = dot(cot, rim_ref[...])
    low, high = rims[:, 0:128], rims[:, 128:256]
    low_ref[144:208, :] = low.astype(BF16)
    high_ref[144:208, :] = high.astype(BF16)
    first = gx == 0
    xlow_ref[32:96, :] = jnp.where(first, pltpu.roll(low, 100, 1), low).astype(BF16)
    xhigh_ref[32:96, :] = jnp.where(first, pltpu.roll(high, 100, 1), high).astype(BF16)
    wide = cot.astype(F32)
    end = jnp.where(first, pltpu.roll(wide[:, 128:256], 32, 1), wide[:, 0:128]).astype(BF16)
    for part in range(4):
        x_ref[32:48, part * 128 : (part + 1) * 128] = end[part * 16 : (part + 1) * 16, :]


def shifted(tile, period, rows, lane):
    size = tile.shape[1]
    z = lane % period
    along = (
        jnp.where(z == 0, 0.0, pltpu.roll(tile, 1, 1)),
        tile,
        jnp.where(z == period - 1, 0.0, pltpu.roll(tile, size - 1, 1)),
    )
    for dy in range(3):
        for dz in range(3):
            moved = along[dz]
            if dy != 1:
                moved = pltpu.roll(moved, period if dy == 0 else size - period, 1)
            yield (dy * 3 + dz) * rows, moved


def split(values):
    top = values.astype(BF16)
    return jnp.concatenate([top, (values - top.astype(F32)).astype(BF16)], axis=0)


def main_kernel(
    rows_y,
    own_ref,
    cot_ref,
    rx_ref,
    rup_ref,
    rdown_ref,
    rxup_ref,
    rxdown_ref,
    w1_ref,
    w2_ref,
    w3_ref,
    pool_first_ref,
    spread_first_ref,
    pool_second_ref,
    spread_own_ref,
    spread_rim_ref,
    spread_end_ref,
    features_ref,
    act_grad_ref,
    grads_ref,
    vol,
    cols_first,
    pre_first,
    half_first,
    act,
    cols_second,
    act_second,
    spread_up,
    grad,
    grad_own,
    cols_grad,
    half_grad,
):
    gx = lax.axis_index("gx")
    block_y = lax.axis_index("yz")

    vol[...] = jnp.zeros_like(vol)
    vol[pl.ds(2 * gx, 17), :, 0:OWN] = own_ref[...].reshape(17, 8, OWN)
    up = rup_ref[0:144, :].astype(F32)[0:136]
    down = rdown_ref[0:144, :].astype(F32)[0:136]
    vol[pl.ds(2 * gx, 17), :, OWN : OWN + 128] = up.reshape(17, 8, 128)
    vol[pl.ds(2 * gx, 17), :, OWN + 128 : FINE] = down.reshape(17, 8, 128)
    end = pl.ds(16 * (1 - gx), 3)
    vol[end, :, 0:OWN] += rx_ref[0:32, :].astype(F32)[0:24].reshape(3, 8, OWN)
    vol[end, :, OWN : OWN + 128] += rxup_ref[0:32, :].astype(F32)[0:24].reshape(3, 8, 128)
    vol[end, :, OWN + 128 : FINE] += rxdown_ref[0:32, :].astype(F32)[0:24].reshape(3, 8, 128)

    own_up = dot(cot_ref[...], spread_own_ref[...])
    rim = jnp.concatenate([rup_ref[144:208, :], rdown_ref[144:208, :]], axis=1)
    rim_up = dot(rim, spread_rim_ref[...])
    for p in range(8):
        spread_up[p + gx, :, 0:128] = own_up[:, p * 128 : (p + 1) * 128]
        spread_up[p + gx, :, 128:256] = rim_up[:, p * 128 : (p + 1) * 128]
    face = jnp.concatenate([rx_ref[32:48, q * 128 : (q + 1) * 128] for q in range(4)], axis=0)
    face = jnp.concatenate([face, rxup_ref[32:96, :], rxdown_ref[32:96, :]], axis=1)
    spread_up[8 * (1 - gx)] = dot(face, spread_end_ref[...])

    lane_fine = lax.broadcasted_iota(jnp.int32, (16, FINE), 1)
    near = lax.broadcasted_iota(jnp.int32, (16, 128), 1) < 64

    def first_layer(j, carry):
        tile = jnp.concatenate([vol[j], vol[j + 1]], axis=0)
        for row, moved in shifted(tile, CZ, 16, lane_fine):
            edge = jnp.where(near, moved[:, OWN : OWN + 128], moved[:, OWN + 128 : FINE])
            cols_first[j, row : row + 16, 0:OWN] = moved[:, 0:OWN].astype(BF16)
            cols_first[j, row : row + 16, OWN:KEPT] = edge.astype(BF16)
        pre = dot(w1_ref[...], cols_first[j])
        pre_first[j] = pre
        sloped = leaky(pre)
        half_first[j] = split(sloped[0:32] + sloped[32:64])
        return carry

    lax.fori_loop(0, NF, first_layer, 0)

    lane = lax.broadcasted_iota(jnp.int32, (32, COARSE), 1)
    valid = jnp.logical_or(
        lane < MID,
        jnp.logical_or(
            jnp.logical_and(lane < 192, block_y < rows_y - 1),
            jnp.logical_and(lane >= 192, block_y > 0),
        ),
    )
    act[...] = jnp.zeros_like(act)

    def pool_planes(step, carry):
        pooled = dot(half_first[pl.ds(3 * step, 3)].reshape(192, KEPT), pool_first_ref[...])
        for k in range(3):
            whole = pooled[k * 64 : k * 64 + 32] + pooled[k * 64 + 32 : k * 64 + 64]
            kept = jnp.where(valid, whole, 0.0).astype(BF16).astype(F32)
            act[3 * step + k + 1 - gx] = kept
        return carry

    lax.fori_loop(0, NF // 3, pool_planes, 0)

    def columns_second(q, carry):
        for row, moved in shifted(act[q], CZ // 2, 32, lane):
            cols_second[q, row : row + 32, :] = moved.astype(BF16)
        return carry

    lax.fori_loop(0, NF + 1, columns_second, 0)

    grad[...] = jnp.zeros_like(grad)

    def second_layer(k, carry):
        pre = dot(w2_ref[...], cols_second[pl.ds(k, 3)].reshape(864, COARSE))
        act_second[k] = leaky(pre[:, 0:MID])
        rounded = (spread_up[(k + gx) // 2] * leaky_slope(pre)).astype(BF16)
        grad[k + 1 - gx] = rounded.astype(F32)
        return carry

    lax.fori_loop(0, NS, second_layer, 0)

    halves = []
    for p in range(8):
        halves.append(split(act_second[2 * p + gx] + act_second[2 * p + 1 + gx]))
    pooled = dot(jnp.concatenate(halves, axis=1), pool_second_ref[...])
    features_ref[...] = (pooled[0:64] + pooled[64:128]).astype(BF16)

    lane_grad = lax.broadcasted_iota(jnp.int32, (64, COARSE), 1)

    def columns_grad(q, carry):
        for row, moved in shifted(grad[q], CZ // 2, 64, lane_grad):
            cols_grad[q, row : row + 64, :] = moved[:, 0:MID].astype(BF16)
        return carry

    lax.fori_loop(0, NF, columns_grad, 0)

    grad_own[...] = jnp.zeros_like(grad_own)
    for m in range(16):
        grad_own[m + 2] = grad[m + 1][:, 0:MID].astype(BF16)

    for m in range(0, 16, 2):
        cols = jnp.concatenate(
            [
                cols_grad[m : m + 3].reshape(1728, MID),
                cols_grad[m + 1 : m + 4].reshape(1728, MID),
            ],
            axis=1,
        )
        back = dot(w3_ref[...], cols)
        act_grad_ref[:, m * MID : (m + 2) * MID] = back
        half_grad[m] = split(back[:, 0:MID])
        half_grad[m + 1] = split(back[:, MID : 2 * MID])

    total = jnp.zeros((288, 192), F32)
    for q in range(0, 18, 2):
        left = jnp.concatenate(
            [cols_second[q + gx][:, 0:MID], cols_second[q + 1 + gx][:, 0:MID]], axis=1
        )
        right = jnp.concatenate(
            [
                grad_own[q : q + 3].reshape(192, MID),
                grad_own[q + 1 : q + 4].reshape(192, MID),
            ],
            axis=1,
        )
        total = total + dot_lanes(left, right)
    grads_ref[:, 0:192] = total

    def first_part(step, total):
        spread = dot(half_grad[pl.ds(4 * step, 4)].reshape(256, MID), spread_first_ref[...])
        for k in range(4):
            m = 4 * step + k + 2 * gx
            whole = spread[k * 64 : k * 64 + 32] + spread[k * 64 + 32 : k * 64 + 64]
            slope = leaky_slope(pre_first[m][:, 0:OWN])
            back = (jnp.concatenate([whole, whole], axis=0) * slope).astype(BF16)
            total = total + dot_lanes(cols_first[m][:, 0:OWN], back)
        return total

    first = lax.fori_loop(0, 4, first_part, jnp.zeros((144, 64), F32))
    grads_ref[0:144, 192:256] = first
    grads_ref[144:288, 192:256] = jnp.zeros((144, 64), F32)


def unpack_kernel(grads_ref, second_ref, first_ref):
    for dx in range(3):
        second_ref[dx] = grads_ref[:, (2 - dx) * 64 : (3 - dx) * 64]
    both = grads_ref[0:144, 192:256]
    for at in range(9):
        part = both[at * 16 : at * 16 + 16]
        for dx in range(3):
            first_ref[dx * 9 + at] = (
                part[4 * dx : 4 * dx + 4, 0:32] + part[4 * dx + 4 : 4 * dx + 8, 32:64]
            )


def call(kernel, outs, scratch=()):
    return pl.pallas_call(
        kernel,
        out_shape=[jax.ShapeDtypeStruct(shape, dtype) for shape, dtype in outs],
        scratch_shapes=[pltpu.VMEM(shape, dtype) for shape, dtype in scratch],
        compiler_params=pltpu.CompilerParams(vmem_limit_bytes=VMEM_LIMIT),
    )


def on_device_kernels(rows_y, volumes, first_kernel, second_kernel, cotangent):
    rim, pool_first, spread_first, pool_second, spread_own, spread_rim, spread_end = constants()
    cot = cotangent.reshape(64, 256)
    own, x_face, low, high, x_low, x_high = call(
        pack_kernel,
        [
            ((136, OWN), F32),
            ((48, OWN), BF16),
            ((208, 128), BF16),
            ((208, 128), BF16),
            ((96, 128), BF16),
            ((96, 128), BF16),
        ],
    )(volumes.reshape(4, CX * OWN), cot, rim)

    below = [(i, i + 1) for i in range(rows_y - 1)]
    above = [(i + 1, i) for i in range(rows_y - 1)]

    def across(routes):
        return [
            (g * rows_y + a, (1 - g) * rows_y + b) for g in range(2) for a, b in routes
        ]

    got_x_down = lax.ppermute(x_high, ("gx", "yz"), across(below))
    got_x_up = lax.ppermute(x_low, ("gx", "yz"), across(above))
    got_down = lax.ppermute(high, "yz", below)
    got_up = lax.ppermute(low, "yz", above)
    got_x = lax.ppermute(x_face, "gx", [(0, 1), (1, 0)])

    by_offset = first_kernel.transpose(0, 3, 4, 2, 1)
    padded = [jnp.pad(by_offset, ((0, 0), (0, 0), (0, 0), (k, 1 - k), (0, 0))) for k in range(2)]
    w1 = jnp.stack(padded).reshape(64, 144)
    w2 = second_kernel.transpose(0, 2, 3, 4, 1).reshape(64, 864)
    w3 = jnp.flip(second_kernel, (2, 3, 4)).transpose(1, 2, 3, 4, 0).reshape(32, 1728)

    features, act_grad, grads = call(
        functools.partial(main_kernel, rows_y),
        [((64, 256), BF16), ((32, 2048), F32), ((288, 256), F32)],
        [
            ((19, 8, FINE), F32),
            ((NF, 144, KEPT), BF16),
            ((NF, 64, KEPT), F32),
            ((NF, 64, KEPT), BF16),
            ((NF + 1, 32, COARSE), F32),
            ((NF + 1, 288, COARSE), BF16),
            ((NS, 64, MID), F32),
            ((9, 64, COARSE), F32),
            ((NF, 64, COARSE), F32),
            ((20, 64, MID), BF16),
            ((NF, 576, MID), BF16),
            ((16, 64, MID), BF16),
        ],
    )(
        own,
        cot,
        got_x,
        got_up,
        got_down,
        got_x_up,
        got_x_down,
        w1,
        w2,
        w3,
        pool_first,
        spread_first,
        pool_second,
        spread_own,
        spread_rim,
        spread_end,
    )
    grads = lax.psum(grads, ("dp", "gx", "yz"))
    second, first = call(unpack_kernel, [((3, 288, 64), F32), ((27, 4, 32), F32)])(grads)
    return (
        features.reshape(1, 64, 1, 1, 256),
        act_grad.reshape(1, 32, 1, 1, 2048),
        first.reshape(3, 3, 3, 4, 32).transpose(4, 3, 0, 1, 2),
        second.reshape(3, 3, 3, 32, 64).transpose(4, 3, 0, 1, 2),
    )


def solution(mesh):
    placed = (P("dp", None, "gx", "yz", None), P(), P(), P("dp", None, "gx", "yz", None))
    rows_y = min(4, mesh.shape["yz"])
    rows_z = mesh.shape["yz"] // rows_y
    if rows_z == 1 and mesh.shape["gx"] == 2:
        body = functools.partial(on_device_kernels, rows_y)
    else:
        body = functools.partial(on_device_plain, rows_y, rows_z)
    return jax.shard_map(
        body,
        mesh=mesh,
        in_specs=placed,
        out_specs=(P("dp", None, "gx", "yz", None), P("dp", None, "gx", "yz", None), P(), P()),
        check_vma=False,
    )
```

```python
import functools

import jax
import jax.numpy as jnp
import numpy as np
from jax import lax
from jax.experimental import pallas as pl
from jax.experimental.pallas import tpu as pltpu
from jax.sharding import PartitionSpec as P

CX = 32
CY = 32
CZ = 16
SLOPE = 0.3
F32 = jnp.float32
BF16 = jnp.bfloat16
VMEM_LIMIT = 56 * 1024 * 1024


def leaky(values):
    return jnp.where(values > 0, values, SLOPE * values)


def leaky_slope(values):
    return jnp.where(values > 0, jnp.float32(1.0), jnp.float32(SLOPE))


def convolve_valid(padded, kernel):
    return lax.conv_general_dilated(
        padded,
        kernel,
        (1, 1, 1),
        "VALID",
        dimension_numbers=("NCDHW", "OIDHW", "NCDHW"),
        preferred_element_type=F32,
    )


def kernel_grad(padded, grad):
    result = lax.conv_general_dilated(
        padded,
        grad,
        (1, 1, 1),
        "VALID",
        dimension_numbers=("CNDHW", "IODHW", "NCDHW"),
        preferred_element_type=F32,
    )
    return result.transpose(1, 0, 2, 3, 4)


def average_pool(values):
    bat, chan, xs, ys, zs = values.shape
    return values.reshape(bat, chan, xs // 2, 2, ys // 2, 2, zs // 2, 2).mean(axis=(3, 5, 7))


def spread_back(values):
    bat, chan, xs, ys, zs = values.shape
    grown = jnp.broadcast_to(
        values[:, :, :, None, :, None, :, None], (bat, chan, xs, 2, ys, 2, zs, 2)
    )
    return grown.reshape(bat, chan, 2 * xs, 2 * ys, 2 * zs) * 0.125


def unflatten(values, factor):
    return values[:, :, 0, 0].reshape(
        values.shape[0], values.shape[1], CX // factor, CY // factor, CZ // factor
    )


def flatten(values):
    return values.reshape(values.shape[0], values.shape[1], 1, 1, -1)


def extend_along(values, dim, axis, routes):
    size = values.shape[dim]
    first = lax.slice_in_dim(values, 0, 1, axis=dim)
    last = lax.slice_in_dim(values, size - 1, size, axis=dim)
    before = lax.ppermute(last, axis, routes)
    after = lax.ppermute(first, axis, [(b, a) for a, b in routes])
    return jnp.concatenate([before, values, after], axis=dim)


def extend(values, rows_y, rows_z):
    planes = lax.axis_size("gx")
    count = rows_y * rows_z
    values = extend_along(values, 2, "gx", [(i, i + 1) for i in range(planes - 1)])
    values = extend_along(values, 3, "yz", [(i, i + rows_z) for i in range(count - rows_z)])
    return extend_along(
        values, 4, "yz", [(i, i + 1) for i in range(count - 1) if (i + 1) % rows_z]
    )


def on_device_plain(rows_y, rows_z, volumes, first_kernel, second_kernel, cotangent):
    upstream = unflatten(cotangent, 4)
    padded_in = extend(unflatten(volumes, 1), rows_y, rows_z)
    pre_first = convolve_valid(padded_in, first_kernel)
    act_first = average_pool(leaky(pre_first)).astype(BF16)
    padded_mid = extend(act_first, rows_y, rows_z)
    pre_second = convolve_valid(padded_mid, second_kernel)
    features = average_pool(leaky(pre_second)).astype(BF16)
    grad_second = (spread_back(upstream.astype(F32)) * leaky_slope(pre_second)).astype(BF16)
    flipped = jnp.flip(second_kernel, (2, 3, 4)).transpose(1, 0, 2, 3, 4)
    act_grad = convolve_valid(extend(grad_second, rows_y, rows_z), flipped)
    grad_first = (spread_back(act_grad) * leaky_slope(pre_first)).astype(BF16)
    first_grad, second_grad = lax.psum(
        (kernel_grad(padded_in, grad_first), kernel_grad(padded_mid, grad_second)),
        ("dp", "gx", "yz"),
    )
    return (flatten(features), flatten(act_grad), first_grad, second_grad)


FINE = 48 * CZ
KEPT = 40 * CZ
OWN = CY * CZ
COARSE = 256
MID = (CY // 2) * (CZ // 2)
NF = 18
NS = 17


def constants():
    kept = np.arange(KEPT)
    row = np.where(kept < OWN + 64, kept // CZ, kept // CZ - 40)
    lane = ((row // 2) * 8 + (kept % CZ) // 2) % COARSE
    pool_first = (lane[:, None] == np.arange(COARSE)[None]) * 0.125
    spread_first = pool_first[:OWN, :MID].T
    mid = np.arange(8 * MID)
    plane, y, z = mid // MID, (mid // 8) % 16, mid % 8
    pooled = plane * 32 + (y // 2) * 4 + z // 2
    pool_second = (pooled[:, None] == np.arange(256)[None]) * 0.125
    spread_own = pool_second.T
    spread_rim = np.zeros((256, 8, 128))
    spread_end = np.zeros((384, 256))
    for z in range(8):
        for p in range(8):
            spread_rim[p * 4 + z // 2, p, z] = 0.125
            spread_rim[128 + p * 4 + z // 2, p, 120 + z] = 0.125
        for y in range(16):
            spread_end[(y // 2) * 4 + z // 2, y * 8 + z] = 0.125
        spread_end[128 + z // 2, 128 + z] = 0.125
        spread_end[256 + z // 2, 248 + z] = 0.125
    rim = np.zeros((256, 256))
    for x in range(8):
        for z in range(4):
            rim[x * 32 + z, x * 4 + z] = 1
            rim[x * 32 + 28 + z, 128 + x * 4 + z] = 1
    made = (
        rim,
        pool_first,
        spread_first,
        pool_second,
        spread_own,
        spread_rim.reshape(256, 1024),
        spread_end,
    )
    return [jnp.asarray(a, BF16) for a in made]


def dot(a, b):
    return jnp.dot(a, b, preferred_element_type=F32)


def dot_lanes(a, b):
    return lax.dot_general(a, b, (((1,), (1,)), ((), ())), preferred_element_type=F32)


def pack_kernel(vol_ref, cot_ref, rim_ref, own_ref, x_ref, low_ref, high_ref, xlow_ref, xhigh_ref):
    gx = lax.axis_index("gx")
    own_ref[0:8, :] = jnp.zeros((8, OWN), F32)
    own_ref[128:136, :] = jnp.zeros((8, OWN), F32)
    for x in range(CX):
        own_ref[4 + 4 * x : 8 + 4 * x, :] = vol_ref[:, x * OWN : (x + 1) * OWN].astype(F32)
    low_ref[0:128, :] = own_ref[0:128, 0:128].astype(BF16)
    high_ref[0:128, :] = own_ref[0:128, OWN - 128 : OWN].astype(BF16)
    blank = jnp.zeros((8, 128), F32)
    low_ref[128:144, :] = jnp.concatenate([own_ref[128:136, 0:128], blank]).astype(BF16)
    high_ref[128:144, :] = jnp.concatenate([own_ref[128:136, OWN - 128 : OWN], blank]).astype(BF16)
    start = pl.multiple_of(112 * (1 - gx), 8)
    face = own_ref[pl.ds(start, 24), :]
    face = jnp.concatenate([face, jnp.zeros((8, OWN), F32)]).astype(BF16)
    x_ref[0:32, :] = face
    xlow_ref[0:32, :] = face[:, 0:128]
    xhigh_ref[0:32, :] = face[:, OWN - 128 : OWN]
    cot = cot_ref[...]
    rims = dot(cot, rim_ref[...])
    low, high = rims[:, 0:128], rims[:, 128:256]
    low_ref[144:208, :] = low.astype(BF16)
    high_ref[144:208, :] = high.astype(BF16)
    first = gx == 0
    xlow_ref[32:96, :] = jnp.where(first, pltpu.roll(low, 100, 1), low).astype(BF16)
    xhigh_ref[32:96, :] = jnp.where(first, pltpu.roll(high, 100, 1), high).astype(BF16)
    wide = cot.astype(F32)
    end = jnp.where(first, pltpu.roll(wide[:, 128:256], 32, 1), wide[:, 0:128]).astype(BF16)
    for part in range(4):
        x_ref[32:48, part * 128 : (part + 1) * 128] = end[part * 16 : (part + 1) * 16, :]


def shifted(tile, period, rows, lane):
    size = tile.shape[1]
    z = lane % period
    along = (
        jnp.where(z == 0, 0.0, pltpu.roll(tile, 1, 1)),
        tile,
        jnp.where(z == period - 1, 0.0, pltpu.roll(tile, size - 1, 1)),
    )
    for dy in range(3):
        for dz in range(3):
            moved = along[dz]
            if dy != 1:
                moved = pltpu.roll(moved, period if dy == 0 else size - period, 1)
            yield (dy * 3 + dz) * rows, moved


def split(values):
    top = values.astype(BF16)
    return jnp.concatenate([top, (values - top.astype(F32)).astype(BF16)], axis=0)


def main_kernel(
    rows_y,
    own_ref,
    cot_ref,
    rx_ref,
    rup_ref,
    rdown_ref,
    rxup_ref,
    rxdown_ref,
    w1_ref,
    w2_ref,
    w3_ref,
    pool_first_ref,
    spread_first_ref,
    pool_second_ref,
    spread_own_ref,
    spread_rim_ref,
    spread_end_ref,
    features_ref,
    act_grad_ref,
    kept_ref,
    sent_ref,
    vol,
    cols_first,
    pre_first,
    half_first,
    act,
    cols_second,
    act_second,
    spread_up,
    grad,
    grad_own,
    cols_grad,
    half_grad,
    grads_ref,
):
    gx = lax.axis_index("gx")
    block_y = lax.axis_index("yz")

    vol[...] = jnp.zeros_like(vol)
    vol[pl.ds(2 * gx, 17), :, 0:OWN] = own_ref[...].reshape(17, 8, OWN)
    up = rup_ref[0:144, :].astype(F32)[0:136]
    down = rdown_ref[0:144, :].astype(F32)[0:136]
    vol[pl.ds(2 * gx, 17), :, OWN : OWN + 128] = up.reshape(17, 8, 128)
    vol[pl.ds(2 * gx, 17), :, OWN + 128 : FINE] = down.reshape(17, 8, 128)
    end = pl.ds(16 * (1 - gx), 3)
    vol[end, :, 0:OWN] += rx_ref[0:32, :].astype(F32)[0:24].reshape(3, 8, OWN)
    vol[end, :, OWN : OWN + 128] += rxup_ref[0:32, :].astype(F32)[0:24].reshape(3, 8, 128)
    vol[end, :, OWN + 128 : FINE] += rxdown_ref[0:32, :].astype(F32)[0:24].reshape(3, 8, 128)

    own_up = dot(cot_ref[...], spread_own_ref[...])
    rim = jnp.concatenate([rup_ref[144:208, :], rdown_ref[144:208, :]], axis=1)
    rim_up = dot(rim, spread_rim_ref[...])
    for p in range(8):
        spread_up[p + gx, :, 0:128] = own_up[:, p * 128 : (p + 1) * 128]
        spread_up[p + gx, :, 128:256] = rim_up[:, p * 128 : (p + 1) * 128]
    face = jnp.concatenate([rx_ref[32:48, q * 128 : (q + 1) * 128] for q in range(4)], axis=0)
    face = jnp.concatenate([face, rxup_ref[32:96, :], rxdown_ref[32:96, :]], axis=1)
    spread_up[8 * (1 - gx)] = dot(face, spread_end_ref[...])

    lane_fine = lax.broadcasted_iota(jnp.int32, (16, FINE), 1)
    near = lax.broadcasted_iota(jnp.int32, (16, 128), 1) < 64

    def first_layer(j, carry):
        tile = jnp.concatenate([vol[j], vol[j + 1]], axis=0)
        for row, moved in shifted(tile, CZ, 16, lane_fine):
            edge = jnp.where(near, moved[:, OWN : OWN + 128], moved[:, OWN + 128 : FINE])
            cols_first[j, row : row + 16, 0:OWN] = moved[:, 0:OWN].astype(BF16)
            cols_first[j, row : row + 16, OWN:KEPT] = edge.astype(BF16)
        pre = dot(w1_ref[...], cols_first[j])
        pre_first[j] = pre
        sloped = leaky(pre)
        half_first[j] = split(sloped[0:32] + sloped[32:64])
        return carry

    lax.fori_loop(0, NF, first_layer, 0)

    lane = lax.broadcasted_iota(jnp.int32, (32, COARSE), 1)
    valid = jnp.logical_or(
        lane < MID,
        jnp.logical_or(
            jnp.logical_and(lane < 192, block_y < rows_y - 1),
            jnp.logical_and(lane >= 192, block_y > 0),
        ),
    )
    act[...] = jnp.zeros_like(act)

    def pool_planes(step, carry):
        pooled = dot(half_first[pl.ds(3 * step, 3)].reshape(192, KEPT), pool_first_ref[...])
        for k in range(3):
            whole = pooled[k * 64 : k * 64 + 32] + pooled[k * 64 + 32 : k * 64 + 64]
            kept = jnp.where(valid, whole, 0.0).astype(BF16).astype(F32)
            act[3 * step + k + 1 - gx] = kept
        return carry

    lax.fori_loop(0, NF // 3, pool_planes, 0)

    def columns_second(q, carry):
        for row, moved in shifted(act[q], CZ // 2, 32, lane):
            cols_second[q, row : row + 32, :] = moved.astype(BF16)
        return carry

    lax.fori_loop(0, NF + 1, columns_second, 0)

    grad[...] = jnp.zeros_like(grad)

    def second_layer(k, carry):
        pre = dot(w2_ref[...], cols_second[pl.ds(k, 3)].reshape(864, COARSE))
        act_second[k] = leaky(pre[:, 0:MID])
        rounded = (spread_up[(k + gx) // 2] * leaky_slope(pre)).astype(BF16)
        grad[k + 1 - gx] = rounded.astype(F32)
        return carry

    lax.fori_loop(0, NS, second_layer, 0)

    halves = []
    for p in range(8):
        halves.append(split(act_second[2 * p + gx] + act_second[2 * p + 1 + gx]))
    pooled = dot(jnp.concatenate(halves, axis=1), pool_second_ref[...])
    features_ref[...] = (pooled[0:64] + pooled[64:128]).astype(BF16)

    lane_grad = lax.broadcasted_iota(jnp.int32, (64, COARSE), 1)

    def columns_grad(q, carry):
        for row, moved in shifted(grad[q], CZ // 2, 64, lane_grad):
            cols_grad[q, row : row + 64, :] = moved[:, 0:MID].astype(BF16)
        return carry

    lax.fori_loop(0, NF, columns_grad, 0)

    grad_own[...] = jnp.zeros_like(grad_own)
    for m in range(16):
        grad_own[m + 2] = grad[m + 1][:, 0:MID].astype(BF16)

    for m in range(0, 16, 2):
        cols = jnp.concatenate(
            [
                cols_grad[m : m + 3].reshape(1728, MID),
                cols_grad[m + 1 : m + 4].reshape(1728, MID),
            ],
            axis=1,
        )
        back = dot(w3_ref[...], cols)
        act_grad_ref[:, m * MID : (m + 2) * MID] = back
        half_grad[m] = split(back[:, 0:MID])
        half_grad[m + 1] = split(back[:, MID : 2 * MID])

    total = jnp.zeros((288, 192), F32)
    for q in range(0, 18, 2):
        left = jnp.concatenate(
            [cols_second[q + gx][:, 0:MID], cols_second[q + 1 + gx][:, 0:MID]], axis=1
        )
        right = jnp.concatenate(
            [
                grad_own[q : q + 3].reshape(192, MID),
                grad_own[q + 1 : q + 4].reshape(192, MID),
            ],
            axis=1,
        )
        total = total + dot_lanes(left, right)
    grads_ref[:, 0:192] = total

    def first_part(step, total):
        spread = dot(half_grad[pl.ds(4 * step, 4)].reshape(256, MID), spread_first_ref[...])
        for k in range(4):
            m = 4 * step + k + 2 * gx
            whole = spread[k * 64 : k * 64 + 32] + spread[k * 64 + 32 : k * 64 + 64]
            slope = leaky_slope(pre_first[m][:, 0:OWN])
            back = (jnp.concatenate([whole, whole], axis=0) * slope).astype(BF16)
            total = total + dot_lanes(cols_first[m][:, 0:OWN], back)
        return total

    first = lax.fori_loop(0, 4, first_part, jnp.zeros((144, 64), F32))
    grads_ref[0:144, 192:256] = first
    grads_ref[144:288, 192:256] = jnp.zeros((144, 64), F32)
    kept_ref[...] = grads_ref[pl.ds(pl.multiple_of(144 * gx, 8), 144), :]
    sent_ref[...] = grads_ref[pl.ds(pl.multiple_of(144 * (1 - gx), 8), 144), :]


def unpack_kernel(mine_ref, other_ref, second_ref, first_ref):
    first = lax.axis_index("gx") == 0
    lower = jnp.where(first, mine_ref[...], other_ref[...])
    upper = jnp.where(first, other_ref[...], mine_ref[...])
    for dx in range(3):
        second_ref[dx, 0:144] = lower[:, (2 - dx) * 64 : (3 - dx) * 64]
        second_ref[dx, 144:288] = upper[:, (2 - dx) * 64 : (3 - dx) * 64]
    both = lower[:, 192:256]
    for at in range(9):
        part = both[at * 16 : at * 16 + 16]
        for dx in range(3):
            first_ref[dx * 9 + at] = (
                part[4 * dx : 4 * dx + 4, 0:32] + part[4 * dx + 4 : 4 * dx + 8, 32:64]
            )


def call(kernel, outs, scratch=()):
    return pl.pallas_call(
        kernel,
        out_shape=[jax.ShapeDtypeStruct(shape, dtype) for shape, dtype in outs],
        scratch_shapes=[pltpu.VMEM(shape, dtype) for shape, dtype in scratch],
        compiler_params=pltpu.CompilerParams(vmem_limit_bytes=VMEM_LIMIT),
    )


def sum_of_group(part, axis):
    count = lax.axis_size(axis)
    terms = [part] + [
        lax.ppermute(part, axis, [(i, i ^ k) for i in range(count)]) for k in range(1, count)
    ]
    terms = [term.astype(F32) for term in terms]
    while len(terms) > 1:
        terms = [terms[i] + terms[i + 1] for i in range(0, len(terms), 2)]
    return terms[0]


def on_device_kernels(rows_y, volumes, first_kernel, second_kernel, cotangent):
    rim, pool_first, spread_first, pool_second, spread_own, spread_rim, spread_end = constants()
    cot = cotangent.reshape(64, 256)
    own, x_face, low, high, x_low, x_high = call(
        pack_kernel,
        [
            ((136, OWN), F32),
            ((48, OWN), BF16),
            ((208, 128), BF16),
            ((208, 128), BF16),
            ((96, 128), BF16),
            ((96, 128), BF16),
        ],
    )(volumes.reshape(4, CX * OWN), cot, rim)

    below = [(i, i + 1) for i in range(rows_y - 1)]
    above = [(i + 1, i) for i in range(rows_y - 1)]

    def across(routes):
        return [
            (g * rows_y + a, (1 - g) * rows_y + b) for g in range(2) for a, b in routes
        ]

    got_x_down = lax.ppermute(x_high, ("gx", "yz"), across(below))
    got_x_up = lax.ppermute(x_low, ("gx", "yz"), across(above))
    got_down = lax.ppermute(high, "yz", below)
    got_up = lax.ppermute(low, "yz", above)
    got_x = lax.ppermute(x_face, "gx", [(0, 1), (1, 0)])

    by_offset = first_kernel.transpose(0, 3, 4, 2, 1)
    padded = [jnp.pad(by_offset, ((0, 0), (0, 0), (0, 0), (k, 1 - k), (0, 0))) for k in range(2)]
    w1 = jnp.stack(padded).reshape(64, 144)
    w2 = second_kernel.transpose(0, 2, 3, 4, 1).reshape(64, 864)
    w3 = jnp.flip(second_kernel, (2, 3, 4)).transpose(1, 2, 3, 4, 0).reshape(32, 1728)

    features, act_grad, kept, sent = call(
        functools.partial(main_kernel, rows_y),
        [((64, 256), BF16), ((32, 2048), F32), ((144, 256), F32), ((144, 256), F32)],
        [
            ((19, 8, FINE), F32),
            ((NF, 144, KEPT), BF16),
            ((NF, 64, KEPT), F32),
            ((NF, 64, KEPT), BF16),
            ((NF + 1, 32, COARSE), F32),
            ((NF + 1, 288, COARSE), BF16),
            ((NS, 64, MID), F32),
            ((9, 64, COARSE), F32),
            ((NF, 64, COARSE), F32),
            ((20, 64, MID), BF16),
            ((NF, 576, MID), BF16),
            ((16, 64, MID), BF16),
            ((288, 256), F32),
        ],
    )(
        own,
        cot,
        got_x,
        got_up,
        got_down,
        got_x_up,
        got_x_down,
        w1,
        w2,
        w3,
        pool_first,
        spread_first,
        pool_second,
        spread_own,
        spread_rim,
        spread_end,
    )
    swap = [(0, 1), (1, 0)]
    part = (kept + lax.ppermute(sent, "gx", swap)).astype(BF16)
    part = sum_of_group(part, "dp").astype(BF16)
    mine = sum_of_group(part, "yz")
    other = lax.ppermute(mine, "gx", swap)
    second, first = call(unpack_kernel, [((3, 288, 64), F32), ((27, 4, 32), F32)])(mine, other)
    return (
        features.reshape(1, 64, 1, 1, 256),
        act_grad.reshape(1, 32, 1, 1, 2048),
        first.reshape(3, 3, 3, 4, 32).transpose(4, 3, 0, 1, 2),
        second.reshape(3, 3, 3, 32, 64).transpose(4, 3, 0, 1, 2),
    )


def solution(mesh):
    placed = (P("dp", None, "gx", "yz", None), P(), P(), P("dp", None, "gx", "yz", None))
    rows_y = min(4, mesh.shape["yz"])
    rows_z = mesh.shape["yz"] // rows_y
    if rows_z == 1 and rows_y in (2, 4) and mesh.shape["gx"] == 2 and mesh.shape["dp"] in (1, 2, 4):
        body = functools.partial(on_device_kernels, rows_y)
    else:
        body = functools.partial(on_device_plain, rows_y, rows_z)
    return jax.shard_map(
        body,
        mesh=mesh,
        in_specs=placed,
        out_specs=(P("dp", None, "gx", "yz", None), P("dp", None, "gx", "yz", None), P(), P()),
        check_vma=False,
    )
```

```python
import functools

import jax
import jax.numpy as jnp
import numpy as np
from jax import lax
from jax.experimental import pallas as pl
from jax.experimental.pallas import tpu as pltpu
from jax.sharding import PartitionSpec as P

CX = 32
CY = 32
CZ = 16
SLOPE = 0.3
F32 = jnp.float32
BF16 = jnp.bfloat16
VMEM_LIMIT = 56 * 1024 * 1024


def leaky(values):
    return jnp.where(values > 0, values, SLOPE * values)


def leaky_slope(values):
    return jnp.where(values > 0, jnp.float32(1.0), jnp.float32(SLOPE))


def convolve_valid(padded, kernel):
    return lax.conv_general_dilated(
        padded,
        kernel,
        (1, 1, 1),
        "VALID",
        dimension_numbers=("NCDHW", "OIDHW", "NCDHW"),
        preferred_element_type=F32,
    )


def kernel_grad(padded, grad):
    result = lax.conv_general_dilated(
        padded,
        grad,
        (1, 1, 1),
        "VALID",
        dimension_numbers=("CNDHW", "IODHW", "NCDHW"),
        preferred_element_type=F32,
    )
    return result.transpose(1, 0, 2, 3, 4)


def average_pool(values):
    bat, chan, xs, ys, zs = values.shape
    return values.reshape(bat, chan, xs // 2, 2, ys // 2, 2, zs // 2, 2).mean(axis=(3, 5, 7))


def spread_back(values):
    bat, chan, xs, ys, zs = values.shape
    grown = jnp.broadcast_to(
        values[:, :, :, None, :, None, :, None], (bat, chan, xs, 2, ys, 2, zs, 2)
    )
    return grown.reshape(bat, chan, 2 * xs, 2 * ys, 2 * zs) * 0.125


def unflatten(values, factor):
    return values[:, :, 0, 0].reshape(
        values.shape[0], values.shape[1], CX // factor, CY // factor, CZ // factor
    )


def flatten(values):
    return values.reshape(values.shape[0], values.shape[1], 1, 1, -1)


def extend_along(values, dim, axis, routes):
    size = values.shape[dim]
    first = lax.slice_in_dim(values, 0, 1, axis=dim)
    last = lax.slice_in_dim(values, size - 1, size, axis=dim)
    before = lax.ppermute(last, axis, routes)
    after = lax.ppermute(first, axis, [(b, a) for a, b in routes])
    return jnp.concatenate([before, values, after], axis=dim)


def extend(values, rows_y, rows_z):
    planes = lax.axis_size("gx")
    count = rows_y * rows_z
    values = extend_along(values, 2, "gx", [(i, i + 1) for i in range(planes - 1)])
    values = extend_along(values, 3, "yz", [(i, i + rows_z) for i in range(count - rows_z)])
    return extend_along(
        values, 4, "yz", [(i, i + 1) for i in range(count - 1) if (i + 1) % rows_z]
    )


def on_device_plain(rows_y, rows_z, volumes, first_kernel, second_kernel, cotangent):
    upstream = unflatten(cotangent, 4)
    padded_in = extend(unflatten(volumes, 1), rows_y, rows_z)
    pre_first = convolve_valid(padded_in, first_kernel)
    act_first = average_pool(leaky(pre_first)).astype(BF16)
    padded_mid = extend(act_first, rows_y, rows_z)
    pre_second = convolve_valid(padded_mid, second_kernel)
    features = average_pool(leaky(pre_second)).astype(BF16)
    grad_second = (spread_back(upstream.astype(F32)) * leaky_slope(pre_second)).astype(BF16)
    flipped = jnp.flip(second_kernel, (2, 3, 4)).transpose(1, 0, 2, 3, 4)
    act_grad = convolve_valid(extend(grad_second, rows_y, rows_z), flipped)
    grad_first = (spread_back(act_grad) * leaky_slope(pre_first)).astype(BF16)
    first_grad, second_grad = lax.psum(
        (kernel_grad(padded_in, grad_first), kernel_grad(padded_mid, grad_second)),
        ("dp", "gx", "yz"),
    )
    return (flatten(features), flatten(act_grad), first_grad, second_grad)


FINE = 48 * CZ
KEPT = 40 * CZ
OWN = CY * CZ
COARSE = 256
MID = (CY // 2) * (CZ // 2)
NF = 18
NS = 17


def constants():
    kept = np.arange(KEPT)
    row = np.where(kept < OWN + 64, kept // CZ, kept // CZ - 40)
    lane = ((row // 2) * 8 + (kept % CZ) // 2) % COARSE
    into = lane[:, None] == np.arange(COARSE)[None]
    corner = (row % 2 == 0) & (kept % 2 == 0)
    pool_first = into * corner[:, None]
    spread_first = into[:OWN, :MID].T * 0.125
    mid = np.arange(8 * MID)
    plane, y, z = mid // MID, (mid // 8) % 16, mid % 8
    pooled = plane * 32 + (y // 2) * 4 + z // 2
    into = pooled[:, None] == np.arange(256)[None]
    pool_second = into * ((y % 2 == 0) & (z % 2 == 0))[:, None]
    spread_own = into.T * 0.125
    spread_rim = np.zeros((256, 8, 128))
    spread_end = np.zeros((384, 256))
    for z in range(8):
        for p in range(8):
            spread_rim[p * 4 + z // 2, p, z] = 0.125
            spread_rim[128 + p * 4 + z // 2, p, 120 + z] = 0.125
        for y in range(16):
            spread_end[(y // 2) * 4 + z // 2, y * 8 + z] = 0.125
        spread_end[128 + z // 2, 128 + z] = 0.125
        spread_end[256 + z // 2, 248 + z] = 0.125
    rim = np.zeros((256, 256))
    for x in range(8):
        for z in range(4):
            rim[x * 32 + z, x * 4 + z] = 1
            rim[x * 32 + 28 + z, 128 + x * 4 + z] = 1
    made = (
        rim,
        pool_first,
        spread_first,
        pool_second,
        spread_own,
        spread_rim.reshape(256, 1024),
        spread_end,
    )
    return [jnp.asarray(a, BF16) for a in made]


def dot(a, b):
    return jnp.dot(a, b, preferred_element_type=F32)


def dot_lanes(a, b):
    return lax.dot_general(a, b, (((1,), (1,)), ((), ())), preferred_element_type=F32)


def pack_kernel(vol_ref, cot_ref, rim_ref, own_ref, x_ref, low_ref, high_ref, xlow_ref, xhigh_ref):
    gx = lax.axis_index("gx")
    own_ref[0:8, :] = jnp.zeros((8, OWN), F32)
    own_ref[128:136, :] = jnp.zeros((8, OWN), F32)
    for x in range(CX):
        own_ref[4 + 4 * x : 8 + 4 * x, :] = vol_ref[:, x * OWN : (x + 1) * OWN].astype(F32)
    low_ref[0:128, :] = own_ref[0:128, 0:128].astype(BF16)
    high_ref[0:128, :] = own_ref[0:128, OWN - 128 : OWN].astype(BF16)
    blank = jnp.zeros((8, 128), F32)
    low_ref[128:144, :] = jnp.concatenate([own_ref[128:136, 0:128], blank]).astype(BF16)
    high_ref[128:144, :] = jnp.concatenate([own_ref[128:136, OWN - 128 : OWN], blank]).astype(BF16)
    start = pl.multiple_of(112 * (1 - gx), 8)
    face = own_ref[pl.ds(start, 24), :]
    face = jnp.concatenate([face, jnp.zeros((8, OWN), F32)]).astype(BF16)
    x_ref[0:32, :] = face
    xlow_ref[0:32, :] = face[:, 0:128]
    xhigh_ref[0:32, :] = face[:, OWN - 128 : OWN]
    cot = cot_ref[...]
    rims = dot(cot, rim_ref[...])
    low, high = rims[:, 0:128], rims[:, 128:256]
    low_ref[144:208, :] = low.astype(BF16)
    high_ref[144:208, :] = high.astype(BF16)
    first = gx == 0
    xlow_ref[32:96, :] = jnp.where(first, pltpu.roll(low, 100, 1), low).astype(BF16)
    xhigh_ref[32:96, :] = jnp.where(first, pltpu.roll(high, 100, 1), high).astype(BF16)
    wide = cot.astype(F32)
    end = jnp.where(first, pltpu.roll(wide[:, 128:256], 32, 1), wide[:, 0:128]).astype(BF16)
    for part in range(4):
        x_ref[32:48, part * 128 : (part + 1) * 128] = end[part * 16 : (part + 1) * 16, :]


def shifted(tile, period, lane):
    size = tile.shape[1]
    z = lane % period
    along = (
        jnp.where(z == 0, 0.0, pltpu.roll(tile, 1, 1)),
        tile,
        jnp.where(z == period - 1, 0.0, pltpu.roll(tile, size - 1, 1)),
    )
    return [
        pltpu.roll(moved, shift, 1) if shift else moved
        for shift in (period, 0, size - period)
        for moved in along
    ]


def pooled(values, period):
    size = values.shape[1]
    values = values + pltpu.roll(values, size - 1, 1)
    values = values + pltpu.roll(values, size - period, 1)
    return (values * 0.125).astype(BF16)


def split(values):
    top = values.astype(BF16)
    return jnp.concatenate([top, (values - top.astype(F32)).astype(BF16)], axis=0)


def main_kernel(
    rows_y,
    own_ref,
    cot_ref,
    rx_ref,
    rup_ref,
    rdown_ref,
    rxup_ref,
    rxdown_ref,
    k1_ref,
    k2_ref,
    pool_first_ref,
    spread_first_ref,
    pool_second_ref,
    spread_own_ref,
    spread_rim_ref,
    spread_end_ref,
    features_ref,
    act_grad_ref,
    kept_ref,
    sent_ref,
    w1_rows,
    vol,
    cols_first,
    pre_first,
    pooled_first,
    cols_second,
    act_second,
    spread_up,
    grad_own,
    cols_grad,
    half_grad,
    grads_ref,
):
    gx = lax.axis_index("gx")
    block_y = lax.axis_index("yz")

    k2 = k2_ref[...].astype(F32)
    w2 = k2.T.astype(BF16)
    w3 = jnp.concatenate([k2[32 * n : 32 * n + 32] for n in range(26, -1, -1)], axis=1)
    w3 = w3.astype(BF16)
    w1_rows[...] = jnp.zeros_like(w1_rows)
    for dx in range(3):
        for at in range(9):
            block = k1_ref[dx * 9 + at].astype(F32)
            for k in range(2):
                row = at * 16 + 4 * (dx + k)
                w1_rows[row : row + 4, 32 * k : 32 * k + 32] = block
    w1 = w1_rows[...].T.astype(BF16)

    vol[...] = jnp.zeros_like(vol)
    vol[pl.ds(2 * gx, 17), :, 0:OWN] = own_ref[...].reshape(17, 8, OWN)
    up = rup_ref[0:144, :].astype(F32)[0:136]
    down = rdown_ref[0:144, :].astype(F32)[0:136]
    vol[pl.ds(2 * gx, 17), :, OWN : OWN + 128] = up.reshape(17, 8, 128)
    vol[pl.ds(2 * gx, 17), :, OWN + 128 : FINE] = down.reshape(17, 8, 128)
    end = pl.ds(16 * (1 - gx), 3)
    vol[end, :, 0:OWN] += rx_ref[0:32, :].astype(F32)[0:24].reshape(3, 8, OWN)
    vol[end, :, OWN : OWN + 128] += rxup_ref[0:32, :].astype(F32)[0:24].reshape(3, 8, 128)
    vol[end, :, OWN + 128 : FINE] += rxdown_ref[0:32, :].astype(F32)[0:24].reshape(3, 8, 128)

    own_up = dot(cot_ref[...], spread_own_ref[...])
    rim = jnp.concatenate([rup_ref[144:208, :], rdown_ref[144:208, :]], axis=1)
    rim_up = dot(rim, spread_rim_ref[...])
    for p in range(8):
        spread_up[p + gx, :, 0:128] = own_up[:, p * 128 : (p + 1) * 128]
        spread_up[p + gx, :, 128:256] = rim_up[:, p * 128 : (p + 1) * 128]
    face = jnp.concatenate([rx_ref[32:48, q * 128 : (q + 1) * 128] for q in range(4)], axis=0)
    face = jnp.concatenate([face, rxup_ref[32:96, :], rxdown_ref[32:96, :]], axis=1)
    spread_up[8 * (1 - gx)] = dot(face, spread_end_ref[...])

    lane_fine = lax.broadcasted_iota(jnp.int32, (16, FINE), 1)
    near = lax.broadcasted_iota(jnp.int32, (16, 128), 1) < 64
    for j in range(NF):
        tile = jnp.concatenate([vol[j], vol[j + 1]], axis=0)
        parts = []
        for moved in shifted(tile, CZ, lane_fine):
            edge = jnp.where(near, moved[:, OWN : OWN + 128], moved[:, OWN + 128 : FINE])
            parts.append(jnp.concatenate([moved[:, 0:OWN], edge], axis=1).astype(BF16))
        cols = jnp.concatenate(parts, axis=0)
        cols_first[j] = cols[:, 0:OWN]
        pre = dot(w1, cols)
        pre_first[j] = pre[:, 0:OWN]
        sloped = leaky(pre)
        pooled_first[j] = pooled(sloped[0:32] + sloped[32:64], CZ)

    lane = lax.broadcasted_iota(jnp.int32, (32, COARSE), 1)
    valid = jnp.logical_or(
        lane < MID,
        jnp.logical_or(
            jnp.logical_and(lane < 192, block_y < rows_y - 1),
            jnp.logical_and(lane >= 192, block_y > 0),
        ),
    )
    cols_second[0] = jnp.zeros((288, COARSE), BF16)
    cols_second[NF + 1] = jnp.zeros((288, COARSE), BF16)
    for step in range(3):
        picked = dot(
            pooled_first[6 * step : 6 * step + 6].reshape(192, KEPT), pool_first_ref[...]
        )
        for k in range(6):
            plane = jnp.where(valid, picked[k * 32 : k * 32 + 32], 0.0)
            parts = [moved.astype(BF16) for moved in shifted(plane, CZ // 2, lane)]
            cols_second[6 * step + k + 1] = jnp.concatenate(parts, axis=0)

    lane_grad = lax.broadcasted_iota(jnp.int32, (64, COARSE), 1)
    cols_grad[0] = jnp.zeros((576, MID), BF16)
    cols_grad[NS + 1] = jnp.zeros((576, MID), BF16)
    for k in (0, 1, 18, 19):
        grad_own[k] = jnp.zeros((64, MID), BF16)
    for k in range(NS):
        pre = dot(w2, cols_second[pl.ds(k + gx, 3)].reshape(864, COARSE))
        act_second[k] = leaky(pre[:, 0:MID])
        rounded = (spread_up[(k + gx) // 2] * leaky_slope(pre)).astype(BF16)
        grad = rounded.astype(F32)
        parts = [moved[:, 0:MID].astype(BF16) for moved in shifted(grad, CZ // 2, lane_grad)]
        cols_grad[k + 1] = jnp.concatenate(parts, axis=0)
        kept = rounded[:, 0:MID]
        if k == 0:
            kept = jnp.where(gx == 0, kept, jnp.zeros_like(kept))
        if k == NS - 1:
            kept = jnp.where(gx == 1, kept, jnp.zeros_like(kept))
        grad_own[k + 2 - gx] = kept

    sums = [
        pooled(act_second[2 * p + gx] + act_second[2 * p + 1 + gx], CZ // 2) for p in range(8)
    ]
    features_ref[...] = dot(jnp.concatenate(sums, axis=1), pool_second_ref[...]).astype(BF16)

    for m in range(0, 16, 2):
        cols = jnp.concatenate(
            [
                cols_grad[pl.ds(m + gx, 3)].reshape(1728, MID),
                cols_grad[pl.ds(m + 1 + gx, 3)].reshape(1728, MID),
            ],
            axis=1,
        )
        back = dot(w3, cols)
        act_grad_ref[:, m * MID : (m + 2) * MID] = back
        half_grad[m] = split(back[:, 0:MID])
        half_grad[m + 1] = split(back[:, MID : 2 * MID])

    total = jnp.zeros((288, 192), F32)
    for q in range(0, 18, 2):
        left = jnp.concatenate(
            [cols_second[q + 2 * gx][:, 0:MID], cols_second[q + 1 + 2 * gx][:, 0:MID]], axis=1
        )
        right = jnp.concatenate(
            [
                grad_own[q : q + 3].reshape(192, MID),
                grad_own[q + 1 : q + 4].reshape(192, MID),
            ],
            axis=1,
        )
        total = total + dot_lanes(left, right)
    grads_ref[:, 0:192] = total

    first = jnp.zeros((144, 64), F32)
    for step in range(4):
        spread = dot(half_grad[4 * step : 4 * step + 4].reshape(256, MID), spread_first_ref[...])
        for k in range(4):
            m = 4 * step + k + 2 * gx
            whole = spread[k * 64 : k * 64 + 32] + spread[k * 64 + 32 : k * 64 + 64]
            slope = leaky_slope(pre_first[m])
            back = (jnp.concatenate([whole, whole], axis=0) * slope).astype(BF16)
            first = first + dot_lanes(cols_first[m], back)
    grads_ref[0:144, 192:256] = first
    grads_ref[144:288, 192:256] = jnp.zeros((144, 64), F32)
    kept_ref[...] = grads_ref[pl.ds(pl.multiple_of(144 * gx, 8), 144), :]
    sent_ref[...] = grads_ref[pl.ds(pl.multiple_of(144 * (1 - gx), 8), 144), :]


def unpack_kernel(mine_ref, other_ref, second_ref, first_ref):
    first = lax.axis_index("gx") == 0
    lower = jnp.where(first, mine_ref[...], other_ref[...])
    upper = jnp.where(first, other_ref[...], mine_ref[...])
    for dx in range(3):
        second_ref[dx, 0:144] = lower[:, (2 - dx) * 64 : (3 - dx) * 64]
        second_ref[dx, 144:288] = upper[:, (2 - dx) * 64 : (3 - dx) * 64]
    both = lower[:, 192:256]
    for at in range(9):
        part = both[at * 16 : at * 16 + 16]
        for dx in range(3):
            first_ref[dx * 9 + at] = (
                part[4 * dx : 4 * dx + 4, 0:32] + part[4 * dx + 4 : 4 * dx + 8, 32:64]
            )


def call(kernel, outs, scratch=()):
    return pl.pallas_call(
        kernel,
        out_shape=[jax.ShapeDtypeStruct(shape, dtype) for shape, dtype in outs],
        scratch_shapes=[pltpu.VMEM(shape, dtype) for shape, dtype in scratch],
        compiler_params=pltpu.CompilerParams(vmem_limit_bytes=VMEM_LIMIT),
    )


def sum_of_group(part, axis):
    count = lax.axis_size(axis)
    terms = [part] + [
        lax.ppermute(part, axis, [(i, i ^ k) for i in range(count)]) for k in range(1, count)
    ]
    terms = [term.astype(F32) for term in terms]
    while len(terms) > 1:
        terms = [terms[i] + terms[i + 1] for i in range(0, len(terms), 2)]
    return terms[0]


def on_device_kernels(rows_y, volumes, first_kernel, second_kernel, cotangent):
    rim, pool_first, spread_first, pool_second, spread_own, spread_rim, spread_end = constants()
    cot = cotangent.reshape(64, 256)
    own, x_face, low, high, x_low, x_high = call(
        pack_kernel,
        [
            ((136, OWN), F32),
            ((48, OWN), BF16),
            ((208, 128), BF16),
            ((208, 128), BF16),
            ((96, 128), BF16),
            ((96, 128), BF16),
        ],
    )(volumes.reshape(4, CX * OWN), cot, rim)

    below = [(i, i + 1) for i in range(rows_y - 1)]
    above = [(i + 1, i) for i in range(rows_y - 1)]

    def across(routes):
        return [
            (g * rows_y + a, (1 - g) * rows_y + b) for g in range(2) for a, b in routes
        ]

    got_x_down = lax.ppermute(x_high, ("gx", "yz"), across(below))
    got_x_up = lax.ppermute(x_low, ("gx", "yz"), across(above))
    got_down = lax.ppermute(high, "yz", below)
    got_up = lax.ppermute(low, "yz", above)
    got_x = lax.ppermute(x_face, "gx", [(0, 1), (1, 0)])

    k1 = first_kernel.transpose(2, 3, 4, 1, 0).reshape(27, 4, 32)
    k2 = second_kernel.transpose(2, 3, 4, 1, 0).reshape(864, 64)

    features, act_grad, kept, sent = call(
        functools.partial(main_kernel, rows_y),
        [((64, 256), BF16), ((32, 2048), F32), ((144, 256), F32), ((144, 256), F32)],
        [
            ((144, 64), F32),
            ((19, 8, FINE), F32),
            ((NF, 144, OWN), BF16),
            ((NF, 64, OWN), F32),
            ((NF, 32, KEPT), BF16),
            ((NF + 2, 288, COARSE), BF16),
            ((NS, 64, MID), F32),
            ((9, 64, COARSE), F32),
            ((20, 64, MID), BF16),
            ((NS + 2, 576, MID), BF16),
            ((16, 64, MID), BF16),
            ((288, 256), F32),
        ],
    )(
        own,
        cot,
        got_x,
        got_up,
        got_down,
        got_x_up,
        got_x_down,
        k1,
        k2,
        pool_first,
        spread_first,
        pool_second,
        spread_own,
        spread_rim,
        spread_end,
    )
    swap = [(0, 1), (1, 0)]
    part = (kept + lax.ppermute(sent, "gx", swap)).astype(BF16)
    part = sum_of_group(part, "dp").astype(BF16)
    mine = sum_of_group(part, "yz")
    other = lax.ppermute(mine, "gx", swap)
    second, first = call(unpack_kernel, [((3, 288, 64), F32), ((27, 4, 32), F32)])(mine, other)
    return (
        features.reshape(1, 64, 1, 1, 256),
        act_grad.reshape(1, 32, 1, 1, 2048),
        first.reshape(3, 3, 3, 4, 32).transpose(4, 3, 0, 1, 2),
        second.reshape(3, 3, 3, 32, 64).transpose(4, 3, 0, 1, 2),
    )


def solution(mesh):
    placed = (P("dp", None, "gx", "yz", None), P(), P(), P("dp", None, "gx", "yz", None))
    rows_y = min(4, mesh.shape["yz"])
    rows_z = mesh.shape["yz"] // rows_y
    if rows_z == 1 and rows_y in (2, 4) and mesh.shape["gx"] == 2 and mesh.shape["dp"] in (1, 2, 4):
        body = functools.partial(on_device_kernels, rows_y)
    else:
        body = functools.partial(on_device_plain, rows_y, rows_z)
    return jax.shard_map(
        body,
        mesh=mesh,
        in_specs=placed,
        out_specs=(P("dp", None, "gx", "yz", None), P("dp", None, "gx", "yz", None), P(), P()),
        check_vma=False,
    )
```

```python
import functools

import jax
import jax.numpy as jnp
import numpy as np
from jax import lax
from jax.experimental import pallas as pl
from jax.experimental.pallas import tpu as pltpu
from jax.sharding import PartitionSpec as P

CX = 32
CY = 32
CZ = 16
SLOPE = 0.3
F32 = jnp.float32
BF16 = jnp.bfloat16


def leaky(values):
    return jnp.where(values > 0, values, SLOPE * values)


def leaky_slope(values):
    return jnp.where(values > 0, jnp.float32(1.0), jnp.float32(SLOPE))


def convolve_valid(padded, kernel):
    return lax.conv_general_dilated(
        padded,
        kernel,
        (1, 1, 1),
        "VALID",
        dimension_numbers=("NCDHW", "OIDHW", "NCDHW"),
        preferred_element_type=F32,
    )


def kernel_grad(padded, grad):
    result = lax.conv_general_dilated(
        padded,
        grad,
        (1, 1, 1),
        "VALID",
        dimension_numbers=("CNDHW", "IODHW", "NCDHW"),
        preferred_element_type=F32,
    )
    return result.transpose(1, 0, 2, 3, 4)


def average_pool(values):
    bat, chan, xs, ys, zs = values.shape
    return values.reshape(bat, chan, xs // 2, 2, ys // 2, 2, zs // 2, 2).mean(axis=(3, 5, 7))


def spread_back(values):
    bat, chan, xs, ys, zs = values.shape
    grown = jnp.broadcast_to(
        values[:, :, :, None, :, None, :, None], (bat, chan, xs, 2, ys, 2, zs, 2)
    )
    return grown.reshape(bat, chan, 2 * xs, 2 * ys, 2 * zs) * 0.125


def unflatten(values, factor):
    return values[:, :, 0, 0].reshape(
        values.shape[0], values.shape[1], CX // factor, CY // factor, CZ // factor
    )


def flatten(values):
    return values.reshape(values.shape[0], values.shape[1], 1, 1, -1)


def extend_along(values, dim, axis, routes):
    size = values.shape[dim]
    first = lax.slice_in_dim(values, 0, 1, axis=dim)
    last = lax.slice_in_dim(values, size - 1, size, axis=dim)
    before = lax.ppermute(last, axis, routes)
    after = lax.ppermute(first, axis, [(b, a) for a, b in routes])
    return jnp.concatenate([before, values, after], axis=dim)


def extend(values, rows_y, rows_z):
    planes = lax.axis_size("gx")
    count = rows_y * rows_z
    values = extend_along(values, 2, "gx", [(i, i + 1) for i in range(planes - 1)])
    values = extend_along(values, 3, "yz", [(i, i + rows_z) for i in range(count - rows_z)])
    return extend_along(
        values, 4, "yz", [(i, i + 1) for i in range(count - 1) if (i + 1) % rows_z]
    )


def on_device_plain(rows_y, rows_z, volumes, first_kernel, second_kernel, cotangent):
    upstream = unflatten(cotangent, 4)
    padded_in = extend(unflatten(volumes, 1), rows_y, rows_z)
    pre_first = convolve_valid(padded_in, first_kernel)
    act_first = average_pool(leaky(pre_first)).astype(BF16)
    padded_mid = extend(act_first, rows_y, rows_z)
    pre_second = convolve_valid(padded_mid, second_kernel)
    features = average_pool(leaky(pre_second)).astype(BF16)
    grad_second = (spread_back(upstream.astype(F32)) * leaky_slope(pre_second)).astype(BF16)
    flipped = jnp.flip(second_kernel, (2, 3, 4)).transpose(1, 0, 2, 3, 4)
    act_grad = convolve_valid(extend(grad_second, rows_y, rows_z), flipped)
    grad_first = (spread_back(act_grad) * leaky_slope(pre_first)).astype(BF16)
    first_grad, second_grad = lax.psum(
        (kernel_grad(padded_in, grad_first), kernel_grad(padded_mid, grad_second)),
        ("dp", "gx", "yz"),
    )
    return (flatten(features), flatten(act_grad), first_grad, second_grad)


FINE = 48 * CZ
KEPT = 40 * CZ
OWN = CY * CZ
COARSE = 256
MID = (CY // 2) * (CZ // 2)
NF = 18
NS = 17


def constants():
    kept = np.arange(KEPT)
    row = np.where(kept < OWN + 64, kept // CZ, kept // CZ - 40)
    lane = ((row // 2) * 8 + (kept % CZ) // 2) % COARSE
    into = lane[:, None] == np.arange(COARSE)[None]
    corner = (row % 2 == 0) & (kept % 2 == 0)
    pool_first = into * corner[:, None]
    spread_first = into[:OWN, :MID].T * 0.125
    mid = np.arange(8 * MID)
    plane, y, z = mid // MID, (mid // 8) % 16, mid % 8
    pooled = plane * 32 + (y // 2) * 4 + z // 2
    into = pooled[:, None] == np.arange(256)[None]
    pool_second = into * ((y % 2 == 0) & (z % 2 == 0))[:, None]
    spread_own = into.T * 0.125
    spread_rim = np.zeros((256, 8, 128))
    spread_end = np.zeros((384, 256))
    for z in range(8):
        for p in range(8):
            spread_rim[p * 4 + z // 2, p, z] = 0.125
            spread_rim[128 + p * 4 + z // 2, p, 120 + z] = 0.125
        for y in range(16):
            spread_end[(y // 2) * 4 + z // 2, y * 8 + z] = 0.125
        spread_end[128 + z // 2, 128 + z] = 0.125
        spread_end[256 + z // 2, 248 + z] = 0.125
    rim = np.zeros((256, 256))
    for x in range(8):
        for z in range(4):
            rim[x * 32 + z, x * 4 + z] = 1
            rim[x * 32 + 28 + z, 128 + x * 4 + z] = 1
    made = (
        rim,
        pool_first,
        spread_first,
        pool_second,
        spread_own,
        spread_rim.reshape(256, 1024),
        spread_end,
    )
    return [jnp.asarray(a, BF16) for a in made]


def dot(a, b):
    return jnp.dot(a, b, preferred_element_type=F32)


def dot_lanes(a, b):
    return lax.dot_general(a, b, (((1,), (1,)), ((), ())), preferred_element_type=F32)


def pack_kernel(
    vol_ref, cot_ref, rim_ref, own_ref, x_ref, near_ref, far_ref, xnear_ref, xfar_ref
):
    gx = lax.axis_index("gx")
    odd = lax.axis_index("yz") % 2
    own_ref[0:8, :] = jnp.zeros((8, OWN), F32)
    own_ref[128:136, :] = jnp.zeros((8, OWN), F32)
    for x in range(CX):
        own_ref[4 + 4 * x : 8 + 4 * x, :] = vol_ref[:, x * OWN : (x + 1) * OWN].astype(F32)
    start = pl.multiple_of(112 * (1 - gx), 8)
    blank = jnp.zeros((8, OWN), F32)
    face = jnp.concatenate([own_ref[pl.ds(start, 24), :], blank])
    x_ref[0:32, :] = face.astype(BF16)
    cot = cot_ref[...]
    wide = cot.astype(F32)
    first = gx == 0
    end = jnp.where(first, pltpu.roll(wide[:, 128:256], 32, 1), wide[:, 0:128]).astype(BF16)
    for part in range(4):
        x_ref[32:48, part * 128 : (part + 1) * 128] = end[part * 16 : (part + 1) * 16, :]
    rims = dot(cot, rim_ref[...])
    for low, side_ref, xside_ref in ((odd, near_ref, xnear_ref), (1 - odd, far_ref, xfar_ref)):
        lanes = pl.ds(pl.multiple_of((OWN - 128) * (1 - low), 128), 128)
        tail = jnp.concatenate([own_ref[128:136, lanes], blank[:, 0:128]])
        side_ref[0:128, :] = own_ref[0:128, lanes].astype(BF16)
        side_ref[128:144, :] = tail.astype(BF16)
        edge = jnp.concatenate([own_ref[pl.ds(start, 24), lanes], blank[:, 0:128]])
        xside_ref[0:32, :] = edge.astype(BF16)
        rim = jnp.where(low == 1, rims[:, 0:128], rims[:, 128:256])
        side_ref[144:208, :] = rim.astype(BF16)
        xside_ref[32:96, :] = jnp.where(first, pltpu.roll(rim, 100, 1), rim).astype(BF16)


def shifted(tile, period, lane):
    size = tile.shape[1]
    z = lane % period
    blank = jnp.zeros_like(tile)
    along = (
        jnp.where(z == 0, blank, pltpu.roll(tile, 1, 1)),
        tile,
        jnp.where(z == period - 1, blank, pltpu.roll(tile, size - 1, 1)),
    )
    return [
        pltpu.roll(moved, shift, 1) if shift else moved
        for shift in (period, 0, size - period)
        for moved in along
    ]


def pooled(values, period):
    size = values.shape[1]
    values = values + pltpu.roll(values, size - 1, 1)
    values = values + pltpu.roll(values, size - period, 1)
    return (values * 0.125).astype(BF16)


def split(values):
    top = values.astype(BF16)
    return jnp.concatenate([top, (values - top.astype(F32)).astype(BF16)], axis=0)


def main_kernel(
    rows_y,
    own_ref,
    cot_ref,
    rx_ref,
    rnear_ref,
    rfar_ref,
    rxnear_ref,
    rxfar_ref,
    k1_ref,
    k2_ref,
    *refs,
):
    consts, refs = refs[:6], refs[6:]
    (
        features_ref,
        act_grad_ref,
        kept_ref,
        sent_ref,
        w1_rows,
        vol,
        cols_first,
        pre_first,
        pooled_first,
        cols_second,
        act_second,
        spread_up,
        grad_own,
        cols_grad,
        half_grad,
        grads_ref,
    ) = refs[:16]
    held, sems = refs[16:22], refs[22]
    copies = [pltpu.make_async_copy(consts[n], held[n], sems.at[n]) for n in range(6)]
    for copy in copies:
        copy.start()
    pool_first_ref, spread_first_ref, pool_second_ref = held[0:3]
    spread_own_ref, spread_rim_ref, spread_end_ref = held[3:6]
    gx = lax.axis_index("gx")
    block_y = lax.axis_index("yz")

    odd = block_y % 2 == 1
    inner = jnp.logical_and(block_y > 0, block_y < rows_y - 1)

    def above_below(near, far):
        near, far = near.astype(F32), far.astype(F32)
        far = jnp.where(inner, far, jnp.zeros_like(far))
        return jnp.where(odd, far, near), jnp.where(odd, near, far)

    w1_rows[...] = jnp.zeros_like(w1_rows)
    for dx in range(3):
        for at in range(9):
            block = k1_ref[dx * 9 + at].astype(F32)
            for k in range(2):
                row = at * 16 + 4 * (dx + k)
                w1_rows[row : row + 4, 32 * k : 32 * k + 32] = block
    w1 = w1_rows[...].T.astype(BF16)

    vol[...] = jnp.zeros_like(vol)
    vol[pl.ds(2 * gx, 17), :, 0:OWN] = own_ref[...].reshape(17, 8, OWN)
    up, down = above_below(rnear_ref[0:144, :], rfar_ref[0:144, :])
    vol[pl.ds(2 * gx, 17), :, OWN : OWN + 128] = up[0:136].reshape(17, 8, 128)
    vol[pl.ds(2 * gx, 17), :, OWN + 128 : FINE] = down[0:136].reshape(17, 8, 128)
    end = pl.ds(16 * (1 - gx), 3)
    vol[end, :, 0:OWN] += rx_ref[0:32, :].astype(F32)[0:24].reshape(3, 8, OWN)
    up, down = above_below(rxnear_ref[0:32, :], rxfar_ref[0:32, :])
    vol[end, :, OWN : OWN + 128] += up[0:24].reshape(3, 8, 128)
    vol[end, :, OWN + 128 : FINE] += down[0:24].reshape(3, 8, 128)

    lane_fine = lax.broadcasted_iota(jnp.int32, (16, FINE), 1)
    near = lax.broadcasted_iota(jnp.int32, (16, 128), 1) < 64
    for j in range(NF):
        tile = jnp.concatenate([vol[j], vol[j + 1]], axis=0).astype(BF16)
        parts = []
        for moved in shifted(tile, CZ, lane_fine):
            edge = jnp.where(near, moved[:, OWN : OWN + 128], moved[:, OWN + 128 : FINE])
            parts.append(jnp.concatenate([moved[:, 0:OWN], edge], axis=1))
        cols = jnp.concatenate(parts, axis=0)
        cols_first[j] = cols[:, 0:OWN]
        pre = dot(w1, cols)
        pre_first[j] = pre[:, 0:OWN]
        sloped = leaky(pre)
        pooled_first[j] = pooled(sloped[0:32] + sloped[32:64], CZ)

    lane = lax.broadcasted_iota(jnp.int32, (32, COARSE), 1)
    valid = jnp.logical_or(
        lane < MID,
        jnp.logical_or(
            jnp.logical_and(lane < 192, block_y < rows_y - 1),
            jnp.logical_and(lane >= 192, block_y > 0),
        ),
    )
    cols_second[0] = jnp.zeros((288, COARSE), BF16)
    cols_second[NF + 1] = jnp.zeros((288, COARSE), BF16)
    copies[0].wait()
    for step in range(3):
        picked = dot(
            pooled_first[6 * step : 6 * step + 6].reshape(192, KEPT), pool_first_ref[...]
        )
        for k in range(6):
            plane = jnp.where(valid, picked[k * 32 : k * 32 + 32], 0.0).astype(BF16)
            parts = shifted(plane, CZ // 2, lane)
            cols_second[6 * step + k + 1] = jnp.concatenate(parts, axis=0)

    for n in (3, 4, 5):
        copies[n].wait()
    own_up = dot(cot_ref[...], spread_own_ref[...])
    up, down = above_below(rnear_ref[144:208, :], rfar_ref[144:208, :])
    rim_up = dot(jnp.concatenate([up, down], axis=1).astype(BF16), spread_rim_ref[...])
    for p in range(8):
        spread_up[p + gx, :, 0:128] = own_up[:, p * 128 : (p + 1) * 128]
        spread_up[p + gx, :, 128:256] = rim_up[:, p * 128 : (p + 1) * 128]
    face = jnp.concatenate([rx_ref[32:48, q * 128 : (q + 1) * 128] for q in range(4)], axis=0)
    up, down = above_below(rxnear_ref[32:96, :], rxfar_ref[32:96, :])
    face = jnp.concatenate([face, up.astype(BF16), down.astype(BF16)], axis=1)
    spread_up[8 * (1 - gx)] = dot(face, spread_end_ref[...])

    k2 = k2_ref[...].astype(F32)
    w2 = k2.T.astype(BF16)
    w3 = jnp.concatenate([k2[32 * n : 32 * n + 32] for n in range(26, -1, -1)], axis=1)
    w3 = w3.astype(BF16)
    lane_grad = lax.broadcasted_iota(jnp.int32, (64, COARSE), 1)
    cols_grad[0] = jnp.zeros((576, MID), BF16)
    cols_grad[NS + 1] = jnp.zeros((576, MID), BF16)
    for k in (0, 1, 18, 19):
        grad_own[k] = jnp.zeros((64, MID), BF16)
    for k in range(NS):
        pre = dot(w2, cols_second[pl.ds(k + gx, 3)].reshape(864, COARSE))
        act_second[k] = leaky(pre[:, 0:MID])
        rounded = (spread_up[(k + gx) // 2] * leaky_slope(pre)).astype(BF16)
        parts = [moved[:, 0:MID] for moved in shifted(rounded, CZ // 2, lane_grad)]
        cols_grad[k + 1] = jnp.concatenate(parts, axis=0)
        kept = rounded[:, 0:MID]
        if k == 0:
            kept = jnp.where(gx == 0, kept, jnp.zeros_like(kept))
        if k == NS - 1:
            kept = jnp.where(gx == 1, kept, jnp.zeros_like(kept))
        grad_own[k + 2 - gx] = kept

    sums = [
        pooled(act_second[2 * p + gx] + act_second[2 * p + 1 + gx], CZ // 2) for p in range(8)
    ]
    copies[2].wait()
    features_ref[...] = dot(jnp.concatenate(sums, axis=1), pool_second_ref[...]).astype(BF16)

    for m in range(0, 16, 2):
        cols = jnp.concatenate(
            [
                cols_grad[pl.ds(m + gx, 3)].reshape(1728, MID),
                cols_grad[pl.ds(m + 1 + gx, 3)].reshape(1728, MID),
            ],
            axis=1,
        )
        back = dot(w3, cols)
        for k in range(2):
            plane = back[:, k * MID : (k + 1) * MID]
            act_grad_ref[:, m + k, :] = plane
            half_grad[m + k] = split(plane)

    total = jnp.zeros((288, 192), F32)
    for q in range(0, 18, 2):
        left = jnp.concatenate(
            [cols_second[q + 2 * gx][:, 0:MID], cols_second[q + 1 + 2 * gx][:, 0:MID]], axis=1
        )
        right = jnp.concatenate(
            [
                grad_own[q : q + 3].reshape(192, MID),
                grad_own[q + 1 : q + 4].reshape(192, MID),
            ],
            axis=1,
        )
        total = total + dot_lanes(left, right)
    grads_ref[:, 0:192] = total

    copies[1].wait()
    first = jnp.zeros((144, 64), F32)
    for step in range(4):
        spread = dot(half_grad[4 * step : 4 * step + 4].reshape(256, MID), spread_first_ref[...])
        for k in range(4):
            m = 4 * step + k + 2 * gx
            whole = spread[k * 64 : k * 64 + 32] + spread[k * 64 + 32 : k * 64 + 64]
            slope = leaky_slope(pre_first[m])
            back = (jnp.concatenate([whole, whole], axis=0) * slope).astype(BF16)
            first = first + dot_lanes(cols_first[m], back)
    grads_ref[0:144, 192:256] = first
    grads_ref[144:288, 192:256] = jnp.zeros((144, 64), F32)
    kept_ref[...] = grads_ref[pl.ds(pl.multiple_of(144 * gx, 8), 144), :]
    sent_ref[...] = grads_ref[pl.ds(pl.multiple_of(144 * (1 - gx), 8), 144), :]


def unpack_kernel(mine_ref, other_ref, second_ref, first_ref):
    first = lax.axis_index("gx") == 0
    lower = jnp.where(first, mine_ref[...], other_ref[...])
    upper = jnp.where(first, other_ref[...], mine_ref[...])
    for dx in range(3):
        second_ref[dx, 0:144] = lower[:, (2 - dx) * 64 : (3 - dx) * 64]
        second_ref[dx, 144:288] = upper[:, (2 - dx) * 64 : (3 - dx) * 64]
    both = lower[:, 192:256]
    for at in range(9):
        part = both[at * 16 : at * 16 + 16]
        for dx in range(3):
            first_ref[dx * 9 + at] = (
                part[4 * dx : 4 * dx + 4, 0:32] + part[4 * dx + 4 : 4 * dx + 8, 32:64]
            )


def call(kernel, outs, limit, scratch=(), semaphores=0, apart=0, operands=0):
    whole = pl.BlockSpec(memory_space=pltpu.VMEM)
    held = [pltpu.VMEM(shape, dtype) for shape, dtype in scratch]
    if semaphores:
        held.append(pltpu.SemaphoreType.DMA((semaphores,)))
    return pl.pallas_call(
        kernel,
        out_shape=[jax.ShapeDtypeStruct(shape, dtype) for shape, dtype in outs],
        in_specs=[whole] * (operands - apart) + [pl.BlockSpec(memory_space=pl.ANY)] * apart,
        out_specs=[whole] * len(outs),
        scratch_shapes=held,
        compiler_params=pltpu.CompilerParams(vmem_limit_bytes=limit * 1024 * 1024),
    )


def sum_of_group(part, axis):
    count = lax.axis_size(axis)
    terms = [part] + [
        lax.ppermute(part, axis, [(i, i ^ k) for i in range(count)]) for k in range(1, count)
    ]
    terms = [term.astype(F32) for term in terms]
    while len(terms) > 1:
        terms = [terms[i] + terms[i + 1] for i in range(0, len(terms), 2)]
    return terms[0]


def on_device_kernels(rows_y, volumes, first_kernel, second_kernel, cotangent):
    rim, *tables = constants()
    cot = cotangent.reshape(64, 256)
    own, x_face, near, far, x_near, x_far = call(
        pack_kernel,
        [
            ((136, OWN), F32),
            ((48, OWN), BF16),
            ((208, 128), BF16),
            ((208, 128), BF16),
            ((96, 128), BF16),
            ((96, 128), BF16),
        ],
        8,
        operands=3,
    )(volumes.reshape(4, CX * OWN), cot, rim)

    def paired(values, k):
        routes = [
            (g * rows_y + i, (1 - g) * rows_y + (i ^ k)) for g in range(2) for i in range(rows_y)
        ]
        return lax.ppermute(values, ("gx", "yz"), routes)

    got_x_near = paired(x_near, 1)
    got_x_far = paired(x_far, 3)
    got_near = lax.ppermute(near, "yz", [(i, i ^ 1) for i in range(rows_y)])
    got_far = lax.ppermute(far, "yz", [(i, i ^ 3) for i in range(rows_y)])
    got_x = lax.ppermute(x_face, "gx", [(0, 1), (1, 0)])

    k1 = first_kernel.transpose(2, 3, 4, 1, 0).reshape(27, 4, 32)
    k2 = second_kernel.transpose(2, 3, 4, 1, 0).reshape(864, 64)

    features, act_grad, kept, sent = call(
        functools.partial(main_kernel, rows_y),
        [((64, 256), BF16), ((32, 16, MID), F32), ((144, 256), F32), ((144, 256), F32)],
        32,
        [
            ((144, 64), F32),
            ((19, 8, FINE), F32),
            ((NF, 144, OWN), BF16),
            ((NF, 64, OWN), F32),
            ((NF, 32, KEPT), BF16),
            ((NF + 2, 288, COARSE), BF16),
            ((NS, 64, MID), F32),
            ((9, 64, COARSE), F32),
            ((20, 64, MID), BF16),
            ((NS + 2, 576, MID), BF16),
            ((16, 64, MID), BF16),
            ((288, 256), F32),
        ]
        + [(table.shape, BF16) for table in tables],
        semaphores=6,
        apart=6,
        operands=15,
    )(
        own,
        cot,
        got_x,
        got_near,
        got_far,
        got_x_near,
        got_x_far,
        k1,
        k2,
        *tables,
    )
    swap = [(0, 1), (1, 0)]
    part = (kept + lax.ppermute(sent, "gx", swap)).astype(BF16)
    part = sum_of_group(part, "dp").astype(BF16)
    mine = sum_of_group(part, "yz")
    other = lax.ppermute(mine, "gx", swap)
    second, first = call(
        unpack_kernel, [((3, 288, 64), F32), ((27, 4, 32), F32)], 8, operands=2
    )(mine, other)
    return (
        features.reshape(1, 64, 1, 1, 256),
        act_grad.reshape(1, 32, 1, 1, 2048),
        first.reshape(3, 3, 3, 4, 32).transpose(4, 3, 0, 1, 2),
        second.reshape(3, 3, 3, 32, 64).transpose(4, 3, 0, 1, 2),
    )


def solution(mesh):
    placed = (P("dp", None, "gx", "yz", None), P(), P(), P("dp", None, "gx", "yz", None))
    rows_y = min(4, mesh.shape["yz"])
    rows_z = mesh.shape["yz"] // rows_y
    if rows_z == 1 and rows_y == 4 and mesh.shape["gx"] == 2 and mesh.shape["dp"] in (1, 2, 4):
        body = functools.partial(on_device_kernels, rows_y)
    else:
        body = functools.partial(on_device_plain, rows_y, rows_z)
    return jax.shard_map(
        body,
        mesh=mesh,
        in_specs=placed,
        out_specs=(P("dp", None, "gx", "yz", None), P("dp", None, "gx", "yz", None), P(), P()),
        check_vma=False,
    )
```

```python
import functools

import jax
import jax.numpy as jnp
from jax import lax
from jax.experimental import pallas as pl
from jax.experimental.pallas import tpu as pltpu
from jax.sharding import PartitionSpec as P

CX = 32
CY = 32
CZ = 16
SLOPE = 0.3
F32 = jnp.float32
BF16 = jnp.bfloat16


def leaky(values):
    return jnp.where(values > 0, values, SLOPE * values)


def leaky_slope(values):
    return jnp.where(values > 0, jnp.float32(1.0), jnp.float32(SLOPE))


def convolve_valid(padded, kernel):
    return lax.conv_general_dilated(
        padded,
        kernel,
        (1, 1, 1),
        "VALID",
        dimension_numbers=("NCDHW", "OIDHW", "NCDHW"),
        preferred_element_type=F32,
    )


def kernel_grad(padded, grad):
    result = lax.conv_general_dilated(
        padded,
        grad,
        (1, 1, 1),
        "VALID",
        dimension_numbers=("CNDHW", "IODHW", "NCDHW"),
        preferred_element_type=F32,
    )
    return result.transpose(1, 0, 2, 3, 4)


def average_pool(values):
    bat, chan, xs, ys, zs = values.shape
    return values.reshape(bat, chan, xs // 2, 2, ys // 2, 2, zs // 2, 2).mean(axis=(3, 5, 7))


def spread_back(values):
    bat, chan, xs, ys, zs = values.shape
    grown = jnp.broadcast_to(
        values[:, :, :, None, :, None, :, None], (bat, chan, xs, 2, ys, 2, zs, 2)
    )
    return grown.reshape(bat, chan, 2 * xs, 2 * ys, 2 * zs) * 0.125


def unflatten(values, factor):
    return values[:, :, 0, 0].reshape(
        values.shape[0], values.shape[1], CX // factor, CY // factor, CZ // factor
    )


def flatten(values):
    return values.reshape(values.shape[0], values.shape[1], 1, 1, -1)


def extend_along(values, dim, axis, routes):
    size = values.shape[dim]
    first = lax.slice_in_dim(values, 0, 1, axis=dim)
    last = lax.slice_in_dim(values, size - 1, size, axis=dim)
    before = lax.ppermute(last, axis, routes)
    after = lax.ppermute(first, axis, [(b, a) for a, b in routes])
    return jnp.concatenate([before, values, after], axis=dim)


def extend(values, rows_y, rows_z):
    planes = lax.axis_size("gx")
    count = rows_y * rows_z
    values = extend_along(values, 2, "gx", [(i, i + 1) for i in range(planes - 1)])
    values = extend_along(values, 3, "yz", [(i, i + rows_z) for i in range(count - rows_z)])
    return extend_along(
        values, 4, "yz", [(i, i + 1) for i in range(count - 1) if (i + 1) % rows_z]
    )


def on_device_plain(rows_y, rows_z, volumes, first_kernel, second_kernel, cotangent):
    upstream = unflatten(cotangent, 4)
    padded_in = extend(unflatten(volumes, 1), rows_y, rows_z)
    pre_first = convolve_valid(padded_in, first_kernel)
    act_first = average_pool(leaky(pre_first)).astype(BF16)
    padded_mid = extend(act_first, rows_y, rows_z)
    pre_second = convolve_valid(padded_mid, second_kernel)
    features = average_pool(leaky(pre_second)).astype(BF16)
    grad_second = (spread_back(upstream.astype(F32)) * leaky_slope(pre_second)).astype(BF16)
    flipped = jnp.flip(second_kernel, (2, 3, 4)).transpose(1, 0, 2, 3, 4)
    act_grad = convolve_valid(extend(grad_second, rows_y, rows_z), flipped)
    grad_first = (spread_back(act_grad) * leaky_slope(pre_first)).astype(BF16)
    first_grad, second_grad = lax.psum(
        (kernel_grad(padded_in, grad_first), kernel_grad(padded_mid, grad_second)),
        ("dp", "gx", "yz"),
    )
    return (flatten(features), flatten(act_grad), first_grad, second_grad)


FINE = 48 * CZ
KEPT = 40 * CZ
OWN = CY * CZ
COARSE = 256
MID = (CY // 2) * (CZ // 2)
NF = 18
NS = 17


def grid(shape):
    return [lax.broadcasted_iota(jnp.int32, shape, dim) for dim in range(2)]


def one_where(condition, value=1.0):
    return jnp.where(condition, value, 0.0).astype(BF16)


def fine_to_mid(lane):
    return (lane >> 5) * 8 + ((lane & 15) >> 1) + jnp.where(lane >= OWN + 64, 96, 0)


def rim_table():
    row, lane = grid((256, 256))
    edge = jnp.where(lane < 128, 0, 7)
    place = (row >> 5) * 4 + (row & 3)
    return one_where(jnp.logical_and(((row >> 2) & 7) == edge, place == (lane & 127)))


def pool_first_table():
    row, lane = grid((KEPT, COARSE))
    place = jnp.where((row & 17) == 0, fine_to_mid(row), -1)
    return one_where(place == lane)


def spread_first_table():
    row, lane = grid((MID, OWN))
    return one_where(fine_to_mid(lane) == row, 0.125)


def pool_second_table():
    row, lane = grid((MID, 128))
    place = jnp.where((row & 9) == 0, (row >> 4) * 4 + ((row & 7) >> 1), -1)
    return one_where(place == lane)


def spread_second_table():
    row, lane = grid((128, COARSE))
    place = jnp.where(lane < MID, (lane >> 4) * 4, jnp.where(lane < 192, 32, 36))
    place = place + ((lane & 7) >> 1)
    used = jnp.logical_or(lane < MID + 8, lane >= COARSE - 8)
    return one_where(jnp.logical_and(used, place == row), 0.125)


def fold_rows(values):
    lane = grid((16, 128))[1]
    kept = [
        jnp.where(lane < 32, values[16 * q : 16 * q + 16], jnp.zeros((16, 128), F32))
        for q in range(4)
    ]
    return kept[0] + sum(pltpu.roll(kept[q], 32 * q, 1) for q in range(1, 4))


def unfold_rows(values):
    parts = [values] + [pltpu.roll(values, 128 - 32 * q, 1) for q in range(1, 4)]
    return jnp.concatenate(parts, axis=0)


def dot(a, b):
    return jnp.dot(a, b, preferred_element_type=F32)


def dot_lanes(a, b):
    return lax.dot_general(a, b, (((1,), (1,)), ((), ())), preferred_element_type=F32)


def pack_kernel(vol_ref, cot_ref, own_ref, x_ref, near_ref, far_ref, xnear_ref, xfar_ref):
    gx = lax.axis_index("gx")
    odd = lax.axis_index("yz") % 2
    own_ref[0:8, :] = jnp.zeros((8, OWN), F32)
    own_ref[128:136, :] = jnp.zeros((8, OWN), F32)
    for x in range(CX):
        own_ref[4 + 4 * x : 8 + 4 * x, :] = vol_ref[:, x * OWN : (x + 1) * OWN].astype(F32)
    start = pl.multiple_of(112 * (1 - gx), 8)
    blank = jnp.zeros((8, OWN), F32)
    face = jnp.concatenate([own_ref[pl.ds(start, 24), :], blank])
    x_ref[0:32, :] = face.astype(BF16)
    cot = cot_ref[...]
    wide = cot.astype(F32)
    first = gx == 0
    end = jnp.where(first, pltpu.roll(wide[:, 128:256], 32, 1), wide[:, 0:128])
    x_ref[32:48, 0:128] = fold_rows(end).astype(BF16)
    x_ref[32:48, 128:OWN] = jnp.zeros((16, OWN - 128), BF16)
    rims = dot(cot, rim_table())
    for low, side_ref, xside_ref in ((odd, near_ref, xnear_ref), (1 - odd, far_ref, xfar_ref)):
        lanes = pl.ds(pl.multiple_of((OWN - 128) * (1 - low), 128), 128)
        tail = jnp.concatenate([own_ref[128:136, lanes], blank[:, 0:128]])
        side_ref[0:128, :] = own_ref[0:128, lanes].astype(BF16)
        side_ref[128:144, :] = tail.astype(BF16)
        edge = jnp.concatenate([own_ref[pl.ds(start, 24), lanes], blank[:, 0:128]])
        xside_ref[0:32, :] = edge.astype(BF16)
        rim = jnp.where(low == 1, rims[:, 0:128], rims[:, 128:256])
        side_ref[144:160, :] = fold_rows(rim).astype(BF16)
        corner = jnp.where(first, pltpu.roll(rim, 100, 1), rim)
        xside_ref[32:48, :] = fold_rows(corner).astype(BF16)


def shifted(tile, period, lane):
    size = tile.shape[1]
    z = lane % period
    blank = jnp.zeros_like(tile)
    along = (
        jnp.where(z == 0, blank, pltpu.roll(tile, 1, 1)),
        tile,
        jnp.where(z == period - 1, blank, pltpu.roll(tile, size - 1, 1)),
    )
    return [
        pltpu.roll(moved, shift, 1) if shift else moved
        for shift in (period, 0, size - period)
        for moved in along
    ]


def pooled(values, period):
    size = values.shape[1]
    values = values + pltpu.roll(values, size - 1, 1)
    values = values + pltpu.roll(values, size - period, 1)
    return (values * 0.125).astype(BF16)


def split(values):
    top = values.astype(BF16)
    return jnp.concatenate([top, (values - top.astype(F32)).astype(BF16)], axis=0)


def main_kernel(
    rows_y,
    own_ref,
    cot_ref,
    rx_ref,
    rnear_ref,
    rfar_ref,
    rxnear_ref,
    rxfar_ref,
    k1_ref,
    k2_ref,
    features_ref,
    act_grad_ref,
    kept_ref,
    sent_ref,
    w1_rows,
    vol,
    cols_first,
    pre_first,
    pooled_first,
    cols_second,
    act_second,
    spread_up,
    grad_own,
    cols_grad,
    half_grad,
    grads_ref,
):
    gx = lax.axis_index("gx")
    block_y = lax.axis_index("yz")

    odd = block_y % 2 == 1
    inner = jnp.logical_and(block_y > 0, block_y < rows_y - 1)

    def above_below(near, far):
        near, far = near.astype(F32), far.astype(F32)
        far = jnp.where(inner, far, jnp.zeros_like(far))
        return jnp.where(odd, far, near), jnp.where(odd, near, far)

    w1_rows[...] = jnp.zeros_like(w1_rows)
    for dx in range(3):
        for at in range(9):
            block = k1_ref[dx * 9 + at].astype(F32)
            for k in range(2):
                row = at * 16 + 4 * (dx + k)
                w1_rows[row : row + 4, 32 * k : 32 * k + 32] = block
    w1 = w1_rows[...].T.astype(BF16)

    vol[...] = jnp.zeros_like(vol)
    vol[pl.ds(2 * gx, 17), :, 0:OWN] = own_ref[...].reshape(17, 8, OWN)
    up, down = above_below(rnear_ref[0:144, :], rfar_ref[0:144, :])
    vol[pl.ds(2 * gx, 17), :, OWN : OWN + 128] = up[0:136].reshape(17, 8, 128)
    vol[pl.ds(2 * gx, 17), :, OWN + 128 : FINE] = down[0:136].reshape(17, 8, 128)
    end = pl.ds(16 * (1 - gx), 3)
    vol[end, :, 0:OWN] += rx_ref[0:32, :].astype(F32)[0:24].reshape(3, 8, OWN)
    up, down = above_below(rxnear_ref[0:32, :], rxfar_ref[0:32, :])
    vol[end, :, OWN : OWN + 128] += up[0:24].reshape(3, 8, 128)
    vol[end, :, OWN + 128 : FINE] += down[0:24].reshape(3, 8, 128)

    lane_fine = lax.broadcasted_iota(jnp.int32, (16, FINE), 1)
    near = lax.broadcasted_iota(jnp.int32, (16, 128), 1) < 64
    for j in range(NF):
        tile = jnp.concatenate([vol[j], vol[j + 1]], axis=0).astype(BF16)
        parts = []
        for moved in shifted(tile, CZ, lane_fine):
            edge = jnp.where(near, moved[:, OWN : OWN + 128], moved[:, OWN + 128 : FINE])
            parts.append(jnp.concatenate([moved[:, 0:OWN], edge], axis=1))
        cols = jnp.concatenate(parts, axis=0)
        cols_first[j] = cols[:, 0:OWN]
        pre = dot(w1, cols)
        pre_first[j] = pre[:, 0:OWN]
        sloped = leaky(pre)
        pooled_first[j] = pooled(sloped[0:32] + sloped[32:64], CZ)

    lane = lax.broadcasted_iota(jnp.int32, (32, COARSE), 1)
    valid = jnp.logical_or(
        lane < MID,
        jnp.logical_or(
            jnp.logical_and(lane < 192, block_y < rows_y - 1),
            jnp.logical_and(lane >= 192, block_y > 0),
        ),
    )
    cols_second[0] = jnp.zeros((288, COARSE), BF16)
    cols_second[NF + 1] = jnp.zeros((288, COARSE), BF16)
    pick = pool_first_table()
    for step in range(3):
        picked = dot(pooled_first[6 * step : 6 * step + 6].reshape(192, KEPT), pick)
        for k in range(6):
            plane = jnp.where(valid, picked[k * 32 : k * 32 + 32], 0.0).astype(BF16)
            parts = shifted(plane, CZ // 2, lane)
            cols_second[6 * step + k + 1] = jnp.concatenate(parts, axis=0)

    slot = grid((64, 128))[1]

    def upstream(plane, up, down):
        return jnp.where(slot < 32, plane, jnp.where(slot < 36, up, down)).astype(BF16)

    def moved_to(values, lane_from, lane_to):
        shift = (lane_to - lane_from) % 128
        return pltpu.roll(values, shift, 1) if shift else values

    cot = cot_ref[...].astype(F32)
    up, down = above_below(rnear_ref[144:160, :], rfar_ref[144:160, :])
    up, down = unfold_rows(up), unfold_rows(down)
    planes = [
        upstream(
            moved_to(cot[:, p // 4 * 128 : p // 4 * 128 + 128], p % 4 * 32, 0),
            moved_to(up, 4 * p, 32),
            moved_to(down, 4 * p, 36),
        )
        for p in range(8)
    ]
    up, down = above_below(rxnear_ref[32:48, :], rxfar_ref[32:48, :])
    planes.append(
        upstream(
            unfold_rows(rx_ref[32:48, 0:128].astype(F32)),
            moved_to(unfold_rows(up), 0, 32),
            moved_to(unfold_rows(down), 0, 36),
        )
    )
    spread = dot(jnp.concatenate(planes, axis=0), spread_second_table())
    for p in range(8):
        spread_up[p + gx] = spread[64 * p : 64 * p + 64]
    spread_up[8 * (1 - gx)] = spread[512:576]

    k2 = k2_ref[...].astype(F32)
    w2 = k2.T.astype(BF16)
    w3 = jnp.concatenate([k2[32 * n : 32 * n + 32] for n in range(26, -1, -1)], axis=1)
    w3 = w3.astype(BF16)
    lane_grad = lax.broadcasted_iota(jnp.int32, (64, COARSE), 1)
    cols_grad[0] = jnp.zeros((576, MID), BF16)
    cols_grad[NS + 1] = jnp.zeros((576, MID), BF16)
    for k in (0, 1, 18, 19):
        grad_own[k] = jnp.zeros((64, MID), BF16)
    for k in range(NS):
        pre = dot(w2, cols_second[pl.ds(k + gx, 3)].reshape(864, COARSE))
        act_second[k] = leaky(pre[:, 0:MID])
        rounded = (spread_up[(k + gx) // 2] * leaky_slope(pre)).astype(BF16)
        parts = [moved[:, 0:MID] for moved in shifted(rounded, CZ // 2, lane_grad)]
        cols_grad[k + 1] = jnp.concatenate(parts, axis=0)
        kept = rounded[:, 0:MID]
        if k == 0:
            kept = jnp.where(gx == 0, kept, jnp.zeros_like(kept))
        if k == NS - 1:
            kept = jnp.where(gx == 1, kept, jnp.zeros_like(kept))
        grad_own[k + 2 - gx] = kept

    sums = [
        pooled(act_second[2 * p + gx] + act_second[2 * p + 1 + gx], CZ // 2) for p in range(8)
    ]
    picked = dot(jnp.concatenate(sums, axis=0), pool_second_table())
    for half in range(2):
        whole = picked[256 * half : 256 * half + 64]
        for k in range(1, 4):
            block = picked[256 * half + 64 * k : 256 * half + 64 * k + 64]
            whole = whole + pltpu.roll(block, 32 * k, 1)
        features_ref[:, 128 * half : 128 * half + 128] = whole.astype(BF16)

    for m in range(0, 16, 2):
        cols = jnp.concatenate(
            [
                cols_grad[pl.ds(m + gx, 3)].reshape(1728, MID),
                cols_grad[pl.ds(m + 1 + gx, 3)].reshape(1728, MID),
            ],
            axis=1,
        )
        back = dot(w3, cols)
        for k in range(2):
            plane = back[:, k * MID : (k + 1) * MID]
            act_grad_ref[:, m + k, :] = plane
            half_grad[m + k] = split(plane)

    total = jnp.zeros((288, 192), F32)
    for q in range(0, 18, 2):
        left = jnp.concatenate(
            [cols_second[q + 2 * gx][:, 0:MID], cols_second[q + 1 + 2 * gx][:, 0:MID]], axis=1
        )
        right = jnp.concatenate(
            [
                grad_own[q : q + 3].reshape(192, MID),
                grad_own[q + 1 : q + 4].reshape(192, MID),
            ],
            axis=1,
        )
        total = total + dot_lanes(left, right)
    grads_ref[:, 0:192] = total

    grow = spread_first_table()
    first = jnp.zeros((144, 64), F32)
    for step in range(4):
        spread = dot(half_grad[4 * step : 4 * step + 4].reshape(256, MID), grow)
        for k in range(4):
            m = 4 * step + k + 2 * gx
            whole = spread[k * 64 : k * 64 + 32] + spread[k * 64 + 32 : k * 64 + 64]
            slope = leaky_slope(pre_first[m])
            back = (jnp.concatenate([whole, whole], axis=0) * slope).astype(BF16)
            first = first + dot_lanes(cols_first[m], back)
    grads_ref[0:144, 192:256] = first
    grads_ref[144:288, 192:256] = jnp.zeros((144, 64), F32)
    kept_ref[...] = grads_ref[pl.ds(pl.multiple_of(144 * gx, 8), 144), :]
    sent_ref[...] = grads_ref[pl.ds(pl.multiple_of(144 * (1 - gx), 8), 144), :]


def unpack_kernel(mine_ref, other_ref, second_ref, first_ref):
    first = lax.axis_index("gx") == 0
    lower = jnp.where(first, mine_ref[...], other_ref[...])
    upper = jnp.where(first, other_ref[...], mine_ref[...])
    for dx in range(3):
        second_ref[dx, 0:144] = lower[:, (2 - dx) * 64 : (3 - dx) * 64]
        second_ref[dx, 144:288] = upper[:, (2 - dx) * 64 : (3 - dx) * 64]
    both = lower[:, 192:256]
    for at in range(9):
        part = both[at * 16 : at * 16 + 16]
        for dx in range(3):
            first_ref[dx * 9 + at] = (
                part[4 * dx : 4 * dx + 4, 0:32] + part[4 * dx + 4 : 4 * dx + 8, 32:64]
            )


def call(kernel, outs, limit, scratch=()):
    return pl.pallas_call(
        kernel,
        out_shape=[jax.ShapeDtypeStruct(shape, dtype) for shape, dtype in outs],
        scratch_shapes=[pltpu.VMEM(shape, dtype) for shape, dtype in scratch],
        compiler_params=pltpu.CompilerParams(vmem_limit_bytes=limit * 1024 * 1024),
    )


def sum_of_group(part, axis):
    count = lax.axis_size(axis)
    terms = [part] + [
        lax.ppermute(part, axis, [(i, i ^ k) for i in range(count)]) for k in range(1, count)
    ]
    terms = [term.astype(F32) for term in terms]
    while len(terms) > 1:
        terms = [terms[i] + terms[i + 1] for i in range(0, len(terms), 2)]
    return terms[0]


def on_device_kernels(rows_y, volumes, first_kernel, second_kernel, cotangent):
    cot = cotangent.reshape(64, 256)
    own, x_face, near, far, x_near, x_far = call(
        pack_kernel,
        [
            ((136, OWN), F32),
            ((48, OWN), BF16),
            ((160, 128), BF16),
            ((160, 128), BF16),
            ((48, 128), BF16),
            ((48, 128), BF16),
        ],
        60,
    )(volumes.reshape(4, CX * OWN), cot)

    def paired(values, partner):
        routes = [
            (g * rows_y + i, partner(g, i)) for g in range(2) for i in range(rows_y)
        ]
        return lax.ppermute(values, ("gx", "yz"), routes)

    def other_side(g, i, across):
        j = i + (1 if i % 2 else -1)
        if 0 <= j < rows_y:
            return (g ^ across) * rows_y + j
        return (1 - g) * rows_y + i

    got_near = lax.ppermute(near, "yz", [(i, i ^ 1) for i in range(rows_y)])
    got_far = paired(far, lambda g, i: other_side(g, i, 0))
    got_x = lax.ppermute(x_face, "gx", [(0, 1), (1, 0)])
    got_x_near = paired(x_near, lambda g, i: (1 - g) * rows_y + (i ^ 1))
    got_x_far = paired(x_far, lambda g, i: other_side(g, i, 1))

    k1 = first_kernel.transpose(2, 3, 4, 1, 0).reshape(27, 4, 32)
    k2 = second_kernel.transpose(2, 3, 4, 1, 0).reshape(864, 64)

    features, act_grad, kept, sent = call(
        functools.partial(main_kernel, rows_y),
        [((64, 256), BF16), ((32, 16, MID), F32), ((144, 256), F32), ((144, 256), F32)],
        32,
        [
            ((144, 64), F32),
            ((19, 8, FINE), F32),
            ((NF, 144, OWN), BF16),
            ((NF, 64, OWN), F32),
            ((NF, 32, KEPT), BF16),
            ((NF + 2, 288, COARSE), BF16),
            ((NS, 64, MID), F32),
            ((9, 64, COARSE), F32),
            ((20, 64, MID), BF16),
            ((NS + 2, 576, MID), BF16),
            ((16, 64, MID), BF16),
            ((288, 256), F32),
        ],
    )(
        own,
        cot,
        got_x,
        got_near,
        got_far,
        got_x_near,
        got_x_far,
        k1,
        k2,
    )
    swap = [(0, 1), (1, 0)]
    part = (kept + lax.ppermute(sent, "gx", swap)).astype(BF16)
    part = sum_of_group(part, "dp").astype(BF16)
    mine = sum_of_group(part, "yz")
    other = lax.ppermute(mine, "gx", swap)
    second, first = call(
        unpack_kernel, [((3, 288, 64), F32), ((27, 4, 32), F32)], 8
    )(mine, other)
    return (
        features.reshape(1, 64, 1, 1, 256),
        act_grad.reshape(1, 32, 1, 1, 2048),
        first.reshape(3, 3, 3, 4, 32).transpose(4, 3, 0, 1, 2),
        second.reshape(3, 3, 3, 32, 64).transpose(4, 3, 0, 1, 2),
    )


def solution(mesh):
    placed = (P("dp", None, "gx", "yz", None), P(), P(), P("dp", None, "gx", "yz", None))
    rows_y = min(4, mesh.shape["yz"])
    rows_z = mesh.shape["yz"] // rows_y
    if rows_z == 1 and rows_y == 4 and mesh.shape["gx"] == 2 and mesh.shape["dp"] in (1, 2, 4):
        body = functools.partial(on_device_kernels, rows_y)
    else:
        body = functools.partial(on_device_plain, rows_y, rows_z)
    return jax.shard_map(
        body,
        mesh=mesh,
        in_specs=placed,
        out_specs=(P("dp", None, "gx", "yz", None), P("dp", None, "gx", "yz", None), P(), P()),
        check_vma=False,
    )
```

```python
import functools

import jax
import jax.numpy as jnp
from jax import lax
from jax.experimental import pallas as pl
from jax.experimental.pallas import tpu as pltpu
from jax.sharding import PartitionSpec as P

CX = 32
CY = 32
CZ = 16
SLOPE = 0.3
F32 = jnp.float32
BF16 = jnp.bfloat16


def leaky(values):
    return jnp.where(values > 0, values, SLOPE * values)


def leaky_slope(values):
    return jnp.where(values > 0, jnp.float32(1.0), jnp.float32(SLOPE))


def convolve_valid(padded, kernel):
    return lax.conv_general_dilated(
        padded,
        kernel,
        (1, 1, 1),
        "VALID",
        dimension_numbers=("NCDHW", "OIDHW", "NCDHW"),
        preferred_element_type=F32,
    )


def kernel_grad(padded, grad):
    result = lax.conv_general_dilated(
        padded,
        grad,
        (1, 1, 1),
        "VALID",
        dimension_numbers=("CNDHW", "IODHW", "NCDHW"),
        preferred_element_type=F32,
    )
    return result.transpose(1, 0, 2, 3, 4)


def average_pool(values):
    bat, chan, xs, ys, zs = values.shape
    return values.reshape(bat, chan, xs // 2, 2, ys // 2, 2, zs // 2, 2).mean(axis=(3, 5, 7))


def spread_back(values):
    bat, chan, xs, ys, zs = values.shape
    grown = jnp.broadcast_to(
        values[:, :, :, None, :, None, :, None], (bat, chan, xs, 2, ys, 2, zs, 2)
    )
    return grown.reshape(bat, chan, 2 * xs, 2 * ys, 2 * zs) * 0.125


def unflatten(values, factor):
    return values[:, :, 0, 0].reshape(
        values.shape[0], values.shape[1], CX // factor, CY // factor, CZ // factor
    )


def flatten(values):
    return values.reshape(values.shape[0], values.shape[1], 1, 1, -1)


def extend_along(values, dim, axis, routes):
    size = values.shape[dim]
    first = lax.slice_in_dim(values, 0, 1, axis=dim)
    last = lax.slice_in_dim(values, size - 1, size, axis=dim)
    before = lax.ppermute(last, axis, routes)
    after = lax.ppermute(first, axis, [(b, a) for a, b in routes])
    return jnp.concatenate([before, values, after], axis=dim)


def extend(values, rows_y, rows_z):
    planes = lax.axis_size("gx")
    count = rows_y * rows_z
    values = extend_along(values, 2, "gx", [(i, i + 1) for i in range(planes - 1)])
    values = extend_along(values, 3, "yz", [(i, i + rows_z) for i in range(count - rows_z)])
    return extend_along(
        values, 4, "yz", [(i, i + 1) for i in range(count - 1) if (i + 1) % rows_z]
    )


def on_device_plain(rows_y, rows_z, volumes, first_kernel, second_kernel, cotangent):
    upstream = unflatten(cotangent, 4)
    padded_in = extend(unflatten(volumes, 1), rows_y, rows_z)
    pre_first = convolve_valid(padded_in, first_kernel)
    act_first = average_pool(leaky(pre_first)).astype(BF16)
    padded_mid = extend(act_first, rows_y, rows_z)
    pre_second = convolve_valid(padded_mid, second_kernel)
    features = average_pool(leaky(pre_second)).astype(BF16)
    grad_second = (spread_back(upstream.astype(F32)) * leaky_slope(pre_second)).astype(BF16)
    flipped = jnp.flip(second_kernel, (2, 3, 4)).transpose(1, 0, 2, 3, 4)
    act_grad = convolve_valid(extend(grad_second, rows_y, rows_z), flipped)
    grad_first = (spread_back(act_grad) * leaky_slope(pre_first)).astype(BF16)
    first_grad, second_grad = lax.psum(
        (kernel_grad(padded_in, grad_first), kernel_grad(padded_mid, grad_second)),
        ("dp", "gx", "yz"),
    )
    return (flatten(features), flatten(act_grad), first_grad, second_grad)


FINE = 48 * CZ
KEPT = 40 * CZ
OWN = CY * CZ
COARSE = 256
MID = (CY // 2) * (CZ // 2)
NF = 18
NS = 17


def grid(shape):
    return [lax.broadcasted_iota(jnp.int32, shape, dim) for dim in range(2)]


def one_where(condition, value=1.0):
    return jnp.where(condition, value, 0.0).astype(BF16)


def fine_to_mid(lane):
    return (lane >> 5) * 8 + ((lane & 15) >> 1) + jnp.where(lane >= OWN + 64, 96, 0)


def rim_table():
    row, lane = grid((256, 256))
    edge = jnp.where(lane < 128, 0, 7)
    place = (row >> 5) * 4 + (row & 3)
    return one_where(jnp.logical_and(((row >> 2) & 7) == edge, place == (lane & 127)))


def pool_first_table():
    row, lane = grid((KEPT, COARSE))
    place = jnp.where((row & 17) == 0, fine_to_mid(row), -1)
    return one_where(place == lane)


def spread_first_table():
    row, lane = grid((MID, OWN))
    return one_where(fine_to_mid(lane) == row, 0.125)


def pool_second_table():
    row, lane = grid((MID, 128))
    place = jnp.where((row & 9) == 0, (row >> 4) * 4 + ((row & 7) >> 1), -1)
    return one_where(place == lane)


def spread_second_table():
    row, lane = grid((128, COARSE))
    place = jnp.where(lane < MID, (lane >> 4) * 4, jnp.where(lane < 192, 32, 36))
    place = place + ((lane & 7) >> 1)
    used = jnp.logical_or(lane < MID + 8, lane >= COARSE - 8)
    return one_where(jnp.logical_and(used, place == row), 0.125)


def fold_rows(values):
    lane = grid((16, 128))[1]
    kept = [
        jnp.where(lane < 32, values[16 * q : 16 * q + 16], jnp.zeros((16, 128), F32))
        for q in range(4)
    ]
    return kept[0] + sum(pltpu.roll(kept[q], 32 * q, 1) for q in range(1, 4))


def unfold_rows(values):
    parts = [values] + [pltpu.roll(values, 128 - 32 * q, 1) for q in range(1, 4)]
    return jnp.concatenate(parts, axis=0)


def dot(a, b):
    return jnp.dot(a, b, preferred_element_type=F32)


def dot_lanes(a, b):
    return lax.dot_general(a, b, (((1,), (1,)), ((), ())), preferred_element_type=F32)


def pack_kernel(vol_ref, cot_ref, own_ref, x_ref, near_ref, far_ref, xnear_ref, xfar_ref):
    gx = lax.axis_index("gx")
    odd = lax.axis_index("yz") % 2
    own_ref[0:8, :] = jnp.zeros((8, OWN), F32)
    own_ref[128:136, :] = jnp.zeros((8, OWN), F32)
    for x in range(CX):
        own_ref[4 + 4 * x : 8 + 4 * x, :] = vol_ref[:, x * OWN : (x + 1) * OWN].astype(F32)
    start = pl.multiple_of(112 * (1 - gx), 8)
    blank = jnp.zeros((8, OWN), F32)
    face = jnp.concatenate([own_ref[pl.ds(start, 24), :], blank])
    x_ref[0:32, :] = face.astype(BF16)
    cot = cot_ref[...]
    wide = cot.astype(F32)
    first = gx == 0
    end = jnp.where(first, pltpu.roll(wide[:, 128:256], 32, 1), wide[:, 0:128])
    x_ref[32:48, 0:128] = fold_rows(end).astype(BF16)
    x_ref[32:48, 128:OWN] = jnp.zeros((16, OWN - 128), BF16)
    rims = dot(cot, rim_table())
    for low, side_ref, xside_ref in ((odd, near_ref, xnear_ref), (1 - odd, far_ref, xfar_ref)):
        lanes = pl.ds(pl.multiple_of((OWN - 128) * (1 - low), 128), 128)
        tail = jnp.concatenate([own_ref[128:136, lanes], blank[:, 0:128]])
        side_ref[0:128, :] = own_ref[0:128, lanes].astype(BF16)
        side_ref[128:144, :] = tail.astype(BF16)
        edge = jnp.concatenate([own_ref[pl.ds(start, 24), lanes], blank[:, 0:128]])
        xside_ref[0:32, :] = edge.astype(BF16)
        rim = jnp.where(low == 1, rims[:, 0:128], rims[:, 128:256])
        side_ref[144:160, :] = fold_rows(rim).astype(BF16)
        corner = jnp.where(first, pltpu.roll(rim, 100, 1), rim)
        xside_ref[32:48, :] = fold_rows(corner).astype(BF16)


def shifted(tile, period, lane):
    size = tile.shape[1]
    z = lane % period
    blank = jnp.zeros_like(tile)
    along = (
        jnp.where(z == 0, blank, pltpu.roll(tile, 1, 1)),
        tile,
        jnp.where(z == period - 1, blank, pltpu.roll(tile, size - 1, 1)),
    )
    return [
        pltpu.roll(moved, shift, 1) if shift else moved
        for shift in (period, 0, size - period)
        for moved in along
    ]


def pooled(values, period):
    size = values.shape[1]
    values = values + pltpu.roll(values, size - 1, 1)
    values = values + pltpu.roll(values, size - period, 1)
    return (values * 0.125).astype(BF16)


def split(values):
    top = values.astype(BF16)
    return jnp.concatenate([top, (values - top.astype(F32)).astype(BF16)], axis=0)


def main_kernel(
    rows_y,
    own_ref,
    cot_ref,
    rx_ref,
    rnear_ref,
    rfar_ref,
    rxnear_ref,
    rxfar_ref,
    k1_ref,
    k2_ref,
    features_ref,
    act_grad_ref,
    kept_ref,
    sent_ref,
    w1_rows,
    vol,
    cols_first,
    pre_first,
    pooled_first,
    cols_second,
    act_second,
    spread_up,
    grad_own,
    cols_grad,
    half_grad,
    grads_ref,
    k2,
    sems,
):
    copy = pltpu.make_async_copy(k2_ref, k2, sems.at[0])
    copy.start()
    gx = lax.axis_index("gx")
    block_y = lax.axis_index("yz")

    odd = block_y % 2 == 1
    inner = jnp.logical_and(block_y > 0, block_y < rows_y - 1)

    def above_below(near, far):
        near, far = near.astype(F32), far.astype(F32)
        far = jnp.where(inner, far, jnp.zeros_like(far))
        return jnp.where(odd, far, near), jnp.where(odd, near, far)

    w1_rows[...] = jnp.zeros_like(w1_rows)
    for dx in range(3):
        for at in range(9):
            block = k1_ref[dx * 9 + at].astype(F32)
            for k in range(2):
                row = at * 16 + 4 * (dx + k)
                w1_rows[row : row + 4, 32 * k : 32 * k + 32] = block
    w1 = w1_rows[...].T.astype(BF16)

    vol[...] = jnp.zeros_like(vol)
    up, down = above_below(rnear_ref[0:144, :], rfar_ref[0:144, :])
    vol[pl.ds(2 * gx, 17), :, OWN : OWN + 128] = up[0:136].reshape(17, 8, 128)
    vol[pl.ds(2 * gx, 17), :, OWN + 128 : FINE] = down[0:136].reshape(17, 8, 128)
    vol[pl.ds(2 * gx, 17), :, 0:OWN] = own_ref[...]
    end = pl.ds(16 * (1 - gx), 3)
    vol[end, :, 0:OWN] += rx_ref[0:32, :].astype(F32)[0:24].reshape(3, 8, OWN)
    up, down = above_below(rxnear_ref[0:32, :], rxfar_ref[0:32, :])
    vol[end, :, OWN : OWN + 128] += up[0:24].reshape(3, 8, 128)
    vol[end, :, OWN + 128 : FINE] += down[0:24].reshape(3, 8, 128)

    lane_fine = lax.broadcasted_iota(jnp.int32, (16, FINE), 1)
    near = lax.broadcasted_iota(jnp.int32, (16, 128), 1) < 64
    for j in range(NF):
        tile = jnp.concatenate([vol[j], vol[j + 1]], axis=0).astype(BF16)
        parts = []
        for moved in shifted(tile, CZ, lane_fine):
            edge = jnp.where(near, moved[:, OWN : OWN + 128], moved[:, OWN + 128 : FINE])
            parts.append(jnp.concatenate([moved[:, 0:OWN], edge], axis=1))
        cols = jnp.concatenate(parts, axis=0)
        cols_first[j] = cols[:, 0:OWN]
        pre = dot(w1, cols)
        pre_first[j] = pre[:, 0:OWN]
        sloped = leaky(pre)
        pooled_first[j] = pooled(sloped[0:32] + sloped[32:64], CZ)

    lane = lax.broadcasted_iota(jnp.int32, (32, COARSE), 1)
    valid = jnp.logical_or(
        lane < MID,
        jnp.logical_or(
            jnp.logical_and(lane < 192, block_y < rows_y - 1),
            jnp.logical_and(lane >= 192, block_y > 0),
        ),
    )
    cols_second[0] = jnp.zeros((288, COARSE), BF16)
    cols_second[NF + 1] = jnp.zeros((288, COARSE), BF16)
    pick = pool_first_table()
    for step in range(3):
        picked = dot(pooled_first[6 * step : 6 * step + 6].reshape(192, KEPT), pick)
        for k in range(6):
            plane = jnp.where(valid, picked[k * 32 : k * 32 + 32], 0.0).astype(BF16)
            parts = shifted(plane, CZ // 2, lane)
            cols_second[6 * step + k + 1] = jnp.concatenate(parts, axis=0)

    slot = grid((64, 128))[1]

    def upstream(plane, up, down):
        return jnp.where(slot < 32, plane, jnp.where(slot < 36, up, down)).astype(BF16)

    def moved_to(values, lane_from, lane_to):
        shift = (lane_to - lane_from) % 128
        return pltpu.roll(values, shift, 1) if shift else values

    cot = cot_ref[...].astype(F32)
    up, down = above_below(rnear_ref[144:160, :], rfar_ref[144:160, :])
    up, down = unfold_rows(up), unfold_rows(down)
    planes = [
        upstream(
            moved_to(cot[:, p // 4 * 128 : p // 4 * 128 + 128], p % 4 * 32, 0),
            moved_to(up, 4 * p, 32),
            moved_to(down, 4 * p, 36),
        )
        for p in range(8)
    ]
    up, down = above_below(rxnear_ref[32:48, :], rxfar_ref[32:48, :])
    planes.append(
        upstream(
            unfold_rows(rx_ref[32:48, 0:128].astype(F32)),
            moved_to(unfold_rows(up), 0, 32),
            moved_to(unfold_rows(down), 0, 36),
        )
    )
    spread = dot(jnp.concatenate(planes, axis=0), spread_second_table())
    for p in range(8):
        spread_up[p + gx] = spread[64 * p : 64 * p + 64]
    spread_up[8 * (1 - gx)] = spread[512:576]

    copy.wait()
    wide = k2[...].astype(F32)
    w2 = wide.T.astype(BF16)
    w3 = jnp.concatenate([wide[32 * n : 32 * n + 32] for n in range(26, -1, -1)], axis=1)
    w3 = w3.astype(BF16)
    lane_grad = lax.broadcasted_iota(jnp.int32, (64, COARSE), 1)
    cols_grad[0] = jnp.zeros((576, MID), BF16)
    cols_grad[NS + 1] = jnp.zeros((576, MID), BF16)
    for k in (0, 1, 18, 19):
        grad_own[k] = jnp.zeros((64, MID), BF16)
    for k in range(NS):
        pre = dot(w2, cols_second[pl.ds(k + gx, 3)].reshape(864, COARSE))
        act_second[k] = leaky(pre[:, 0:MID])
        rounded = (spread_up[(k + gx) // 2] * leaky_slope(pre)).astype(BF16)
        parts = [moved[:, 0:MID] for moved in shifted(rounded, CZ // 2, lane_grad)]
        cols_grad[k + 1] = jnp.concatenate(parts, axis=0)
        kept = rounded[:, 0:MID]
        if k == 0:
            kept = jnp.where(gx == 0, kept, jnp.zeros_like(kept))
        if k == NS - 1:
            kept = jnp.where(gx == 1, kept, jnp.zeros_like(kept))
        grad_own[k + 2 - gx] = kept

    sums = [
        pooled(act_second[2 * p + gx] + act_second[2 * p + 1 + gx], CZ // 2) for p in range(8)
    ]
    picked = dot(jnp.concatenate(sums, axis=0), pool_second_table())
    for half in range(2):
        whole = picked[256 * half : 256 * half + 64]
        for k in range(1, 4):
            block = picked[256 * half + 64 * k : 256 * half + 64 * k + 64]
            whole = whole + pltpu.roll(block, 32 * k, 1)
        features_ref[:, 128 * half : 128 * half + 128] = whole.astype(BF16)

    for m in range(0, 16, 2):
        cols = jnp.concatenate(
            [
                cols_grad[pl.ds(m + gx, 3)].reshape(1728, MID),
                cols_grad[pl.ds(m + 1 + gx, 3)].reshape(1728, MID),
            ],
            axis=1,
        )
        back = dot(w3, cols)
        for k in range(2):
            plane = back[:, k * MID : (k + 1) * MID]
            act_grad_ref[:, m + k, :] = plane
            half_grad[m + k] = split(plane)

    total = jnp.zeros((288, 192), F32)
    for q in range(0, 18, 2):
        left = jnp.concatenate(
            [cols_second[q + 2 * gx][:, 0:MID], cols_second[q + 1 + 2 * gx][:, 0:MID]], axis=1
        )
        right = jnp.concatenate(
            [
                grad_own[q : q + 3].reshape(192, MID),
                grad_own[q + 1 : q + 4].reshape(192, MID),
            ],
            axis=1,
        )
        total = total + dot_lanes(left, right)
    grads_ref[:, 0:192] = total

    grow = spread_first_table()
    first = jnp.zeros((144, 64), F32)
    for step in range(4):
        spread = dot(half_grad[4 * step : 4 * step + 4].reshape(256, MID), grow)
        for k in range(4):
            m = 4 * step + k + 2 * gx
            whole = spread[k * 64 : k * 64 + 32] + spread[k * 64 + 32 : k * 64 + 64]
            slope = leaky_slope(pre_first[m])
            back = (jnp.concatenate([whole, whole], axis=0) * slope).astype(BF16)
            first = first + dot_lanes(cols_first[m], back)
    grads_ref[0:144, 192:256] = first
    grads_ref[144:288, 192:256] = jnp.zeros((144, 64), F32)
    for half_ref, half in ((kept_ref, gx), (sent_ref, 1 - gx)):
        for piece in range(4):
            rows = pl.ds(pl.multiple_of(144 * half + 72 * (piece // 2), 8), 72)
            half_ref[piece] = grads_ref[rows, 128 * (piece % 2) : 128 * (piece % 2) + 128]


def unpack_kernel(mine_ref, other_ref, second_ref, first_ref, halves):
    gx = lax.axis_index("gx")
    dp = lax.axis_index("dp")
    for k in range(4):
        halves[gx, dp ^ k] = mine_ref[k].astype(F32)
        halves[1 - gx, dp ^ k] = other_ref[k].astype(F32)
    for half in range(2):
        for k in range(2):
            rows = slice(half * 144 + k * 72, half * 144 + k * 72 + 72)
            second_ref[2, rows] = halves[half, 2 * k, :, 0:64]
            second_ref[1, rows] = halves[half, 2 * k, :, 64:128]
            second_ref[0, rows] = halves[half, 2 * k + 1, :, 0:64]
    both = jnp.concatenate([halves[0, 1], halves[0, 3]], axis=0)[:, 64:128]
    for at in range(9):
        part = both[at * 16 : at * 16 + 16]
        for dx in range(3):
            first_ref[dx * 9 + at] = (
                part[4 * dx : 4 * dx + 4, 0:32] + part[4 * dx + 4 : 4 * dx + 8, 32:64]
            )


def call(kernel, outs, limit, scratch=(), in_specs=None, semaphores=0):
    held = [pltpu.VMEM(shape, dtype) for shape, dtype in scratch]
    if semaphores:
        held.append(pltpu.SemaphoreType.DMA((semaphores,)))
    return pl.pallas_call(
        kernel,
        out_shape=[jax.ShapeDtypeStruct(shape, dtype) for shape, dtype in outs],
        scratch_shapes=held,
        compiler_params=pltpu.CompilerParams(vmem_limit_bytes=limit * 1024 * 1024),
        **({} if in_specs is None else {"in_specs": in_specs}),
    )


def in_hbm(values):
    return pltpu.with_memory_space_constraint(values, pltpu.HBM)


def swapped(values, axis, k):
    return lax.ppermute(values, axis, [(i, i ^ k) for i in range(lax.axis_size(axis))])


def added(terms):
    terms = [term.astype(F32) for term in terms]
    return ((terms[0] + terms[1]) + (terms[2] + terms[3])).astype(BF16)


def on_device_kernels(rows_y, volumes, first_kernel, second_kernel, cotangent):
    cot = cotangent.reshape(64, 256)
    own, x_face, near, far, x_near, x_far = call(
        pack_kernel,
        [
            ((136, OWN), F32),
            ((48, OWN), BF16),
            ((160, 128), BF16),
            ((160, 128), BF16),
            ((48, 128), BF16),
            ((48, 128), BF16),
        ],
        16,
    )(in_hbm(volumes.reshape(4, CX * OWN)), in_hbm(cot))

    def paired(values, partner):
        routes = [
            (g * rows_y + i, partner(g, i)) for g in range(2) for i in range(rows_y)
        ]
        return lax.ppermute(values, ("gx", "yz"), routes)

    def other_side(g, i, across):
        j = i + (1 if i % 2 else -1)
        if 0 <= j < rows_y:
            return (g ^ across) * rows_y + j
        return (1 - g) * rows_y + i

    got_near = lax.ppermute(near, "yz", [(i, i ^ 1) for i in range(rows_y)])
    got_far = paired(far, lambda g, i: other_side(g, i, 0))
    got_x = lax.ppermute(x_face, "gx", [(0, 1), (1, 0)])
    got_x_near = paired(x_near, lambda g, i: (1 - g) * rows_y + (i ^ 1))
    got_x_far = paired(x_far, lambda g, i: other_side(g, i, 1))

    k1 = first_kernel.transpose(2, 3, 4, 1, 0).reshape(27, 4, 32)
    k2 = second_kernel.transpose(2, 3, 4, 1, 0).reshape(864, 64)

    whole = pl.BlockSpec(memory_space=pltpu.VMEM)
    apart = pl.BlockSpec(memory_space=pltpu.HBM)
    features, act_grad, kept, sent = call(
        functools.partial(main_kernel, rows_y),
        [((64, 256), BF16), ((32, 16, MID), F32), ((4, 72, 128), F32), ((4, 72, 128), F32)],
        32,
        [
            ((144, 64), F32),
            ((19, 8, FINE), F32),
            ((NF, 144, OWN), BF16),
            ((NF, 64, OWN), F32),
            ((NF, 32, KEPT), BF16),
            ((NF + 2, 288, COARSE), BF16),
            ((NS, 64, MID), F32),
            ((9, 64, COARSE), F32),
            ((20, 64, MID), BF16),
            ((NS + 2, 576, MID), BF16),
            ((16, 64, MID), BF16),
            ((288, 256), F32),
            ((864, 64), BF16),
        ],
        [whole] * 8 + [apart],
        1,
    )(
        own.reshape(17, 8, OWN),
        cot,
        got_x,
        got_near,
        got_far,
        got_x_near,
        got_x_far,
        k1,
        in_hbm(k2),
    )
    pieces = (kept + swapped(sent, "gx", 1)).astype(BF16)
    place = lax.axis_index("dp")

    def piece_of(k):
        return lax.dynamic_index_in_dim(pieces, place ^ k, 0, keepdims=False)

    piece = added([piece_of(0)] + [swapped(piece_of(k), "dp", k) for k in range(1, 4)])
    piece = added([piece] + [swapped(piece, "yz", k) for k in range(1, 4)])
    mine = jnp.stack([piece] + [swapped(piece, "dp", k) for k in range(1, 4)])
    other = swapped(mine, "gx", 1)
    second, first = call(
        unpack_kernel,
        [((3, 288, 64), F32), ((27, 4, 32), F32)],
        8,
        [((2, 4, 72, 128), F32)],
    )(mine, other)
    return (
        features.reshape(1, 64, 1, 1, 256),
        act_grad.reshape(1, 32, 1, 1, 2048),
        first.reshape(3, 3, 3, 4, 32).transpose(4, 3, 0, 1, 2),
        second.reshape(3, 3, 3, 32, 64).transpose(4, 3, 0, 1, 2),
    )


def solution(mesh):
    placed = (P("dp", None, "gx", "yz", None), P(), P(), P("dp", None, "gx", "yz", None))
    rows_y = min(4, mesh.shape["yz"])
    rows_z = mesh.shape["yz"] // rows_y
    if rows_z == 1 and rows_y == 4 and mesh.shape["gx"] == 2 and mesh.shape["dp"] == 4:
        body = functools.partial(on_device_kernels, rows_y)
    else:
        body = functools.partial(on_device_plain, rows_y, rows_z)
    return jax.shard_map(
        body,
        mesh=mesh,
        in_specs=placed,
        out_specs=(P("dp", None, "gx", "yz", None), P("dp", None, "gx", "yz", None), P(), P()),
        check_vma=False,
    )
```

```python
import functools

import jax
import jax.numpy as jnp
from jax import lax
from jax.experimental import pallas as pl
from jax.experimental.pallas import tpu as pltpu
from jax.sharding import PartitionSpec as P

CX = 32
CY = 32
CZ = 16
SLOPE = 0.3
F32 = jnp.float32
BF16 = jnp.bfloat16


def leaky(values):
    return jnp.where(values > 0, values, SLOPE * values)


def leaky_slope(values):
    return jnp.where(values > 0, jnp.float32(1.0), jnp.float32(SLOPE))


def convolve_valid(padded, kernel):
    return lax.conv_general_dilated(
        padded,
        kernel,
        (1, 1, 1),
        "VALID",
        dimension_numbers=("NCDHW", "OIDHW", "NCDHW"),
        preferred_element_type=F32,
    )


def kernel_grad(padded, grad):
    result = lax.conv_general_dilated(
        padded,
        grad,
        (1, 1, 1),
        "VALID",
        dimension_numbers=("CNDHW", "IODHW", "NCDHW"),
        preferred_element_type=F32,
    )
    return result.transpose(1, 0, 2, 3, 4)


def average_pool(values):
    bat, chan, xs, ys, zs = values.shape
    return values.reshape(bat, chan, xs // 2, 2, ys // 2, 2, zs // 2, 2).mean(axis=(3, 5, 7))


def spread_back(values):
    bat, chan, xs, ys, zs = values.shape
    grown = jnp.broadcast_to(
        values[:, :, :, None, :, None, :, None], (bat, chan, xs, 2, ys, 2, zs, 2)
    )
    return grown.reshape(bat, chan, 2 * xs, 2 * ys, 2 * zs) * 0.125


def unflatten(values, factor):
    return values[:, :, 0, 0].reshape(
        values.shape[0], values.shape[1], CX // factor, CY // factor, CZ // factor
    )


def flatten(values):
    return values.reshape(values.shape[0], values.shape[1], 1, 1, -1)


def extend_along(values, dim, axis, routes):
    size = values.shape[dim]
    first = lax.slice_in_dim(values, 0, 1, axis=dim)
    last = lax.slice_in_dim(values, size - 1, size, axis=dim)
    before = lax.ppermute(last, axis, routes)
    after = lax.ppermute(first, axis, [(b, a) for a, b in routes])
    return jnp.concatenate([before, values, after], axis=dim)


def extend(values, rows_y, rows_z):
    planes = lax.axis_size("gx")
    count = rows_y * rows_z
    values = extend_along(values, 2, "gx", [(i, i + 1) for i in range(planes - 1)])
    values = extend_along(values, 3, "yz", [(i, i + rows_z) for i in range(count - rows_z)])
    return extend_along(
        values, 4, "yz", [(i, i + 1) for i in range(count - 1) if (i + 1) % rows_z]
    )


def on_device_plain(rows_y, rows_z, volumes, first_kernel, second_kernel, cotangent):
    upstream = unflatten(cotangent, 4)
    padded_in = extend(unflatten(volumes, 1), rows_y, rows_z)
    pre_first = convolve_valid(padded_in, first_kernel)
    act_first = average_pool(leaky(pre_first)).astype(BF16)
    padded_mid = extend(act_first, rows_y, rows_z)
    pre_second = convolve_valid(padded_mid, second_kernel)
    features = average_pool(leaky(pre_second)).astype(BF16)
    grad_second = (spread_back(upstream.astype(F32)) * leaky_slope(pre_second)).astype(BF16)
    flipped = jnp.flip(second_kernel, (2, 3, 4)).transpose(1, 0, 2, 3, 4)
    act_grad = convolve_valid(extend(grad_second, rows_y, rows_z), flipped)
    grad_first = (spread_back(act_grad) * leaky_slope(pre_first)).astype(BF16)
    first_grad, second_grad = lax.psum(
        (kernel_grad(padded_in, grad_first), kernel_grad(padded_mid, grad_second)),
        ("dp", "gx", "yz"),
    )
    return (flatten(features), flatten(act_grad), first_grad, second_grad)


FINE = 48 * CZ
KEPT = 40 * CZ
OWN = CY * CZ
COARSE = 256
MID = (CY // 2) * (CZ // 2)
NF = 18
NS = 17


def grid(shape):
    return [lax.broadcasted_iota(jnp.int32, shape, dim) for dim in range(2)]


def one_where(condition, value=1.0):
    return jnp.where(condition, value, 0.0).astype(BF16)


def fine_to_mid(lane):
    return (lane >> 5) * 8 + ((lane & 15) >> 1) + jnp.where(lane >= OWN + 64, 96, 0)


def rim_table():
    row, lane = grid((256, 256))
    edge = jnp.where(lane < 128, 0, 7)
    place = (row >> 5) * 4 + (row & 3)
    return one_where(jnp.logical_and(((row >> 2) & 7) == edge, place == (lane & 127)))


def pool_first_table():
    row, lane = grid((KEPT, COARSE))
    place = jnp.where((row & 17) == 0, fine_to_mid(row), -1)
    return one_where(place == lane)


def spread_first_table():
    row, lane = grid((MID, OWN))
    return one_where(fine_to_mid(lane) == row, 0.125)


def pool_second_table():
    row, lane = grid((MID, 128))
    place = jnp.where((row & 9) == 0, (row >> 4) * 4 + ((row & 7) >> 1), -1)
    return one_where(place == lane)


def spread_second_table():
    row, lane = grid((128, COARSE))
    place = jnp.where(lane < MID, (lane >> 4) * 4, jnp.where(lane < 192, 32, 36))
    place = place + ((lane & 7) >> 1)
    used = jnp.logical_or(lane < MID + 8, lane >= COARSE - 8)
    return one_where(jnp.logical_and(used, place == row), 0.125)


def fold_rows(values):
    lane = grid((16, 128))[1]
    kept = [
        jnp.where(lane < 32, values[16 * q : 16 * q + 16], jnp.zeros((16, 128), F32))
        for q in range(4)
    ]
    return kept[0] + sum(pltpu.roll(kept[q], 32 * q, 1) for q in range(1, 4))


def unfold_rows(values):
    parts = [values] + [pltpu.roll(values, 128 - 32 * q, 1) for q in range(1, 4)]
    return jnp.concatenate(parts, axis=0)


def dot(a, b):
    return jnp.dot(a, b, preferred_element_type=F32)


def dot_lanes(a, b):
    return lax.dot_general(a, b, (((1,), (1,)), ((), ())), preferred_element_type=F32)


def pack_kernel(vol_ref, cot_ref, own_ref, x_ref, near_ref, far_ref, xnear_ref, xfar_ref):
    gx = lax.axis_index("gx")
    odd = lax.axis_index("yz") % 2
    own_ref[0:8, :] = jnp.zeros((8, OWN), F32)
    own_ref[128:136, :] = jnp.zeros((8, OWN), F32)
    for x in range(CX):
        own_ref[4 + 4 * x : 8 + 4 * x, :] = vol_ref[:, x * OWN : (x + 1) * OWN].astype(F32)
    start = pl.multiple_of(112 * (1 - gx), 8)
    blank = jnp.zeros((8, OWN), F32)
    face = jnp.concatenate([own_ref[pl.ds(start, 24), :], blank])
    x_ref[0:32, :] = face.astype(BF16)
    cot = cot_ref[...]
    wide = cot.astype(F32)
    first = gx == 0
    end = jnp.where(first, pltpu.roll(wide[:, 128:256], 32, 1), wide[:, 0:128])
    x_ref[32:48, 0:128] = fold_rows(end).astype(BF16)
    x_ref[32:48, 128:OWN] = jnp.zeros((16, OWN - 128), BF16)
    rims = dot(cot, rim_table())
    for low, side_ref, xside_ref in ((odd, near_ref, xnear_ref), (1 - odd, far_ref, xfar_ref)):
        lanes = pl.ds(pl.multiple_of((OWN - 128) * (1 - low), 128), 128)
        tail = jnp.concatenate([own_ref[128:136, lanes], blank[:, 0:128]])
        side_ref[0:128, :] = own_ref[0:128, lanes].astype(BF16)
        side_ref[128:144, :] = tail.astype(BF16)
        edge = jnp.concatenate([own_ref[pl.ds(start, 24), lanes], blank[:, 0:128]])
        xside_ref[0:32, :] = edge.astype(BF16)
        rim = jnp.where(low == 1, rims[:, 0:128], rims[:, 128:256])
        side_ref[144:160, :] = fold_rows(rim).astype(BF16)
        corner = jnp.where(first, pltpu.roll(rim, 100, 1), rim)
        xside_ref[32:48, :] = fold_rows(corner).astype(BF16)


def shifted(tile, period, lane):
    size = tile.shape[1]
    z = lane % period
    blank = jnp.zeros_like(tile)
    along = (
        jnp.where(z == 0, blank, pltpu.roll(tile, 1, 1)),
        tile,
        jnp.where(z == period - 1, blank, pltpu.roll(tile, size - 1, 1)),
    )
    return [
        pltpu.roll(moved, shift, 1) if shift else moved
        for shift in (period, 0, size - period)
        for moved in along
    ]


def pooled(values, period):
    size = values.shape[1]
    values = values + pltpu.roll(values, size - 1, 1)
    values = values + pltpu.roll(values, size - period, 1)
    return (values * 0.125).astype(BF16)


def split(values):
    top = values.astype(BF16)
    return jnp.concatenate([top, (values - top.astype(F32)).astype(BF16)], axis=0)


def main_kernel(
    rows_y,
    own_ref,
    cot_ref,
    rx_ref,
    rnear_ref,
    rfar_ref,
    rxnear_ref,
    rxfar_ref,
    k1_ref,
    k2_ref,
    features_ref,
    act_grad_ref,
    pieces_ref,
    w1_rows,
    vol,
    cols_first,
    pre_first,
    pooled_first,
    cols_second,
    act_second,
    spread_up,
    grad_own,
    cols_grad,
    half_grad,
    grads_ref,
):
    gx = lax.axis_index("gx")
    block_y = lax.axis_index("yz")

    odd = block_y % 2 == 1
    inner = jnp.logical_and(block_y > 0, block_y < rows_y - 1)

    def above_below(near, far):
        near, far = near.astype(F32), far.astype(F32)
        far = jnp.where(inner, far, jnp.zeros_like(far))
        return jnp.where(odd, far, near), jnp.where(odd, near, far)

    w1_rows[...] = jnp.zeros_like(w1_rows)
    for dx in range(3):
        for at in range(9):
            block = k1_ref[dx * 9 + at].astype(F32)
            for k in range(2):
                row = at * 16 + 4 * (dx + k)
                w1_rows[row : row + 4, 32 * k : 32 * k + 32] = block
    w1 = w1_rows[...].T.astype(BF16)

    vol[...] = jnp.zeros_like(vol)
    up, down = above_below(rnear_ref[0:144, :], rfar_ref[0:144, :])
    vol[pl.ds(2 * gx, 17), :, OWN : OWN + 128] = up[0:136].reshape(17, 8, 128)
    vol[pl.ds(2 * gx, 17), :, OWN + 128 : FINE] = down[0:136].reshape(17, 8, 128)
    vol[pl.ds(2 * gx, 17), :, 0:OWN] = own_ref[...]
    end = pl.ds(16 * (1 - gx), 3)
    vol[end, :, 0:OWN] += rx_ref[0:32, :].astype(F32)[0:24].reshape(3, 8, OWN)
    up, down = above_below(rxnear_ref[0:32, :], rxfar_ref[0:32, :])
    vol[end, :, OWN : OWN + 128] += up[0:24].reshape(3, 8, 128)
    vol[end, :, OWN + 128 : FINE] += down[0:24].reshape(3, 8, 128)

    lane_fine = lax.broadcasted_iota(jnp.int32, (16, FINE), 1)
    near = lax.broadcasted_iota(jnp.int32, (16, 128), 1) < 64
    for j in range(NF):
        tile = jnp.concatenate([vol[j], vol[j + 1]], axis=0).astype(BF16)
        parts = []
        for moved in shifted(tile, CZ, lane_fine):
            edge = jnp.where(near, moved[:, OWN : OWN + 128], moved[:, OWN + 128 : FINE])
            parts.append(jnp.concatenate([moved[:, 0:OWN], edge], axis=1))
        cols = jnp.concatenate(parts, axis=0)
        cols_first[j] = cols[:, 0:OWN]
        pre = dot(w1, cols)
        pre_first[j] = pre[:, 0:OWN]
        sloped = leaky(pre)
        pooled_first[j] = pooled(sloped[0:32] + sloped[32:64], CZ)

    lane = lax.broadcasted_iota(jnp.int32, (32, COARSE), 1)
    valid = jnp.logical_or(
        lane < MID,
        jnp.logical_or(
            jnp.logical_and(lane < 192, block_y < rows_y - 1),
            jnp.logical_and(lane >= 192, block_y > 0),
        ),
    )
    cols_second[0] = jnp.zeros((288, COARSE), BF16)
    cols_second[NF + 1] = jnp.zeros((288, COARSE), BF16)
    pick = pool_first_table()
    for step in range(3):
        picked = dot(pooled_first[6 * step : 6 * step + 6].reshape(192, KEPT), pick)
        for k in range(6):
            plane = jnp.where(valid, picked[k * 32 : k * 32 + 32], 0.0).astype(BF16)
            parts = shifted(plane, CZ // 2, lane)
            cols_second[6 * step + k + 1] = jnp.concatenate(parts, axis=0)

    slot = grid((64, 128))[1]

    def upstream(plane, up, down):
        return jnp.where(slot < 32, plane, jnp.where(slot < 36, up, down)).astype(BF16)

    def moved_to(values, lane_from, lane_to):
        shift = (lane_to - lane_from) % 128
        return pltpu.roll(values, shift, 1) if shift else values

    cot = cot_ref[...].astype(F32)
    up, down = above_below(rnear_ref[144:160, :], rfar_ref[144:160, :])
    up, down = unfold_rows(up), unfold_rows(down)
    planes = [
        upstream(
            moved_to(cot[:, p // 4 * 128 : p // 4 * 128 + 128], p % 4 * 32, 0),
            moved_to(up, 4 * p, 32),
            moved_to(down, 4 * p, 36),
        )
        for p in range(8)
    ]
    up, down = above_below(rxnear_ref[32:48, :], rxfar_ref[32:48, :])
    planes.append(
        upstream(
            unfold_rows(rx_ref[32:48, 0:128].astype(F32)),
            moved_to(unfold_rows(up), 0, 32),
            moved_to(unfold_rows(down), 0, 36),
        )
    )
    spread = dot(jnp.concatenate(planes, axis=0), spread_second_table())
    for p in range(8):
        spread_up[p + gx] = spread[64 * p : 64 * p + 64]
    spread_up[8 * (1 - gx)] = spread[512:576]

    wide = k2_ref[...].astype(F32)
    w2 = wide.T.astype(BF16)
    w3 = jnp.concatenate([wide[32 * n : 32 * n + 32] for n in range(26, -1, -1)], axis=1)
    w3 = w3.astype(BF16)
    lane_grad = lax.broadcasted_iota(jnp.int32, (64, COARSE), 1)
    cols_grad[0] = jnp.zeros((576, MID), BF16)
    cols_grad[NS + 1] = jnp.zeros((576, MID), BF16)
    for k in (0, 1, 18, 19):
        grad_own[k] = jnp.zeros((64, MID), BF16)
    for k in range(NS):
        pre = dot(w2, cols_second[pl.ds(k + gx, 3)].reshape(864, COARSE))
        act_second[k] = leaky(pre[:, 0:MID])
        rounded = (spread_up[(k + gx) // 2] * leaky_slope(pre)).astype(BF16)
        parts = [moved[:, 0:MID] for moved in shifted(rounded, CZ // 2, lane_grad)]
        cols_grad[k + 1] = jnp.concatenate(parts, axis=0)
        kept = rounded[:, 0:MID]
        if k == 0:
            kept = jnp.where(gx == 0, kept, jnp.zeros_like(kept))
        if k == NS - 1:
            kept = jnp.where(gx == 1, kept, jnp.zeros_like(kept))
        grad_own[k + 2 - gx] = kept

    sums = [
        pooled(act_second[2 * p + gx] + act_second[2 * p + 1 + gx], CZ // 2) for p in range(8)
    ]
    picked = dot(jnp.concatenate(sums, axis=0), pool_second_table())
    for half in range(2):
        whole = picked[256 * half : 256 * half + 64]
        for k in range(1, 4):
            block = picked[256 * half + 64 * k : 256 * half + 64 * k + 64]
            whole = whole + pltpu.roll(block, 32 * k, 1)
        features_ref[:, 128 * half : 128 * half + 128] = whole.astype(BF16)

    for m in range(0, 16, 2):
        cols = jnp.concatenate(
            [
                cols_grad[pl.ds(m + gx, 3)].reshape(1728, MID),
                cols_grad[pl.ds(m + 1 + gx, 3)].reshape(1728, MID),
            ],
            axis=1,
        )
        back = dot(w3, cols)
        for k in range(2):
            plane = back[:, k * MID : (k + 1) * MID]
            act_grad_ref[:, m + k, :] = plane
            half_grad[m + k] = split(plane)

    total = jnp.zeros((288, 192), F32)
    for q in range(0, 18, 2):
        left = jnp.concatenate(
            [cols_second[q + 2 * gx][:, 0:MID], cols_second[q + 1 + 2 * gx][:, 0:MID]], axis=1
        )
        right = jnp.concatenate(
            [
                grad_own[q : q + 3].reshape(192, MID),
                grad_own[q + 1 : q + 4].reshape(192, MID),
            ],
            axis=1,
        )
        total = total + dot_lanes(left, right)
    grads_ref[:, 0:192] = total

    grow = spread_first_table()
    first = jnp.zeros((144, 64), F32)
    for step in range(4):
        spread = dot(half_grad[4 * step : 4 * step + 4].reshape(256, MID), grow)
        for k in range(4):
            m = 4 * step + k + 2 * gx
            whole = spread[k * 64 : k * 64 + 32] + spread[k * 64 + 32 : k * 64 + 64]
            slope = leaky_slope(pre_first[m])
            back = (jnp.concatenate([whole, whole], axis=0) * slope).astype(BF16)
            first = first + dot_lanes(cols_first[m], back)
    grads_ref[0:144, 192:256] = first
    grads_ref[144:288, 192:256] = jnp.zeros((144, 64), F32)
    for piece in range(8):
        rows, lanes = 72 * (piece // 2), 128 * (piece % 2)
        pieces_ref[piece] = grads_ref[rows : rows + 72, lanes : lanes + 128].astype(BF16)


def unpack_kernel(pieces_ref, second_ref, first_ref):
    for k in range(4):
        rows = slice(k * 72, k * 72 + 72)
        left = pieces_ref[2 * k].astype(F32)
        second_ref[2, rows] = left[:, 0:64]
        second_ref[1, rows] = left[:, 64:128]
        second_ref[0, rows] = pieces_ref[2 * k + 1].astype(F32)[:, 0:64]
    both = jnp.concatenate([pieces_ref[1].astype(F32), pieces_ref[3].astype(F32)], axis=0)
    both = both[:, 64:128]
    for at in range(9):
        part = both[at * 16 : at * 16 + 16]
        for dx in range(3):
            first_ref[dx * 9 + at] = (
                part[4 * dx : 4 * dx + 4, 0:32] + part[4 * dx + 4 : 4 * dx + 8, 32:64]
            )


def call(kernel, outs, limit, scratch=()):
    return pl.pallas_call(
        kernel,
        out_shape=[jax.ShapeDtypeStruct(shape, dtype) for shape, dtype in outs],
        scratch_shapes=[pltpu.VMEM(shape, dtype) for shape, dtype in scratch],
        compiler_params=pltpu.CompilerParams(vmem_limit_bytes=limit * 1024 * 1024),
    )


def in_hbm(values):
    return pltpu.with_memory_space_constraint(values, pltpu.HBM)


def to_all(pieces, axes):
    return lax.all_to_all(pieces, axes, 0, 0)


def summed(pieces):
    return pieces.astype(F32).sum(axis=0).astype(BF16)


def copies_of(piece, axes):
    return jnp.broadcast_to(piece[None], (lax.axis_size(axes),) + piece.shape)


def on_device_kernels(rows_y, volumes, first_kernel, second_kernel, cotangent):
    cot = cotangent.reshape(64, 256)
    own, x_face, near, far, x_near, x_far = call(
        pack_kernel,
        [
            ((136, OWN), F32),
            ((48, OWN), BF16),
            ((160, 128), BF16),
            ((160, 128), BF16),
            ((48, 128), BF16),
            ((48, 128), BF16),
        ],
        16,
    )(in_hbm(volumes.reshape(4, CX * OWN)), in_hbm(cot))

    def paired(values, partner):
        routes = [
            (g * rows_y + i, partner(g, i)) for g in range(2) for i in range(rows_y)
        ]
        return lax.ppermute(values, ("gx", "yz"), routes)

    def other_side(g, i, across):
        j = i + (1 if i % 2 else -1)
        if 0 <= j < rows_y:
            return (g ^ across) * rows_y + j
        return (1 - g) * rows_y + i

    got_near = lax.ppermute(near, "yz", [(i, i ^ 1) for i in range(rows_y)])
    got_far = paired(far, lambda g, i: other_side(g, i, 0))
    got_x = lax.ppermute(x_face, "gx", [(0, 1), (1, 0)])
    got_x_near = paired(x_near, lambda g, i: (1 - g) * rows_y + (i ^ 1))
    got_x_far = paired(x_far, lambda g, i: other_side(g, i, 1))

    k1 = first_kernel.transpose(2, 3, 4, 1, 0).reshape(27, 4, 32)
    k2 = second_kernel.transpose(2, 3, 4, 1, 0).reshape(864, 64)

    features, act_grad, pieces = call(
        functools.partial(main_kernel, rows_y),
        [((64, 256), BF16), ((32, 16, MID), F32), ((8, 72, 128), BF16)],
        32,
        [
            ((144, 64), F32),
            ((19, 8, FINE), F32),
            ((NF, 144, OWN), BF16),
            ((NF, 64, OWN), F32),
            ((NF, 32, KEPT), BF16),
            ((NF + 2, 288, COARSE), BF16),
            ((NS, 64, MID), F32),
            ((9, 64, COARSE), F32),
            ((20, 64, MID), BF16),
            ((NS + 2, 576, MID), BF16),
            ((16, 64, MID), BF16),
            ((288, 256), F32),
        ],
    )(
        own.reshape(17, 8, OWN),
        cot,
        got_x,
        got_near,
        got_far,
        got_x_near,
        got_x_far,
        k1,
        in_hbm(k2),
    )
    plane = ("dp", "gx")
    piece = summed(to_all(pieces, plane))
    piece = summed(to_all(copies_of(piece, "yz"), "yz"))
    pieces = to_all(copies_of(piece, plane), plane)
    second, first = call(unpack_kernel, [((3, 288, 64), F32), ((27, 4, 32), F32)], 8)(pieces)
    return (
        features.reshape(1, 64, 1, 1, 256),
        act_grad.reshape(1, 32, 1, 1, 2048),
        first.reshape(3, 3, 3, 4, 32).transpose(4, 3, 0, 1, 2),
        second.reshape(3, 3, 3, 32, 64).transpose(4, 3, 0, 1, 2),
    )


def solution(mesh):
    placed = (P("dp", None, "gx", "yz", None), P(), P(), P("dp", None, "gx", "yz", None))
    rows_y = min(4, mesh.shape["yz"])
    rows_z = mesh.shape["yz"] // rows_y
    if rows_z == 1 and rows_y == 4 and mesh.shape["gx"] == 2 and mesh.shape["dp"] == 4:
        body = functools.partial(on_device_kernels, rows_y)
    else:
        body = functools.partial(on_device_plain, rows_y, rows_z)
    return jax.shard_map(
        body,
        mesh=mesh,
        in_specs=placed,
        out_specs=(P("dp", None, "gx", "yz", None), P("dp", None, "gx", "yz", None), P(), P()),
        check_vma=False,
    )
```

```python
import functools

import jax
import jax.numpy as jnp
import numpy as np
from jax import lax
from jax.experimental import pallas as pl
from jax.experimental.pallas import tpu as pltpu
from jax.sharding import PartitionSpec as P

CX = 32
CY = 32
CZ = 16
SLOPE = 0.3
F32 = jnp.float32
BF16 = jnp.bfloat16


def leaky(values):
    return jnp.where(values > 0, values, SLOPE * values)


def leaky_slope(values):
    return jnp.where(values > 0, jnp.float32(1.0), jnp.float32(SLOPE))


def convolve_valid(padded, kernel):
    return lax.conv_general_dilated(
        padded,
        kernel,
        (1, 1, 1),
        "VALID",
        dimension_numbers=("NCDHW", "OIDHW", "NCDHW"),
        preferred_element_type=F32,
    )


def kernel_grad(padded, grad):
    result = lax.conv_general_dilated(
        padded,
        grad,
        (1, 1, 1),
        "VALID",
        dimension_numbers=("CNDHW", "IODHW", "NCDHW"),
        preferred_element_type=F32,
    )
    return result.transpose(1, 0, 2, 3, 4)


def average_pool(values):
    bat, chan, xs, ys, zs = values.shape
    return values.reshape(bat, chan, xs // 2, 2, ys // 2, 2, zs // 2, 2).mean(axis=(3, 5, 7))


def spread_back(values):
    bat, chan, xs, ys, zs = values.shape
    grown = jnp.broadcast_to(
        values[:, :, :, None, :, None, :, None], (bat, chan, xs, 2, ys, 2, zs, 2)
    )
    return grown.reshape(bat, chan, 2 * xs, 2 * ys, 2 * zs) * 0.125


def unflatten(values, factor):
    return values[:, :, 0, 0].reshape(
        values.shape[0], values.shape[1], CX // factor, CY // factor, CZ // factor
    )


def flatten(values):
    return values.reshape(values.shape[0], values.shape[1], 1, 1, -1)


def extend_along(values, dim, axis, routes):
    size = values.shape[dim]
    first = lax.slice_in_dim(values, 0, 1, axis=dim)
    last = lax.slice_in_dim(values, size - 1, size, axis=dim)
    before = lax.ppermute(last, axis, routes)
    after = lax.ppermute(first, axis, [(b, a) for a, b in routes])
    return jnp.concatenate([before, values, after], axis=dim)


def extend(values, rows_y, rows_z):
    planes = lax.axis_size("gx")
    count = rows_y * rows_z
    values = extend_along(values, 2, "gx", [(i, i + 1) for i in range(planes - 1)])
    values = extend_along(values, 3, "yz", [(i, i + rows_z) for i in range(count - rows_z)])
    return extend_along(
        values, 4, "yz", [(i, i + 1) for i in range(count - 1) if (i + 1) % rows_z]
    )


def on_device_plain(rows_y, rows_z, volumes, first_kernel, second_kernel, cotangent):
    upstream = unflatten(cotangent, 4)
    padded_in = extend(unflatten(volumes, 1), rows_y, rows_z)
    pre_first = convolve_valid(padded_in, first_kernel)
    act_first = average_pool(leaky(pre_first)).astype(BF16)
    padded_mid = extend(act_first, rows_y, rows_z)
    pre_second = convolve_valid(padded_mid, second_kernel)
    features = average_pool(leaky(pre_second)).astype(BF16)
    grad_second = (spread_back(upstream.astype(F32)) * leaky_slope(pre_second)).astype(BF16)
    flipped = jnp.flip(second_kernel, (2, 3, 4)).transpose(1, 0, 2, 3, 4)
    act_grad = convolve_valid(extend(grad_second, rows_y, rows_z), flipped)
    grad_first = (spread_back(act_grad) * leaky_slope(pre_first)).astype(BF16)
    first_grad, second_grad = lax.psum(
        (kernel_grad(padded_in, grad_first), kernel_grad(padded_mid, grad_second)),
        ("dp", "gx", "yz"),
    )
    return (flatten(features), flatten(act_grad), first_grad, second_grad)


FINE = 48 * CZ
KEPT = 40 * CZ
OWN = CY * CZ
COARSE = 256
MID = (CY // 2) * (CZ // 2)
NF = 18
NS = 17


def grid(shape):
    return [lax.broadcasted_iota(jnp.int32, shape, dim) for dim in range(2)]


def one_where(condition, value=1.0):
    return jnp.where(condition, value, 0.0).astype(BF16)


def fine_to_mid(lane):
    return (lane >> 5) * 8 + ((lane & 15) >> 1) + jnp.where(lane >= OWN + 64, 96, 0)


def rim_table():
    row, lane = grid((256, 256))
    edge = jnp.where(lane < 128, 0, 7)
    place = (row >> 5) * 4 + (row & 3)
    return one_where(jnp.logical_and(((row >> 2) & 7) == edge, place == (lane & 127)))


def pool_first_table():
    row, lane = grid((KEPT, COARSE))
    place = jnp.where((row & 17) == 0, fine_to_mid(row), -1)
    return one_where(place == lane)


def spread_first_table():
    row, lane = grid((MID, OWN))
    return one_where(fine_to_mid(lane) == row, 0.125)


def pool_second_table():
    row, lane = grid((MID, 128))
    place = jnp.where((row & 9) == 0, (row >> 4) * 4 + ((row & 7) >> 1), -1)
    return one_where(place == lane)


def spread_second_table():
    row, lane = grid((128, COARSE))
    place = jnp.where(lane < MID, (lane >> 4) * 4, jnp.where(lane < 192, 32, 36))
    place = place + ((lane & 7) >> 1)
    used = jnp.logical_or(lane < MID + 8, lane >= COARSE - 8)
    return one_where(jnp.logical_and(used, place == row), 0.125)


def fold_rows(values):
    lane = grid((16, 128))[1]
    kept = [
        jnp.where(lane < 32, values[16 * q : 16 * q + 16], jnp.zeros((16, 128), F32))
        for q in range(4)
    ]
    return kept[0] + sum(pltpu.roll(kept[q], 32 * q, 1) for q in range(1, 4))


def unfold_rows(values):
    parts = [values] + [pltpu.roll(values, 128 - 32 * q, 1) for q in range(1, 4)]
    return jnp.concatenate(parts, axis=0)


def dot(a, b):
    return jnp.dot(a, b, preferred_element_type=F32)


def dot_lanes(a, b):
    return lax.dot_general(a, b, (((1,), (1,)), ((), ())), preferred_element_type=F32)


def pack_kernel(vol_ref, cot_ref, own_ref, x_ref, near_ref, far_ref, xnear_ref, xfar_ref):
    gx = lax.axis_index("gx")
    odd = lax.axis_index("yz") % 2
    own_ref[0:8, :] = jnp.zeros((8, OWN), F32)
    own_ref[128:136, :] = jnp.zeros((8, OWN), F32)
    for x in range(CX):
        own_ref[4 + 4 * x : 8 + 4 * x, :] = vol_ref[:, x * OWN : (x + 1) * OWN].astype(F32)
    start = pl.multiple_of(112 * (1 - gx), 8)
    blank = jnp.zeros((8, OWN), F32)
    face = jnp.concatenate([own_ref[pl.ds(start, 24), :], blank])
    x_ref[0:32, :] = face.astype(BF16)
    cot = cot_ref[...]
    wide = cot.astype(F32)
    first = gx == 0
    end = jnp.where(first, pltpu.roll(wide[:, 128:256], 32, 1), wide[:, 0:128])
    x_ref[32:48, 0:128] = fold_rows(end).astype(BF16)
    x_ref[32:48, 128:OWN] = jnp.zeros((16, OWN - 128), BF16)
    rims = dot(cot, rim_table())
    for low, side_ref, xside_ref in ((odd, near_ref, xnear_ref), (1 - odd, far_ref, xfar_ref)):
        lanes = pl.ds(pl.multiple_of((OWN - 128) * (1 - low), 128), 128)
        tail = jnp.concatenate([own_ref[128:136, lanes], blank[:, 0:128]])
        side_ref[0:128, :] = own_ref[0:128, lanes].astype(BF16)
        side_ref[128:144, :] = tail.astype(BF16)
        edge = jnp.concatenate([own_ref[pl.ds(start, 24), lanes], blank[:, 0:128]])
        xside_ref[0:32, :] = edge.astype(BF16)
        rim = jnp.where(low == 1, rims[:, 0:128], rims[:, 128:256])
        side_ref[144:160, :] = fold_rows(rim).astype(BF16)
        corner = jnp.where(first, pltpu.roll(rim, 100, 1), rim)
        xside_ref[32:48, :] = fold_rows(corner).astype(BF16)


def shifted(tile, period, lane):
    size = tile.shape[1]
    z = lane % period
    blank = jnp.zeros_like(tile)
    along = (
        jnp.where(z == 0, blank, pltpu.roll(tile, 1, 1)),
        tile,
        jnp.where(z == period - 1, blank, pltpu.roll(tile, size - 1, 1)),
    )
    return [
        pltpu.roll(moved, shift, 1) if shift else moved
        for shift in (period, 0, size - period)
        for moved in along
    ]


def pooled(values, period):
    size = values.shape[1]
    values = values + pltpu.roll(values, size - 1, 1)
    values = values + pltpu.roll(values, size - period, 1)
    return (values * 0.125).astype(BF16)


def split(values):
    top = values.astype(BF16)
    return jnp.concatenate([top, (values - top.astype(F32)).astype(BF16)], axis=0)


def main_kernel(
    rows_y,
    own_ref,
    cot_ref,
    rx_ref,
    rnear_ref,
    rfar_ref,
    rxnear_ref,
    rxfar_ref,
    k1_ref,
    k2_ref,
    features_ref,
    act_grad_ref,
    kept_ref,
    sent_ref,
    w1_rows,
    vol,
    cols_first,
    pre_first,
    pooled_first,
    cols_second,
    act_second,
    spread_up,
    grad_own,
    cols_grad,
    half_grad,
    grads_ref,
):
    gx = lax.axis_index("gx")
    block_y = lax.axis_index("yz")

    odd = block_y % 2 == 1
    inner = jnp.logical_and(block_y > 0, block_y < rows_y - 1)

    def above_below(near, far):
        near, far = near.astype(F32), far.astype(F32)
        far = jnp.where(inner, far, jnp.zeros_like(far))
        return jnp.where(odd, far, near), jnp.where(odd, near, far)

    w1_rows[...] = jnp.zeros_like(w1_rows)
    for dx in range(3):
        for at in range(9):
            block = k1_ref[dx * 9 + at].astype(F32)
            for k in range(2):
                row = at * 16 + 4 * (dx + k)
                w1_rows[row : row + 4, 32 * k : 32 * k + 32] = block
    w1 = w1_rows[...].T.astype(BF16)

    vol[...] = jnp.zeros_like(vol)
    up, down = above_below(rnear_ref[0:144, :], rfar_ref[0:144, :])
    vol[pl.ds(2 * gx, 17), :, OWN : OWN + 128] = up[0:136].reshape(17, 8, 128)
    vol[pl.ds(2 * gx, 17), :, OWN + 128 : FINE] = down[0:136].reshape(17, 8, 128)
    vol[pl.ds(2 * gx, 17), :, 0:OWN] = own_ref[...]
    end = pl.ds(16 * (1 - gx), 3)
    vol[end, :, 0:OWN] += rx_ref[0:32, :].astype(F32)[0:24].reshape(3, 8, OWN)
    up, down = above_below(rxnear_ref[0:32, :], rxfar_ref[0:32, :])
    vol[end, :, OWN : OWN + 128] += up[0:24].reshape(3, 8, 128)
    vol[end, :, OWN + 128 : FINE] += down[0:24].reshape(3, 8, 128)

    lane_fine = lax.broadcasted_iota(jnp.int32, (16, FINE), 1)
    near = lax.broadcasted_iota(jnp.int32, (16, 128), 1) < 64
    for j in range(NF):
        tile = jnp.concatenate([vol[j], vol[j + 1]], axis=0).astype(BF16)
        parts = []
        for moved in shifted(tile, CZ, lane_fine):
            edge = jnp.where(near, moved[:, OWN : OWN + 128], moved[:, OWN + 128 : FINE])
            parts.append(jnp.concatenate([moved[:, 0:OWN], edge], axis=1))
        cols = jnp.concatenate(parts, axis=0)
        cols_first[j] = cols[:, 0:OWN]
        pre = dot(w1, cols)
        pre_first[j] = pre[:, 0:OWN]
        sloped = leaky(pre)
        pooled_first[j] = pooled(sloped[0:32] + sloped[32:64], CZ)

    lane = lax.broadcasted_iota(jnp.int32, (32, COARSE), 1)
    valid = jnp.logical_or(
        lane < MID,
        jnp.logical_or(
            jnp.logical_and(lane < 192, block_y < rows_y - 1),
            jnp.logical_and(lane >= 192, block_y > 0),
        ),
    )
    cols_second[0] = jnp.zeros((288, COARSE), BF16)
    cols_second[NF + 1] = jnp.zeros((288, COARSE), BF16)
    pick = pool_first_table()
    for step in range(3):
        picked = dot(pooled_first[6 * step : 6 * step + 6].reshape(192, KEPT), pick)
        for k in range(6):
            plane = jnp.where(valid, picked[k * 32 : k * 32 + 32], 0.0).astype(BF16)
            parts = shifted(plane, CZ // 2, lane)
            cols_second[6 * step + k + 1] = jnp.concatenate(parts, axis=0)

    slot = grid((64, 128))[1]

    def upstream(plane, up, down):
        return jnp.where(slot < 32, plane, jnp.where(slot < 36, up, down)).astype(BF16)

    def moved_to(values, lane_from, lane_to):
        shift = (lane_to - lane_from) % 128
        return pltpu.roll(values, shift, 1) if shift else values

    cot = cot_ref[...].astype(F32)
    up, down = above_below(rnear_ref[144:160, :], rfar_ref[144:160, :])
    up, down = unfold_rows(up), unfold_rows(down)
    planes = [
        upstream(
            moved_to(cot[:, p // 4 * 128 : p // 4 * 128 + 128], p % 4 * 32, 0),
            moved_to(up, 4 * p, 32),
            moved_to(down, 4 * p, 36),
        )
        for p in range(8)
    ]
    up, down = above_below(rxnear_ref[32:48, :], rxfar_ref[32:48, :])
    planes.append(
        upstream(
            unfold_rows(rx_ref[32:48, 0:128].astype(F32)),
            moved_to(unfold_rows(up), 0, 32),
            moved_to(unfold_rows(down), 0, 36),
        )
    )
    spread = dot(jnp.concatenate(planes, axis=0), spread_second_table())
    for p in range(8):
        spread_up[p + gx] = spread[64 * p : 64 * p + 64]
    spread_up[8 * (1 - gx)] = spread[512:576]

    wide = k2_ref[...].astype(F32)
    w2 = wide.T.astype(BF16)
    w3 = jnp.concatenate([wide[32 * n : 32 * n + 32] for n in range(26, -1, -1)], axis=1)
    w3 = w3.astype(BF16)
    lane_grad = lax.broadcasted_iota(jnp.int32, (64, COARSE), 1)
    cols_grad[0] = jnp.zeros((576, MID), BF16)
    cols_grad[NS + 1] = jnp.zeros((576, MID), BF16)
    for k in (0, 1, 18, 19):
        grad_own[k] = jnp.zeros((64, MID), BF16)
    for k in range(NS):
        pre = dot(w2, cols_second[pl.ds(k + gx, 3)].reshape(864, COARSE))
        act_second[k] = leaky(pre[:, 0:MID])
        rounded = (spread_up[(k + gx) // 2] * leaky_slope(pre)).astype(BF16)
        parts = [moved[:, 0:MID] for moved in shifted(rounded, CZ // 2, lane_grad)]
        cols_grad[k + 1] = jnp.concatenate(parts, axis=0)
        kept = rounded[:, 0:MID]
        if k == 0:
            kept = jnp.where(gx == 0, kept, jnp.zeros_like(kept))
        if k == NS - 1:
            kept = jnp.where(gx == 1, kept, jnp.zeros_like(kept))
        grad_own[k + 2 - gx] = kept

    sums = [
        pooled(act_second[2 * p + gx] + act_second[2 * p + 1 + gx], CZ // 2) for p in range(8)
    ]
    picked = dot(jnp.concatenate(sums, axis=0), pool_second_table())
    for half in range(2):
        whole = picked[256 * half : 256 * half + 64]
        for k in range(1, 4):
            block = picked[256 * half + 64 * k : 256 * half + 64 * k + 64]
            whole = whole + pltpu.roll(block, 32 * k, 1)
        features_ref[:, 128 * half : 128 * half + 128] = whole.astype(BF16)

    for m in range(0, 16, 2):
        cols = jnp.concatenate(
            [
                cols_grad[pl.ds(m + gx, 3)].reshape(1728, MID),
                cols_grad[pl.ds(m + 1 + gx, 3)].reshape(1728, MID),
            ],
            axis=1,
        )
        back = dot(w3, cols)
        for k in range(2):
            plane = back[:, k * MID : (k + 1) * MID]
            act_grad_ref[:, m + k, :] = plane
            half_grad[m + k] = split(plane)

    total = jnp.zeros((288, 192), F32)
    for q in range(0, 18, 2):
        left = jnp.concatenate(
            [cols_second[q + 2 * gx][:, 0:MID], cols_second[q + 1 + 2 * gx][:, 0:MID]], axis=1
        )
        right = jnp.concatenate(
            [
                grad_own[q : q + 3].reshape(192, MID),
                grad_own[q + 1 : q + 4].reshape(192, MID),
            ],
            axis=1,
        )
        total = total + dot_lanes(left, right)
    grads_ref[:, 0:192] = total

    grow = spread_first_table()
    first = jnp.zeros((144, 64), F32)
    for step in range(4):
        spread = dot(half_grad[4 * step : 4 * step + 4].reshape(256, MID), grow)
        for k in range(4):
            m = 4 * step + k + 2 * gx
            whole = spread[k * 64 : k * 64 + 32] + spread[k * 64 + 32 : k * 64 + 64]
            slope = leaky_slope(pre_first[m])
            back = (jnp.concatenate([whole, whole], axis=0) * slope).astype(BF16)
            first = first + dot_lanes(cols_first[m], back)
    grads_ref[0:144, 192:256] = first
    grads_ref[144:288, 192:256] = jnp.zeros((144, 64), F32)
    kept_ref[...] = grads_ref[pl.ds(pl.multiple_of(144 * gx, 8), 144), :]
    sent_ref[...] = grads_ref[pl.ds(pl.multiple_of(144 * (1 - gx), 8), 144), :]


def unpack_kernel(mine_ref, other_ref, second_ref, first_ref):
    first = lax.axis_index("gx") == 0
    lower = jnp.where(first, mine_ref[...], other_ref[...])
    upper = jnp.where(first, other_ref[...], mine_ref[...])
    for dx in range(3):
        second_ref[dx, 0:144] = lower[:, (2 - dx) * 64 : (3 - dx) * 64]
        second_ref[dx, 144:288] = upper[:, (2 - dx) * 64 : (3 - dx) * 64]
    both = lower[:, 192:256]
    for at in range(9):
        part = both[at * 16 : at * 16 + 16]
        for dx in range(3):
            first_ref[dx * 9 + at] = (
                part[4 * dx : 4 * dx + 4, 0:32] + part[4 * dx + 4 : 4 * dx + 8, 32:64]
            )


def call(kernel, outs, limit, scratch=()):
    return pl.pallas_call(
        kernel,
        out_shape=[jax.ShapeDtypeStruct(shape, dtype) for shape, dtype in outs],
        scratch_shapes=[pltpu.VMEM(shape, dtype) for shape, dtype in scratch],
        compiler_params=pltpu.CompilerParams(vmem_limit_bytes=limit * 1024 * 1024),
    )


def in_hbm(values):
    return pltpu.with_memory_space_constraint(values, pltpu.HBM)


def swap_cores(values):
    return lax.ppermute(values, "gx", [(0, 1), (1, 0)])


def sum_in_pairs(part):
    sizes = [lax.axis_size(axis) for axis in ("dp", "gx", "yz")]
    steps = [[(axis, 1 << bit) for bit in range(sizes[axis].bit_length() - 1)] for axis in (0, 2)]
    orders = (steps[0] + steps[1], steps[1] + steps[0])
    for step in range(len(orders[0])):
        routes = []
        for at in np.ndindex(*sizes):
            axis, bit = orders[at[1]][step]
            to = list(at)
            to[axis] ^= bit
            routes.append(
                tuple((d * sizes[1] + g) * sizes[2] + z for d, g, z in (at, tuple(to)))
            )
        part = part.astype(BF16)
        came = lax.ppermute(part, ("dp", "gx", "yz"), routes)
        part = part.astype(F32) + came.astype(F32)
    return part


def on_device_kernels(rows_y, volumes, first_kernel, second_kernel, cotangent):
    cot = cotangent.reshape(64, 256)
    own, x_face, near, far, x_near, x_far = call(
        pack_kernel,
        [
            ((136, OWN), F32),
            ((48, OWN), BF16),
            ((160, 128), BF16),
            ((160, 128), BF16),
            ((48, 128), BF16),
            ((48, 128), BF16),
        ],
        16,
    )(in_hbm(volumes.reshape(4, CX * OWN)), in_hbm(cot))

    def paired(values, partner):
        routes = [
            (g * rows_y + i, partner(g, i)) for g in range(2) for i in range(rows_y)
        ]
        return lax.ppermute(values, ("gx", "yz"), routes)

    def other_side(g, i, across):
        j = i + (1 if i % 2 else -1)
        if 0 <= j < rows_y:
            return (g ^ across) * rows_y + j
        return (1 - g) * rows_y + i

    got_near = lax.ppermute(near, "yz", [(i, i ^ 1) for i in range(rows_y)])
    got_far = paired(far, lambda g, i: other_side(g, i, 0))
    got_x = lax.ppermute(x_face, "gx", [(0, 1), (1, 0)])
    got_x_near = paired(x_near, lambda g, i: (1 - g) * rows_y + (i ^ 1))
    got_x_far = paired(x_far, lambda g, i: other_side(g, i, 1))

    k1 = first_kernel.transpose(2, 3, 4, 1, 0).reshape(27, 4, 32)
    k2 = second_kernel.transpose(2, 3, 4, 1, 0).reshape(864, 64)

    features, act_grad, kept, sent = call(
        functools.partial(main_kernel, rows_y),
        [((64, 256), BF16), ((32, 16, MID), F32), ((144, 256), F32), ((144, 256), F32)],
        32,
        [
            ((144, 64), F32),
            ((19, 8, FINE), F32),
            ((NF, 144, OWN), BF16),
            ((NF, 64, OWN), F32),
            ((NF, 32, KEPT), BF16),
            ((NF + 2, 288, COARSE), BF16),
            ((NS, 64, MID), F32),
            ((9, 64, COARSE), F32),
            ((20, 64, MID), BF16),
            ((NS + 2, 576, MID), BF16),
            ((16, 64, MID), BF16),
            ((288, 256), F32),
        ],
    )(
        own.reshape(17, 8, OWN),
        cot,
        got_x,
        got_near,
        got_far,
        got_x_near,
        got_x_far,
        k1,
        k2,
    )
    mine = sum_in_pairs(kept + swap_cores(sent))
    second, first = call(unpack_kernel, [((3, 288, 64), F32), ((27, 4, 32), F32)], 8)(
        mine, swap_cores(mine)
    )
    return (
        features.reshape(1, 64, 1, 1, 256),
        act_grad.reshape(1, 32, 1, 1, 2048),
        first.reshape(3, 3, 3, 4, 32).transpose(4, 3, 0, 1, 2),
        second.reshape(3, 3, 3, 32, 64).transpose(4, 3, 0, 1, 2),
    )


def solution(mesh):
    placed = (P("dp", None, "gx", "yz", None), P(), P(), P("dp", None, "gx", "yz", None))
    rows_y = min(4, mesh.shape["yz"])
    rows_z = mesh.shape["yz"] // rows_y
    if rows_z == 1 and rows_y == 4 and mesh.shape["gx"] == 2 and mesh.shape["dp"] == 4:
        body = functools.partial(on_device_kernels, rows_y)
    else:
        body = functools.partial(on_device_plain, rows_y, rows_z)
    return jax.shard_map(
        body,
        mesh=mesh,
        in_specs=placed,
        out_specs=(P("dp", None, "gx", "yz", None), P("dp", None, "gx", "yz", None), P(), P()),
        check_vma=False,
    )
```

```python
import functools

import jax
import jax.numpy as jnp
from jax import lax
from jax.experimental import pallas as pl
from jax.experimental.pallas import tpu as pltpu
from jax.sharding import PartitionSpec as P

CX = 32
CY = 32
CZ = 16
SLOPE = 0.3
F32 = jnp.float32
BF16 = jnp.bfloat16


def leaky(values):
    return jnp.where(values > 0, values, SLOPE * values)


def leaky_slope(values):
    return jnp.where(values > 0, jnp.float32(1.0), jnp.float32(SLOPE))


def convolve_valid(padded, kernel):
    return lax.conv_general_dilated(
        padded,
        kernel,
        (1, 1, 1),
        "VALID",
        dimension_numbers=("NCDHW", "OIDHW", "NCDHW"),
        preferred_element_type=F32,
    )


def kernel_grad(padded, grad):
    result = lax.conv_general_dilated(
        padded,
        grad,
        (1, 1, 1),
        "VALID",
        dimension_numbers=("CNDHW", "IODHW", "NCDHW"),
        preferred_element_type=F32,
    )
    return result.transpose(1, 0, 2, 3, 4)


def average_pool(values):
    bat, chan, xs, ys, zs = values.shape
    return values.reshape(bat, chan, xs // 2, 2, ys // 2, 2, zs // 2, 2).mean(axis=(3, 5, 7))


def spread_back(values):
    bat, chan, xs, ys, zs = values.shape
    grown = jnp.broadcast_to(
        values[:, :, :, None, :, None, :, None], (bat, chan, xs, 2, ys, 2, zs, 2)
    )
    return grown.reshape(bat, chan, 2 * xs, 2 * ys, 2 * zs) * 0.125


def unflatten(values, factor):
    return values[:, :, 0, 0].reshape(
        values.shape[0], values.shape[1], CX // factor, CY // factor, CZ // factor
    )


def flatten(values):
    return values.reshape(values.shape[0], values.shape[1], 1, 1, -1)


def extend_along(values, dim, axis, routes):
    size = values.shape[dim]
    first = lax.slice_in_dim(values, 0, 1, axis=dim)
    last = lax.slice_in_dim(values, size - 1, size, axis=dim)
    before = lax.ppermute(last, axis, routes)
    after = lax.ppermute(first, axis, [(b, a) for a, b in routes])
    return jnp.concatenate([before, values, after], axis=dim)


def extend(values, rows_y, rows_z):
    planes = lax.axis_size("gx")
    count = rows_y * rows_z
    values = extend_along(values, 2, "gx", [(i, i + 1) for i in range(planes - 1)])
    values = extend_along(values, 3, "yz", [(i, i + rows_z) for i in range(count - rows_z)])
    return extend_along(
        values, 4, "yz", [(i, i + 1) for i in range(count - 1) if (i + 1) % rows_z]
    )


def on_device_plain(rows_y, rows_z, volumes, first_kernel, second_kernel, cotangent):
    upstream = unflatten(cotangent, 4)
    padded_in = extend(unflatten(volumes, 1), rows_y, rows_z)
    pre_first = convolve_valid(padded_in, first_kernel)
    act_first = average_pool(leaky(pre_first)).astype(BF16)
    padded_mid = extend(act_first, rows_y, rows_z)
    pre_second = convolve_valid(padded_mid, second_kernel)
    features = average_pool(leaky(pre_second)).astype(BF16)
    grad_second = (spread_back(upstream.astype(F32)) * leaky_slope(pre_second)).astype(BF16)
    flipped = jnp.flip(second_kernel, (2, 3, 4)).transpose(1, 0, 2, 3, 4)
    act_grad = convolve_valid(extend(grad_second, rows_y, rows_z), flipped)
    grad_first = (spread_back(act_grad) * leaky_slope(pre_first)).astype(BF16)
    first_grad, second_grad = lax.psum(
        (kernel_grad(padded_in, grad_first), kernel_grad(padded_mid, grad_second)),
        ("dp", "gx", "yz"),
    )
    return (flatten(features), flatten(act_grad), first_grad, second_grad)


FINE = 48 * CZ
KEPT = 40 * CZ
OWN = CY * CZ
COARSE = 256
MID = (CY // 2) * (CZ // 2)
NF = 18
NS = 17


def grid(shape):
    return [lax.broadcasted_iota(jnp.int32, shape, dim) for dim in range(2)]


def one_where(condition, value=1.0):
    return jnp.where(condition, value, 0.0).astype(BF16)


def fine_to_mid(lane):
    return (lane >> 5) * 8 + ((lane & 15) >> 1) + jnp.where(lane >= OWN + 64, 96, 0)


def rim_table():
    row, lane = grid((256, 256))
    edge = jnp.where(lane < 128, 0, 7)
    place = (row >> 5) * 4 + (row & 3)
    return one_where(jnp.logical_and(((row >> 2) & 7) == edge, place == (lane & 127)))


def pool_first_table():
    row, lane = grid((KEPT, COARSE))
    place = jnp.where((row & 17) == 0, fine_to_mid(row), -1)
    return one_where(place == lane)


def spread_first_table():
    row, lane = grid((MID, OWN))
    return one_where(fine_to_mid(lane) == row, 0.125)


def pool_second_table():
    row, lane = grid((MID, 128))
    place = jnp.where((row & 9) == 0, (row >> 4) * 4 + ((row & 7) >> 1), -1)
    return one_where(place == lane)


def spread_second_table():
    row, lane = grid((128, COARSE))
    place = jnp.where(lane < MID, (lane >> 4) * 4, jnp.where(lane < 192, 32, 36))
    place = place + ((lane & 7) >> 1)
    used = jnp.logical_or(lane < MID + 8, lane >= COARSE - 8)
    return one_where(jnp.logical_and(used, place == row), 0.125)


def fold_rows(values):
    lane = grid((16, 128))[1]
    kept = [
        jnp.where(lane < 32, values[16 * q : 16 * q + 16], jnp.zeros((16, 128), F32))
        for q in range(4)
    ]
    return kept[0] + sum(pltpu.roll(kept[q], 32 * q, 1) for q in range(1, 4))


def unfold_rows(values):
    parts = [values] + [pltpu.roll(values, 128 - 32 * q, 1) for q in range(1, 4)]
    return jnp.concatenate(parts, axis=0)


def dot(a, b):
    return jnp.dot(a, b, preferred_element_type=F32)


def dot_lanes(a, b):
    return lax.dot_general(a, b, (((1,), (1,)), ((), ())), preferred_element_type=F32)


def pack_kernel(
    vol_ref,
    cot_ref,
    k1_ref,
    k2_ref,
    own_ref,
    x_ref,
    near_ref,
    far_ref,
    xnear_ref,
    xfar_ref,
    w1_ref,
    w2_ref,
    w3_ref,
    w1_rows,
):
    gx = lax.axis_index("gx")
    odd = lax.axis_index("yz") % 2
    own_ref[0:8, :] = jnp.zeros((8, OWN), F32)
    own_ref[128:136, :] = jnp.zeros((8, OWN), F32)
    for x in range(CX):
        own_ref[4 + 4 * x : 8 + 4 * x, :] = vol_ref[:, x * OWN : (x + 1) * OWN].astype(F32)
    start = pl.multiple_of(112 * (1 - gx), 8)
    blank = jnp.zeros((8, OWN), F32)
    face = jnp.concatenate([own_ref[pl.ds(start, 24), :], blank])
    x_ref[0:32, :] = face.astype(BF16)
    cot = cot_ref[...]
    wide = cot.astype(F32)
    first = gx == 0
    end = jnp.where(first, pltpu.roll(wide[:, 128:256], 32, 1), wide[:, 0:128])
    x_ref[32:48, 0:128] = fold_rows(end).astype(BF16)
    x_ref[32:48, 128:OWN] = jnp.zeros((16, OWN - 128), BF16)
    rims = dot(cot, rim_table())
    for low, side_ref, xside_ref in ((odd, near_ref, xnear_ref), (1 - odd, far_ref, xfar_ref)):
        lanes = pl.ds(pl.multiple_of((OWN - 128) * (1 - low), 128), 128)
        tail = jnp.concatenate([own_ref[128:136, lanes], blank[:, 0:128]])
        side_ref[0:128, :] = own_ref[0:128, lanes].astype(BF16)
        side_ref[128:144, :] = tail.astype(BF16)
        edge = jnp.concatenate([own_ref[pl.ds(start, 24), lanes], blank[:, 0:128]])
        xside_ref[0:32, :] = edge.astype(BF16)
        rim = jnp.where(low == 1, rims[:, 0:128], rims[:, 128:256])
        side_ref[144:160, :] = fold_rows(rim).astype(BF16)
        corner = jnp.where(first, pltpu.roll(rim, 100, 1), rim)
        xside_ref[32:48, :] = fold_rows(corner).astype(BF16)

    w1_rows[...] = jnp.zeros_like(w1_rows)
    for dx in range(3):
        for at in range(9):
            block = k1_ref[dx * 9 + at].astype(F32)
            for k in range(2):
                row = at * 16 + 4 * (dx + k)
                w1_rows[row : row + 4, 32 * k : 32 * k + 32] = block
    w1_ref[...] = w1_rows[...].T.astype(BF16)
    k2 = k2_ref[...].astype(F32)
    flipped = jnp.concatenate([k2[32 * n : 32 * n + 32] for n in range(26, -1, -1)], axis=1)
    for out_ref, one in ((w2_ref, k2.T), (w3_ref, flipped)):
        high, wide = one.shape
        for r in range(4):
            parts = [jnp.zeros((high, wide // 3 * r), F32)] if r else []
            parts.append(one)
            if r < 3:
                parts.append(jnp.zeros((high, wide // 3 * (3 - r)), F32))
            row = jnp.concatenate(parts, axis=1)
            out_ref[high * r : high * r + high, :] = row.astype(BF16)


def shifted(tile, period, lane):
    size = tile.shape[1]
    z = lane % period
    blank = jnp.zeros_like(tile)
    along = (
        jnp.where(z == 0, blank, pltpu.roll(tile, 1, 1)),
        tile,
        jnp.where(z == period - 1, blank, pltpu.roll(tile, size - 1, 1)),
    )
    return [
        pltpu.roll(moved, shift, 1) if shift else moved
        for shift in (period, 0, size - period)
        for moved in along
    ]


def pooled(values, period):
    size = values.shape[1]
    values = values + pltpu.roll(values, size - 1, 1)
    values = values + pltpu.roll(values, size - period, 1)
    return (values * 0.125).astype(BF16)


def split(values):
    top = values.astype(BF16)
    return jnp.concatenate([top, (values - top.astype(F32)).astype(BF16)], axis=0)


def main_kernel(
    rows_y,
    own_ref,
    cot_ref,
    rx_ref,
    rnear_ref,
    rfar_ref,
    rxnear_ref,
    rxfar_ref,
    w1_ref,
    w2_ref,
    w3_ref,
    features_ref,
    act_grad_ref,
    kept_ref,
    sent_ref,
    vol,
    cols_first,
    pre_first,
    pooled_first,
    cols_second,
    act_second,
    spread_up,
    grad_own,
    cols_grad,
    half_grad,
    grads_ref,
):
    gx = lax.axis_index("gx")
    block_y = lax.axis_index("yz")

    odd = block_y % 2 == 1
    inner = jnp.logical_and(block_y > 0, block_y < rows_y - 1)

    def above_below(near, far):
        near, far = near.astype(F32), far.astype(F32)
        far = jnp.where(inner, far, jnp.zeros_like(far))
        return jnp.where(odd, far, near), jnp.where(odd, near, far)

    vol[...] = jnp.zeros_like(vol)
    up, down = above_below(rnear_ref[0:144, :], rfar_ref[0:144, :])
    vol[pl.ds(2 * gx, 17), :, OWN : OWN + 128] = up[0:136].reshape(17, 8, 128)
    vol[pl.ds(2 * gx, 17), :, OWN + 128 : FINE] = down[0:136].reshape(17, 8, 128)
    vol[pl.ds(2 * gx, 17), :, 0:OWN] = own_ref[...]
    end = pl.ds(16 * (1 - gx), 3)
    vol[end, :, 0:OWN] += rx_ref[0:32, :].astype(F32)[0:24].reshape(3, 8, OWN)
    up, down = above_below(rxnear_ref[0:32, :], rxfar_ref[0:32, :])
    vol[end, :, OWN : OWN + 128] += up[0:24].reshape(3, 8, 128)
    vol[end, :, OWN + 128 : FINE] += down[0:24].reshape(3, 8, 128)

    lane_fine = lax.broadcasted_iota(jnp.int32, (16, FINE), 1)
    near = lax.broadcasted_iota(jnp.int32, (16, 128), 1) < 64
    for j in range(NF):
        tile = jnp.concatenate([vol[j], vol[j + 1]], axis=0).astype(BF16)
        parts = []
        for moved in shifted(tile, CZ, lane_fine):
            edge = jnp.where(near, moved[:, OWN : OWN + 128], moved[:, OWN + 128 : FINE])
            parts.append(jnp.concatenate([moved[:, 0:OWN], edge], axis=1))
        cols = jnp.concatenate(parts, axis=0)
        cols_first[j] = cols[:, 0:OWN]
        pre = dot(w1_ref[...], cols)
        pre_first[j] = pre[:, 0:OWN]
        sloped = leaky(pre)
        pooled_first[j] = pooled(sloped[0:32] + sloped[32:64], CZ)

    lane = lax.broadcasted_iota(jnp.int32, (32, COARSE), 1)
    valid = jnp.logical_or(
        lane < MID,
        jnp.logical_or(
            jnp.logical_and(lane < 192, block_y < rows_y - 1),
            jnp.logical_and(lane >= 192, block_y > 0),
        ),
    )
    cols_second[0] = jnp.zeros((288, COARSE), BF16)
    cols_second[NF + 1] = jnp.zeros((288, COARSE), BF16)
    pick = pool_first_table()
    for step in range(3):
        picked = dot(pooled_first[6 * step : 6 * step + 6].reshape(192, KEPT), pick)
        for k in range(6):
            plane = jnp.where(valid, picked[k * 32 : k * 32 + 32], 0.0).astype(BF16)
            parts = shifted(plane, CZ // 2, lane)
            cols_second[6 * step + k + 1] = jnp.concatenate(parts, axis=0)

    slot = grid((64, 128))[1]

    def upstream(plane, up, down):
        return jnp.where(slot < 32, plane, jnp.where(slot < 36, up, down)).astype(BF16)

    def moved_to(values, lane_from, lane_to):
        shift = (lane_to - lane_from) % 128
        return pltpu.roll(values, shift, 1) if shift else values

    cot = cot_ref[...].astype(F32)
    up, down = above_below(rnear_ref[144:160, :], rfar_ref[144:160, :])
    up, down = unfold_rows(up), unfold_rows(down)
    planes = [
        upstream(
            moved_to(cot[:, p // 4 * 128 : p // 4 * 128 + 128], p % 4 * 32, 0),
            moved_to(up, 4 * p, 32),
            moved_to(down, 4 * p, 36),
        )
        for p in range(8)
    ]
    up, down = above_below(rxnear_ref[32:48, :], rxfar_ref[32:48, :])
    planes.append(
        upstream(
            unfold_rows(rx_ref[32:48, 0:128].astype(F32)),
            moved_to(unfold_rows(up), 0, 32),
            moved_to(unfold_rows(down), 0, 36),
        )
    )
    spread = dot(jnp.concatenate(planes, axis=0), spread_second_table())
    for p in range(8):
        spread_up[p + gx] = spread[64 * p : 64 * p + 64]
    spread_up[8 * (1 - gx)] = spread[512:576]

    lane_grad = lax.broadcasted_iota(jnp.int32, (64, COARSE), 1)
    cols_grad[0] = jnp.zeros((576, MID), BF16)
    cols_grad[NS + 1] = jnp.zeros((576, MID), BF16)
    for k in (0, 1, 18, 19):
        grad_own[k] = jnp.zeros((64, MID), BF16)
    def second_layer(k, pre):
        act_second[k] = leaky(pre[:, 0:MID])
        rounded = (spread_up[(k + gx) // 2] * leaky_slope(pre)).astype(BF16)
        parts = [moved[:, 0:MID] for moved in shifted(rounded, CZ // 2, lane_grad)]
        cols_grad[k + 1] = jnp.concatenate(parts, axis=0)
        kept = rounded[:, 0:MID]
        if k == 0:
            kept = jnp.where(gx == 0, kept, jnp.zeros_like(kept))
        if k == NS - 1:
            kept = jnp.where(gx == 1, kept, jnp.zeros_like(kept))
        grad_own[k + 2 - gx] = kept

    for k in range(0, NS - 1, 4):
        four = dot(w2_ref[...], cols_second[pl.ds(k + gx, 6)].reshape(1728, COARSE))
        for r in range(4):
            second_layer(k + r, four[64 * r : 64 * r + 64])
    last = cols_second[pl.ds(NS - 1 + gx, 3)].reshape(864, COARSE)
    second_layer(NS - 1, dot(w2_ref[0:64, 0:864], last))

    sums = [
        pooled(act_second[2 * p + gx] + act_second[2 * p + 1 + gx], CZ // 2) for p in range(8)
    ]
    picked = dot(jnp.concatenate(sums, axis=0), pool_second_table())
    for half in range(2):
        whole = picked[256 * half : 256 * half + 64]
        for k in range(1, 4):
            block = picked[256 * half + 64 * k : 256 * half + 64 * k + 64]
            whole = whole + pltpu.roll(block, 32 * k, 1)
        features_ref[:, 128 * half : 128 * half + 128] = whole.astype(BF16)

    for base in (0, 8):
        cols = jnp.concatenate(
            [
                cols_grad[pl.ds(base + gx, 6)].reshape(3456, MID),
                cols_grad[pl.ds(base + 4 + gx, 6)].reshape(3456, MID),
            ],
            axis=1,
        )
        back = dot(w3_ref[...], cols)
        for m in range(8):
            row, lanes = 32 * (m % 4), MID * (m // 4)
            plane = back[row : row + 32, lanes : lanes + MID]
            act_grad_ref[:, base + m, :] = plane
            half_grad[base + m] = split(plane)

    left = jnp.concatenate([cols_second[q + 2 * gx][:, 0:MID] for q in range(18)], axis=1)
    right = jnp.concatenate([grad_own[q : q + 3].reshape(192, MID) for q in range(18)], axis=1)
    grads_ref[:, 0:192] = dot_lanes(left, right)

    grow = spread_first_table()
    first = jnp.zeros((144, 64), F32)
    for step in range(4):
        spread = dot(half_grad[4 * step : 4 * step + 4].reshape(256, MID), grow)
        for k in range(4):
            m = 4 * step + k + 2 * gx
            whole = spread[k * 64 : k * 64 + 32] + spread[k * 64 + 32 : k * 64 + 64]
            slope = leaky_slope(pre_first[m])
            back = (jnp.concatenate([whole, whole], axis=0) * slope).astype(BF16)
            first = first + dot_lanes(cols_first[m], back)
    grads_ref[0:144, 192:256] = first
    grads_ref[144:288, 192:256] = jnp.zeros((144, 64), F32)
    kept_ref[...] = grads_ref[pl.ds(pl.multiple_of(144 * gx, 8), 144), :]
    sent_ref[...] = grads_ref[pl.ds(pl.multiple_of(144 * (1 - gx), 8), 144), :]


def unpack_kernel(mine_ref, other_ref, second_ref, first_ref):
    first = lax.axis_index("gx") == 0
    lower = jnp.where(first, mine_ref[...], other_ref[...])
    upper = jnp.where(first, other_ref[...], mine_ref[...])
    for dx in range(3):
        second_ref[dx, 0:144] = lower[:, (2 - dx) * 64 : (3 - dx) * 64]
        second_ref[dx, 144:288] = upper[:, (2 - dx) * 64 : (3 - dx) * 64]
    both = lower[:, 192:256]
    for at in range(9):
        part = both[at * 16 : at * 16 + 16]
        for dx in range(3):
            first_ref[dx * 9 + at] = (
                part[4 * dx : 4 * dx + 4, 0:32] + part[4 * dx + 4 : 4 * dx + 8, 32:64]
            )


def call(kernel, outs, limit, scratch=()):
    return pl.pallas_call(
        kernel,
        out_shape=[jax.ShapeDtypeStruct(shape, dtype) for shape, dtype in outs],
        scratch_shapes=[pltpu.VMEM(shape, dtype) for shape, dtype in scratch],
        compiler_params=pltpu.CompilerParams(vmem_limit_bytes=limit * 1024 * 1024),
    )


def in_hbm(values):
    return pltpu.with_memory_space_constraint(values, pltpu.HBM)


def swap_cores(values):
    return lax.ppermute(values, "gx", [(0, 1), (1, 0)])


def sum_of_four(part, axis):
    came = [lax.ppermute(part, axis, [(i, i ^ k) for i in range(4)]) for k in range(1, 4)]
    terms = [term.astype(F32) for term in [part] + came]
    return (terms[0] + terms[1]) + (terms[2] + terms[3])


def on_device_kernels(rows_y, volumes, first_kernel, second_kernel, cotangent):
    cot = cotangent.reshape(64, 256)
    k1 = first_kernel.transpose(2, 3, 4, 1, 0).reshape(27, 4, 32)
    k2 = second_kernel.transpose(2, 3, 4, 1, 0).reshape(864, 64)
    own, x_face, near, far, x_near, x_far, w1, w2, w3 = call(
        pack_kernel,
        [
            ((136, OWN), F32),
            ((48, OWN), BF16),
            ((160, 128), BF16),
            ((160, 128), BF16),
            ((48, 128), BF16),
            ((48, 128), BF16),
            ((64, 144), BF16),
            ((256, 1728), BF16),
            ((128, 3456), BF16),
        ],
        16,
        [((144, 64), F32)],
    )(in_hbm(volumes.reshape(4, CX * OWN)), in_hbm(cot), in_hbm(k1), in_hbm(k2))

    def paired(values, partner):
        routes = [
            (g * rows_y + i, partner(g, i)) for g in range(2) for i in range(rows_y)
        ]
        return lax.ppermute(values, ("gx", "yz"), routes)

    def other_side(g, i, across):
        j = i + (1 if i % 2 else -1)
        if 0 <= j < rows_y:
            return (g ^ across) * rows_y + j
        return (1 - g) * rows_y + i

    got_near = lax.ppermute(near, "yz", [(i, i ^ 1) for i in range(rows_y)])
    got_far = paired(far, lambda g, i: other_side(g, i, 0))
    got_x = lax.ppermute(x_face, "gx", [(0, 1), (1, 0)])
    got_x_near = paired(x_near, lambda g, i: (1 - g) * rows_y + (i ^ 1))
    got_x_far = paired(x_far, lambda g, i: other_side(g, i, 1))

    features, act_grad, kept, sent = call(
        functools.partial(main_kernel, rows_y),
        [((64, 256), BF16), ((32, 16, MID), F32), ((144, 256), F32), ((144, 256), F32)],
        32,
        [
            ((19, 8, FINE), F32),
            ((NF, 144, OWN), BF16),
            ((NF, 64, OWN), F32),
            ((NF, 32, KEPT), BF16),
            ((NF + 2, 288, COARSE), BF16),
            ((NS, 64, MID), F32),
            ((9, 64, COARSE), F32),
            ((20, 64, MID), BF16),
            ((NS + 2, 576, MID), BF16),
            ((16, 64, MID), BF16),
            ((288, 256), F32),
        ],
    )(
        own.reshape(17, 8, OWN),
        cot,
        got_x,
        got_near,
        got_far,
        got_x_near,
        got_x_far,
        w1,
        w2,
        w3,
    )
    part = (kept + swap_cores(sent)).astype(BF16)
    mine = sum_of_four(sum_of_four(part, "dp").astype(BF16), "yz")
    second, first = call(unpack_kernel, [((3, 288, 64), F32), ((27, 4, 32), F32)], 8)(
        mine, swap_cores(mine)
    )
    return (
        features.reshape(1, 64, 1, 1, 256),
        act_grad.reshape(1, 32, 1, 1, 2048),
        first.reshape(3, 3, 3, 4, 32).transpose(4, 3, 0, 1, 2),
        second.reshape(3, 3, 3, 32, 64).transpose(4, 3, 0, 1, 2),
    )


def solution(mesh):
    placed = (P("dp", None, "gx", "yz", None), P(), P(), P("dp", None, "gx", "yz", None))
    rows_y = min(4, mesh.shape["yz"])
    rows_z = mesh.shape["yz"] // rows_y
    if rows_z == 1 and rows_y == 4 and mesh.shape["gx"] == 2 and mesh.shape["dp"] == 4:
        body = functools.partial(on_device_kernels, rows_y)
    else:
        body = functools.partial(on_device_plain, rows_y, rows_z)
    return jax.shard_map(
        body,
        mesh=mesh,
        in_specs=placed,
        out_specs=(P("dp", None, "gx", "yz", None), P("dp", None, "gx", "yz", None), P(), P()),
        check_vma=False,
    )
```

```python
import functools

import jax
import jax.numpy as jnp
from jax import lax
from jax.experimental import pallas as pl
from jax.experimental.pallas import tpu as pltpu
from jax.sharding import PartitionSpec as P

CX = 32
CY = 32
CZ = 16
SLOPE = 0.3
F32 = jnp.float32
BF16 = jnp.bfloat16


def leaky(values):
    return jnp.maximum(values, SLOPE * values)


def leaky_slope(values):
    return jnp.where(values > 0, jnp.float32(1.0), jnp.float32(SLOPE))


def convolve_valid(padded, kernel):
    return lax.conv_general_dilated(
        padded,
        kernel,
        (1, 1, 1),
        "VALID",
        dimension_numbers=("NCDHW", "OIDHW", "NCDHW"),
        preferred_element_type=F32,
    )


def kernel_grad(padded, grad):
    result = lax.conv_general_dilated(
        padded,
        grad,
        (1, 1, 1),
        "VALID",
        dimension_numbers=("CNDHW", "IODHW", "NCDHW"),
        preferred_element_type=F32,
    )
    return result.transpose(1, 0, 2, 3, 4)


def average_pool(values):
    bat, chan, xs, ys, zs = values.shape
    return values.reshape(bat, chan, xs // 2, 2, ys // 2, 2, zs // 2, 2).mean(axis=(3, 5, 7))


def spread_back(values):
    bat, chan, xs, ys, zs = values.shape
    grown = jnp.broadcast_to(
        values[:, :, :, None, :, None, :, None], (bat, chan, xs, 2, ys, 2, zs, 2)
    )
    return grown.reshape(bat, chan, 2 * xs, 2 * ys, 2 * zs) * 0.125


def unflatten(values, factor):
    return values[:, :, 0, 0].reshape(
        values.shape[0], values.shape[1], CX // factor, CY // factor, CZ // factor
    )


def flatten(values):
    return values.reshape(values.shape[0], values.shape[1], 1, 1, -1)


def extend_along(values, dim, axis, routes):
    size = values.shape[dim]
    first = lax.slice_in_dim(values, 0, 1, axis=dim)
    last = lax.slice_in_dim(values, size - 1, size, axis=dim)
    before = lax.ppermute(last, axis, routes)
    after = lax.ppermute(first, axis, [(b, a) for a, b in routes])
    return jnp.concatenate([before, values, after], axis=dim)


def extend(values, rows_y, rows_z):
    planes = lax.axis_size("gx")
    count = rows_y * rows_z
    values = extend_along(values, 2, "gx", [(i, i + 1) for i in range(planes - 1)])
    values = extend_along(values, 3, "yz", [(i, i + rows_z) for i in range(count - rows_z)])
    return extend_along(
        values, 4, "yz", [(i, i + 1) for i in range(count - 1) if (i + 1) % rows_z]
    )


def on_device_plain(rows_y, rows_z, volumes, first_kernel, second_kernel, cotangent):
    upstream = unflatten(cotangent, 4)
    padded_in = extend(unflatten(volumes, 1), rows_y, rows_z)
    pre_first = convolve_valid(padded_in, first_kernel)
    act_first = average_pool(leaky(pre_first)).astype(BF16)
    padded_mid = extend(act_first, rows_y, rows_z)
    pre_second = convolve_valid(padded_mid, second_kernel)
    features = average_pool(leaky(pre_second)).astype(BF16)
    grad_second = (spread_back(upstream.astype(F32)) * leaky_slope(pre_second)).astype(BF16)
    flipped = jnp.flip(second_kernel, (2, 3, 4)).transpose(1, 0, 2, 3, 4)
    act_grad = convolve_valid(extend(grad_second, rows_y, rows_z), flipped)
    grad_first = (spread_back(act_grad) * leaky_slope(pre_first)).astype(BF16)
    first_grad, second_grad = lax.psum(
        (kernel_grad(padded_in, grad_first), kernel_grad(padded_mid, grad_second)),
        ("dp", "gx", "yz"),
    )
    return (flatten(features), flatten(act_grad), first_grad, second_grad)


FINE = 48 * CZ
KEPT = 40 * CZ
OWN = CY * CZ
COARSE = 256
MID = (CY // 2) * (CZ // 2)
NF = 18
NS = 17


def grid(shape):
    return [lax.broadcasted_iota(jnp.int32, shape, dim) for dim in range(2)]


def one_where(condition, value=1.0):
    return jnp.where(condition, value, 0.0).astype(BF16)


def fine_to_mid(lane):
    return (lane >> 5) * 8 + ((lane & 15) >> 1) + jnp.where(lane >= OWN + 64, 96, 0)


def rim_table():
    row, lane = grid((256, 256))
    edge = jnp.where(lane < 128, 0, 7)
    place = (row >> 5) * 4 + (row & 3)
    return one_where(jnp.logical_and(((row >> 2) & 7) == edge, place == (lane & 127)))


def pool_first_table():
    row, lane = grid((KEPT, COARSE))
    place = jnp.where((row & 17) == 0, fine_to_mid(row), -1)
    return one_where(place == lane, 0.125)


def spread_first_table():
    row, lane = grid((MID, OWN))
    return one_where(fine_to_mid(lane) == row, 0.125)


def pool_second_table():
    row, lane = grid((MID, 128))
    place = jnp.where((row & 9) == 0, (row >> 4) * 4 + ((row & 7) >> 1), -1)
    return one_where(place == lane, 0.125)


def spread_second_table():
    row, lane = grid((128, COARSE))
    place = jnp.where(lane < MID, (lane >> 4) * 4, jnp.where(lane < 192, 32, 36))
    place = place + ((lane & 7) >> 1)
    used = jnp.logical_or(lane < MID + 8, lane >= COARSE - 8)
    return one_where(jnp.logical_and(used, place == row), 0.125)


def fold_rows(values):
    lane = grid((16, 128))[1]
    kept = [
        jnp.where(lane < 32, values[16 * q : 16 * q + 16], jnp.zeros((16, 128), F32))
        for q in range(4)
    ]
    return kept[0] + sum(pltpu.roll(kept[q], 32 * q, 1) for q in range(1, 4))


def unfold_rows(values):
    parts = [values] + [pltpu.roll(values, 128 - 32 * q, 1) for q in range(1, 4)]
    return jnp.concatenate(parts, axis=0)


def dot(a, b):
    return jnp.dot(a, b, preferred_element_type=F32)


def dot_lanes(a, b):
    return lax.dot_general(a, b, (((1,), (1,)), ((), ())), preferred_element_type=F32)


def pack_kernel(vol_ref, cot_ref, own_ref, x_ref, near_ref, far_ref, xnear_ref, xfar_ref):
    gx = lax.axis_index("gx")
    odd = lax.axis_index("yz") % 2
    own_ref[0:8, :] = jnp.zeros((8, OWN), F32)
    own_ref[128:136, :] = jnp.zeros((8, OWN), F32)
    for x in range(CX):
        own_ref[4 + 4 * x : 8 + 4 * x, :] = vol_ref[:, x * OWN : (x + 1) * OWN].astype(F32)
    start = pl.multiple_of(112 * (1 - gx), 8)
    blank = jnp.zeros((8, OWN), F32)
    face = jnp.concatenate([own_ref[pl.ds(start, 24), :], blank])
    x_ref[0:32, :] = face.astype(BF16)
    cot = cot_ref[...]
    wide = cot.astype(F32)
    first = gx == 0
    end = jnp.where(first, pltpu.roll(wide[:, 128:256], 32, 1), wide[:, 0:128])
    x_ref[32:48, 0:128] = fold_rows(end).astype(BF16)
    x_ref[32:48, 128:OWN] = jnp.zeros((16, OWN - 128), BF16)
    rims = dot(cot, rim_table())
    for low, side_ref, xside_ref in ((odd, near_ref, xnear_ref), (1 - odd, far_ref, xfar_ref)):
        lanes = pl.ds(pl.multiple_of((OWN - 128) * (1 - low), 128), 128)
        tail = jnp.concatenate([own_ref[128:136, lanes], blank[:, 0:128]])
        side_ref[0:128, :] = own_ref[0:128, lanes].astype(BF16)
        side_ref[128:144, :] = tail.astype(BF16)
        edge = jnp.concatenate([own_ref[pl.ds(start, 24), lanes], blank[:, 0:128]])
        xside_ref[0:32, :] = edge.astype(BF16)
        rim = jnp.where(low == 1, rims[:, 0:128], rims[:, 128:256])
        side_ref[144:160, :] = fold_rows(rim).astype(BF16)
        corner = jnp.where(first, pltpu.roll(rim, 100, 1), rim)
        xside_ref[32:48, :] = fold_rows(corner).astype(BF16)


def prepare_kernel(
    after_ref,
    k1_ref,
    k2_ref,
    w1_ref,
    w2_ref,
    w3_ref,
    pool_first_ref,
    spread_first_ref,
    pool_second_ref,
    spread_second_ref,
    w1_rows,
):
    del after_ref
    pool_first_ref[...] = pool_first_table()
    spread_first_ref[...] = spread_first_table()
    pool_second_ref[...] = pool_second_table()
    spread_second_ref[...] = spread_second_table()
    w1_rows[...] = jnp.zeros_like(w1_rows)
    for dx in range(3):
        for at in range(9):
            block = k1_ref[dx * 9 + at].astype(F32)
            for k in range(2):
                row = at * 16 + 4 * (dx + k)
                w1_rows[row : row + 4, 32 * k : 32 * k + 32] = block
    w1_ref[...] = w1_rows[...].T.astype(BF16)
    k2 = k2_ref[...].astype(F32)
    flipped = jnp.concatenate([k2[32 * n : 32 * n + 32] for n in range(26, -1, -1)], axis=1)
    for out_ref, one in ((w2_ref, k2.T), (w3_ref, flipped)):
        high, wide = one.shape
        for r in range(4):
            parts = [jnp.zeros((high, wide // 3 * r), F32)] if r else []
            parts.append(one)
            if r < 3:
                parts.append(jnp.zeros((high, wide // 3 * (3 - r)), F32))
            row = jnp.concatenate(parts, axis=1)
            out_ref[high * r : high * r + high, :] = row.astype(BF16)


def shifted(tile, period, lane):
    size = tile.shape[1]
    z = lane % period
    blank = jnp.zeros_like(tile)
    along = (
        jnp.where(z == 0, blank, pltpu.roll(tile, 1, 1)),
        tile,
        jnp.where(z == period - 1, blank, pltpu.roll(tile, size - 1, 1)),
    )
    return [
        pltpu.roll(moved, shift, 1) if shift else moved
        for shift in (period, 0, size - period)
        for moved in along
    ]


def pooled(values, period):
    blocks = []
    for at in range(0, values.shape[1], 128):
        block = values[:, at : at + 128]
        block = block + pltpu.roll(block, 127, 1)
        blocks.append(block + pltpu.roll(block, 128 - period, 1))
    return jnp.concatenate(blocks, axis=1).astype(BF16)


def split(values):
    top = values.astype(BF16)
    return jnp.concatenate([top, (values - top.astype(F32)).astype(BF16)], axis=0)


def main_kernel(
    rows_y,
    own_ref,
    cot_ref,
    rx_ref,
    rnear_ref,
    rfar_ref,
    rxnear_ref,
    rxfar_ref,
    w1_ref,
    w2_ref,
    w3_ref,
    pool_first_ref,
    spread_first_ref,
    pool_second_ref,
    spread_second_ref,
    features_ref,
    act_grad_ref,
    kept_ref,
    sent_ref,
    vol,
    cols_first,
    pre_first,
    pooled_first,
    cols_second,
    act_second,
    spread_up,
    grad_own,
    cols_grad,
    half_grad,
    grads_ref,
):
    gx = lax.axis_index("gx")
    block_y = lax.axis_index("yz")

    odd = block_y % 2 == 1
    inner = jnp.logical_and(block_y > 0, block_y < rows_y - 1)

    def above_below(near, far):
        near, far = near.astype(F32), far.astype(F32)
        far = jnp.where(inner, far, jnp.zeros_like(far))
        return jnp.where(odd, far, near), jnp.where(odd, near, far)

    vol[...] = jnp.zeros_like(vol)
    up, down = above_below(rnear_ref[0:144, :], rfar_ref[0:144, :])
    vol[pl.ds(2 * gx, 17), :, OWN : OWN + 128] = up[0:136].reshape(17, 8, 128)
    vol[pl.ds(2 * gx, 17), :, OWN + 128 : FINE] = down[0:136].reshape(17, 8, 128)
    vol[pl.ds(2 * gx, 17), :, 0:OWN] = own_ref[...]
    end = pl.ds(16 * (1 - gx), 3)
    vol[end, :, 0:OWN] += rx_ref[0:32, :].astype(F32)[0:24].reshape(3, 8, OWN)
    up, down = above_below(rxnear_ref[0:32, :], rxfar_ref[0:32, :])
    vol[end, :, OWN : OWN + 128] += up[0:24].reshape(3, 8, 128)
    vol[end, :, OWN + 128 : FINE] += down[0:24].reshape(3, 8, 128)

    lane_fine = lax.broadcasted_iota(jnp.int32, (16, FINE), 1)
    near = lax.broadcasted_iota(jnp.int32, (16, 128), 1) < 64
    for j in range(NF):
        tile = jnp.concatenate([vol[j], vol[j + 1]], axis=0).astype(BF16)
        parts = []
        for moved in shifted(tile, CZ, lane_fine):
            edge = jnp.where(near, moved[:, OWN : OWN + 128], moved[:, OWN + 128 : FINE])
            parts.append(jnp.concatenate([moved[:, 0:OWN], edge], axis=1))
        cols = jnp.concatenate(parts, axis=0)
        cols_first[j] = cols[:, 0:OWN]
        pre = dot(w1_ref[...], cols)
        pre_first[j] = pre[:, 0:OWN]
        sloped = leaky(pre)
        pooled_first[j] = pooled(sloped[0:32] + sloped[32:64], CZ)

    lane = lax.broadcasted_iota(jnp.int32, (32, COARSE), 1)
    valid = jnp.logical_or(
        lane < MID,
        jnp.logical_or(
            jnp.logical_and(lane < 192, block_y < rows_y - 1),
            jnp.logical_and(lane >= 192, block_y > 0),
        ),
    )
    cols_second[0] = jnp.zeros((288, COARSE), BF16)
    cols_second[NF + 1] = jnp.zeros((288, COARSE), BF16)
    pick = pool_first_ref[...]
    for step in range(3):
        picked = dot(pooled_first[6 * step : 6 * step + 6].reshape(192, KEPT), pick)
        for k in range(6):
            plane = jnp.where(valid, picked[k * 32 : k * 32 + 32], 0.0).astype(BF16)
            parts = shifted(plane, CZ // 2, lane)
            cols_second[6 * step + k + 1] = jnp.concatenate(parts, axis=0)

    slot = grid((64, 128))[1]

    def upstream(plane, up, down):
        return jnp.where(slot < 32, plane, jnp.where(slot < 36, up, down)).astype(BF16)

    def moved_to(values, lane_from, lane_to):
        shift = (lane_to - lane_from) % 128
        return pltpu.roll(values, shift, 1) if shift else values

    cot = cot_ref[...].astype(F32)
    up, down = above_below(rnear_ref[144:160, :], rfar_ref[144:160, :])
    up, down = unfold_rows(up), unfold_rows(down)
    planes = [
        upstream(
            moved_to(cot[:, p // 4 * 128 : p // 4 * 128 + 128], p % 4 * 32, 0),
            moved_to(up, 4 * p, 32),
            moved_to(down, 4 * p, 36),
        )
        for p in range(8)
    ]
    up, down = above_below(rxnear_ref[32:48, :], rxfar_ref[32:48, :])
    planes.append(
        upstream(
            unfold_rows(rx_ref[32:48, 0:128].astype(F32)),
            moved_to(unfold_rows(up), 0, 32),
            moved_to(unfold_rows(down), 0, 36),
        )
    )
    spread = dot(jnp.concatenate(planes, axis=0), spread_second_ref[...])
    for p in range(8):
        spread_up[p + gx] = spread[64 * p : 64 * p + 64]
    spread_up[8 * (1 - gx)] = spread[512:576]

    lane_grad = lax.broadcasted_iota(jnp.int32, (64, COARSE), 1)
    cols_grad[0] = jnp.zeros((576, MID), BF16)
    cols_grad[NS + 1] = jnp.zeros((576, MID), BF16)
    for k in (0, 1, 18, 19):
        grad_own[k] = jnp.zeros((64, MID), BF16)
    def second_layer(k, pre):
        act_second[k] = leaky(pre[:, 0:MID])
        given = spread_up[(k + gx) // 2]
        rounded = jnp.where(pre > 0, given, SLOPE * given).astype(BF16)
        parts = [moved[:, 0:MID] for moved in shifted(rounded, CZ // 2, lane_grad)]
        cols_grad[k + 1] = jnp.concatenate(parts, axis=0)
        kept = rounded[:, 0:MID]
        if k == 0:
            kept = jnp.where(gx == 0, kept, jnp.zeros_like(kept))
        if k == NS - 1:
            kept = jnp.where(gx == 1, kept, jnp.zeros_like(kept))
        grad_own[k + 2 - gx] = kept

    for k in range(0, NS - 1, 4):
        four = dot(w2_ref[...], cols_second[pl.ds(k + gx, 6)].reshape(1728, COARSE))
        for r in range(4):
            second_layer(k + r, four[64 * r : 64 * r + 64])
    last = cols_second[pl.ds(NS - 1 + gx, 3)].reshape(864, COARSE)
    second_layer(NS - 1, dot(w2_ref[0:64, 0:864], last))

    sums = [
        pooled(act_second[2 * p + gx] + act_second[2 * p + 1 + gx], CZ // 2) for p in range(8)
    ]
    picked = dot(jnp.concatenate(sums, axis=0), pool_second_ref[...])
    for half in range(2):
        whole = picked[256 * half : 256 * half + 64]
        for k in range(1, 4):
            block = picked[256 * half + 64 * k : 256 * half + 64 * k + 64]
            whole = whole + pltpu.roll(block, 32 * k, 1)
        features_ref[:, 128 * half : 128 * half + 128] = whole.astype(BF16)

    for base in (0, 8):
        cols = jnp.concatenate(
            [
                cols_grad[pl.ds(base + gx, 6)].reshape(3456, MID),
                cols_grad[pl.ds(base + 4 + gx, 6)].reshape(3456, MID),
            ],
            axis=1,
        )
        back = dot(w3_ref[...], cols)
        for m in range(8):
            row, lanes = 32 * (m % 4), MID * (m // 4)
            plane = back[row : row + 32, lanes : lanes + MID]
            act_grad_ref[:, base + m, :] = plane
            half_grad[base + m] = split(plane)

    left = jnp.concatenate([cols_second[q + 2 * gx][:, 0:MID] for q in range(18)], axis=1)
    right = jnp.concatenate([grad_own[q : q + 3].reshape(192, MID) for q in range(18)], axis=1)
    grads_ref[:, 0:192] = dot_lanes(left, right)

    grow = spread_first_ref[...]
    first = jnp.zeros((144, 64), F32)
    for step in range(4):
        spread = dot(half_grad[4 * step : 4 * step + 4].reshape(256, MID), grow)
        for k in range(4):
            m = 4 * step + k + 2 * gx
            whole = spread[k * 64 : k * 64 + 32] + spread[k * 64 + 32 : k * 64 + 64]
            less = SLOPE * whole
            pre = pre_first[m]
            back = jnp.concatenate(
                [
                    jnp.where(pre[0:32] > 0, whole, less),
                    jnp.where(pre[32:64] > 0, whole, less),
                ],
                axis=0,
            ).astype(BF16)
            first = first + dot_lanes(cols_first[m], back)
    grads_ref[0:144, 192:256] = first
    grads_ref[144:288, 192:256] = jnp.zeros((144, 64), F32)
    kept_ref[...] = grads_ref[pl.ds(pl.multiple_of(144 * gx, 8), 144), :]
    sent = grads_ref[pl.ds(pl.multiple_of(144 * (1 - gx), 8), 144), :]
    sent_ref[...] = sent.astype(BF16)


def unpack_kernel(mine_ref, other_ref, second_ref, first_ref):
    first = lax.axis_index("gx") == 0
    mine, other = mine_ref[...].astype(F32), other_ref[...].astype(F32)
    lower, upper = jnp.where(first, mine, other), jnp.where(first, other, mine)
    for dx in range(3):
        second_ref[dx, 0:144] = lower[:, (2 - dx) * 64 : (3 - dx) * 64]
        second_ref[dx, 144:288] = upper[:, (2 - dx) * 64 : (3 - dx) * 64]
    both = lower[:, 192:256]
    for at in range(9):
        part = both[at * 16 : at * 16 + 16]
        for dx in range(3):
            first_ref[dx * 9 + at] = (
                part[4 * dx : 4 * dx + 4, 0:32] + part[4 * dx + 4 : 4 * dx + 8, 32:64]
            )


def call(kernel, outs, limit, scratch=(), cost=None, in_vmem=False):
    return pl.pallas_call(
        kernel,
        out_shape=[
            pltpu.VMEM(shape, dtype) if in_vmem else jax.ShapeDtypeStruct(shape, dtype)
            for shape, dtype in outs
        ],
        cost_estimate=cost,
        scratch_shapes=[pltpu.VMEM(shape, dtype) for shape, dtype in scratch],
        compiler_params=pltpu.CompilerParams(vmem_limit_bytes=limit * 1024 * 1024),
    )


def in_hbm(values):
    return pltpu.with_memory_space_constraint(values, pltpu.HBM)


def swap_cores(values):
    return lax.ppermute(values, "gx", [(0, 1), (1, 0)])


def sum_of_four(part, axis):
    came = [lax.ppermute(part, axis, [(i, i ^ k) for i in range(4)]) for k in range(1, 4)]
    terms = [term.astype(F32) for term in [part] + came]
    return ((terms[0] + terms[1]) + (terms[2] + terms[3])).astype(BF16)


def on_device_kernels(rows_y, volumes, first_kernel, second_kernel, cotangent):
    cot = cotangent.reshape(64, 256)
    k1 = first_kernel.transpose(2, 3, 4, 1, 0).reshape(27, 4, 32)
    k2 = second_kernel.transpose(2, 3, 4, 1, 0).reshape(864, 64)
    own, x_face, near, far, x_near, x_far = call(
        pack_kernel,
        [
            ((136, OWN), F32),
            ((48, OWN), BF16),
            ((160, 128), BF16),
            ((160, 128), BF16),
            ((48, 128), BF16),
            ((48, 128), BF16),
        ],
        16,
    )(in_hbm(volumes.reshape(4, CX * OWN)), in_hbm(cot))
    prepared = call(
        prepare_kernel,
        [
            ((64, 144), BF16),
            ((256, 1728), BF16),
            ((128, 3456), BF16),
            ((KEPT, COARSE), BF16),
            ((MID, OWN), BF16),
            ((MID, 128), BF16),
            ((128, COARSE), BF16),
        ],
        16,
        [((144, 64), F32)],
        pl.CostEstimate(flops=10**9, bytes_accessed=6 * 10**6, transcendentals=0),
    )(x_far, in_hbm(k1), in_hbm(k2))

    def paired(values, partner):
        routes = [
            (g * rows_y + i, partner(g, i)) for g in range(2) for i in range(rows_y)
        ]
        return lax.ppermute(values, ("gx", "yz"), routes)

    def other_side(g, i, across):
        j = i + (1 if i % 2 else -1)
        if 0 <= j < rows_y:
            return (g ^ across) * rows_y + j
        return (1 - g) * rows_y + i

    got_near = lax.ppermute(near, "yz", [(i, i ^ 1) for i in range(rows_y)])
    got_far = paired(far, lambda g, i: other_side(g, i, 0))
    got_x = lax.ppermute(x_face, "gx", [(0, 1), (1, 0)])
    got_x_near = paired(x_near, lambda g, i: (1 - g) * rows_y + (i ^ 1))
    got_x_far = paired(x_far, lambda g, i: other_side(g, i, 1))

    features, act_grad, kept, sent = call(
        functools.partial(main_kernel, rows_y),
        [((64, 256), BF16), ((32, 16, MID), F32), ((144, 256), F32), ((144, 256), BF16)],
        32,
        [
            ((19, 8, FINE), F32),
            ((NF, 144, OWN), BF16),
            ((NF, 64, OWN), F32),
            ((NF, 32, KEPT), BF16),
            ((NF + 2, 288, COARSE), BF16),
            ((NS, 64, MID), F32),
            ((9, 64, COARSE), F32),
            ((20, 64, MID), BF16),
            ((NS + 2, 576, MID), BF16),
            ((16, 64, MID), BF16),
            ((288, 256), F32),
        ],
        in_vmem=True,
    )(
        own.reshape(17, 8, OWN),
        cot,
        got_x,
        got_near,
        got_far,
        got_x_near,
        got_x_far,
        *prepared,
    )
    part = (kept + swap_cores(sent).astype(F32)).astype(BF16)
    mine = sum_of_four(sum_of_four(part, "dp"), "yz")
    second, first = call(unpack_kernel, [((3, 288, 64), F32), ((27, 4, 32), F32)], 8)(
        mine, swap_cores(mine)
    )
    return (
        features.reshape(1, 64, 1, 1, 256),
        act_grad.reshape(1, 32, 1, 1, 2048),
        first.reshape(3, 3, 3, 4, 32).transpose(4, 3, 0, 1, 2),
        second.reshape(3, 3, 3, 32, 64).transpose(4, 3, 0, 1, 2),
    )


def solution(mesh):
    placed = (P("dp", None, "gx", "yz", None), P(), P(), P("dp", None, "gx", "yz", None))
    rows_y = min(4, mesh.shape["yz"])
    rows_z = mesh.shape["yz"] // rows_y
    if rows_z == 1 and rows_y == 4 and mesh.shape["gx"] == 2 and mesh.shape["dp"] == 4:
        body = functools.partial(on_device_kernels, rows_y)
    else:
        body = functools.partial(on_device_plain, rows_y, rows_z)
    return jax.shard_map(
        body,
        mesh=mesh,
        in_specs=placed,
        out_specs=(P("dp", None, "gx", "yz", None), P("dp", None, "gx", "yz", None), P(), P()),
        check_vma=False,
    )
```

```python
import functools

import jax
import jax.numpy as jnp
from jax import lax
from jax.experimental import pallas as pl
from jax.experimental.pallas import tpu as pltpu
from jax.sharding import PartitionSpec as P

CX = 32
CY = 32
CZ = 16
SLOPE = 0.3
F32 = jnp.float32
BF16 = jnp.bfloat16


def leaky(values):
    return jnp.maximum(values, SLOPE * values)


def leaky_slope(values):
    return jnp.where(values > 0, jnp.float32(1.0), jnp.float32(SLOPE))


def convolve_valid(padded, kernel):
    return lax.conv_general_dilated(
        padded,
        kernel,
        (1, 1, 1),
        "VALID",
        dimension_numbers=("NCDHW", "OIDHW", "NCDHW"),
        preferred_element_type=F32,
    )


def kernel_grad(padded, grad):
    result = lax.conv_general_dilated(
        padded,
        grad,
        (1, 1, 1),
        "VALID",
        dimension_numbers=("CNDHW", "IODHW", "NCDHW"),
        preferred_element_type=F32,
    )
    return result.transpose(1, 0, 2, 3, 4)


def average_pool(values):
    bat, chan, xs, ys, zs = values.shape
    return values.reshape(bat, chan, xs // 2, 2, ys // 2, 2, zs // 2, 2).mean(axis=(3, 5, 7))


def spread_back(values):
    bat, chan, xs, ys, zs = values.shape
    grown = jnp.broadcast_to(
        values[:, :, :, None, :, None, :, None], (bat, chan, xs, 2, ys, 2, zs, 2)
    )
    return grown.reshape(bat, chan, 2 * xs, 2 * ys, 2 * zs) * 0.125


def unflatten(values, factor):
    return values[:, :, 0, 0].reshape(
        values.shape[0], values.shape[1], CX // factor, CY // factor, CZ // factor
    )


def flatten(values):
    return values.reshape(values.shape[0], values.shape[1], 1, 1, -1)


def extend_along(values, dim, axis, routes):
    size = values.shape[dim]
    first = lax.slice_in_dim(values, 0, 1, axis=dim)
    last = lax.slice_in_dim(values, size - 1, size, axis=dim)
    before = lax.ppermute(last, axis, routes)
    after = lax.ppermute(first, axis, [(b, a) for a, b in routes])
    return jnp.concatenate([before, values, after], axis=dim)


def extend(values, rows_y, rows_z):
    planes = lax.axis_size("gx")
    count = rows_y * rows_z
    values = extend_along(values, 2, "gx", [(i, i + 1) for i in range(planes - 1)])
    values = extend_along(values, 3, "yz", [(i, i + rows_z) for i in range(count - rows_z)])
    return extend_along(
        values, 4, "yz", [(i, i + 1) for i in range(count - 1) if (i + 1) % rows_z]
    )


def on_device_plain(rows_y, rows_z, volumes, first_kernel, second_kernel, cotangent):
    upstream = unflatten(cotangent, 4)
    padded_in = extend(unflatten(volumes, 1), rows_y, rows_z)
    pre_first = convolve_valid(padded_in, first_kernel)
    act_first = average_pool(leaky(pre_first)).astype(BF16)
    padded_mid = extend(act_first, rows_y, rows_z)
    pre_second = convolve_valid(padded_mid, second_kernel)
    features = average_pool(leaky(pre_second)).astype(BF16)
    grad_second = (spread_back(upstream.astype(F32)) * leaky_slope(pre_second)).astype(BF16)
    flipped = jnp.flip(second_kernel, (2, 3, 4)).transpose(1, 0, 2, 3, 4)
    act_grad = convolve_valid(extend(grad_second, rows_y, rows_z), flipped)
    grad_first = (spread_back(act_grad) * leaky_slope(pre_first)).astype(BF16)
    first_grad, second_grad = lax.psum(
        (kernel_grad(padded_in, grad_first), kernel_grad(padded_mid, grad_second)),
        ("dp", "gx", "yz"),
    )
    return (flatten(features), flatten(act_grad), first_grad, second_grad)


FINE = 48 * CZ
KEPT = 40 * CZ
OWN = CY * CZ
COARSE = 256
MID = (CY // 2) * (CZ // 2)
NF = 18
NS = 17


def grid(shape):
    return [lax.broadcasted_iota(jnp.int32, shape, dim) for dim in range(2)]


def one_where(condition, value=1.0):
    return jnp.where(condition, value, 0.0).astype(BF16)


def fine_to_mid(lane):
    return (lane >> 5) * 8 + ((lane & 15) >> 1) + jnp.where(lane >= OWN + 64, 96, 0)


def rim_table():
    row, lane = grid((256, 256))
    edge = jnp.where(lane < 128, 0, 7)
    place = (row >> 5) * 4 + (row & 3)
    return one_where(jnp.logical_and(((row >> 2) & 7) == edge, place == (lane & 127)))


def pool_first_table():
    row, lane = grid((KEPT, COARSE))
    place = jnp.where((row & 17) == 0, fine_to_mid(row), -1)
    return one_where(place == lane, 0.125)


def spread_first_table():
    row, lane = grid((MID, OWN))
    return one_where(fine_to_mid(lane) == row, 0.125)


def pool_second_table():
    row, lane = grid((MID, 128))
    place = jnp.where((row & 9) == 0, (row >> 4) * 4 + ((row & 7) >> 1), -1)
    return one_where(place == lane, 0.125)


def spread_second_table():
    row, lane = grid((128, COARSE))
    place = jnp.where(lane < MID, (lane >> 4) * 4, jnp.where(lane < 192, 32, 36))
    place = place + ((lane & 7) >> 1)
    used = jnp.logical_or(lane < MID + 8, lane >= COARSE - 8)
    return one_where(jnp.logical_and(used, place == row), 0.125)


def fold_rows(values):
    lane = grid((16, 128))[1]
    kept = [
        jnp.where(lane < 32, values[16 * q : 16 * q + 16], jnp.zeros((16, 128), F32))
        for q in range(4)
    ]
    return kept[0] + sum(pltpu.roll(kept[q], 32 * q, 1) for q in range(1, 4))


def unfold_rows(values):
    parts = [values] + [pltpu.roll(values, 128 - 32 * q, 1) for q in range(1, 4)]
    return jnp.concatenate(parts, axis=0)


def dot(a, b):
    return jnp.dot(a, b, preferred_element_type=F32)


def dot_lanes(a, b):
    return lax.dot_general(a, b, (((1,), (1,)), ((), ())), preferred_element_type=F32)


def pack_kernel(vol_ref, cot_ref, own_ref, x_ref, near_ref, far_ref, xnear_ref, xfar_ref):
    gx = lax.axis_index("gx")
    odd = lax.axis_index("yz") % 2
    own_ref[0:8, :] = jnp.zeros((8, OWN), F32)
    own_ref[128:136, :] = jnp.zeros((8, OWN), F32)
    for x in range(CX):
        own_ref[4 + 4 * x : 8 + 4 * x, :] = vol_ref[:, x * OWN : (x + 1) * OWN].astype(F32)
    start = pl.multiple_of(112 * (1 - gx), 8)
    blank = jnp.zeros((8, OWN), F32)
    face = jnp.concatenate([own_ref[pl.ds(start, 24), :], blank])
    x_ref[0:32, :] = face.astype(BF16)
    cot = cot_ref[...]
    wide = cot.astype(F32)
    first = gx == 0
    end = jnp.where(first, pltpu.roll(wide[:, 128:256], 32, 1), wide[:, 0:128])
    x_ref[32:48, 0:128] = fold_rows(end).astype(BF16)
    x_ref[32:48, 128:OWN] = jnp.zeros((16, OWN - 128), BF16)
    rims = dot(cot, rim_table())
    for low, side_ref, xside_ref in ((odd, near_ref, xnear_ref), (1 - odd, far_ref, xfar_ref)):
        lanes = pl.ds(pl.multiple_of((OWN - 128) * (1 - low), 128), 128)
        tail = jnp.concatenate([own_ref[128:136, lanes], blank[:, 0:128]])
        side_ref[0:128, :] = own_ref[0:128, lanes].astype(BF16)
        side_ref[128:144, :] = tail.astype(BF16)
        edge = jnp.concatenate([own_ref[pl.ds(start, 24), lanes], blank[:, 0:128]])
        xside_ref[0:32, :] = edge.astype(BF16)
        rim = jnp.where(low == 1, rims[:, 0:128], rims[:, 128:256])
        side_ref[144:160, :] = fold_rows(rim).astype(BF16)
        corner = jnp.where(first, pltpu.roll(rim, 100, 1), rim)
        xside_ref[32:48, :] = fold_rows(corner).astype(BF16)


def prepare_kernel(
    after_ref,
    k1_ref,
    k2_ref,
    w1_ref,
    w2_ref,
    w3_ref,
    pool_first_ref,
    spread_first_ref,
    pool_second_ref,
    spread_second_ref,
    w1_rows,
):
    del after_ref
    pool_first_ref[...] = pool_first_table()
    spread_first_ref[...] = spread_first_table()
    pool_second_ref[...] = pool_second_table()
    spread_second_ref[...] = spread_second_table()
    w1_rows[...] = jnp.zeros_like(w1_rows)
    for dx in range(3):
        for at in range(9):
            block = k1_ref[dx * 9 + at].astype(F32)
            for k in range(2):
                row = at * 16 + 4 * (dx + k)
                w1_rows[row : row + 4, 32 * k : 32 * k + 32] = block
    w1_ref[...] = w1_rows[...].T.astype(BF16)
    k2 = k2_ref[...].astype(F32)
    flipped = jnp.concatenate([k2[32 * n : 32 * n + 32] for n in range(26, -1, -1)], axis=1)
    for out_ref, one in ((w2_ref, k2.T), (w3_ref, flipped)):
        high, wide = one.shape
        for r in range(4):
            parts = [jnp.zeros((high, wide // 3 * r), F32)] if r else []
            parts.append(one)
            if r < 3:
                parts.append(jnp.zeros((high, wide // 3 * (3 - r)), F32))
            row = jnp.concatenate(parts, axis=1)
            out_ref[high * r : high * r + high, :] = row.astype(BF16)


def shifted(tile, period, lane):
    size = tile.shape[1]
    z = lane % period
    blank = jnp.zeros_like(tile)
    along = (
        jnp.where(z == 0, blank, pltpu.roll(tile, 1, 1)),
        tile,
        jnp.where(z == period - 1, blank, pltpu.roll(tile, size - 1, 1)),
    )
    return [
        pltpu.roll(moved, shift, 1) if shift else moved
        for shift in (period, 0, size - period)
        for moved in along
    ]


def pooled(values, period):
    blocks = []
    for at in range(0, values.shape[1], 128):
        block = values[:, at : at + 128]
        block = block + pltpu.roll(block, 127, 1)
        blocks.append(block + pltpu.roll(block, 128 - period, 1))
    return jnp.concatenate(blocks, axis=1).astype(BF16)


def split(values):
    top = values.astype(BF16)
    return jnp.concatenate([top, (values - top.astype(F32)).astype(BF16)], axis=0)


def main_kernel(
    rows_y,
    own_ref,
    cot_ref,
    rx_ref,
    rnear_ref,
    rfar_ref,
    rxnear_ref,
    rxfar_ref,
    w1_ref,
    w2_ref,
    w3_ref,
    pool_first_ref,
    spread_first_ref,
    spread_second_ref,
    act_second,
    act_grad_ref,
    kept_ref,
    sent_ref,
    vol,
    cols_first,
    pre_first,
    pooled_first,
    cols_second,
    spread_up,
    grad_own,
    cols_grad,
    half_grad,
    grads_ref,
    sums_ref,
):
    gx = lax.axis_index("gx")
    block_y = lax.axis_index("yz")

    odd = block_y % 2 == 1
    inner = jnp.logical_and(block_y > 0, block_y < rows_y - 1)

    def above_below(near, far):
        near, far = near.astype(F32), far.astype(F32)
        far = jnp.where(inner, far, jnp.zeros_like(far))
        return jnp.where(odd, far, near), jnp.where(odd, near, far)

    vol[...] = jnp.zeros_like(vol)
    up, down = above_below(rnear_ref[0:144, :], rfar_ref[0:144, :])
    vol[pl.ds(2 * gx, 17), :, OWN : OWN + 128] = up[0:136].reshape(17, 8, 128)
    vol[pl.ds(2 * gx, 17), :, OWN + 128 : FINE] = down[0:136].reshape(17, 8, 128)
    vol[pl.ds(2 * gx, 17), :, 0:OWN] = own_ref[...]
    end = pl.ds(16 * (1 - gx), 3)
    vol[end, :, 0:OWN] += rx_ref[0:32, :].astype(F32)[0:24].reshape(3, 8, OWN)
    up, down = above_below(rxnear_ref[0:32, :], rxfar_ref[0:32, :])
    vol[end, :, OWN : OWN + 128] += up[0:24].reshape(3, 8, 128)
    vol[end, :, OWN + 128 : FINE] += down[0:24].reshape(3, 8, 128)

    lane_fine = lax.broadcasted_iota(jnp.int32, (16, FINE), 1)
    near = lax.broadcasted_iota(jnp.int32, (16, 128), 1) < 64
    for j in range(NF):
        tile = jnp.concatenate([vol[j], vol[j + 1]], axis=0).astype(BF16)
        parts = []
        for moved in shifted(tile, CZ, lane_fine):
            edge = jnp.where(near, moved[:, OWN : OWN + 128], moved[:, OWN + 128 : FINE])
            parts.append(jnp.concatenate([moved[:, 0:OWN], edge], axis=1))
        cols = jnp.concatenate(parts, axis=0)
        cols_first[j] = cols[:, 0:OWN]
        pre = dot(w1_ref[...], cols)
        pre_first[j] = pre[:, 0:OWN]
        sloped = leaky(pre)
        pooled_first[j] = pooled(sloped[0:32] + sloped[32:64], CZ)

    lane = lax.broadcasted_iota(jnp.int32, (32, COARSE), 1)
    valid = jnp.logical_or(
        lane < MID,
        jnp.logical_or(
            jnp.logical_and(lane < 192, block_y < rows_y - 1),
            jnp.logical_and(lane >= 192, block_y > 0),
        ),
    )
    cols_second[0] = jnp.zeros((288, COARSE), BF16)
    cols_second[NF + 1] = jnp.zeros((288, COARSE), BF16)
    pick = pool_first_ref[...]
    for step in range(3):
        picked = dot(pooled_first[6 * step : 6 * step + 6].reshape(192, KEPT), pick)
        for k in range(6):
            plane = jnp.where(valid, picked[k * 32 : k * 32 + 32], 0.0).astype(BF16)
            parts = shifted(plane, CZ // 2, lane)
            cols_second[6 * step + k + 1] = jnp.concatenate(parts, axis=0)

    slot = grid((64, 128))[1]

    def upstream(plane, up, down):
        return jnp.where(slot < 32, plane, jnp.where(slot < 36, up, down)).astype(BF16)

    def moved_to(values, lane_from, lane_to):
        shift = (lane_to - lane_from) % 128
        return pltpu.roll(values, shift, 1) if shift else values

    cot = cot_ref[...].astype(F32)
    up, down = above_below(rnear_ref[144:160, :], rfar_ref[144:160, :])
    up, down = unfold_rows(up), unfold_rows(down)
    planes = [
        upstream(
            moved_to(cot[:, p // 4 * 128 : p // 4 * 128 + 128], p % 4 * 32, 0),
            moved_to(up, 4 * p, 32),
            moved_to(down, 4 * p, 36),
        )
        for p in range(8)
    ]
    up, down = above_below(rxnear_ref[32:48, :], rxfar_ref[32:48, :])
    planes.append(
        upstream(
            unfold_rows(rx_ref[32:48, 0:128].astype(F32)),
            moved_to(unfold_rows(up), 0, 32),
            moved_to(unfold_rows(down), 0, 36),
        )
    )
    spread = dot(jnp.concatenate(planes, axis=0), spread_second_ref[...])
    for p in range(8):
        spread_up[p + gx] = spread[64 * p : 64 * p + 64]
    spread_up[8 * (1 - gx)] = spread[512:576]

    lane_grad = lax.broadcasted_iota(jnp.int32, (64, COARSE), 1)
    cols_grad[0] = jnp.zeros((576, MID), BF16)
    cols_grad[NS + 1] = jnp.zeros((576, MID), BF16)
    for k in (0, 1, 18, 19):
        grad_own[k] = jnp.zeros((64, MID), BF16)
    def second_layer(k, pre):
        act_second[k] = leaky(pre[:, 0:MID])
        given = spread_up[(k + gx) // 2]
        rounded = jnp.where(pre > 0, given, SLOPE * given).astype(BF16)
        parts = [moved[:, 0:MID] for moved in shifted(rounded, CZ // 2, lane_grad)]
        cols_grad[k + 1] = jnp.concatenate(parts, axis=0)
        kept = rounded[:, 0:MID]
        if k == 0:
            kept = jnp.where(gx == 0, kept, jnp.zeros_like(kept))
        if k == NS - 1:
            kept = jnp.where(gx == 1, kept, jnp.zeros_like(kept))
        grad_own[k + 2 - gx] = kept

    for k in range(0, NS - 1, 4):
        four = dot(w2_ref[...], cols_second[pl.ds(k + gx, 6)].reshape(1728, COARSE))
        for r in range(4):
            second_layer(k + r, four[64 * r : 64 * r + 64])
    last = cols_second[pl.ds(NS - 1 + gx, 3)].reshape(864, COARSE)
    second_layer(NS - 1, dot(w2_ref[0:64, 0:864], last))

    for base in (0, 8):
        cols = jnp.concatenate(
            [
                cols_grad[pl.ds(base + gx, 6)].reshape(3456, MID),
                cols_grad[pl.ds(base + 4 + gx, 6)].reshape(3456, MID),
            ],
            axis=1,
        )
        back = dot(w3_ref[...], cols)
        for m in range(8):
            row, lanes = 32 * (m % 4), MID * (m // 4)
            plane = back[row : row + 32, lanes : lanes + MID]
            act_grad_ref[:, base + m, :] = plane
            half_grad[base + m] = split(plane)

    left = jnp.concatenate([cols_second[q + 2 * gx][:, 0:MID] for q in range(18)], axis=1)
    right = jnp.concatenate([grad_own[q : q + 3].reshape(192, MID) for q in range(18)], axis=1)
    grads_ref[:, 0:192] = dot_lanes(left, right)

    grow = spread_first_ref[...]
    first = jnp.zeros((144, 64), F32)
    for step in range(4):
        spread = dot(half_grad[4 * step : 4 * step + 4].reshape(256, MID), grow)
        for k in range(4):
            m = 4 * step + k + 2 * gx
            whole = spread[k * 64 : k * 64 + 32] + spread[k * 64 + 32 : k * 64 + 64]
            less = SLOPE * whole
            pre = pre_first[m]
            back = jnp.concatenate(
                [
                    jnp.where(pre[0:32] > 0, whole, less),
                    jnp.where(pre[32:64] > 0, whole, less),
                ],
                axis=0,
            ).astype(BF16)
            first = first + dot_lanes(cols_first[m], back)
    grads_ref[0:144, 192:256] = first
    both = pltpu.roll(grads_ref[0:144, 128:256], 64, 1)
    sums_ref[...] = both + pltpu.roll(pltpu.roll(both, 96, 1), 140, 0)
    slot = grid((72, 128))[1]
    place = grid((24, 128))[1] // 32

    def folded(half):
        rows = pl.multiple_of(144 * half, 8)
        right = grads_ref[pl.ds(rows, 72), 128:256]
        right_next = pltpu.roll(grads_ref[pl.ds(rows + 72, 72), 128:256], 64, 1)
        parts = [
            sums_ref[pl.ds(pl.multiple_of(72 * half + 24 * q, 8), 24), :] for q in range(3)
        ]
        last = jnp.where(place == 2, pltpu.roll(parts[2], 64, 1), jnp.zeros((24, 128), F32))
        last = jnp.where(place == 1, pltpu.roll(parts[1], 32, 1), last)
        last = jnp.where(place == 0, parts[0], last)
        return [grads_ref[pl.ds(rows, 144), 0:128], jnp.where(slot < 64, right, right_next), last]

    for half_ref, half in ((kept_ref, gx), (sent_ref, 1 - gx)):
        row = 0
        for part in folded(half):
            half_ref[row : row + part.shape[0], :] = part.astype(half_ref.dtype)
            row += part.shape[0]


def features_kernel(act_second_ref, pool_second_ref, features_ref):
    gx = lax.axis_index("gx")
    sums = [
        pooled(act_second_ref[2 * p + gx] + act_second_ref[2 * p + 1 + gx], CZ // 2)
        for p in range(8)
    ]
    picked = dot(jnp.concatenate(sums, axis=0), pool_second_ref[...])
    for half in range(2):
        whole = picked[256 * half : 256 * half + 64]
        for k in range(1, 4):
            block = picked[256 * half + 64 * k : 256 * half + 64 * k + 64]
            whole = whole + pltpu.roll(block, 32 * k, 1)
        features_ref[:, 128 * half : 128 * half + 128] = whole.astype(BF16)


def unpack_kernel(mine_ref, other_ref, second_ref, first_ref):
    first = lax.axis_index("gx") == 0
    mine, other = mine_ref[...].astype(F32), other_ref[...].astype(F32)
    halves = jnp.where(first, mine, other), jnp.where(first, other, mine)
    for h, half in enumerate(halves):
        row = 144 * h
        second_ref[2, row : row + 144] = half[0:144, 0:64]
        second_ref[1, row : row + 144] = half[0:144, 64:128]
        second_ref[0, row : row + 72] = half[144:216, 0:64]
        second_ref[0, row + 72 : row + 144] = half[144:216, 64:128]
    for at in range(9):
        for dx in range(3):
            h, row = divmod(at * 16 + 4 * dx, 72)
            q, row = divmod(row, 24)
            first_ref[dx * 9 + at] = halves[h][216 + row : 220 + row, 32 * q : 32 * q + 32]


def call(kernel, outs, limit, scratch=(), cost=None, in_vmem=False):
    return pl.pallas_call(
        kernel,
        out_shape=[
            pltpu.VMEM(shape, dtype) if in_vmem else jax.ShapeDtypeStruct(shape, dtype)
            for shape, dtype in outs
        ],
        cost_estimate=cost,
        scratch_shapes=[pltpu.VMEM(shape, dtype) for shape, dtype in scratch],
        compiler_params=pltpu.CompilerParams(vmem_limit_bytes=limit * 1024 * 1024),
    )


def in_hbm(values):
    return pltpu.with_memory_space_constraint(values, pltpu.HBM)


def swap_cores(values):
    return lax.ppermute(values, "gx", [(0, 1), (1, 0)])


def sum_of_four(part, axis):
    came = [lax.ppermute(part, axis, [(i, i ^ k) for i in range(4)]) for k in range(1, 4)]
    terms = [term.astype(F32) for term in [part] + came]
    return ((terms[0] + terms[1]) + (terms[2] + terms[3])).astype(BF16)


def on_device_kernels(rows_y, volumes, first_kernel, second_kernel, cotangent):
    cot = cotangent.reshape(64, 256)
    k1 = first_kernel.transpose(2, 3, 4, 1, 0).reshape(27, 4, 32)
    k2 = second_kernel.transpose(2, 3, 4, 1, 0).reshape(864, 64)
    own, x_face, near, far, x_near, x_far = call(
        pack_kernel,
        [
            ((136, OWN), F32),
            ((48, OWN), BF16),
            ((160, 128), BF16),
            ((160, 128), BF16),
            ((48, 128), BF16),
            ((48, 128), BF16),
        ],
        16,
    )(in_hbm(volumes.reshape(4, CX * OWN)), in_hbm(cot))
    *weights, pool_first, spread_first, pool_second, spread_second = call(
        prepare_kernel,
        [
            ((64, 144), BF16),
            ((256, 1728), BF16),
            ((128, 3456), BF16),
            ((KEPT, COARSE), BF16),
            ((MID, OWN), BF16),
            ((MID, 128), BF16),
            ((128, COARSE), BF16),
        ],
        16,
        [((144, 64), F32)],
        pl.CostEstimate(flops=10**8, bytes_accessed=2 * 10**6, transcendentals=0),
    )(x_far, in_hbm(k1), in_hbm(k2))

    def paired(values, partner):
        routes = [
            (g * rows_y + i, partner(g, i)) for g in range(2) for i in range(rows_y)
        ]
        return lax.ppermute(values, ("gx", "yz"), routes)

    def other_side(g, i, across):
        j = i + (1 if i % 2 else -1)
        if 0 <= j < rows_y:
            return (g ^ across) * rows_y + j
        return (1 - g) * rows_y + i

    got_near = lax.ppermute(near, "yz", [(i, i ^ 1) for i in range(rows_y)])
    got_far = paired(far, lambda g, i: other_side(g, i, 0))
    got_x = lax.ppermute(x_face, "gx", [(0, 1), (1, 0)])
    got_x_near = paired(x_near, lambda g, i: (1 - g) * rows_y + (i ^ 1))
    got_x_far = paired(x_far, lambda g, i: other_side(g, i, 1))

    act_second, act_grad, kept, sent = call(
        functools.partial(main_kernel, rows_y),
        [
            ((NS, 64, MID), F32),
            ((32, 16, MID), F32),
            ((240, 128), F32),
            ((240, 128), BF16),
        ],
        32,
        [
            ((19, 8, FINE), F32),
            ((NF, 144, OWN), BF16),
            ((NF, 64, OWN), F32),
            ((NF, 32, KEPT), BF16),
            ((NF + 2, 288, COARSE), BF16),
            ((9, 64, COARSE), F32),
            ((20, 64, MID), BF16),
            ((NS + 2, 576, MID), BF16),
            ((16, 64, MID), BF16),
            ((288, 256), F32),
            ((144, 128), F32),
        ],
        in_vmem=True,
    )(
        own.reshape(17, 8, OWN),
        cot,
        got_x,
        got_near,
        got_far,
        got_x_near,
        got_x_far,
        *weights,
        pool_first,
        spread_first,
        spread_second,
    )
    [features] = call(features_kernel, [((64, 256), BF16)], 8)(act_second, pool_second)
    part = (kept + swap_cores(sent).astype(F32)).astype(BF16)
    mine = sum_of_four(sum_of_four(part, "dp"), "yz")
    second, first = call(unpack_kernel, [((3, 288, 64), F32), ((27, 4, 32), F32)], 8)(
        mine, swap_cores(mine)
    )
    return (
        features.reshape(1, 64, 1, 1, 256),
        act_grad.reshape(1, 32, 1, 1, 2048),
        first.reshape(3, 3, 3, 4, 32).transpose(4, 3, 0, 1, 2),
        second.reshape(3, 3, 3, 32, 64).transpose(4, 3, 0, 1, 2),
    )


def solution(mesh):
    placed = (P("dp", None, "gx", "yz", None), P(), P(), P("dp", None, "gx", "yz", None))
    rows_y = min(4, mesh.shape["yz"])
    rows_z = mesh.shape["yz"] // rows_y
    if rows_z == 1 and rows_y == 4 and mesh.shape["gx"] == 2 and mesh.shape["dp"] == 4:
        body = functools.partial(on_device_kernels, rows_y)
    else:
        body = functools.partial(on_device_plain, rows_y, rows_z)
    return jax.shard_map(
        body,
        mesh=mesh,
        in_specs=placed,
        out_specs=(P("dp", None, "gx", "yz", None), P("dp", None, "gx", "yz", None), P(), P()),
        check_vma=False,
    )
```

```python
import functools

import jax
import jax.numpy as jnp
import numpy as np
from jax import lax
from jax.experimental import pallas as pl
from jax.experimental.pallas import tpu as pltpu
from jax.sharding import PartitionSpec as P

CX = 32
CY = 32
CZ = 16
SLOPE = 0.3
F32 = jnp.float32
BF16 = jnp.bfloat16


def leaky(values):
    return jnp.maximum(values, SLOPE * values)


def leaky_slope(values):
    return jnp.where(values > 0, jnp.float32(1.0), jnp.float32(SLOPE))


def convolve_valid(padded, kernel):
    return lax.conv_general_dilated(
        padded,
        kernel,
        (1, 1, 1),
        "VALID",
        dimension_numbers=("NCDHW", "OIDHW", "NCDHW"),
        preferred_element_type=F32,
    )


def kernel_grad(padded, grad):
    result = lax.conv_general_dilated(
        padded,
        grad,
        (1, 1, 1),
        "VALID",
        dimension_numbers=("CNDHW", "IODHW", "NCDHW"),
        preferred_element_type=F32,
    )
    return result.transpose(1, 0, 2, 3, 4)


def average_pool(values):
    bat, chan, xs, ys, zs = values.shape
    return values.reshape(bat, chan, xs // 2, 2, ys // 2, 2, zs // 2, 2).mean(axis=(3, 5, 7))


def spread_back(values):
    bat, chan, xs, ys, zs = values.shape
    grown = jnp.broadcast_to(
        values[:, :, :, None, :, None, :, None], (bat, chan, xs, 2, ys, 2, zs, 2)
    )
    return grown.reshape(bat, chan, 2 * xs, 2 * ys, 2 * zs) * 0.125


def unflatten(values, factor):
    return values[:, :, 0, 0].reshape(
        values.shape[0], values.shape[1], CX // factor, CY // factor, CZ // factor
    )


def flatten(values):
    return values.reshape(values.shape[0], values.shape[1], 1, 1, -1)


def extend_along(values, dim, axis, routes):
    size = values.shape[dim]
    first = lax.slice_in_dim(values, 0, 1, axis=dim)
    last = lax.slice_in_dim(values, size - 1, size, axis=dim)
    before = lax.ppermute(last, axis, routes)
    after = lax.ppermute(first, axis, [(b, a) for a, b in routes])
    return jnp.concatenate([before, values, after], axis=dim)


def extend(values, rows_y, rows_z):
    planes = lax.axis_size("gx")
    count = rows_y * rows_z
    values = extend_along(values, 2, "gx", [(i, i + 1) for i in range(planes - 1)])
    values = extend_along(values, 3, "yz", [(i, i + rows_z) for i in range(count - rows_z)])
    return extend_along(
        values, 4, "yz", [(i, i + 1) for i in range(count - 1) if (i + 1) % rows_z]
    )


def on_device_plain(rows_y, rows_z, volumes, first_kernel, second_kernel, cotangent):
    upstream = unflatten(cotangent, 4)
    padded_in = extend(unflatten(volumes, 1), rows_y, rows_z)
    pre_first = convolve_valid(padded_in, first_kernel)
    act_first = average_pool(leaky(pre_first)).astype(BF16)
    padded_mid = extend(act_first, rows_y, rows_z)
    pre_second = convolve_valid(padded_mid, second_kernel)
    features = average_pool(leaky(pre_second)).astype(BF16)
    grad_second = (spread_back(upstream.astype(F32)) * leaky_slope(pre_second)).astype(BF16)
    flipped = jnp.flip(second_kernel, (2, 3, 4)).transpose(1, 0, 2, 3, 4)
    act_grad = convolve_valid(extend(grad_second, rows_y, rows_z), flipped)
    grad_first = (spread_back(act_grad) * leaky_slope(pre_first)).astype(BF16)
    first_grad, second_grad = lax.psum(
        (kernel_grad(padded_in, grad_first), kernel_grad(padded_mid, grad_second)),
        ("dp", "gx", "yz"),
    )
    return (flatten(features), flatten(act_grad), first_grad, second_grad)


FINE = 48 * CZ
KEPT = 40 * CZ
OWN = CY * CZ
COARSE = 256
MID = (CY // 2) * (CZ // 2)
NF = 18
NS = 17


def grid(shape):
    return [lax.broadcasted_iota(jnp.int32, shape, dim) for dim in range(2)]


def one_where(condition, value=1.0):
    return jnp.where(condition, value, 0.0).astype(BF16)


def fine_to_mid(lane):
    return (lane >> 5) * 8 + ((lane & 15) >> 1) + jnp.where(lane >= OWN + 64, 96, 0)


def rim_table():
    row, lane = grid((256, 256))
    edge = jnp.where(lane < 128, 0, 7)
    place = (row >> 5) * 4 + (row & 3)
    return one_where(jnp.logical_and(((row >> 2) & 7) == edge, place == (lane & 127)))


def pool_first_table():
    row, lane = grid((KEPT, COARSE))
    place = jnp.where((row & 17) == 0, fine_to_mid(row), -1)
    return one_where(place == lane, 0.125)


def spread_first_table():
    row, lane = grid((MID, OWN))
    return one_where(fine_to_mid(lane) == row, 0.125)


def pool_second_table():
    row, lane = grid((MID, 128))
    place = jnp.where((row & 9) == 0, (row >> 4) * 4 + ((row & 7) >> 1), -1)
    return one_where(place == lane, 0.125)


def spread_second_table():
    row, lane = grid((128, COARSE))
    place = jnp.where(lane < MID, (lane >> 4) * 4, jnp.where(lane < 192, 32, 36))
    place = place + ((lane & 7) >> 1)
    used = jnp.logical_or(lane < MID + 8, lane >= COARSE - 8)
    return one_where(jnp.logical_and(used, place == row), 0.125)


def fold_rows(values):
    lane = grid((16, 128))[1]
    kept = [
        jnp.where(lane < 32, values[16 * q : 16 * q + 16], jnp.zeros((16, 128), F32))
        for q in range(4)
    ]
    return kept[0] + sum(pltpu.roll(kept[q], 32 * q, 1) for q in range(1, 4))


def unfold_rows(values):
    parts = [values] + [pltpu.roll(values, 128 - 32 * q, 1) for q in range(1, 4)]
    return jnp.concatenate(parts, axis=0)


def dot(a, b):
    return jnp.dot(a, b, preferred_element_type=F32)


def dot_lanes(a, b):
    return lax.dot_general(a, b, (((1,), (1,)), ((), ())), preferred_element_type=F32)


def pack_kernel(vol_ref, cot_ref, own_ref, x_ref, near_ref, far_ref, xnear_ref, xfar_ref):
    gx = lax.axis_index("gx")
    odd = lax.axis_index("yz") % 2
    own_ref[0:8, :] = jnp.zeros((8, OWN), F32)
    own_ref[128:136, :] = jnp.zeros((8, OWN), F32)
    for x in range(CX):
        own_ref[4 + 4 * x : 8 + 4 * x, :] = vol_ref[:, x * OWN : (x + 1) * OWN].astype(F32)
    start = pl.multiple_of(112 * (1 - gx), 8)
    blank = jnp.zeros((8, OWN), F32)
    face = jnp.concatenate([own_ref[pl.ds(start, 24), :], blank])
    x_ref[0:32, :] = face.astype(BF16)
    cot = cot_ref[...]
    wide = cot.astype(F32)
    first = gx == 0
    end = jnp.where(first, pltpu.roll(wide[:, 128:256], 32, 1), wide[:, 0:128])
    x_ref[32:48, 0:128] = fold_rows(end).astype(BF16)
    x_ref[32:48, 128:OWN] = jnp.zeros((16, OWN - 128), BF16)
    rims = dot(cot, rim_table())
    for low, side_ref, xside_ref in ((odd, near_ref, xnear_ref), (1 - odd, far_ref, xfar_ref)):
        lanes = pl.ds(pl.multiple_of((OWN - 128) * (1 - low), 128), 128)
        tail = jnp.concatenate([own_ref[128:136, lanes], blank[:, 0:128]])
        side_ref[0:128, :] = own_ref[0:128, lanes].astype(BF16)
        side_ref[128:144, :] = tail.astype(BF16)
        edge = jnp.concatenate([own_ref[pl.ds(start, 24), lanes], blank[:, 0:128]])
        xside_ref[0:32, :] = edge.astype(BF16)
        rim = jnp.where(low == 1, rims[:, 0:128], rims[:, 128:256])
        side_ref[144:160, :] = fold_rows(rim).astype(BF16)
        corner = jnp.where(first, pltpu.roll(rim, 100, 1), rim)
        xside_ref[32:48, :] = fold_rows(corner).astype(BF16)


def prepare_kernel(
    after_ref,
    k1_ref,
    k2_ref,
    w1_ref,
    w2_ref,
    w3_ref,
    pool_first_ref,
    spread_first_ref,
    pool_second_ref,
    spread_second_ref,
    w1_rows,
):
    del after_ref
    pool_first_ref[...] = pool_first_table()
    spread_first_ref[...] = spread_first_table()
    pool_second_ref[...] = pool_second_table()
    spread_second_ref[...] = spread_second_table()
    w1_rows[...] = jnp.zeros_like(w1_rows)
    for dx in range(3):
        for at in range(9):
            block = k1_ref[dx * 9 + at].astype(F32)
            for k in range(2):
                row = at * 16 + 4 * (dx + k)
                w1_rows[row : row + 4, 32 * k : 32 * k + 32] = block
    w1_ref[...] = w1_rows[...].T.astype(BF16)
    k2 = k2_ref[...].astype(F32)
    flipped = jnp.concatenate([k2[32 * n : 32 * n + 32] for n in range(26, -1, -1)], axis=1)
    for out_ref, one in ((w2_ref, k2.T), (w3_ref, flipped)):
        high, wide = one.shape
        for r in range(4):
            parts = [jnp.zeros((high, wide // 3 * r), F32)] if r else []
            parts.append(one)
            if r < 3:
                parts.append(jnp.zeros((high, wide // 3 * (3 - r)), F32))
            row = jnp.concatenate(parts, axis=1)
            out_ref[high * r : high * r + high, :] = row.astype(BF16)


def shifted(tile, period, lane):
    size = tile.shape[1]
    z = lane % period
    blank = jnp.zeros_like(tile)
    along = (
        jnp.where(z == 0, blank, pltpu.roll(tile, 1, 1)),
        tile,
        jnp.where(z == period - 1, blank, pltpu.roll(tile, size - 1, 1)),
    )
    return [
        pltpu.roll(moved, shift, 1) if shift else moved
        for shift in (period, 0, size - period)
        for moved in along
    ]


def pooled(values, period):
    blocks = []
    for at in range(0, values.shape[1], 128):
        block = values[:, at : at + 128]
        block = block + pltpu.roll(block, 127, 1)
        blocks.append(block + pltpu.roll(block, 128 - period, 1))
    return jnp.concatenate(blocks, axis=1).astype(BF16)


def split(values):
    top = values.astype(BF16)
    return jnp.concatenate([top, (values - top.astype(F32)).astype(BF16)], axis=0)


def main_kernel(
    rows_y,
    own_ref,
    cot_ref,
    rx_ref,
    rnear_ref,
    rfar_ref,
    rxnear_ref,
    rxfar_ref,
    w1_ref,
    w2_ref,
    w3_ref,
    pool_first_ref,
    spread_first_ref,
    spread_second_ref,
    act_second,
    act_grad_ref,
    kept_ref,
    sent_ref,
    vol,
    cols_first,
    pre_first,
    pooled_first,
    cols_second,
    spread_up,
    grad_own,
    cols_grad,
    half_grad,
    grads_ref,
    sums_ref,
):
    gx = lax.axis_index("gx")
    block_y = lax.axis_index("yz")

    odd = block_y % 2 == 1
    inner = jnp.logical_and(block_y > 0, block_y < rows_y - 1)

    def above_below(near, far):
        near, far = near.astype(F32), far.astype(F32)
        far = jnp.where(inner, far, jnp.zeros_like(far))
        return jnp.where(odd, far, near), jnp.where(odd, near, far)

    vol[...] = jnp.zeros_like(vol)
    up, down = above_below(rnear_ref[0:144, :], rfar_ref[0:144, :])
    vol[pl.ds(2 * gx, 17), :, OWN : OWN + 128] = up[0:136].reshape(17, 8, 128)
    vol[pl.ds(2 * gx, 17), :, OWN + 128 : FINE] = down[0:136].reshape(17, 8, 128)
    vol[pl.ds(2 * gx, 17), :, 0:OWN] = own_ref[...]
    end = pl.ds(16 * (1 - gx), 3)
    vol[end, :, 0:OWN] += rx_ref[0:32, :].astype(F32)[0:24].reshape(3, 8, OWN)
    up, down = above_below(rxnear_ref[0:32, :], rxfar_ref[0:32, :])
    vol[end, :, OWN : OWN + 128] += up[0:24].reshape(3, 8, 128)
    vol[end, :, OWN + 128 : FINE] += down[0:24].reshape(3, 8, 128)

    lane_fine = lax.broadcasted_iota(jnp.int32, (16, FINE), 1)
    near = lax.broadcasted_iota(jnp.int32, (16, 128), 1) < 64
    for j in range(NF):
        tile = jnp.concatenate([vol[j], vol[j + 1]], axis=0).astype(BF16)
        parts = []
        for moved in shifted(tile, CZ, lane_fine):
            edge = jnp.where(near, moved[:, OWN : OWN + 128], moved[:, OWN + 128 : FINE])
            parts.append(jnp.concatenate([moved[:, 0:OWN], edge], axis=1))
        cols = jnp.concatenate(parts, axis=0)
        cols_first[j] = cols[:, 0:OWN]
        pre = dot(w1_ref[...], cols)
        pre_first[j] = pre[:, 0:OWN]
        sloped = leaky(pre)
        pooled_first[j] = pooled(sloped[0:32] + sloped[32:64], CZ)

    lane = lax.broadcasted_iota(jnp.int32, (32, COARSE), 1)
    valid = jnp.logical_or(
        lane < MID,
        jnp.logical_or(
            jnp.logical_and(lane < 192, block_y < rows_y - 1),
            jnp.logical_and(lane >= 192, block_y > 0),
        ),
    )
    cols_second[0] = jnp.zeros((288, COARSE), BF16)
    cols_second[NF + 1] = jnp.zeros((288, COARSE), BF16)
    pick = pool_first_ref[...]
    for step in range(3):
        picked = dot(pooled_first[6 * step : 6 * step + 6].reshape(192, KEPT), pick)
        for k in range(6):
            plane = jnp.where(valid, picked[k * 32 : k * 32 + 32], 0.0).astype(BF16)
            parts = shifted(plane, CZ // 2, lane)
            cols_second[6 * step + k + 1] = jnp.concatenate(parts, axis=0)

    slot = grid((64, 128))[1]

    def upstream(plane, up, down):
        return jnp.where(slot < 32, plane, jnp.where(slot < 36, up, down)).astype(BF16)

    def moved_to(values, lane_from, lane_to):
        shift = (lane_to - lane_from) % 128
        return pltpu.roll(values, shift, 1) if shift else values

    cot = cot_ref[...].astype(F32)
    up, down = above_below(rnear_ref[144:160, :], rfar_ref[144:160, :])
    up, down = unfold_rows(up), unfold_rows(down)
    planes = [
        upstream(
            moved_to(cot[:, p // 4 * 128 : p // 4 * 128 + 128], p % 4 * 32, 0),
            moved_to(up, 4 * p, 32),
            moved_to(down, 4 * p, 36),
        )
        for p in range(8)
    ]
    up, down = above_below(rxnear_ref[32:48, :], rxfar_ref[32:48, :])
    planes.append(
        upstream(
            unfold_rows(rx_ref[32:48, 0:128].astype(F32)),
            moved_to(unfold_rows(up), 0, 32),
            moved_to(unfold_rows(down), 0, 36),
        )
    )
    spread = dot(jnp.concatenate(planes, axis=0), spread_second_ref[...])
    for p in range(8):
        spread_up[p + gx] = spread[64 * p : 64 * p + 64]
    spread_up[8 * (1 - gx)] = spread[512:576]

    lane_grad = lax.broadcasted_iota(jnp.int32, (64, COARSE), 1)
    cols_grad[0] = jnp.zeros((576, MID), BF16)
    cols_grad[NS + 1] = jnp.zeros((576, MID), BF16)
    for k in (0, 1, 18, 19):
        grad_own[k] = jnp.zeros((64, MID), BF16)
    def second_layer(k, pre):
        act_second[k] = leaky(pre[:, 0:MID])
        given = spread_up[(k + gx) // 2]
        rounded = jnp.where(pre > 0, given, SLOPE * given).astype(BF16)
        parts = [moved[:, 0:MID] for moved in shifted(rounded, CZ // 2, lane_grad)]
        cols_grad[k + 1] = jnp.concatenate(parts, axis=0)
        kept = rounded[:, 0:MID]
        if k == 0:
            kept = jnp.where(gx == 0, kept, jnp.zeros_like(kept))
        if k == NS - 1:
            kept = jnp.where(gx == 1, kept, jnp.zeros_like(kept))
        grad_own[k + 2 - gx] = kept

    for k in range(0, NS - 1, 4):
        four = dot(w2_ref[...], cols_second[pl.ds(k + gx, 6)].reshape(1728, COARSE))
        for r in range(4):
            second_layer(k + r, four[64 * r : 64 * r + 64])
    last = cols_second[pl.ds(NS - 1 + gx, 3)].reshape(864, COARSE)
    second_layer(NS - 1, dot(w2_ref[0:64, 0:864], last))

    for base in (0, 8):
        cols = jnp.concatenate(
            [
                cols_grad[pl.ds(base + gx, 6)].reshape(3456, MID),
                cols_grad[pl.ds(base + 4 + gx, 6)].reshape(3456, MID),
            ],
            axis=1,
        )
        back = dot(w3_ref[...], cols)
        for m in range(8):
            row, lanes = 32 * (m % 4), MID * (m // 4)
            plane = back[row : row + 32, lanes : lanes + MID]
            act_grad_ref[:, base + m, :] = plane
            half_grad[base + m] = split(plane)

    left = jnp.concatenate([cols_second[q + 2 * gx][:, 0:MID] for q in range(18)], axis=1)
    right = jnp.concatenate([grad_own[q : q + 3].reshape(192, MID) for q in range(18)], axis=1)
    grads_ref[:, 0:192] = dot_lanes(left, right)

    grow = spread_first_ref[...]
    first = jnp.zeros((144, 64), F32)
    for step in range(4):
        spread = dot(half_grad[4 * step : 4 * step + 4].reshape(256, MID), grow)
        for k in range(4):
            m = 4 * step + k + 2 * gx
            whole = spread[k * 64 : k * 64 + 32] + spread[k * 64 + 32 : k * 64 + 64]
            less = SLOPE * whole
            pre = pre_first[m]
            back = jnp.concatenate(
                [
                    jnp.where(pre[0:32] > 0, whole, less),
                    jnp.where(pre[32:64] > 0, whole, less),
                ],
                axis=0,
            ).astype(BF16)
            first = first + dot_lanes(cols_first[m], back)
    grads_ref[0:144, 192:256] = first
    both = pltpu.roll(grads_ref[0:144, 128:256], 64, 1)
    sums_ref[...] = both + pltpu.roll(pltpu.roll(both, 96, 1), 140, 0)
    slot = grid((72, 128))[1]
    place = grid((24, 128))[1] // 32

    def folded(half):
        rows = pl.multiple_of(144 * half, 8)
        right = grads_ref[pl.ds(rows, 72), 128:256]
        right_next = pltpu.roll(grads_ref[pl.ds(rows + 72, 72), 128:256], 64, 1)
        parts = [
            sums_ref[pl.ds(pl.multiple_of(72 * half + 24 * q, 8), 24), :] for q in range(3)
        ]
        last = jnp.where(place == 2, pltpu.roll(parts[2], 64, 1), jnp.zeros((24, 128), F32))
        last = jnp.where(place == 1, pltpu.roll(parts[1], 32, 1), last)
        last = jnp.where(place == 0, parts[0], last)
        return [grads_ref[pl.ds(rows, 144), 0:128], jnp.where(slot < 64, right, right_next), last]

    for half_ref, half in ((kept_ref, gx), (sent_ref, 1 - gx)):
        row = 0
        for part in folded(half):
            half_ref[row : row + part.shape[0], :] = part.astype(half_ref.dtype)
            row += part.shape[0]


def features_kernel(act_second_ref, pool_second_ref, features_ref):
    gx = lax.axis_index("gx")
    sums = [
        pooled(act_second_ref[2 * p + gx] + act_second_ref[2 * p + 1 + gx], CZ // 2)
        for p in range(8)
    ]
    picked = dot(jnp.concatenate(sums, axis=0), pool_second_ref[...])
    for half in range(2):
        whole = picked[256 * half : 256 * half + 64]
        for k in range(1, 4):
            block = picked[256 * half + 64 * k : 256 * half + 64 * k + 64]
            whole = whole + pltpu.roll(block, 32 * k, 1)
        features_ref[:, 128 * half : 128 * half + 128] = whole.astype(BF16)


def unpack_kernel(mine_ref, other_ref, second_ref, first_ref):
    first = lax.axis_index("gx") == 0
    mine, other = mine_ref[...].astype(F32), other_ref[...].astype(F32)
    halves = jnp.where(first, mine, other), jnp.where(first, other, mine)
    for h, half in enumerate(halves):
        row = 144 * h
        second_ref[2, row : row + 144] = half[0:144, 0:64]
        second_ref[1, row : row + 144] = half[0:144, 64:128]
        second_ref[0, row : row + 72] = half[144:216, 0:64]
        second_ref[0, row + 72 : row + 144] = half[144:216, 64:128]
    for at in range(9):
        for dx in range(3):
            h, row = divmod(at * 16 + 4 * dx, 72)
            q, row = divmod(row, 24)
            first_ref[dx * 9 + at] = halves[h][216 + row : 220 + row, 32 * q : 32 * q + 32]


def call(kernel, outs, limit, scratch=(), cost=None, in_vmem=False):
    return pl.pallas_call(
        kernel,
        out_shape=[
            pltpu.VMEM(shape, dtype) if in_vmem else jax.ShapeDtypeStruct(shape, dtype)
            for shape, dtype in outs
        ],
        cost_estimate=cost,
        scratch_shapes=[pltpu.VMEM(shape, dtype) for shape, dtype in scratch],
        compiler_params=pltpu.CompilerParams(vmem_limit_bytes=limit * 1024 * 1024),
    )


def in_hbm(values):
    return pltpu.with_memory_space_constraint(values, pltpu.HBM)


def swap_cores(values):
    return lax.ppermute(values, "gx", [(0, 1), (1, 0)])


def sum_of_four(part, axis, orders):
    names = ("dp", "gx", "yz")
    sizes = [lax.axis_size(name) for name in names]
    terms = [part]
    for step in range(3):
        routes = []
        for at in np.ndindex(*sizes):
            to = list(at)
            to[names.index(axis)] ^= orders[at[1]][step]
            routes.append(
                tuple((d * sizes[1] + g) * sizes[2] + z for d, g, z in (at, tuple(to)))
            )
        terms.append(lax.ppermute(part, names, routes))
    terms = [term.astype(F32) for term in terms]
    return ((terms[0] + terms[1]) + (terms[2] + terms[3])).astype(BF16)


def on_device_kernels(rows_y, volumes, first_kernel, second_kernel, cotangent):
    cot = cotangent.reshape(64, 256)
    k1 = first_kernel.transpose(2, 3, 4, 1, 0).reshape(27, 4, 32)
    k2 = second_kernel.transpose(2, 3, 4, 1, 0).reshape(864, 64)
    own, x_face, near, far, x_near, x_far = call(
        pack_kernel,
        [
            ((136, OWN), F32),
            ((48, OWN), BF16),
            ((160, 128), BF16),
            ((160, 128), BF16),
            ((48, 128), BF16),
            ((48, 128), BF16),
        ],
        16,
    )(in_hbm(volumes.reshape(4, CX * OWN)), in_hbm(cot))
    *weights, pool_first, spread_first, pool_second, spread_second = call(
        prepare_kernel,
        [
            ((64, 144), BF16),
            ((256, 1728), BF16),
            ((128, 3456), BF16),
            ((KEPT, COARSE), BF16),
            ((MID, OWN), BF16),
            ((MID, 128), BF16),
            ((128, COARSE), BF16),
        ],
        16,
        [((144, 64), F32)],
        pl.CostEstimate(flops=10**8, bytes_accessed=2 * 10**6, transcendentals=0),
    )(x_far, in_hbm(k1), in_hbm(k2))

    def paired(values, partner):
        routes = [
            (g * rows_y + i, partner(g, i)) for g in range(2) for i in range(rows_y)
        ]
        return lax.ppermute(values, ("gx", "yz"), routes)

    def other_side(g, i, across):
        j = i + (1 if i % 2 else -1)
        if 0 <= j < rows_y:
            return (g ^ across) * rows_y + j
        return (1 - g) * rows_y + i

    got_near = lax.ppermute(near, "yz", [(i, i ^ 1) for i in range(rows_y)])
    got_far = paired(far, lambda g, i: other_side(g, i, 0))
    got_x = lax.ppermute(x_face, "gx", [(0, 1), (1, 0)])
    got_x_near = paired(x_near, lambda g, i: (1 - g) * rows_y + (i ^ 1))
    got_x_far = paired(x_far, lambda g, i: other_side(g, i, 1))

    act_second, act_grad, kept, sent = call(
        functools.partial(main_kernel, rows_y),
        [
            ((NS, 64, MID), F32),
            ((32, 16, MID), F32),
            ((240, 128), F32),
            ((240, 128), BF16),
        ],
        32,
        [
            ((19, 8, FINE), F32),
            ((NF, 144, OWN), BF16),
            ((NF, 64, OWN), F32),
            ((NF, 32, KEPT), BF16),
            ((NF + 2, 288, COARSE), BF16),
            ((9, 64, COARSE), F32),
            ((20, 64, MID), BF16),
            ((NS + 2, 576, MID), BF16),
            ((16, 64, MID), BF16),
            ((288, 256), F32),
            ((144, 128), F32),
        ],
        in_vmem=True,
    )(
        own.reshape(17, 8, OWN),
        cot,
        got_x,
        got_near,
        got_far,
        got_x_near,
        got_x_far,
        *weights,
        pool_first,
        spread_first,
        spread_second,
    )
    [features] = call(features_kernel, [((64, 256), BF16)], 8)(act_second, pool_second)
    part = (kept + swap_cores(sent).astype(F32)).astype(BF16)
    part = sum_of_four(part, "dp", ((1, 2, 3), (2, 1, 3)))
    part, features = lax.optimization_barrier((part, features))
    mine = sum_of_four(part, "yz", ((3, 2, 1), (1, 2, 3)))
    second, first = call(unpack_kernel, [((3, 288, 64), F32), ((27, 4, 32), F32)], 8)(
        mine, swap_cores(mine)
    )
    return (
        features.reshape(1, 64, 1, 1, 256),
        act_grad.reshape(1, 32, 1, 1, 2048),
        first.reshape(3, 3, 3, 4, 32).transpose(4, 3, 0, 1, 2),
        second.reshape(3, 3, 3, 32, 64).transpose(4, 3, 0, 1, 2),
    )


def solution(mesh):
    placed = (P("dp", None, "gx", "yz", None), P(), P(), P("dp", None, "gx", "yz", None))
    rows_y = min(4, mesh.shape["yz"])
    rows_z = mesh.shape["yz"] // rows_y
    if rows_z == 1 and rows_y == 4 and mesh.shape["gx"] == 2 and mesh.shape["dp"] == 4:
        body = functools.partial(on_device_kernels, rows_y)
    else:
        body = functools.partial(on_device_plain, rows_y, rows_z)
    return jax.shard_map(
        body,
        mesh=mesh,
        in_specs=placed,
        out_specs=(P("dp", None, "gx", "yz", None), P("dp", None, "gx", "yz", None), P(), P()),
        check_vma=False,
    )
```

```python
import functools

import jax
import jax.numpy as jnp
from jax import lax
from jax.experimental import pallas as pl
from jax.experimental.pallas import tpu as pltpu
from jax.sharding import PartitionSpec as P

CX = 32
CY = 32
CZ = 16
SLOPE = 0.3
F32 = jnp.float32
BF16 = jnp.bfloat16


def leaky(values):
    return jnp.maximum(values, SLOPE * values)


def leaky_slope(values):
    return jnp.where(values > 0, jnp.float32(1.0), jnp.float32(SLOPE))


def convolve_valid(padded, kernel):
    return lax.conv_general_dilated(
        padded,
        kernel,
        (1, 1, 1),
        "VALID",
        dimension_numbers=("NCDHW", "OIDHW", "NCDHW"),
        preferred_element_type=F32,
    )


def kernel_grad(padded, grad):
    result = lax.conv_general_dilated(
        padded,
        grad,
        (1, 1, 1),
        "VALID",
        dimension_numbers=("CNDHW", "IODHW", "NCDHW"),
        preferred_element_type=F32,
    )
    return result.transpose(1, 0, 2, 3, 4)


def average_pool(values):
    bat, chan, xs, ys, zs = values.shape
    return values.reshape(bat, chan, xs // 2, 2, ys // 2, 2, zs // 2, 2).mean(axis=(3, 5, 7))


def spread_back(values):
    bat, chan, xs, ys, zs = values.shape
    grown = jnp.broadcast_to(
        values[:, :, :, None, :, None, :, None], (bat, chan, xs, 2, ys, 2, zs, 2)
    )
    return grown.reshape(bat, chan, 2 * xs, 2 * ys, 2 * zs) * 0.125


def unflatten(values, factor):
    return values[:, :, 0, 0].reshape(
        values.shape[0], values.shape[1], CX // factor, CY // factor, CZ // factor
    )


def flatten(values):
    return values.reshape(values.shape[0], values.shape[1], 1, 1, -1)


def extend_along(values, dim, axis, routes):
    size = values.shape[dim]
    first = lax.slice_in_dim(values, 0, 1, axis=dim)
    last = lax.slice_in_dim(values, size - 1, size, axis=dim)
    before = lax.ppermute(last, axis, routes)
    after = lax.ppermute(first, axis, [(b, a) for a, b in routes])
    return jnp.concatenate([before, values, after], axis=dim)


def extend(values, rows_y, rows_z):
    planes = lax.axis_size("gx")
    count = rows_y * rows_z
    values = extend_along(values, 2, "gx", [(i, i + 1) for i in range(planes - 1)])
    values = extend_along(values, 3, "yz", [(i, i + rows_z) for i in range(count - rows_z)])
    return extend_along(
        values, 4, "yz", [(i, i + 1) for i in range(count - 1) if (i + 1) % rows_z]
    )


def on_device_plain(rows_y, rows_z, volumes, first_kernel, second_kernel, cotangent):
    upstream = unflatten(cotangent, 4)
    padded_in = extend(unflatten(volumes, 1), rows_y, rows_z)
    pre_first = convolve_valid(padded_in, first_kernel)
    act_first = average_pool(leaky(pre_first)).astype(BF16)
    padded_mid = extend(act_first, rows_y, rows_z)
    pre_second = convolve_valid(padded_mid, second_kernel)
    features = average_pool(leaky(pre_second)).astype(BF16)
    grad_second = (spread_back(upstream.astype(F32)) * leaky_slope(pre_second)).astype(BF16)
    flipped = jnp.flip(second_kernel, (2, 3, 4)).transpose(1, 0, 2, 3, 4)
    act_grad = convolve_valid(extend(grad_second, rows_y, rows_z), flipped)
    grad_first = (spread_back(act_grad) * leaky_slope(pre_first)).astype(BF16)
    first_grad, second_grad = lax.psum(
        (kernel_grad(padded_in, grad_first), kernel_grad(padded_mid, grad_second)),
        ("dp", "gx", "yz"),
    )
    return (flatten(features), flatten(act_grad), first_grad, second_grad)


FINE = 48 * CZ
KEPT = 40 * CZ
OWN = CY * CZ
COARSE = 256
MID = (CY // 2) * (CZ // 2)
NF = 18
NS = 17


def grid(shape):
    return [lax.broadcasted_iota(jnp.int32, shape, dim) for dim in range(2)]


def one_where(condition, value=1.0):
    return jnp.where(condition, value, 0.0).astype(BF16)


def fine_to_mid(lane):
    return (lane >> 5) * 8 + ((lane & 15) >> 1) + jnp.where(lane >= OWN + 64, 96, 0)


def rim_table():
    row, lane = grid((256, 256))
    edge = jnp.where(lane < 128, 0, 7)
    place = (row >> 5) * 4 + (row & 3)
    return one_where(jnp.logical_and(((row >> 2) & 7) == edge, place == (lane & 127)))


def pool_first_table():
    row, lane = grid((KEPT, COARSE))
    place = jnp.where((row & 17) == 0, fine_to_mid(row), -1)
    return one_where(place == lane, 0.125)


def spread_first_table():
    row, lane = grid((MID, OWN))
    return one_where(fine_to_mid(lane) == row, 0.125)


def pool_second_table():
    row, lane = grid((MID, 128))
    place = jnp.where((row & 9) == 0, (row >> 4) * 4 + ((row & 7) >> 1), -1)
    return one_where(place == lane, 0.125)


def spread_second_table():
    row, lane = grid((128, COARSE))
    place = jnp.where(lane < MID, (lane >> 4) * 4, jnp.where(lane < 192, 32, 36))
    place = place + ((lane & 7) >> 1)
    used = jnp.logical_or(lane < MID + 8, lane >= COARSE - 8)
    return one_where(jnp.logical_and(used, place == row), 0.125)


def fold_rows(values):
    lane = grid((16, 128))[1]
    kept = [
        jnp.where(lane < 32, values[16 * q : 16 * q + 16], jnp.zeros((16, 128), F32))
        for q in range(4)
    ]
    return kept[0] + sum(pltpu.roll(kept[q], 32 * q, 1) for q in range(1, 4))


def unfold_rows(values):
    parts = [values] + [pltpu.roll(values, 128 - 32 * q, 1) for q in range(1, 4)]
    return jnp.concatenate(parts, axis=0)


def dot(a, b):
    return jnp.dot(a, b, preferred_element_type=F32)


def dot_lanes(a, b):
    return lax.dot_general(a, b, (((1,), (1,)), ((), ())), preferred_element_type=F32)


def pack_kernel(vol_ref, cot_ref, own_ref, x_ref, near_ref, far_ref, xnear_ref, xfar_ref):
    gx = lax.axis_index("gx")
    odd = lax.axis_index("yz") % 2
    own_ref[0:8, :] = jnp.zeros((8, OWN), F32)
    own_ref[128:136, :] = jnp.zeros((8, OWN), F32)
    for x in range(CX):
        own_ref[4 + 4 * x : 8 + 4 * x, :] = vol_ref[:, x * OWN : (x + 1) * OWN].astype(F32)
    start = pl.multiple_of(112 * (1 - gx), 8)
    blank = jnp.zeros((8, OWN), F32)
    face = jnp.concatenate([own_ref[pl.ds(start, 24), :], blank])
    x_ref[0:32, :] = face.astype(BF16)
    cot = cot_ref[...]
    wide = cot.astype(F32)
    first = gx == 0
    end = jnp.where(first, pltpu.roll(wide[:, 128:256], 32, 1), wide[:, 0:128])
    x_ref[32:48, 0:128] = fold_rows(end).astype(BF16)
    x_ref[32:48, 128:OWN] = jnp.zeros((16, OWN - 128), BF16)
    rims = dot(cot, rim_table())
    for low, side_ref, xside_ref in ((odd, near_ref, xnear_ref), (1 - odd, far_ref, xfar_ref)):
        lanes = pl.ds(pl.multiple_of((OWN - 128) * (1 - low), 128), 128)
        tail = jnp.concatenate([own_ref[128:136, lanes], blank[:, 0:128]])
        side_ref[0:128, :] = own_ref[0:128, lanes].astype(BF16)
        side_ref[128:144, :] = tail.astype(BF16)
        edge = jnp.concatenate([own_ref[pl.ds(start, 24), lanes], blank[:, 0:128]])
        xside_ref[0:32, :] = edge.astype(BF16)
        rim = jnp.where(low == 1, rims[:, 0:128], rims[:, 128:256])
        side_ref[144:160, :] = fold_rows(rim).astype(BF16)
        corner = jnp.where(first, pltpu.roll(rim, 100, 1), rim)
        xside_ref[32:48, :] = fold_rows(corner).astype(BF16)


def prepare_kernel(
    after_ref,
    k1_ref,
    k2_ref,
    w1_ref,
    w2_ref,
    w3_ref,
    pool_first_ref,
    spread_first_ref,
    pool_second_ref,
    spread_second_ref,
    w1_rows,
):
    del after_ref
    pool_first_ref[...] = pool_first_table()
    spread_first_ref[...] = spread_first_table()
    pool_second_ref[...] = pool_second_table()
    spread_second_ref[...] = spread_second_table()
    w1_rows[...] = jnp.zeros_like(w1_rows)
    for dx in range(3):
        for at in range(9):
            block = k1_ref[dx * 9 + at].astype(F32)
            for k in range(2):
                row = at * 16 + 4 * (dx + k)
                w1_rows[row : row + 4, 32 * k : 32 * k + 32] = block
    w1_ref[...] = w1_rows[...].T.astype(BF16)
    k2 = k2_ref[...].astype(F32)
    flipped = jnp.concatenate([k2[32 * n : 32 * n + 32] for n in range(26, -1, -1)], axis=1)
    for out_ref, one in ((w2_ref, k2.T), (w3_ref, flipped)):
        high, wide = one.shape
        for r in range(4):
            parts = [jnp.zeros((high, wide // 3 * r), F32)] if r else []
            parts.append(one)
            if r < 3:
                parts.append(jnp.zeros((high, wide // 3 * (3 - r)), F32))
            row = jnp.concatenate(parts, axis=1)
            out_ref[high * r : high * r + high, :] = row.astype(BF16)


def shifted(tile, period, lane):
    size = tile.shape[1]
    z = lane % period
    blank = jnp.zeros_like(tile)
    along = (
        jnp.where(z == 0, blank, pltpu.roll(tile, 1, 1)),
        tile,
        jnp.where(z == period - 1, blank, pltpu.roll(tile, size - 1, 1)),
    )
    return [
        pltpu.roll(moved, shift, 1) if shift else moved
        for shift in (period, 0, size - period)
        for moved in along
    ]


def pooled(values, period):
    blocks = []
    for at in range(0, values.shape[1], 128):
        block = values[:, at : at + 128]
        block = block + pltpu.roll(block, 127, 1)
        blocks.append(block + pltpu.roll(block, 128 - period, 1))
    return jnp.concatenate(blocks, axis=1).astype(BF16)


def split(values):
    top = values.astype(BF16)
    return jnp.concatenate([top, (values - top.astype(F32)).astype(BF16)], axis=0)


def main_kernel(
    rows_y,
    own_ref,
    cot_ref,
    rx_ref,
    rnear_ref,
    rfar_ref,
    rxnear_ref,
    rxfar_ref,
    w1_ref,
    w2_ref,
    w3_ref,
    pool_first_ref,
    spread_first_ref,
    spread_second_ref,
    act_second,
    act_grad_ref,
    kept_ref,
    sent_ref,
    vol,
    cols_first,
    pre_first,
    pooled_first,
    cols_second,
    spread_up,
    grad_own,
    cols_grad,
    half_grad,
    grads_ref,
    sums_ref,
):
    gx = lax.axis_index("gx")
    block_y = lax.axis_index("yz")

    odd = block_y % 2 == 1
    inner = jnp.logical_and(block_y > 0, block_y < rows_y - 1)

    def above_below(near, far):
        near, far = near.astype(F32), far.astype(F32)
        far = jnp.where(inner, far, jnp.zeros_like(far))
        return jnp.where(odd, far, near), jnp.where(odd, near, far)

    vol[...] = jnp.zeros_like(vol)
    up, down = above_below(rnear_ref[0:144, :], rfar_ref[0:144, :])
    vol[pl.ds(2 * gx, 17), :, OWN : OWN + 128] = up[0:136].reshape(17, 8, 128)
    vol[pl.ds(2 * gx, 17), :, OWN + 128 : FINE] = down[0:136].reshape(17, 8, 128)
    vol[pl.ds(2 * gx, 17), :, 0:OWN] = own_ref[...]
    end = pl.ds(16 * (1 - gx), 3)
    vol[end, :, 0:OWN] += rx_ref[0:32, :].astype(F32)[0:24].reshape(3, 8, OWN)
    up, down = above_below(rxnear_ref[0:32, :], rxfar_ref[0:32, :])
    vol[end, :, OWN : OWN + 128] += up[0:24].reshape(3, 8, 128)
    vol[end, :, OWN + 128 : FINE] += down[0:24].reshape(3, 8, 128)

    slot = grid((64, 128))[1]

    def upstream(plane, up, down):
        return jnp.where(slot < 32, plane, jnp.where(slot < 36, up, down)).astype(BF16)

    def moved_to(values, lane_from, lane_to):
        shift = (lane_to - lane_from) % 128
        return pltpu.roll(values, shift, 1) if shift else values

    cot = cot_ref[...].astype(F32)
    up, down = above_below(rnear_ref[144:160, :], rfar_ref[144:160, :])
    up, down = unfold_rows(up), unfold_rows(down)
    planes = [
        upstream(
            moved_to(cot[:, p // 4 * 128 : p // 4 * 128 + 128], p % 4 * 32, 0),
            moved_to(up, 4 * p, 32),
            moved_to(down, 4 * p, 36),
        )
        for p in range(8)
    ]
    up, down = above_below(rxnear_ref[32:48, :], rxfar_ref[32:48, :])
    planes.append(
        upstream(
            unfold_rows(rx_ref[32:48, 0:128].astype(F32)),
            moved_to(unfold_rows(up), 0, 32),
            moved_to(unfold_rows(down), 0, 36),
        )
    )
    spread = dot(jnp.concatenate(planes, axis=0), spread_second_ref[...])
    for p in range(8):
        spread_up[p + gx] = spread[64 * p : 64 * p + 64]
    spread_up[8 * (1 - gx)] = spread[512:576]

    lane_fine = lax.broadcasted_iota(jnp.int32, (16, FINE), 1)
    near = lax.broadcasted_iota(jnp.int32, (16, 128), 1) < 64

    def first_layer(j):
        tile = jnp.concatenate([vol[j], vol[j + 1]], axis=0).astype(BF16)
        parts = []
        for moved in shifted(tile, CZ, lane_fine):
            edge = jnp.where(near, moved[:, OWN : OWN + 128], moved[:, OWN + 128 : FINE])
            parts.append(jnp.concatenate([moved[:, 0:OWN], edge], axis=1))
        cols = jnp.concatenate(parts, axis=0)
        cols_first[j] = cols[:, 0:OWN]
        pre = dot(w1_ref[...], cols)
        pre_first[j] = pre[:, 0:OWN]
        sloped = leaky(pre)
        pooled_first[j] = pooled(sloped[0:32] + sloped[32:64], CZ)

    lane = lax.broadcasted_iota(jnp.int32, (32, COARSE), 1)
    valid = jnp.logical_or(
        lane < MID,
        jnp.logical_or(
            jnp.logical_and(lane < 192, block_y < rows_y - 1),
            jnp.logical_and(lane >= 192, block_y > 0),
        ),
    )

    def columns_second(step):
        six = pooled_first[6 * step : 6 * step + 6].reshape(192, KEPT)
        picked = dot(six, pool_first_ref[...])
        for k in range(6):
            plane = jnp.where(valid, picked[k * 32 : k * 32 + 32], 0.0).astype(BF16)
            parts = shifted(plane, CZ // 2, lane)
            cols_second[6 * step + k + 1] = jnp.concatenate(parts, axis=0)

    lane_grad = lax.broadcasted_iota(jnp.int32, (64, COARSE), 1)

    def second_layer(k, pre):
        act_second[k] = leaky(pre[:, 0:MID])
        given = spread_up[(k + gx) // 2]
        rounded = jnp.where(pre > 0, given, SLOPE * given).astype(BF16)
        parts = [moved[:, 0:MID] for moved in shifted(rounded, CZ // 2, lane_grad)]
        cols_grad[k + 1] = jnp.concatenate(parts, axis=0)
        kept = rounded[:, 0:MID]
        if k == 0:
            kept = jnp.where(gx == 0, kept, jnp.zeros_like(kept))
        if k == NS - 1:
            kept = jnp.where(gx == 1, kept, jnp.zeros_like(kept))
        grad_own[k + 2 - gx] = kept

    def four_second(k):
        four = dot(w2_ref[...], cols_second[pl.ds(k + gx, 6)].reshape(1728, COARSE))
        for r in range(4):
            second_layer(k + r, four[64 * r : 64 * r + 64])

    def eight_back(base):
        cols = jnp.concatenate(
            [
                cols_grad[pl.ds(base + gx, 6)].reshape(3456, MID),
                cols_grad[pl.ds(base + 4 + gx, 6)].reshape(3456, MID),
            ],
            axis=1,
        )
        back = dot(w3_ref[...], cols)
        for m in range(8):
            row, lanes = 32 * (m % 4), MID * (m // 4)
            plane = back[row : row + 32, lanes : lanes + MID]
            act_grad_ref[:, base + m, :] = plane
            half_grad[base + m] = split(plane)

    def four_first(step):
        spread = dot(
            half_grad[4 * step : 4 * step + 4].reshape(256, MID), spread_first_ref[...]
        )
        backs = []
        for k in range(4):
            whole = spread[k * 64 : k * 64 + 32] + spread[k * 64 + 32 : k * 64 + 64]
            less = SLOPE * whole
            pre = pre_first[4 * step + k + 2 * gx]
            parts = [jnp.where(pre[r : r + 32] > 0, whole, less) for r in (0, 32)]
            backs.append(jnp.concatenate(parts, axis=0).astype(BF16))
        cols = [cols_first[4 * step + k + 2 * gx] for k in range(4)]
        return dot_lanes(jnp.concatenate(cols, axis=1), jnp.concatenate(backs, axis=1))

    cols_second[0] = jnp.zeros((288, COARSE), BF16)
    cols_second[NF + 1] = jnp.zeros((288, COARSE), BF16)
    cols_grad[0] = jnp.zeros((576, MID), BF16)
    cols_grad[NS + 1] = jnp.zeros((576, MID), BF16)
    for k in (0, 1, 18, 19):
        grad_own[k] = jnp.zeros((64, MID), BF16)

    for step in range(3):
        for j in range(6 * step, 6 * step + 6):
            first_layer(j)
        columns_second(step)
        four_second(4 * step)
    eight_back(0)
    four_second(12)
    last = cols_second[pl.ds(NS - 1 + gx, 3)].reshape(864, COARSE)
    second_layer(NS - 1, dot(w2_ref[0:64, 0:864], last))
    first = four_first(0) + four_first(1)
    eight_back(8)
    left = jnp.concatenate([cols_second[q + 2 * gx][:, 0:MID] for q in range(18)], axis=1)
    right = jnp.concatenate([grad_own[q : q + 3].reshape(192, MID) for q in range(18)], axis=1)
    grads_ref[:, 0:192] = dot_lanes(left, right)
    first = first + four_first(2) + four_first(3)
    grads_ref[0:144, 192:256] = first

    both = pltpu.roll(grads_ref[0:144, 128:256], 64, 1)
    sums_ref[...] = both + pltpu.roll(pltpu.roll(both, 96, 1), 140, 0)
    slot = grid((72, 128))[1]
    place = grid((24, 128))[1] // 32

    def folded(half):
        rows = pl.multiple_of(144 * half, 8)
        right = grads_ref[pl.ds(rows, 72), 128:256]
        right_next = pltpu.roll(grads_ref[pl.ds(rows + 72, 72), 128:256], 64, 1)
        parts = [
            sums_ref[pl.ds(pl.multiple_of(72 * half + 24 * q, 8), 24), :] for q in range(3)
        ]
        last = jnp.where(place == 2, pltpu.roll(parts[2], 64, 1), jnp.zeros((24, 128), F32))
        last = jnp.where(place == 1, pltpu.roll(parts[1], 32, 1), last)
        last = jnp.where(place == 0, parts[0], last)
        return [grads_ref[pl.ds(rows, 144), 0:128], jnp.where(slot < 64, right, right_next), last]

    for half_ref, half in ((kept_ref, gx), (sent_ref, 1 - gx)):
        row = 0
        for part in folded(half):
            half_ref[row : row + part.shape[0], :] = part.astype(half_ref.dtype)
            row += part.shape[0]


def features_kernel(act_second_ref, pool_second_ref, features_ref):
    gx = lax.axis_index("gx")
    sums = [
        pooled(act_second_ref[2 * p + gx] + act_second_ref[2 * p + 1 + gx], CZ // 2)
        for p in range(8)
    ]
    picked = dot(jnp.concatenate(sums, axis=0), pool_second_ref[...])
    for half in range(2):
        whole = picked[256 * half : 256 * half + 64]
        for k in range(1, 4):
            block = picked[256 * half + 64 * k : 256 * half + 64 * k + 64]
            whole = whole + pltpu.roll(block, 32 * k, 1)
        features_ref[:, 128 * half : 128 * half + 128] = whole.astype(BF16)


def unpack_kernel(mine_ref, other_ref, second_ref, first_ref):
    first = lax.axis_index("gx") == 0
    mine, other = mine_ref[...].astype(F32), other_ref[...].astype(F32)
    halves = jnp.where(first, mine, other), jnp.where(first, other, mine)
    for h, half in enumerate(halves):
        row = 144 * h
        second_ref[2, row : row + 144] = half[0:144, 0:64]
        second_ref[1, row : row + 144] = half[0:144, 64:128]
        second_ref[0, row : row + 72] = half[144:216, 0:64]
        second_ref[0, row + 72 : row + 144] = half[144:216, 64:128]
    for at in range(9):
        for dx in range(3):
            h, row = divmod(at * 16 + 4 * dx, 72)
            q, row = divmod(row, 24)
            first_ref[dx * 9 + at] = halves[h][216 + row : 220 + row, 32 * q : 32 * q + 32]


def call(kernel, outs, limit, scratch=(), cost=None, in_vmem=False):
    return pl.pallas_call(
        kernel,
        out_shape=[
            pltpu.VMEM(shape, dtype) if in_vmem else jax.ShapeDtypeStruct(shape, dtype)
            for shape, dtype in outs
        ],
        cost_estimate=cost,
        scratch_shapes=[pltpu.VMEM(shape, dtype) for shape, dtype in scratch],
        compiler_params=pltpu.CompilerParams(vmem_limit_bytes=limit * 1024 * 1024),
    )


def in_hbm(values):
    return pltpu.with_memory_space_constraint(values, pltpu.HBM)


def swap_cores(values):
    return lax.ppermute(values, "gx", [(0, 1), (1, 0)])


def sum_of_four(part, axis):
    came = [lax.ppermute(part, axis, [(i, i ^ k) for i in range(4)]) for k in range(1, 4)]
    terms = [term.astype(F32) for term in [part] + came]
    return ((terms[0] + terms[1]) + (terms[2] + terms[3])).astype(BF16)


def on_device_kernels(rows_y, volumes, first_kernel, second_kernel, cotangent):
    cot = cotangent.reshape(64, 256)
    k1 = first_kernel.transpose(2, 3, 4, 1, 0).reshape(27, 4, 32)
    k2 = second_kernel.transpose(2, 3, 4, 1, 0).reshape(864, 64)
    own, x_face, near, far, x_near, x_far = call(
        pack_kernel,
        [
            ((136, OWN), F32),
            ((48, OWN), BF16),
            ((160, 128), BF16),
            ((160, 128), BF16),
            ((48, 128), BF16),
            ((48, 128), BF16),
        ],
        16,
    )(in_hbm(volumes.reshape(4, CX * OWN)), in_hbm(cot))
    *weights, pool_first, spread_first, pool_second, spread_second = call(
        prepare_kernel,
        [
            ((64, 144), BF16),
            ((256, 1728), BF16),
            ((128, 3456), BF16),
            ((KEPT, COARSE), BF16),
            ((MID, OWN), BF16),
            ((MID, 128), BF16),
            ((128, COARSE), BF16),
        ],
        16,
        [((144, 64), F32)],
        pl.CostEstimate(flops=10**8, bytes_accessed=2 * 10**6, transcendentals=0),
    )(x_far, in_hbm(k1), in_hbm(k2))

    def paired(values, partner):
        routes = [
            (g * rows_y + i, partner(g, i)) for g in range(2) for i in range(rows_y)
        ]
        return lax.ppermute(values, ("gx", "yz"), routes)

    def other_side(g, i, across):
        j = i + (1 if i % 2 else -1)
        if 0 <= j < rows_y:
            return (g ^ across) * rows_y + j
        return (1 - g) * rows_y + i

    got_near = lax.ppermute(near, "yz", [(i, i ^ 1) for i in range(rows_y)])
    got_far = paired(far, lambda g, i: other_side(g, i, 0))
    got_x = lax.ppermute(x_face, "gx", [(0, 1), (1, 0)])
    got_x_near = paired(x_near, lambda g, i: (1 - g) * rows_y + (i ^ 1))
    got_x_far = paired(x_far, lambda g, i: other_side(g, i, 1))

    act_second, act_grad, kept, sent = call(
        functools.partial(main_kernel, rows_y),
        [
            ((NS, 64, MID), F32),
            ((32, 16, MID), F32),
            ((240, 128), F32),
            ((240, 128), BF16),
        ],
        32,
        [
            ((19, 8, FINE), F32),
            ((NF, 144, OWN), BF16),
            ((NF, 64, OWN), F32),
            ((NF, 32, KEPT), BF16),
            ((NF + 2, 288, COARSE), BF16),
            ((9, 64, COARSE), F32),
            ((20, 64, MID), BF16),
            ((NS + 2, 576, MID), BF16),
            ((16, 64, MID), BF16),
            ((288, 256), F32),
            ((144, 128), F32),
        ],
        in_vmem=True,
    )(
        own.reshape(17, 8, OWN),
        cot,
        got_x,
        got_near,
        got_far,
        got_x_near,
        got_x_far,
        *weights,
        pool_first,
        spread_first,
        spread_second,
    )
    [features] = call(features_kernel, [((64, 256), BF16)], 8)(act_second, pool_second)
    part = (kept + swap_cores(sent).astype(F32)).astype(BF16)
    part = sum_of_four(part, "dp")
    part, features = lax.optimization_barrier((part, features))
    mine = sum_of_four(part, "yz")
    second, first = call(unpack_kernel, [((3, 288, 64), F32), ((27, 4, 32), F32)], 8)(
        mine, swap_cores(mine)
    )
    return (
        features.reshape(1, 64, 1, 1, 256),
        act_grad.reshape(1, 32, 1, 1, 2048),
        first.reshape(3, 3, 3, 4, 32).transpose(4, 3, 0, 1, 2),
        second.reshape(3, 3, 3, 32, 64).transpose(4, 3, 0, 1, 2),
    )


def solution(mesh):
    placed = (P("dp", None, "gx", "yz", None), P(), P(), P("dp", None, "gx", "yz", None))
    rows_y = min(4, mesh.shape["yz"])
    rows_z = mesh.shape["yz"] // rows_y
    if rows_z == 1 and rows_y == 4 and mesh.shape["gx"] == 2 and mesh.shape["dp"] == 4:
        body = functools.partial(on_device_kernels, rows_y)
    else:
        body = functools.partial(on_device_plain, rows_y, rows_z)
    return jax.shard_map(
        body,
        mesh=mesh,
        in_specs=placed,
        out_specs=(P("dp", None, "gx", "yz", None), P("dp", None, "gx", "yz", None), P(), P()),
        check_vma=False,
    )
```

```python
import functools

import jax
import jax.numpy as jnp
from jax import lax
from jax.experimental import pallas as pl
from jax.experimental.pallas import tpu as pltpu
from jax.sharding import PartitionSpec as P

CX = 32
CY = 32
CZ = 16
SLOPE = 0.3
F32 = jnp.float32
BF16 = jnp.bfloat16


def leaky(values):
    return jnp.maximum(values, SLOPE * values)


def leaky_slope(values):
    return jnp.where(values > 0, jnp.float32(1.0), jnp.float32(SLOPE))


def convolve_valid(padded, kernel):
    return lax.conv_general_dilated(
        padded,
        kernel,
        (1, 1, 1),
        "VALID",
        dimension_numbers=("NCDHW", "OIDHW", "NCDHW"),
        preferred_element_type=F32,
    )


def kernel_grad(padded, grad):
    result = lax.conv_general_dilated(
        padded,
        grad,
        (1, 1, 1),
        "VALID",
        dimension_numbers=("CNDHW", "IODHW", "NCDHW"),
        preferred_element_type=F32,
    )
    return result.transpose(1, 0, 2, 3, 4)


def average_pool(values):
    bat, chan, xs, ys, zs = values.shape
    return values.reshape(bat, chan, xs // 2, 2, ys // 2, 2, zs // 2, 2).mean(axis=(3, 5, 7))


def spread_back(values):
    bat, chan, xs, ys, zs = values.shape
    grown = jnp.broadcast_to(
        values[:, :, :, None, :, None, :, None], (bat, chan, xs, 2, ys, 2, zs, 2)
    )
    return grown.reshape(bat, chan, 2 * xs, 2 * ys, 2 * zs) * 0.125


def unflatten(values, factor):
    return values[:, :, 0, 0].reshape(
        values.shape[0], values.shape[1], CX // factor, CY // factor, CZ // factor
    )


def flatten(values):
    return values.reshape(values.shape[0], values.shape[1], 1, 1, -1)


def extend_along(values, dim, axis, routes):
    size = values.shape[dim]
    first = lax.slice_in_dim(values, 0, 1, axis=dim)
    last = lax.slice_in_dim(values, size - 1, size, axis=dim)
    before = lax.ppermute(last, axis, routes)
    after = lax.ppermute(first, axis, [(b, a) for a, b in routes])
    return jnp.concatenate([before, values, after], axis=dim)


def extend(values, rows_y, rows_z):
    planes = lax.axis_size("gx")
    count = rows_y * rows_z
    values = extend_along(values, 2, "gx", [(i, i + 1) for i in range(planes - 1)])
    values = extend_along(values, 3, "yz", [(i, i + rows_z) for i in range(count - rows_z)])
    return extend_along(
        values, 4, "yz", [(i, i + 1) for i in range(count - 1) if (i + 1) % rows_z]
    )


def on_device_plain(rows_y, rows_z, volumes, first_kernel, second_kernel, cotangent):
    upstream = unflatten(cotangent, 4)
    padded_in = extend(unflatten(volumes, 1), rows_y, rows_z)
    pre_first = convolve_valid(padded_in, first_kernel)
    act_first = average_pool(leaky(pre_first)).astype(BF16)
    padded_mid = extend(act_first, rows_y, rows_z)
    pre_second = convolve_valid(padded_mid, second_kernel)
    features = average_pool(leaky(pre_second)).astype(BF16)
    grad_second = (spread_back(upstream.astype(F32)) * leaky_slope(pre_second)).astype(BF16)
    flipped = jnp.flip(second_kernel, (2, 3, 4)).transpose(1, 0, 2, 3, 4)
    act_grad = convolve_valid(extend(grad_second, rows_y, rows_z), flipped)
    grad_first = (spread_back(act_grad) * leaky_slope(pre_first)).astype(BF16)
    first_grad, second_grad = lax.psum(
        (kernel_grad(padded_in, grad_first), kernel_grad(padded_mid, grad_second)),
        ("dp", "gx", "yz"),
    )
    return (flatten(features), flatten(act_grad), first_grad, second_grad)


FINE = 48 * CZ
KEPT = 40 * CZ
OWN = CY * CZ
COARSE = 256
MID = (CY // 2) * (CZ // 2)
NF = 18
NS = 17


def grid(shape):
    return [lax.broadcasted_iota(jnp.int32, shape, dim) for dim in range(2)]


def one_where(condition, value=1.0):
    return jnp.where(condition, value, 0.0).astype(BF16)


def fine_to_mid(lane):
    return (lane >> 5) * 8 + ((lane & 15) >> 1) + jnp.where(lane >= OWN + 64, 96, 0)


def rim_table():
    row, lane = grid((256, 256))
    edge = jnp.where(lane < 128, 0, 7)
    place = (row >> 5) * 4 + (row & 3)
    return one_where(jnp.logical_and(((row >> 2) & 7) == edge, place == (lane & 127)))


def pool_first_table():
    row, lane = grid((KEPT, COARSE))
    place = jnp.where((row & 17) == 0, fine_to_mid(row), -1)
    return one_where(place == lane, 0.125)


def spread_first_table():
    row, lane = grid((MID, OWN))
    return one_where(fine_to_mid(lane) == row, 0.125)


def pool_second_table():
    row, lane = grid((MID, 128))
    place = jnp.where((row & 9) == 0, (row >> 4) * 4 + ((row & 7) >> 1), -1)
    return one_where(place == lane, 0.125)


def spread_second_table():
    row, lane = grid((128, COARSE))
    place = jnp.where(lane < MID, (lane >> 4) * 4, jnp.where(lane < 192, 32, 36))
    place = place + ((lane & 7) >> 1)
    used = jnp.logical_or(lane < MID + 8, lane >= COARSE - 8)
    return one_where(jnp.logical_and(used, place == row), 0.125)


def fold_rows(values):
    lane = grid((16, 128))[1]
    kept = [
        jnp.where(lane < 32, values[16 * q : 16 * q + 16], jnp.zeros((16, 128), F32))
        for q in range(4)
    ]
    return kept[0] + sum(pltpu.roll(kept[q], 32 * q, 1) for q in range(1, 4))


def unfold_rows(values):
    parts = [values] + [pltpu.roll(values, 128 - 32 * q, 1) for q in range(1, 4)]
    return jnp.concatenate(parts, axis=0)


def dot(a, b):
    return jnp.dot(a, b, preferred_element_type=F32)


def dot_lanes(a, b):
    return lax.dot_general(a, b, (((1,), (1,)), ((), ())), preferred_element_type=F32)


def pack_kernel(vol_ref, cot_ref, own_ref, x_ref, near_ref, far_ref):
    gx = lax.axis_index("gx")
    odd = lax.axis_index("yz") % 2
    own_ref[0:8, :] = jnp.zeros((8, OWN), F32)
    own_ref[128:136, :] = jnp.zeros((8, OWN), F32)
    for x in range(CX):
        own_ref[4 + 4 * x : 8 + 4 * x, :] = vol_ref[:, x * OWN : (x + 1) * OWN].astype(F32)
    start = pl.multiple_of(112 * (1 - gx), 8)
    blank = jnp.zeros((8, OWN), F32)
    face = jnp.concatenate([own_ref[pl.ds(start, 24), :], blank])
    x_ref[0:32, :] = face.astype(BF16)
    cot = cot_ref[...]
    wide = cot.astype(F32)
    first = gx == 0
    end = jnp.where(first, pltpu.roll(wide[:, 128:256], 32, 1), wide[:, 0:128])
    x_ref[32:48, 0:128] = fold_rows(end).astype(BF16)
    x_ref[32:48, 128:OWN] = jnp.zeros((16, OWN - 128), BF16)
    rims = dot(cot, rim_table())
    for low, side_ref in ((odd, near_ref), (1 - odd, far_ref)):
        lanes = pl.ds(pl.multiple_of((OWN - 128) * (1 - low), 128), 128)
        tail = jnp.concatenate([own_ref[128:136, lanes], blank[:, 0:128]])
        side_ref[0:128, :] = own_ref[0:128, lanes].astype(BF16)
        side_ref[128:144, :] = tail.astype(BF16)
        rim = jnp.where(low == 1, rims[:, 0:128], rims[:, 128:256])
        side_ref[144:160, :] = fold_rows(rim).astype(BF16)


def prepare_kernel(
    after_ref,
    k1_ref,
    k2_ref,
    w1_ref,
    w2_ref,
    w3_ref,
    pool_first_ref,
    spread_first_ref,
    pool_second_ref,
    spread_second_ref,
    w1_rows,
):
    del after_ref
    pool_first_ref[...] = pool_first_table()
    spread_first_ref[...] = spread_first_table()
    pool_second_ref[...] = pool_second_table()
    spread_second_ref[...] = spread_second_table()
    w1_rows[...] = jnp.zeros_like(w1_rows)
    for dx in range(3):
        for at in range(9):
            block = k1_ref[dx * 9 + at].astype(F32)
            for k in range(2):
                row = at * 16 + 4 * (dx + k)
                w1_rows[row : row + 4, 32 * k : 32 * k + 32] = block
    w1_ref[...] = w1_rows[...].T.astype(BF16)
    k2 = k2_ref[...].astype(F32)
    flipped = jnp.concatenate([k2[32 * n : 32 * n + 32] for n in range(26, -1, -1)], axis=1)
    for out_ref, one in ((w2_ref, k2.T), (w3_ref, flipped)):
        high, wide = one.shape
        for r in range(4):
            parts = [jnp.zeros((high, wide // 3 * r), F32)] if r else []
            parts.append(one)
            if r < 3:
                parts.append(jnp.zeros((high, wide // 3 * (3 - r)), F32))
            row = jnp.concatenate(parts, axis=1)
            out_ref[high * r : high * r + high, :] = row.astype(BF16)


def shifted(tile, period, lane):
    size = tile.shape[1]
    z = lane % period
    blank = jnp.zeros_like(tile)
    along = (
        jnp.where(z == 0, blank, pltpu.roll(tile, 1, 1)),
        tile,
        jnp.where(z == period - 1, blank, pltpu.roll(tile, size - 1, 1)),
    )
    return [
        pltpu.roll(moved, shift, 1) if shift else moved
        for shift in (period, 0, size - period)
        for moved in along
    ]


def pooled(values, period):
    blocks = []
    for at in range(0, values.shape[1], 128):
        block = values[:, at : at + 128]
        block = block + pltpu.roll(block, 127, 1)
        blocks.append(block + pltpu.roll(block, 128 - period, 1))
    return jnp.concatenate(blocks, axis=1).astype(BF16)


def split(values):
    top = values.astype(BF16)
    return jnp.concatenate([top, (values - top.astype(F32)).astype(BF16)], axis=0)


def main_kernel(
    rows_y,
    own_ref,
    cot_ref,
    rx_ref,
    rnear_ref,
    rfar_ref,
    w1_ref,
    w2_ref,
    w3_ref,
    pool_first_ref,
    spread_first_ref,
    spread_second_ref,
    act_second,
    act_grad_ref,
    kept_ref,
    sent_ref,
    vol,
    cols_first,
    pre_first,
    pooled_first,
    cols_second,
    spread_up,
    grad_own,
    cols_grad,
    half_grad,
    grads_ref,
    sums_ref,
):
    gx = lax.axis_index("gx")
    block_y = lax.axis_index("yz")

    odd = block_y % 2 == 1
    inner = jnp.logical_and(block_y > 0, block_y < rows_y - 1)

    def above_below(near, far):
        near, far = near.astype(F32), far.astype(F32)
        far = jnp.where(inner, far, jnp.zeros_like(far))
        return jnp.where(odd, far, near), jnp.where(odd, near, far)

    vol[...] = jnp.zeros_like(vol)
    up, down = above_below(rnear_ref[0:144, :], rfar_ref[0:144, :])
    vol[pl.ds(2 * gx, 17), :, OWN : OWN + 128] = up[0:136].reshape(17, 8, 128)
    vol[pl.ds(2 * gx, 17), :, OWN + 128 : FINE] = down[0:136].reshape(17, 8, 128)
    vol[pl.ds(2 * gx, 17), :, 0:OWN] = own_ref[...]
    end = pl.ds(16 * (1 - gx), 3)
    vol[end, :, 0:OWN] += rx_ref[0:32, 0:OWN].astype(F32)[0:24].reshape(3, 8, OWN)
    up, down = above_below(rx_ref[0:32, OWN : OWN + 128], rx_ref[0:32, OWN + 128 : FINE])
    vol[end, :, OWN : OWN + 128] += up[0:24].reshape(3, 8, 128)
    vol[end, :, OWN + 128 : FINE] += down[0:24].reshape(3, 8, 128)

    slot = grid((64, 128))[1]

    def upstream(plane, up, down):
        return jnp.where(slot < 32, plane, jnp.where(slot < 36, up, down)).astype(BF16)

    def moved_to(values, lane_from, lane_to):
        shift = (lane_to - lane_from) % 128
        return pltpu.roll(values, shift, 1) if shift else values

    cot = cot_ref[...].astype(F32)
    up, down = above_below(rnear_ref[144:160, :], rfar_ref[144:160, :])
    up, down = unfold_rows(up), unfold_rows(down)
    planes = [
        upstream(
            moved_to(cot[:, p // 4 * 128 : p // 4 * 128 + 128], p % 4 * 32, 0),
            moved_to(up, 4 * p, 32),
            moved_to(down, 4 * p, 36),
        )
        for p in range(8)
    ]
    up, down = above_below(rx_ref[32:48, OWN : OWN + 128], rx_ref[32:48, OWN + 128 : FINE])
    up, down = unfold_rows(up), unfold_rows(down)
    planes.append(
        upstream(
            unfold_rows(rx_ref[32:48, 0:128].astype(F32)),
            jnp.where(gx == 0, moved_to(up, 0, 32), moved_to(up, 28, 32)),
            jnp.where(gx == 0, moved_to(down, 0, 36), moved_to(down, 28, 36)),
        )
    )
    spread = dot(jnp.concatenate(planes, axis=0), spread_second_ref[...])
    for p in range(8):
        spread_up[p + gx] = spread[64 * p : 64 * p + 64]
    spread_up[8 * (1 - gx)] = spread[512:576]

    lane_fine = lax.broadcasted_iota(jnp.int32, (16, FINE), 1)
    near = lax.broadcasted_iota(jnp.int32, (16, 128), 1) < 64

    def two_first(first):
        both = []
        for j in (first, first + 1):
            tile = jnp.concatenate([vol[j], vol[j + 1]], axis=0).astype(BF16)
            parts = []
            for moved in shifted(tile, CZ, lane_fine):
                edge = jnp.where(near, moved[:, OWN : OWN + 128], moved[:, OWN + 128 : FINE])
                parts.append(jnp.concatenate([moved[:, 0:OWN], edge], axis=1))
            both.append(jnp.concatenate(parts, axis=0))
            cols_first[j] = both[-1][:, 0:OWN]
        wide = dot(w1_ref[...], jnp.concatenate(both, axis=1))
        for k in range(2):
            pre = wide[:, KEPT * k : KEPT * k + KEPT]
            pre_first[first + k] = pre[:, 0:OWN]
            sloped = leaky(pre)
            pooled_first[first + k] = pooled(sloped[0:32] + sloped[32:64], CZ)

    lane = lax.broadcasted_iota(jnp.int32, (32, COARSE), 1)
    valid = jnp.logical_or(
        lane < MID,
        jnp.logical_or(
            jnp.logical_and(lane < 192, block_y < rows_y - 1),
            jnp.logical_and(lane >= 192, block_y > 0),
        ),
    )

    def columns_second(start, count):
        planes = pooled_first[start : start + count].reshape(32 * count, KEPT)
        picked = dot(planes, pool_first_ref[...])
        for k in range(count):
            plane = jnp.where(valid, picked[k * 32 : k * 32 + 32], 0.0).astype(BF16)
            parts = shifted(plane, CZ // 2, lane)
            cols_second[start + k + 1] = jnp.concatenate(parts, axis=0)

    lane_grad = lax.broadcasted_iota(jnp.int32, (64, COARSE), 1)

    def second_layer(k, pre):
        act_second[k] = leaky(pre[:, 0:MID])
        given = spread_up[(k + gx) // 2]
        rounded = jnp.where(pre > 0, given, SLOPE * given).astype(BF16)
        parts = [moved[:, 0:MID] for moved in shifted(rounded, CZ // 2, lane_grad)]
        cols_grad[k + 1] = jnp.concatenate(parts, axis=0)
        kept = rounded[:, 0:MID]
        if k == 0:
            kept = jnp.where(gx == 0, kept, jnp.zeros_like(kept))
        if k == NS - 1:
            kept = jnp.where(gx == 1, kept, jnp.zeros_like(kept))
        grad_own[k + 2 - gx] = kept

    def four_second(k):
        four = dot(w2_ref[...], cols_second[pl.ds(k + gx, 6)].reshape(1728, COARSE))
        for r in range(4):
            second_layer(k + r, four[64 * r : 64 * r + 64])

    def eight_back(base):
        cols = jnp.concatenate(
            [
                cols_grad[pl.ds(base + gx, 6)].reshape(3456, MID),
                cols_grad[pl.ds(base + 4 + gx, 6)].reshape(3456, MID),
            ],
            axis=1,
        )
        back = dot(w3_ref[...], cols)
        for m in range(8):
            row, lanes = 32 * (m % 4), MID * (m // 4)
            plane = back[row : row + 32, lanes : lanes + MID]
            act_grad_ref[:, base + m, :] = plane
            half_grad[base + m] = split(plane)

    def four_first(step):
        spread = dot(
            half_grad[4 * step : 4 * step + 4].reshape(256, MID), spread_first_ref[...]
        )
        backs = []
        for k in range(4):
            whole = spread[k * 64 : k * 64 + 32] + spread[k * 64 + 32 : k * 64 + 64]
            less = SLOPE * whole
            pre = pre_first[4 * step + k + 2 * gx]
            parts = [jnp.where(pre[r : r + 32] > 0, whole, less) for r in (0, 32)]
            backs.append(jnp.concatenate(parts, axis=0).astype(BF16))
        cols = [cols_first[4 * step + k + 2 * gx] for k in range(4)]
        return dot_lanes(jnp.concatenate(cols, axis=1), jnp.concatenate(backs, axis=1))

    cols_second[0] = jnp.zeros((288, COARSE), BF16)
    cols_second[NF + 1] = jnp.zeros((288, COARSE), BF16)
    cols_grad[0] = jnp.zeros((576, MID), BF16)
    cols_grad[NS + 1] = jnp.zeros((576, MID), BF16)
    for k in (0, 1, 18, 19):
        grad_own[k] = jnp.zeros((64, MID), BF16)

    for start, count in ((0, 10), (10, 8)):
        for j in range(start, start + count, 2):
            two_first(j)
        columns_second(start, count)
        four_second(start // 10 * 8)
        if not start:
            four_second(4)
    eight_back(0)
    four_second(12)
    last = cols_second[pl.ds(NS - 1 + gx, 3)].reshape(864, COARSE)
    second_layer(NS - 1, dot(w2_ref[0:64, 0:864], last))
    first = four_first(0) + four_first(1)
    eight_back(8)
    left = jnp.concatenate([cols_second[q + 2 * gx][:, 0:MID] for q in range(18)], axis=1)
    right = jnp.concatenate([grad_own[q : q + 3].reshape(192, MID) for q in range(18)], axis=1)
    grads_ref[:, 0:192] = dot_lanes(left, right)
    first = first + four_first(2) + four_first(3)
    grads_ref[0:144, 192:256] = first

    both = pltpu.roll(grads_ref[0:144, 128:256], 64, 1)
    sums_ref[...] = both + pltpu.roll(pltpu.roll(both, 96, 1), 140, 0)
    slot = grid((72, 128))[1]
    place = grid((24, 128))[1] // 32

    def folded(half):
        rows = pl.multiple_of(144 * half, 8)
        right = grads_ref[pl.ds(rows, 72), 128:256]
        right_next = pltpu.roll(grads_ref[pl.ds(rows + 72, 72), 128:256], 64, 1)
        parts = [
            sums_ref[pl.ds(pl.multiple_of(72 * half + 24 * q, 8), 24), :] for q in range(3)
        ]
        last = jnp.where(place == 2, pltpu.roll(parts[2], 64, 1), jnp.zeros((24, 128), F32))
        last = jnp.where(place == 1, pltpu.roll(parts[1], 32, 1), last)
        last = jnp.where(place == 0, parts[0], last)
        return [grads_ref[pl.ds(rows, 144), 0:128], jnp.where(slot < 64, right, right_next), last]

    for half_ref, half in ((kept_ref, gx), (sent_ref, 1 - gx)):
        row = 0
        for part in folded(half):
            half_ref[row : row + part.shape[0], :] = part.astype(half_ref.dtype)
            row += part.shape[0]


def features_kernel(act_second_ref, pool_second_ref, features_ref):
    gx = lax.axis_index("gx")
    sums = [
        pooled(act_second_ref[2 * p + gx] + act_second_ref[2 * p + 1 + gx], CZ // 2)
        for p in range(8)
    ]
    picked = dot(jnp.concatenate(sums, axis=0), pool_second_ref[...])
    for half in range(2):
        whole = picked[256 * half : 256 * half + 64]
        for k in range(1, 4):
            block = picked[256 * half + 64 * k : 256 * half + 64 * k + 64]
            whole = whole + pltpu.roll(block, 32 * k, 1)
        features_ref[:, 128 * half : 128 * half + 128] = whole.astype(BF16)


def unpack_kernel(mine_ref, other_ref, second_ref, first_ref):
    first = lax.axis_index("gx") == 0
    mine, other = mine_ref[...].astype(F32), other_ref[...].astype(F32)
    halves = jnp.where(first, mine, other), jnp.where(first, other, mine)
    for h, half in enumerate(halves):
        row = 144 * h
        second_ref[2, row : row + 144] = half[0:144, 0:64]
        second_ref[1, row : row + 144] = half[0:144, 64:128]
        second_ref[0, row : row + 72] = half[144:216, 0:64]
        second_ref[0, row + 72 : row + 144] = half[144:216, 64:128]
    for at in range(9):
        for dx in range(3):
            h, row = divmod(at * 16 + 4 * dx, 72)
            q, row = divmod(row, 24)
            first_ref[dx * 9 + at] = halves[h][216 + row : 220 + row, 32 * q : 32 * q + 32]


def call(kernel, outs, limit, scratch=(), cost=None, in_vmem=False):
    return pl.pallas_call(
        kernel,
        out_shape=[
            pltpu.VMEM(shape, dtype) if in_vmem else jax.ShapeDtypeStruct(shape, dtype)
            for shape, dtype in outs
        ],
        cost_estimate=cost,
        scratch_shapes=[pltpu.VMEM(shape, dtype) for shape, dtype in scratch],
        compiler_params=pltpu.CompilerParams(vmem_limit_bytes=limit * 1024 * 1024),
    )


def in_hbm(values):
    return pltpu.with_memory_space_constraint(values, pltpu.HBM)


def swap_cores(values):
    return lax.ppermute(values, "gx", [(0, 1), (1, 0)])


def sum_of_four(part, axis):
    came = [lax.ppermute(part, axis, [(i, i ^ k) for i in range(4)]) for k in range(1, 4)]
    terms = [term.astype(F32) for term in [part] + came]
    return ((terms[0] + terms[1]) + (terms[2] + terms[3])).astype(BF16)


def on_device_kernels(rows_y, volumes, first_kernel, second_kernel, cotangent):
    cot = cotangent.reshape(64, 256)
    k1 = first_kernel.transpose(2, 3, 4, 1, 0).reshape(27, 4, 32)
    k2 = second_kernel.transpose(2, 3, 4, 1, 0).reshape(864, 64)
    own, x_face, near, far = call(
        pack_kernel,
        [
            ((136, OWN), F32),
            ((48, OWN), BF16),
            ((160, 128), BF16),
            ((160, 128), BF16),
        ],
        16,
    )(in_hbm(volumes.reshape(4, CX * OWN)), in_hbm(cot))
    *weights, pool_first, spread_first, pool_second, spread_second = call(
        prepare_kernel,
        [
            ((64, 144), BF16),
            ((256, 1728), BF16),
            ((128, 3456), BF16),
            ((KEPT, COARSE), BF16),
            ((MID, OWN), BF16),
            ((MID, 128), BF16),
            ((128, COARSE), BF16),
        ],
        16,
        [((144, 64), F32)],
        pl.CostEstimate(flops=10**8, bytes_accessed=2 * 10**6, transcendentals=0),
    )(far, in_hbm(k1), in_hbm(k2))

    def other_side(g, i):
        j = i + (1 if i % 2 else -1)
        return g * rows_y + j if 0 <= j < rows_y else (1 - g) * rows_y + i

    routes = [(g * rows_y + i, other_side(g, i)) for g in range(2) for i in range(rows_y)]
    got_near = lax.ppermute(near, "yz", [(i, i ^ 1) for i in range(rows_y)])
    got_far = lax.ppermute(far, ("gx", "yz"), routes)
    x_face, spread_first = lax.optimization_barrier((x_face, spread_first))
    start = 112 * (1 - lax.axis_index("gx"))
    strips = [
        jnp.concatenate([lax.dynamic_slice(got, (start, 0), (32, 128)), got[144:160]])
        for got in (got_near, got_far)
    ]
    got_x = swap_cores(jnp.concatenate([x_face] + strips, axis=1))

    act_second, act_grad, kept, sent = call(
        functools.partial(main_kernel, rows_y),
        [
            ((NS, 64, MID), F32),
            ((32, 16, MID), F32),
            ((240, 128), F32),
            ((240, 128), BF16),
        ],
        32,
        [
            ((19, 8, FINE), F32),
            ((NF, 144, OWN), BF16),
            ((NF, 64, OWN), F32),
            ((NF, 32, KEPT), BF16),
            ((NF + 2, 288, COARSE), BF16),
            ((9, 64, COARSE), F32),
            ((20, 64, MID), BF16),
            ((NS + 2, 576, MID), BF16),
            ((16, 64, MID), BF16),
            ((288, 256), F32),
            ((144, 128), F32),
        ],
        in_vmem=True,
    )(
        own.reshape(17, 8, OWN),
        cot,
        got_x,
        got_near,
        got_far,
        *weights,
        pool_first,
        spread_first,
        spread_second,
    )
    [features] = call(features_kernel, [((64, 256), BF16)], 8)(act_second, pool_second)
    part = (kept + swap_cores(sent).astype(F32)).astype(BF16)
    part = sum_of_four(part, "dp")
    part, features = lax.optimization_barrier((part, features))
    mine = sum_of_four(part, "yz")
    second, first = call(unpack_kernel, [((3, 288, 64), F32), ((27, 4, 32), F32)], 8)(
        mine, swap_cores(mine)
    )
    return (
        features.reshape(1, 64, 1, 1, 256),
        act_grad.reshape(1, 32, 1, 1, 2048),
        first.reshape(3, 3, 3, 4, 32).transpose(4, 3, 0, 1, 2),
        second.reshape(3, 3, 3, 32, 64).transpose(4, 3, 0, 1, 2),
    )


def solution(mesh):
    placed = (P("dp", None, "gx", "yz", None), P(), P(), P("dp", None, "gx", "yz", None))
    rows_y = min(4, mesh.shape["yz"])
    rows_z = mesh.shape["yz"] // rows_y
    if rows_z == 1 and rows_y == 4 and mesh.shape["gx"] == 2 and mesh.shape["dp"] == 4:
        body = functools.partial(on_device_kernels, rows_y)
    else:
        body = functools.partial(on_device_plain, rows_y, rows_z)
    return jax.shard_map(
        body,
        mesh=mesh,
        in_specs=placed,
        out_specs=(P("dp", None, "gx", "yz", None), P("dp", None, "gx", "yz", None), P(), P()),
        check_vma=False,
    )
```

```python
import functools

import jax
import jax.numpy as jnp
from jax import lax
from jax.experimental import pallas as pl
from jax.experimental.pallas import tpu as pltpu
from jax.sharding import PartitionSpec as P

CX = 32
CY = 32
CZ = 16
SLOPE = 0.3
F32 = jnp.float32
BF16 = jnp.bfloat16


def leaky(values):
    return jnp.maximum(values, SLOPE * values)


def leaky_slope(values):
    return jnp.where(values > 0, jnp.float32(1.0), jnp.float32(SLOPE))


def convolve_valid(padded, kernel):
    return lax.conv_general_dilated(
        padded,
        kernel,
        (1, 1, 1),
        "VALID",
        dimension_numbers=("NCDHW", "OIDHW", "NCDHW"),
        preferred_element_type=F32,
    )


def kernel_grad(padded, grad):
    result = lax.conv_general_dilated(
        padded,
        grad,
        (1, 1, 1),
        "VALID",
        dimension_numbers=("CNDHW", "IODHW", "NCDHW"),
        preferred_element_type=F32,
    )
    return result.transpose(1, 0, 2, 3, 4)


def average_pool(values):
    bat, chan, xs, ys, zs = values.shape
    return values.reshape(bat, chan, xs // 2, 2, ys // 2, 2, zs // 2, 2).mean(axis=(3, 5, 7))


def spread_back(values):
    bat, chan, xs, ys, zs = values.shape
    grown = jnp.broadcast_to(
        values[:, :, :, None, :, None, :, None], (bat, chan, xs, 2, ys, 2, zs, 2)
    )
    return grown.reshape(bat, chan, 2 * xs, 2 * ys, 2 * zs) * 0.125


def unflatten(values, factor):
    return values[:, :, 0, 0].reshape(
        values.shape[0], values.shape[1], CX // factor, CY // factor, CZ // factor
    )


def flatten(values):
    return values.reshape(values.shape[0], values.shape[1], 1, 1, -1)


def extend_along(values, dim, axis, routes):
    size = values.shape[dim]
    first = lax.slice_in_dim(values, 0, 1, axis=dim)
    last = lax.slice_in_dim(values, size - 1, size, axis=dim)
    before = lax.ppermute(last, axis, routes)
    after = lax.ppermute(first, axis, [(b, a) for a, b in routes])
    return jnp.concatenate([before, values, after], axis=dim)


def extend(values, rows_y, rows_z):
    planes = lax.axis_size("gx")
    count = rows_y * rows_z
    values = extend_along(values, 2, "gx", [(i, i + 1) for i in range(planes - 1)])
    values = extend_along(values, 3, "yz", [(i, i + rows_z) for i in range(count - rows_z)])
    return extend_along(
        values, 4, "yz", [(i, i + 1) for i in range(count - 1) if (i + 1) % rows_z]
    )


def on_device_plain(rows_y, rows_z, volumes, first_kernel, second_kernel, cotangent):
    upstream = unflatten(cotangent, 4)
    padded_in = extend(unflatten(volumes, 1), rows_y, rows_z)
    pre_first = convolve_valid(padded_in, first_kernel)
    act_first = average_pool(leaky(pre_first)).astype(BF16)
    padded_mid = extend(act_first, rows_y, rows_z)
    pre_second = convolve_valid(padded_mid, second_kernel)
    features = average_pool(leaky(pre_second)).astype(BF16)
    grad_second = (spread_back(upstream.astype(F32)) * leaky_slope(pre_second)).astype(BF16)
    flipped = jnp.flip(second_kernel, (2, 3, 4)).transpose(1, 0, 2, 3, 4)
    act_grad = convolve_valid(extend(grad_second, rows_y, rows_z), flipped)
    grad_first = (spread_back(act_grad) * leaky_slope(pre_first)).astype(BF16)
    first_grad, second_grad = lax.psum(
        (kernel_grad(padded_in, grad_first), kernel_grad(padded_mid, grad_second)),
        ("dp", "gx", "yz"),
    )
    return (flatten(features), flatten(act_grad), first_grad, second_grad)


FINE = 48 * CZ
KEPT = 40 * CZ
OWN = CY * CZ
COARSE = 256
MID = (CY // 2) * (CZ // 2)
NF = 18
NS = 17


def grid(shape):
    return [lax.broadcasted_iota(jnp.int32, shape, dim) for dim in range(2)]


def one_where(condition, value=1.0):
    return jnp.where(condition, value, 0.0).astype(BF16)


def fine_to_mid(lane):
    return (lane >> 5) * 8 + ((lane & 15) >> 1) + jnp.where(lane >= OWN + 64, 96, 0)


def rim_table():
    row, lane = grid((256, 256))
    edge = jnp.where(lane < 128, 0, 7)
    place = (row >> 5) * 4 + (row & 3)
    return one_where(jnp.logical_and(((row >> 2) & 7) == edge, place == (lane & 127)))


def pool_first_table():
    row, lane = grid((KEPT, COARSE))
    place = jnp.where((row & 17) == 0, fine_to_mid(row), -1)
    return one_where(place == lane, 0.125)


def spread_first_table():
    row, lane = grid((MID, OWN))
    return one_where(fine_to_mid(lane) == row, 0.125)


def pool_second_table():
    row, lane = grid((MID, 128))
    place = jnp.where((row & 9) == 0, (row >> 4) * 4 + ((row & 7) >> 1), -1)
    return one_where(place == lane, 0.125)


def spread_second_table():
    row, lane = grid((128, COARSE))
    place = jnp.where(lane < MID, (lane >> 4) * 4, jnp.where(lane < 192, 32, 36))
    place = place + ((lane & 7) >> 1)
    used = jnp.logical_or(lane < MID + 8, lane >= COARSE - 8)
    return one_where(jnp.logical_and(used, place == row), 0.125)


def fold_rows(values):
    lane = grid((16, 128))[1]
    kept = [
        jnp.where(lane < 32, values[16 * q : 16 * q + 16], jnp.zeros((16, 128), F32))
        for q in range(4)
    ]
    return kept[0] + sum(pltpu.roll(kept[q], 32 * q, 1) for q in range(1, 4))


def unfold_rows(values):
    parts = [values] + [pltpu.roll(values, 128 - 32 * q, 1) for q in range(1, 4)]
    return jnp.concatenate(parts, axis=0)


def dot(a, b):
    return jnp.dot(a, b, preferred_element_type=F32)


def dot_lanes(a, b):
    return lax.dot_general(a, b, (((1,), (1,)), ((), ())), preferred_element_type=F32)


def pack_kernel(vol_ref, cot_ref, own_ref, x_ref, near_ref, far_ref, xnear_ref, xfar_ref):
    gx = lax.axis_index("gx")
    odd = lax.axis_index("yz") % 2
    own_ref[0:8, :] = jnp.zeros((8, OWN), F32)
    own_ref[128:136, :] = jnp.zeros((8, OWN), F32)
    for x in range(CX):
        own_ref[4 + 4 * x : 8 + 4 * x, :] = vol_ref[:, x * OWN : (x + 1) * OWN].astype(F32)
    start = pl.multiple_of(112 * (1 - gx), 8)
    blank = jnp.zeros((8, OWN), F32)
    face = jnp.concatenate([own_ref[pl.ds(start, 24), :], blank])
    x_ref[0:32, :] = face.astype(BF16)
    cot = cot_ref[...]
    wide = cot.astype(F32)
    first = gx == 0
    end = jnp.where(first, pltpu.roll(wide[:, 128:256], 32, 1), wide[:, 0:128])
    x_ref[32:48, 0:128] = fold_rows(end).astype(BF16)
    x_ref[32:48, 128:OWN] = jnp.zeros((16, OWN - 128), BF16)
    rims = dot(cot, rim_table())
    for low, side_ref, xside_ref in ((odd, near_ref, xnear_ref), (1 - odd, far_ref, xfar_ref)):
        lanes = pl.ds(pl.multiple_of((OWN - 128) * (1 - low), 128), 128)
        tail = jnp.concatenate([own_ref[128:136, lanes], blank[:, 0:128]])
        side_ref[0:128, :] = own_ref[0:128, lanes].astype(BF16)
        side_ref[128:144, :] = tail.astype(BF16)
        edge = jnp.concatenate([own_ref[pl.ds(start, 24), lanes], blank[:, 0:128]])
        xside_ref[0:32, :] = edge.astype(BF16)
        rim = jnp.where(low == 1, rims[:, 0:128], rims[:, 128:256])
        side_ref[144:160, :] = fold_rows(rim).astype(BF16)
        corner = jnp.where(first, pltpu.roll(rim, 100, 1), rim)
        xside_ref[32:48, :] = fold_rows(corner).astype(BF16)


def prepare_kernel(
    after_ref,
    k1_ref,
    k2_ref,
    w1_ref,
    w2_ref,
    w3_ref,
    pool_first_ref,
    spread_first_ref,
    pool_second_ref,
    spread_second_ref,
    w1_rows,
):
    del after_ref
    pool_first_ref[...] = pool_first_table()
    spread_first_ref[...] = spread_first_table()
    pool_second_ref[...] = pool_second_table()
    spread_second_ref[...] = spread_second_table()
    w1_rows[...] = jnp.zeros_like(w1_rows)
    for dx in range(3):
        for at in range(9):
            block = k1_ref[dx * 9 + at].astype(F32)
            for k in range(2):
                row = at * 16 + 4 * (dx + k)
                w1_rows[row : row + 4, 32 * k : 32 * k + 32] = block
    w1_ref[...] = w1_rows[...].T.astype(BF16)
    k2 = k2_ref[...].astype(F32)
    flipped = jnp.concatenate([k2[32 * n : 32 * n + 32] for n in range(26, -1, -1)], axis=1)
    for out_ref, one in ((w2_ref, k2.T), (w3_ref, flipped)):
        high, wide = one.shape
        for r in range(4):
            parts = [jnp.zeros((high, wide // 3 * r), F32)] if r else []
            parts.append(one)
            if r < 3:
                parts.append(jnp.zeros((high, wide // 3 * (3 - r)), F32))
            row = jnp.concatenate(parts, axis=1)
            out_ref[high * r : high * r + high, :] = row.astype(BF16)


def shifted(tile, period, lane):
    size = tile.shape[1]
    z = lane % period
    blank = jnp.zeros_like(tile)
    along = (
        jnp.where(z == 0, blank, pltpu.roll(tile, 1, 1)),
        tile,
        jnp.where(z == period - 1, blank, pltpu.roll(tile, size - 1, 1)),
    )
    for shift in (period, 0, size - period):
        for moved in along:
            yield pltpu.roll(moved, shift, 1) if shift else moved


def pooled(values, period):
    blocks = []
    for at in range(0, values.shape[1], 128):
        block = values[:, at : at + 128]
        block = block + pltpu.roll(block, 127, 1)
        blocks.append(block + pltpu.roll(block, 128 - period, 1))
    return jnp.concatenate(blocks, axis=1).astype(BF16)


def split(values):
    top = values.astype(BF16)
    return jnp.concatenate([top, (values - top.astype(F32)).astype(BF16)], axis=0)


def main_kernel(
    rows_y,
    own_ref,
    cot_ref,
    rx_ref,
    rnear_ref,
    rfar_ref,
    rxnear_ref,
    rxfar_ref,
    w1_ref,
    w2_ref,
    w3_ref,
    pool_first_ref,
    spread_first_ref,
    spread_second_ref,
    act_second,
    act_grad_ref,
    kept_ref,
    sent_ref,
    vol,
    cols_first,
    pre_first,
    pooled_first,
    cols_second,
    spread_up,
    grad_own,
    cols_grad,
    half_grad,
    grads_ref,
    sums_ref,
):
    gx = lax.axis_index("gx")
    block_y = lax.axis_index("yz")

    odd = block_y % 2 == 1
    inner = jnp.logical_and(block_y > 0, block_y < rows_y - 1)

    def above_below(near, far):
        near, far = near.astype(F32), far.astype(F32)
        far = jnp.where(inner, far, jnp.zeros_like(far))
        return jnp.where(odd, far, near), jnp.where(odd, near, far)

    vol[...] = jnp.zeros_like(vol)
    up, down = above_below(rnear_ref[0:144, :], rfar_ref[0:144, :])
    vol[pl.ds(2 * gx, 17), :, OWN : OWN + 128] = up[0:136].reshape(17, 8, 128)
    vol[pl.ds(2 * gx, 17), :, OWN + 128 : FINE] = down[0:136].reshape(17, 8, 128)
    vol[pl.ds(2 * gx, 17), :, 0:OWN] = own_ref[...]
    end = pl.ds(16 * (1 - gx), 3)
    vol[end, :, 0:OWN] += rx_ref[0:32, :].astype(F32)[0:24].reshape(3, 8, OWN)
    up, down = above_below(rxnear_ref[0:32, :], rxfar_ref[0:32, :])
    vol[end, :, OWN : OWN + 128] += up[0:24].reshape(3, 8, 128)
    vol[end, :, OWN + 128 : FINE] += down[0:24].reshape(3, 8, 128)

    slot = grid((64, 128))[1]

    def upstream(plane, up, down):
        return jnp.where(slot < 32, plane, jnp.where(slot < 36, up, down)).astype(BF16)

    def moved_to(values, lane_from, lane_to):
        shift = (lane_to - lane_from) % 128
        return pltpu.roll(values, shift, 1) if shift else values

    cot = cot_ref[...].astype(F32)
    up, down = above_below(rnear_ref[144:160, :], rfar_ref[144:160, :])
    up, down = unfold_rows(up), unfold_rows(down)
    planes = [
        upstream(
            moved_to(cot[:, p // 4 * 128 : p // 4 * 128 + 128], p % 4 * 32, 0),
            moved_to(up, 4 * p, 32),
            moved_to(down, 4 * p, 36),
        )
        for p in range(8)
    ]
    up, down = above_below(rxnear_ref[32:48, :], rxfar_ref[32:48, :])
    planes.append(
        upstream(
            unfold_rows(rx_ref[32:48, 0:128].astype(F32)),
            moved_to(unfold_rows(up), 0, 32),
            moved_to(unfold_rows(down), 0, 36),
        )
    )
    spread = dot(jnp.concatenate(planes, axis=0), spread_second_ref[...])
    for p in range(8):
        spread_up[p + gx] = spread[64 * p : 64 * p + 64]
    spread_up[8 * (1 - gx)] = spread[512:576]

    lane_fine = lax.broadcasted_iota(jnp.int32, (16, FINE), 1)
    near = lax.broadcasted_iota(jnp.int32, (16, 128), 1) < 64

    def first_layer(j):
        tile = jnp.concatenate([vol[j], vol[j + 1]], axis=0).astype(BF16)
        for n, moved in enumerate(shifted(tile, CZ, lane_fine)):
            edge = jnp.where(near, moved[:, OWN : OWN + 128], moved[:, OWN + 128 : FINE])
            cols_first[j, 16 * n : 16 * n + 16, 0:OWN] = moved[:, 0:OWN]
            cols_first[j, 16 * n : 16 * n + 16, OWN:KEPT] = edge
        pre = dot(w1_ref[...], cols_first[j])
        pre_first[j] = pre[:, 0:OWN]
        sloped = leaky(pre)
        pooled_first[j] = pooled(sloped[0:32] + sloped[32:64], CZ)

    lane = lax.broadcasted_iota(jnp.int32, (32, COARSE), 1)
    valid = jnp.logical_or(
        lane < MID,
        jnp.logical_or(
            jnp.logical_and(lane < 192, block_y < rows_y - 1),
            jnp.logical_and(lane >= 192, block_y > 0),
        ),
    )

    def columns_second(step):
        six = pooled_first[6 * step : 6 * step + 6].reshape(192, KEPT)
        picked = dot(six, pool_first_ref[...])
        for k in range(6):
            plane = jnp.where(valid, picked[k * 32 : k * 32 + 32], 0.0).astype(BF16)
            for n, moved in enumerate(shifted(plane, CZ // 2, lane)):
                cols_second[6 * step + k + 1, 32 * n : 32 * n + 32, :] = moved

    lane_grad = lax.broadcasted_iota(jnp.int32, (64, COARSE), 1)

    def second_layer(k, pre):
        act_second[k] = leaky(pre[:, 0:MID])
        given = spread_up[(k + gx) // 2]
        rounded = jnp.where(pre > 0, given, SLOPE * given).astype(BF16)
        for n, moved in enumerate(shifted(rounded, CZ // 2, lane_grad)):
            cols_grad[k + 1, 64 * n : 64 * n + 64, :] = moved[:, 0:MID]
        kept = rounded[:, 0:MID]
        if k == 0:
            kept = jnp.where(gx == 0, kept, jnp.zeros_like(kept))
        if k == NS - 1:
            kept = jnp.where(gx == 1, kept, jnp.zeros_like(kept))
        grad_own[k + 2 - gx] = kept

    def four_second(k):
        four = dot(w2_ref[...], cols_second[pl.ds(k + gx, 6)].reshape(1728, COARSE))
        for r in range(4):
            second_layer(k + r, four[64 * r : 64 * r + 64])

    def eight_back(base):
        cols = jnp.concatenate(
            [
                cols_grad[pl.ds(base + gx, 6)].reshape(3456, MID),
                cols_grad[pl.ds(base + 4 + gx, 6)].reshape(3456, MID),
            ],
            axis=1,
        )
        back = dot(w3_ref[...], cols)
        for m in range(8):
            row, lanes = 32 * (m % 4), MID * (m // 4)
            plane = back[row : row + 32, lanes : lanes + MID]
            act_grad_ref[:, base + m, :] = plane
            half_grad[base + m] = split(plane)

    def four_first(step):
        spread = dot(
            half_grad[4 * step : 4 * step + 4].reshape(256, MID), spread_first_ref[...]
        )
        backs = []
        for k in range(4):
            whole = spread[k * 64 : k * 64 + 32] + spread[k * 64 + 32 : k * 64 + 64]
            less = SLOPE * whole
            pre = pre_first[4 * step + k + 2 * gx]
            parts = [jnp.where(pre[r : r + 32] > 0, whole, less) for r in (0, 32)]
            backs.append(jnp.concatenate(parts, axis=0).astype(BF16))
        cols = [cols_first[4 * step + k + 2 * gx][:, 0:OWN] for k in range(4)]
        return dot_lanes(jnp.concatenate(cols, axis=1), jnp.concatenate(backs, axis=1))

    cols_second[0] = jnp.zeros((288, COARSE), BF16)
    cols_second[NF + 1] = jnp.zeros((288, COARSE), BF16)
    cols_grad[0] = jnp.zeros((576, MID), BF16)
    cols_grad[NS + 1] = jnp.zeros((576, MID), BF16)
    for k in (0, 1, 18, 19):
        grad_own[k] = jnp.zeros((64, MID), BF16)

    for step in range(3):
        for j in range(6 * step, 6 * step + 6):
            first_layer(j)
        columns_second(step)
        four_second(4 * step)
    eight_back(0)
    four_second(12)
    last = cols_second[pl.ds(NS - 1 + gx, 3)].reshape(864, COARSE)
    second_layer(NS - 1, dot(w2_ref[0:64, 0:864], last))
    first = four_first(0) + four_first(1)
    eight_back(8)
    left = jnp.concatenate([cols_second[q + 2 * gx][:, 0:MID] for q in range(18)], axis=1)
    right = jnp.concatenate([grad_own[q : q + 3].reshape(192, MID) for q in range(18)], axis=1)
    grads_ref[:, 0:192] = dot_lanes(left, right)
    first = first + four_first(2) + four_first(3)
    grads_ref[0:144, 192:256] = first

    both = pltpu.roll(grads_ref[0:144, 128:256], 64, 1)
    sums_ref[...] = both + pltpu.roll(pltpu.roll(both, 96, 1), 140, 0)
    slot = grid((72, 128))[1]
    place = grid((24, 128))[1] // 32

    def folded(half):
        rows = pl.multiple_of(144 * half, 8)
        right = grads_ref[pl.ds(rows, 72), 128:256]
        right_next = pltpu.roll(grads_ref[pl.ds(rows + 72, 72), 128:256], 64, 1)
        parts = [
            sums_ref[pl.ds(pl.multiple_of(72 * half + 24 * q, 8), 24), :] for q in range(3)
        ]
        last = jnp.where(place == 2, pltpu.roll(parts[2], 64, 1), jnp.zeros((24, 128), F32))
        last = jnp.where(place == 1, pltpu.roll(parts[1], 32, 1), last)
        last = jnp.where(place == 0, parts[0], last)
        return [grads_ref[pl.ds(rows, 144), 0:128], jnp.where(slot < 64, right, right_next), last]

    for half_ref, half in ((kept_ref, gx), (sent_ref, 1 - gx)):
        row = 0
        for part in folded(half):
            half_ref[row : row + part.shape[0], :] = part.astype(half_ref.dtype)
            row += part.shape[0]


def features_kernel(act_second_ref, pool_second_ref, features_ref):
    gx = lax.axis_index("gx")
    sums = [
        pooled(act_second_ref[2 * p + gx] + act_second_ref[2 * p + 1 + gx], CZ // 2)
        for p in range(8)
    ]
    picked = dot(jnp.concatenate(sums, axis=0), pool_second_ref[...])
    for half in range(2):
        whole = picked[256 * half : 256 * half + 64]
        for k in range(1, 4):
            block = picked[256 * half + 64 * k : 256 * half + 64 * k + 64]
            whole = whole + pltpu.roll(block, 32 * k, 1)
        features_ref[:, 128 * half : 128 * half + 128] = whole.astype(BF16)


def unpack_kernel(mine_ref, other_ref, second_ref, first_ref):
    first = lax.axis_index("gx") == 0
    mine, other = mine_ref[...].astype(F32), other_ref[...].astype(F32)
    halves = jnp.where(first, mine, other), jnp.where(first, other, mine)
    for h, half in enumerate(halves):
        row = 144 * h
        second_ref[2, row : row + 144] = half[0:144, 0:64]
        second_ref[1, row : row + 144] = half[0:144, 64:128]
        second_ref[0, row : row + 72] = half[144:216, 0:64]
        second_ref[0, row + 72 : row + 144] = half[144:216, 64:128]
    for at in range(9):
        for dx in range(3):
            h, row = divmod(at * 16 + 4 * dx, 72)
            q, row = divmod(row, 24)
            first_ref[dx * 9 + at] = halves[h][216 + row : 220 + row, 32 * q : 32 * q + 32]


def call(kernel, outs, limit, scratch=(), cost=None, in_vmem=False):
    return pl.pallas_call(
        kernel,
        out_shape=[
            pltpu.VMEM(shape, dtype) if in_vmem else jax.ShapeDtypeStruct(shape, dtype)
            for shape, dtype in outs
        ],
        cost_estimate=cost,
        scratch_shapes=[pltpu.VMEM(shape, dtype) for shape, dtype in scratch],
        compiler_params=pltpu.CompilerParams(vmem_limit_bytes=limit * 1024 * 1024),
    )


def in_hbm(values):
    return pltpu.with_memory_space_constraint(values, pltpu.HBM)


def swap_cores(values):
    return lax.ppermute(values, "gx", [(0, 1), (1, 0)])


def sum_of_four(part, axis):
    came = [lax.ppermute(part, axis, [(i, i ^ k) for i in range(4)]) for k in range(1, 4)]
    terms = [term.astype(F32) for term in [part] + came]
    return ((terms[0] + terms[1]) + (terms[2] + terms[3])).astype(BF16)


def on_device_kernels(rows_y, volumes, first_kernel, second_kernel, cotangent):
    cot = cotangent.reshape(64, 256)
    k1 = first_kernel.transpose(2, 3, 4, 1, 0).reshape(27, 4, 32)
    k2 = second_kernel.transpose(2, 3, 4, 1, 0).reshape(864, 64)
    own, x_face, near, far, x_near, x_far = call(
        pack_kernel,
        [
            ((136, OWN), F32),
            ((48, OWN), BF16),
            ((160, 128), BF16),
            ((160, 128), BF16),
            ((48, 128), BF16),
            ((48, 128), BF16),
        ],
        16,
    )(in_hbm(volumes.reshape(4, CX * OWN)), in_hbm(cot))
    *weights, pool_first, spread_first, pool_second, spread_second = call(
        prepare_kernel,
        [
            ((64, 144), BF16),
            ((256, 1728), BF16),
            ((128, 3456), BF16),
            ((KEPT, COARSE), BF16),
            ((MID, OWN), BF16),
            ((MID, 128), BF16),
            ((128, COARSE), BF16),
        ],
        16,
        [((144, 64), F32)],
        pl.CostEstimate(flops=10**8, bytes_accessed=2 * 10**6, transcendentals=0),
    )(x_far, in_hbm(k1), in_hbm(k2))

    def paired(values, partner):
        routes = [
            (g * rows_y + i, partner(g, i)) for g in range(2) for i in range(rows_y)
        ]
        return lax.ppermute(values, ("gx", "yz"), routes)

    def other_side(g, i, across):
        j = i + (1 if i % 2 else -1)
        if 0 <= j < rows_y:
            return (g ^ across) * rows_y + j
        return (1 - g) * rows_y + i

    got_near = lax.ppermute(near, "yz", [(i, i ^ 1) for i in range(rows_y)])
    got_far = paired(far, lambda g, i: other_side(g, i, 0))
    got_x = lax.ppermute(x_face, "gx", [(0, 1), (1, 0)])
    got_x_near = paired(x_near, lambda g, i: (1 - g) * rows_y + (i ^ 1))
    got_x_far = paired(x_far, lambda g, i: other_side(g, i, 1))

    act_second, act_grad, kept, sent = call(
        functools.partial(main_kernel, rows_y),
        [
            ((NS, 64, MID), F32),
            ((32, 16, MID), F32),
            ((240, 128), F32),
            ((240, 128), BF16),
        ],
        32,
        [
            ((19, 8, FINE), F32),
            ((NF, 144, KEPT), BF16),
            ((NF, 64, OWN), F32),
            ((NF, 32, KEPT), BF16),
            ((NF + 2, 288, COARSE), BF16),
            ((9, 64, COARSE), F32),
            ((20, 64, MID), BF16),
            ((NS + 2, 576, MID), BF16),
            ((16, 64, MID), BF16),
            ((288, 256), F32),
            ((144, 128), F32),
        ],
        in_vmem=True,
    )(
        own.reshape(17, 8, OWN),
        cot,
        got_x,
        got_near,
        got_far,
        got_x_near,
        got_x_far,
        *weights,
        pool_first,
        spread_first,
        spread_second,
    )
    [features] = call(features_kernel, [((64, 256), BF16)], 8)(act_second, pool_second)
    part = (kept + swap_cores(sent).astype(F32)).astype(BF16)
    part = sum_of_four(part, "dp")
    part, features = lax.optimization_barrier((part, features))
    mine = sum_of_four(part, "yz")
    second, first = call(unpack_kernel, [((3, 288, 64), F32), ((27, 4, 32), F32)], 8)(
        mine, swap_cores(mine)
    )
    return (
        features.reshape(1, 64, 1, 1, 256),
        act_grad.reshape(1, 32, 1, 1, 2048),
        first.reshape(3, 3, 3, 4, 32).transpose(4, 3, 0, 1, 2),
        second.reshape(3, 3, 3, 32, 64).transpose(4, 3, 0, 1, 2),
    )


def solution(mesh):
    placed = (P("dp", None, "gx", "yz", None), P(), P(), P("dp", None, "gx", "yz", None))
    rows_y = min(4, mesh.shape["yz"])
    rows_z = mesh.shape["yz"] // rows_y
    if rows_z == 1 and rows_y == 4 and mesh.shape["gx"] == 2 and mesh.shape["dp"] == 4:
        body = functools.partial(on_device_kernels, rows_y)
    else:
        body = functools.partial(on_device_plain, rows_y, rows_z)
    return jax.shard_map(
        body,
        mesh=mesh,
        in_specs=placed,
        out_specs=(P("dp", None, "gx", "yz", None), P("dp", None, "gx", "yz", None), P(), P()),
        check_vma=False,
    )
```

```python
import functools

import jax
import jax.numpy as jnp
from jax import lax
from jax.experimental import pallas as pl
from jax.experimental.pallas import tpu as pltpu
from jax.sharding import PartitionSpec as P

CX = 32
CY = 32
CZ = 16
SLOPE = 0.3
F32 = jnp.float32
BF16 = jnp.bfloat16


def leaky(values):
    return jnp.maximum(values, SLOPE * values)


def leaky_slope(values):
    return jnp.where(values > 0, jnp.float32(1.0), jnp.float32(SLOPE))


def convolve_valid(padded, kernel):
    return lax.conv_general_dilated(
        padded,
        kernel,
        (1, 1, 1),
        "VALID",
        dimension_numbers=("NCDHW", "OIDHW", "NCDHW"),
        preferred_element_type=F32,
    )


def kernel_grad(padded, grad):
    result = lax.conv_general_dilated(
        padded,
        grad,
        (1, 1, 1),
        "VALID",
        dimension_numbers=("CNDHW", "IODHW", "NCDHW"),
        preferred_element_type=F32,
    )
    return result.transpose(1, 0, 2, 3, 4)


def average_pool(values):
    bat, chan, xs, ys, zs = values.shape
    return values.reshape(bat, chan, xs // 2, 2, ys // 2, 2, zs // 2, 2).mean(axis=(3, 5, 7))


def spread_back(values):
    bat, chan, xs, ys, zs = values.shape
    grown = jnp.broadcast_to(
        values[:, :, :, None, :, None, :, None], (bat, chan, xs, 2, ys, 2, zs, 2)
    )
    return grown.reshape(bat, chan, 2 * xs, 2 * ys, 2 * zs) * 0.125


def unflatten(values, factor):
    return values[:, :, 0, 0].reshape(
        values.shape[0], values.shape[1], CX // factor, CY // factor, CZ // factor
    )


def flatten(values):
    return values.reshape(values.shape[0], values.shape[1], 1, 1, -1)


def extend_along(values, dim, axis, routes):
    size = values.shape[dim]
    first = lax.slice_in_dim(values, 0, 1, axis=dim)
    last = lax.slice_in_dim(values, size - 1, size, axis=dim)
    before = lax.ppermute(last, axis, routes)
    after = lax.ppermute(first, axis, [(b, a) for a, b in routes])
    return jnp.concatenate([before, values, after], axis=dim)


def extend(values, rows_y, rows_z):
    planes = lax.axis_size("gx")
    count = rows_y * rows_z
    values = extend_along(values, 2, "gx", [(i, i + 1) for i in range(planes - 1)])
    values = extend_along(values, 3, "yz", [(i, i + rows_z) for i in range(count - rows_z)])
    return extend_along(
        values, 4, "yz", [(i, i + 1) for i in range(count - 1) if (i + 1) % rows_z]
    )


def on_device_plain(rows_y, rows_z, volumes, first_kernel, second_kernel, cotangent):
    upstream = unflatten(cotangent, 4)
    padded_in = extend(unflatten(volumes, 1), rows_y, rows_z)
    pre_first = convolve_valid(padded_in, first_kernel)
    act_first = average_pool(leaky(pre_first)).astype(BF16)
    padded_mid = extend(act_first, rows_y, rows_z)
    pre_second = convolve_valid(padded_mid, second_kernel)
    features = average_pool(leaky(pre_second)).astype(BF16)
    grad_second = (spread_back(upstream.astype(F32)) * leaky_slope(pre_second)).astype(BF16)
    flipped = jnp.flip(second_kernel, (2, 3, 4)).transpose(1, 0, 2, 3, 4)
    act_grad = convolve_valid(extend(grad_second, rows_y, rows_z), flipped)
    grad_first = (spread_back(act_grad) * leaky_slope(pre_first)).astype(BF16)
    first_grad, second_grad = lax.psum(
        (kernel_grad(padded_in, grad_first), kernel_grad(padded_mid, grad_second)),
        ("dp", "gx", "yz"),
    )
    return (flatten(features), flatten(act_grad), first_grad, second_grad)


FINE = 48 * CZ
KEPT = 40 * CZ
OWN = CY * CZ
COARSE = 256
MID = (CY // 2) * (CZ // 2)
NF = 18
NS = 17


def grid(shape):
    return [lax.broadcasted_iota(jnp.int32, shape, dim) for dim in range(2)]


def one_where(condition, value=1.0):
    return jnp.where(condition, value, 0.0).astype(BF16)


def fine_to_mid(lane):
    return (lane >> 5) * 8 + ((lane & 15) >> 1) + jnp.where(lane >= OWN + 64, 96, 0)


def rim_table():
    row, lane = grid((256, 256))
    edge = jnp.where(lane < 128, 0, 7)
    place = (row >> 5) * 4 + (row & 3)
    return one_where(jnp.logical_and(((row >> 2) & 7) == edge, place == (lane & 127)))


def pool_first_table():
    row, lane = grid((KEPT, COARSE))
    place = jnp.where((row & 17) == 0, fine_to_mid(row), -1)
    return one_where(place == lane, 0.125)


def spread_first_table():
    row, lane = grid((MID, OWN))
    return one_where(fine_to_mid(lane) == row, 0.125)


def pool_second_table():
    row, lane = grid((MID, 128))
    place = jnp.where((row & 9) == 0, (row >> 4) * 4 + ((row & 7) >> 1), -1)
    return one_where(place == lane, 0.125)


def spread_second_table():
    row, lane = grid((128, COARSE))
    place = jnp.where(lane < MID, (lane >> 4) * 4, jnp.where(lane < 192, 32, 36))
    place = place + ((lane & 7) >> 1)
    used = jnp.logical_or(lane < MID + 8, lane >= COARSE - 8)
    return one_where(jnp.logical_and(used, place == row), 0.125)


def fold_rows(values):
    lane = grid((16, 128))[1]
    kept = [
        jnp.where(lane < 32, values[16 * q : 16 * q + 16], jnp.zeros((16, 128), F32))
        for q in range(4)
    ]
    return kept[0] + sum(pltpu.roll(kept[q], 32 * q, 1) for q in range(1, 4))


def unfold_rows(values):
    parts = [values] + [pltpu.roll(values, 128 - 32 * q, 1) for q in range(1, 4)]
    return jnp.concatenate(parts, axis=0)


def dot(a, b):
    return jnp.dot(a, b, preferred_element_type=F32)


def dot_lanes(a, b):
    return lax.dot_general(a, b, (((1,), (1,)), ((), ())), preferred_element_type=F32)


def pack_kernel(vol_ref, cot_ref, own_ref, x_ref, near_ref, far_ref, xnear_ref, xfar_ref):
    gx = lax.axis_index("gx")
    odd = lax.axis_index("yz") % 2
    own_ref[0:8, :] = jnp.zeros((8, OWN), F32)
    own_ref[128:136, :] = jnp.zeros((8, OWN), F32)
    for x in range(CX):
        own_ref[4 + 4 * x : 8 + 4 * x, :] = vol_ref[:, x * OWN : (x + 1) * OWN].astype(F32)
    start = pl.multiple_of(112 * (1 - gx), 8)
    blank = jnp.zeros((8, OWN), F32)
    face = jnp.concatenate([own_ref[pl.ds(start, 24), :], blank])
    x_ref[0:32, :] = face.astype(BF16)
    cot = cot_ref[...]
    wide = cot.astype(F32)
    first = gx == 0
    end = jnp.where(first, pltpu.roll(wide[:, 128:256], 32, 1), wide[:, 0:128])
    x_ref[32:48, 0:128] = fold_rows(end).astype(BF16)
    x_ref[32:48, 128:OWN] = jnp.zeros((16, OWN - 128), BF16)
    rims = dot(cot, rim_table())
    for low, side_ref, xside_ref in ((odd, near_ref, xnear_ref), (1 - odd, far_ref, xfar_ref)):
        lanes = pl.ds(pl.multiple_of((OWN - 128) * (1 - low), 128), 128)
        tail = jnp.concatenate([own_ref[128:136, lanes], blank[:, 0:128]])
        side_ref[0:128, :] = own_ref[0:128, lanes].astype(BF16)
        side_ref[128:144, :] = tail.astype(BF16)
        edge = jnp.concatenate([own_ref[pl.ds(start, 24), lanes], blank[:, 0:128]])
        xside_ref[0:32, :] = edge.astype(BF16)
        rim = jnp.where(low == 1, rims[:, 0:128], rims[:, 128:256])
        side_ref[144:160, :] = fold_rows(rim).astype(BF16)
        corner = jnp.where(first, pltpu.roll(rim, 100, 1), rim)
        xside_ref[32:48, :] = fold_rows(corner).astype(BF16)


def prepare_kernel(
    after_ref,
    k1_ref,
    k2_ref,
    w1_ref,
    w2_ref,
    w3_ref,
    pool_first_ref,
    spread_first_ref,
    pool_second_ref,
    spread_second_ref,
    w1_rows,
):
    del after_ref
    pool_first_ref[...] = pool_first_table()
    spread_first_ref[...] = spread_first_table()
    pool_second_ref[...] = pool_second_table()
    spread_second_ref[...] = spread_second_table()
    w1_rows[...] = jnp.zeros_like(w1_rows)
    for dx in range(3):
        for at in range(9):
            block = k1_ref[dx * 9 + at].astype(F32)
            for k in range(2):
                row = at * 16 + 4 * (dx + k)
                w1_rows[row : row + 4, 32 * k : 32 * k + 32] = block
    w1_ref[...] = w1_rows[...].T.astype(BF16)
    k2 = k2_ref[...].astype(F32)
    flipped = jnp.concatenate([k2[32 * n : 32 * n + 32] for n in range(26, -1, -1)], axis=1)
    for out_ref, one in ((w2_ref, k2.T), (w3_ref, flipped)):
        high, wide = one.shape
        for r in range(4):
            parts = [jnp.zeros((high, wide // 3 * r), F32)] if r else []
            parts.append(one)
            if r < 3:
                parts.append(jnp.zeros((high, wide // 3 * (3 - r)), F32))
            row = jnp.concatenate(parts, axis=1)
            out_ref[high * r : high * r + high, :] = row.astype(BF16)


def shifted(tile, period, lane):
    size = tile.shape[1]
    z = lane % period
    blank = jnp.zeros_like(tile)
    along = (
        jnp.where(z == 0, blank, pltpu.roll(tile, 1, 1)),
        tile,
        jnp.where(z == period - 1, blank, pltpu.roll(tile, size - 1, 1)),
    )
    for shift in (period, 0, size - period):
        for moved in along:
            yield pltpu.roll(moved, shift, 1) if shift else moved


def pooled(values, period):
    blocks = []
    for at in range(0, values.shape[1], 128):
        block = values[:, at : at + 128]
        block = block + pltpu.roll(block, 127, 1)
        blocks.append(block + pltpu.roll(block, 128 - period, 1))
    return jnp.concatenate(blocks, axis=1).astype(BF16)


def split(values):
    top = values.astype(BF16)
    return jnp.concatenate([top, (values - top.astype(F32)).astype(BF16)], axis=0)


def main_kernel(
    rows_y,
    own_ref,
    cot_ref,
    rx_ref,
    rnear_ref,
    rfar_ref,
    rxnear_ref,
    rxfar_ref,
    w1_ref,
    w2_ref,
    w3_ref,
    pool_first_ref,
    spread_first_ref,
    spread_second_ref,
    act_second,
    act_grad_ref,
    kept_ref,
    sent_ref,
    vol,
    cols_first,
    pre_first,
    pooled_first,
    cols_second,
    spread_up,
    grad_own,
    cols_grad,
    half_grad,
    grads_ref,
    sums_ref,
):
    gx = lax.axis_index("gx")
    block_y = lax.axis_index("yz")

    odd = block_y % 2 == 1
    inner = jnp.logical_and(block_y > 0, block_y < rows_y - 1)

    def above_below(near, far):
        near, far = near.astype(F32), far.astype(F32)
        far = jnp.where(inner, far, jnp.zeros_like(far))
        return jnp.where(odd, far, near), jnp.where(odd, near, far)

    vol[...] = jnp.zeros_like(vol)
    up, down = above_below(rnear_ref[0:144, :], rfar_ref[0:144, :])
    vol[pl.ds(2 * gx, 17), :, OWN : OWN + 128] = up[0:136].reshape(17, 8, 128)
    vol[pl.ds(2 * gx, 17), :, OWN + 128 : FINE] = down[0:136].reshape(17, 8, 128)
    vol[pl.ds(2 * gx, 17), :, 0:OWN] = own_ref[...]
    end = pl.ds(16 * (1 - gx), 3)
    vol[end, :, 0:OWN] += rx_ref[0:32, :].astype(F32)[0:24].reshape(3, 8, OWN)
    up, down = above_below(rxnear_ref[0:32, :], rxfar_ref[0:32, :])
    vol[end, :, OWN : OWN + 128] += up[0:24].reshape(3, 8, 128)
    vol[end, :, OWN + 128 : FINE] += down[0:24].reshape(3, 8, 128)

    slot = grid((64, 128))[1]

    def upstream(plane, up, down):
        return jnp.where(slot < 32, plane, jnp.where(slot < 36, up, down)).astype(BF16)

    def moved_to(values, lane_from, lane_to):
        shift = (lane_to - lane_from) % 128
        return pltpu.roll(values, shift, 1) if shift else values

    cot = cot_ref[...].astype(F32)
    up, down = above_below(rnear_ref[144:160, :], rfar_ref[144:160, :])
    up, down = unfold_rows(up), unfold_rows(down)
    planes = [
        upstream(
            moved_to(cot[:, p // 4 * 128 : p // 4 * 128 + 128], p % 4 * 32, 0),
            moved_to(up, 4 * p, 32),
            moved_to(down, 4 * p, 36),
        )
        for p in range(8)
    ]
    up, down = above_below(rxnear_ref[32:48, :], rxfar_ref[32:48, :])
    planes.append(
        upstream(
            unfold_rows(rx_ref[32:48, 0:128].astype(F32)),
            moved_to(unfold_rows(up), 0, 32),
            moved_to(unfold_rows(down), 0, 36),
        )
    )
    spread = dot(jnp.concatenate(planes, axis=0), spread_second_ref[...])
    for p in range(8):
        spread_up[p + gx] = spread[64 * p : 64 * p + 64]
    spread_up[8 * (1 - gx)] = spread[512:576]

    lane_fine = lax.broadcasted_iota(jnp.int32, (16, FINE), 1)
    near = lax.broadcasted_iota(jnp.int32, (16, 128), 1) < 64

    def first_layer(j):
        tile = jnp.concatenate([vol[j], vol[j + 1]], axis=0).astype(BF16)
        for n, moved in enumerate(shifted(tile, CZ, lane_fine)):
            edge = jnp.where(near, moved[:, OWN : OWN + 128], moved[:, OWN + 128 : FINE])
            cols_first[j, 16 * n : 16 * n + 16, 0:OWN] = moved[:, 0:OWN]
            cols_first[j, 16 * n : 16 * n + 16, OWN:KEPT] = edge
        pre = dot(w1_ref[...], cols_first[j])
        pre_first[j] = pre[:, 0:OWN]
        sloped = leaky(pre)
        pooled_first[j] = pooled(sloped[0:32] + sloped[32:64], CZ)

    lane = lax.broadcasted_iota(jnp.int32, (32, COARSE), 1)
    valid = jnp.logical_or(
        lane < MID,
        jnp.logical_or(
            jnp.logical_and(lane < 192, block_y < rows_y - 1),
            jnp.logical_and(lane >= 192, block_y > 0),
        ),
    )

    def columns_second(step):
        six = pooled_first[6 * step : 6 * step + 6].reshape(192, KEPT)
        picked = dot(six, pool_first_ref[...])
        for k in range(6):
            plane = jnp.where(valid, picked[k * 32 : k * 32 + 32], 0.0).astype(BF16)
            for n, moved in enumerate(shifted(plane, CZ // 2, lane)):
                cols_second[6 * step + k + 1, 32 * n : 32 * n + 32, :] = moved

    lane_grad = lax.broadcasted_iota(jnp.int32, (64, COARSE), 1)

    def second_layer(k, pre):
        act_second[k] = leaky(pre[:, 0:MID])
        given = spread_up[(k + gx) // 2]
        rounded = jnp.where(pre > 0, given, SLOPE * given).astype(BF16)
        for n, moved in enumerate(shifted(rounded, CZ // 2, lane_grad)):
            cols_grad[k + 1, 64 * n : 64 * n + 64, :] = moved[:, 0:MID]
        kept = rounded[:, 0:MID]
        if k == 0:
            kept = jnp.where(gx == 0, kept, jnp.zeros_like(kept))
        if k == NS - 1:
            kept = jnp.where(gx == 1, kept, jnp.zeros_like(kept))
        grad_own[k + 2 - gx] = kept

    def four_second(k):
        four = dot(w2_ref[...], cols_second[pl.ds(k + gx, 6)].reshape(1728, COARSE))
        for r in range(4):
            second_layer(k + r, four[64 * r : 64 * r + 64])

    def eight_back(base):
        cols = jnp.concatenate(
            [
                cols_grad[pl.ds(base + gx, 6)].reshape(3456, MID),
                cols_grad[pl.ds(base + 4 + gx, 6)].reshape(3456, MID),
            ],
            axis=1,
        )
        back = dot(w3_ref[...], cols)
        for m in range(8):
            row, lanes = 32 * (m % 4), MID * (m // 4)
            plane = back[row : row + 32, lanes : lanes + MID]
            act_grad_ref[:, base + m, :] = plane
            half_grad[base + m] = split(plane)

    def four_first(step):
        spread = dot(
            half_grad[4 * step : 4 * step + 4].reshape(256, MID), spread_first_ref[...]
        )
        backs = []
        for k in range(4):
            whole = spread[k * 64 : k * 64 + 32] + spread[k * 64 + 32 : k * 64 + 64]
            less = SLOPE * whole
            pre = pre_first[4 * step + k + 2 * gx]
            parts = [jnp.where(pre[r : r + 32] > 0, whole, less) for r in (0, 32)]
            backs.append(jnp.concatenate(parts, axis=0).astype(BF16))
        cols = [cols_first[4 * step + k + 2 * gx][:, 0:OWN] for k in range(4)]
        return dot_lanes(jnp.concatenate(cols, axis=1), jnp.concatenate(backs, axis=1))

    cols_second[0] = jnp.zeros((288, COARSE), BF16)
    cols_second[NF + 1] = jnp.zeros((288, COARSE), BF16)
    cols_grad[0] = jnp.zeros((576, MID), BF16)
    cols_grad[NS + 1] = jnp.zeros((576, MID), BF16)
    for k in (0, 1, 18, 19):
        grad_own[k] = jnp.zeros((64, MID), BF16)

    for step in range(3):
        for j in range(6 * step, 6 * step + 6):
            first_layer(j)
        columns_second(step)
        four_second(4 * step)
    eight_back(0)
    four_second(12)
    last = cols_second[pl.ds(NS - 1 + gx, 3)].reshape(864, COARSE)
    second_layer(NS - 1, dot(w2_ref[0:64, 0:864], last))
    first = four_first(0) + four_first(1)
    eight_back(8)
    left = jnp.concatenate([cols_second[q + 2 * gx][:, 0:MID] for q in range(18)], axis=1)
    right = jnp.concatenate([grad_own[q : q + 3].reshape(192, MID) for q in range(18)], axis=1)
    grads_ref[:, 0:192] = dot_lanes(left, right)
    first = first + four_first(2) + four_first(3)
    grads_ref[0:144, 192:256] = first

    both = pltpu.roll(grads_ref[0:144, 128:256], 64, 1)
    sums_ref[...] = both + pltpu.roll(pltpu.roll(both, 96, 1), 140, 0)
    slot = grid((72, 128))[1]
    place = grid((24, 128))[1] // 32

    def folded(half):
        rows = pl.multiple_of(144 * half, 8)
        right = grads_ref[pl.ds(rows, 72), 128:256]
        right_next = pltpu.roll(grads_ref[pl.ds(rows + 72, 72), 128:256], 64, 1)
        parts = [
            sums_ref[pl.ds(pl.multiple_of(72 * half + 24 * q, 8), 24), :] for q in range(3)
        ]
        last = jnp.where(place == 2, pltpu.roll(parts[2], 64, 1), jnp.zeros((24, 128), F32))
        last = jnp.where(place == 1, pltpu.roll(parts[1], 32, 1), last)
        last = jnp.where(place == 0, parts[0], last)
        return [grads_ref[pl.ds(rows, 144), 0:128], jnp.where(slot < 64, right, right_next), last]

    for half_ref, half in ((kept_ref, gx), (sent_ref, 1 - gx)):
        row = 0
        for part in folded(half):
            half_ref[row : row + part.shape[0], :] = part.astype(half_ref.dtype)
            row += part.shape[0]


def features_kernel(act_second_ref, pool_second_ref, features_ref):
    gx = lax.axis_index("gx")
    sums = [
        pooled(act_second_ref[2 * p + gx] + act_second_ref[2 * p + 1 + gx], CZ // 2)
        for p in range(8)
    ]
    picked = dot(jnp.concatenate(sums, axis=0), pool_second_ref[...])
    for half in range(2):
        whole = picked[256 * half : 256 * half + 64]
        for k in range(1, 4):
            block = picked[256 * half + 64 * k : 256 * half + 64 * k + 64]
            whole = whole + pltpu.roll(block, 32 * k, 1)
        features_ref[:, 128 * half : 128 * half + 128] = whole.astype(BF16)


def unpack_kernel(mine_ref, other_ref, second_ref, first_ref):
    first = lax.axis_index("gx") == 0
    mine, other = mine_ref[...].astype(F32), other_ref[...].astype(F32)
    halves = jnp.where(first, mine, other), jnp.where(first, other, mine)
    for h, half in enumerate(halves):
        row = 144 * h
        second_ref[2, row : row + 144] = half[0:144, 0:64]
        second_ref[1, row : row + 144] = half[0:144, 64:128]
        second_ref[0, row : row + 72] = half[144:216, 0:64]
        second_ref[0, row + 72 : row + 144] = half[144:216, 64:128]
    for at in range(9):
        for dx in range(3):
            h, row = divmod(at * 16 + 4 * dx, 72)
            q, row = divmod(row, 24)
            first_ref[dx * 9 + at] = halves[h][216 + row : 220 + row, 32 * q : 32 * q + 32]


def call(kernel, outs, limit, scratch=(), cost=None, in_vmem=False):
    return pl.pallas_call(
        kernel,
        out_shape=[
            pltpu.VMEM(shape, dtype) if in_vmem else jax.ShapeDtypeStruct(shape, dtype)
            for shape, dtype in outs
        ],
        cost_estimate=cost,
        scratch_shapes=[pltpu.VMEM(shape, dtype) for shape, dtype in scratch],
        compiler_params=pltpu.CompilerParams(vmem_limit_bytes=limit * 1024 * 1024),
    )


def in_hbm(values):
    return pltpu.with_memory_space_constraint(values, pltpu.HBM)


def swap_cores(values):
    return lax.ppermute(values, "gx", [(0, 1), (1, 0)])


def sum_of_four(part, axis):
    came = [lax.ppermute(part, axis, [(i, i ^ k) for i in range(4)]) for k in range(1, 4)]
    terms = [term.astype(F32) for term in [part] + came]
    return ((terms[0] + terms[1]) + (terms[2] + terms[3])).astype(BF16)


def on_device_kernels(rows_y, volumes, first_kernel, second_kernel, cotangent):
    cot = cotangent.reshape(64, 256)
    k1 = first_kernel.transpose(2, 3, 4, 1, 0).reshape(27, 4, 32)
    k2 = second_kernel.transpose(2, 3, 4, 1, 0).reshape(864, 64)
    own, x_face, near, far, x_near, x_far = call(
        pack_kernel,
        [
            ((136, OWN), F32),
            ((48, OWN), BF16),
            ((160, 128), BF16),
            ((160, 128), BF16),
            ((48, 128), BF16),
            ((48, 128), BF16),
        ],
        16,
    )(in_hbm(volumes.reshape(4, CX * OWN)), in_hbm(cot))
    *weights, pool_first, spread_first, pool_second, spread_second = call(
        prepare_kernel,
        [
            ((64, 144), BF16),
            ((256, 1728), BF16),
            ((128, 3456), BF16),
            ((KEPT, COARSE), BF16),
            ((MID, OWN), BF16),
            ((MID, 128), BF16),
            ((128, COARSE), BF16),
        ],
        16,
        [((144, 64), F32)],
        pl.CostEstimate(flops=10**8, bytes_accessed=2 * 10**6, transcendentals=0),
    )(x_far, in_hbm(k1), in_hbm(k2))

    def paired(values, partner):
        routes = [
            (g * rows_y + i, partner(g, i)) for g in range(2) for i in range(rows_y)
        ]
        return lax.ppermute(values, ("gx", "yz"), routes)

    def other_side(g, i, across):
        j = i + (1 if i % 2 else -1)
        if 0 <= j < rows_y:
            return (g ^ across) * rows_y + j
        return (1 - g) * rows_y + i

    got_near = lax.ppermute(near, "yz", [(i, i ^ 1) for i in range(rows_y)])
    got_far = paired(far, lambda g, i: other_side(g, i, 0))
    got_x = lax.ppermute(x_face, "gx", [(0, 1), (1, 0)])
    got_x_near = paired(x_near, lambda g, i: (1 - g) * rows_y + (i ^ 1))
    got_x_far = paired(x_far, lambda g, i: other_side(g, i, 1))

    act_second, act_grad, kept, sent = call(
        functools.partial(main_kernel, rows_y),
        [
            ((NS, 64, MID), F32),
            ((32, 16, MID), F32),
            ((240, 128), F32),
            ((240, 128), BF16),
        ],
        32,
        [
            ((19, 8, FINE), F32),
            ((NF, 144, KEPT), BF16),
            ((NF, 64, OWN), F32),
            ((NF, 32, KEPT), BF16),
            ((NF + 2, 288, COARSE), BF16),
            ((9, 64, COARSE), F32),
            ((20, 64, MID), BF16),
            ((NS + 2, 576, MID), BF16),
            ((16, 64, MID), BF16),
            ((288, 256), F32),
            ((144, 128), F32),
        ],
        in_vmem=True,
    )(
        own.reshape(17, 8, OWN),
        cot,
        got_x,
        got_near,
        got_far,
        got_x_near,
        got_x_far,
        *weights,
        pool_first,
        spread_first,
        spread_second,
    )
    [features] = call(features_kernel, [((64, 256), BF16)], 8)(act_second, pool_second)
    part = (kept + swap_cores(sent).astype(F32)).astype(BF16)
    part = sum_of_four(part, "yz")
    part, features = lax.optimization_barrier((part, features))
    mine = sum_of_four(part, "dp")
    second, first = call(unpack_kernel, [((3, 288, 64), F32), ((27, 4, 32), F32)], 8)(
        mine, swap_cores(mine)
    )
    return (
        features.reshape(1, 64, 1, 1, 256),
        act_grad.reshape(1, 32, 1, 1, 2048),
        first.reshape(3, 3, 3, 4, 32).transpose(4, 3, 0, 1, 2),
        second.reshape(3, 3, 3, 32, 64).transpose(4, 3, 0, 1, 2),
    )


def solution(mesh):
    placed = (P("dp", None, "gx", "yz", None), P(), P(), P("dp", None, "gx", "yz", None))
    rows_y = min(4, mesh.shape["yz"])
    rows_z = mesh.shape["yz"] // rows_y
    if rows_z == 1 and rows_y == 4 and mesh.shape["gx"] == 2 and mesh.shape["dp"] == 4:
        body = functools.partial(on_device_kernels, rows_y)
    else:
        body = functools.partial(on_device_plain, rows_y, rows_z)
    return jax.shard_map(
        body,
        mesh=mesh,
        in_specs=placed,
        out_specs=(P("dp", None, "gx", "yz", None), P("dp", None, "gx", "yz", None), P(), P()),
        check_vma=False,
    )
```

```python
import functools

import jax
import jax.numpy as jnp
from jax import lax
from jax.experimental import pallas as pl
from jax.experimental.pallas import tpu as pltpu
from jax.sharding import PartitionSpec as P

CX = 32
CY = 32
CZ = 16
SLOPE = 0.3
F32 = jnp.float32
BF16 = jnp.bfloat16


def leaky(values):
    return jnp.maximum(values, SLOPE * values)


def leaky_slope(values):
    return jnp.where(values > 0, jnp.float32(1.0), jnp.float32(SLOPE))


def convolve_valid(padded, kernel):
    return lax.conv_general_dilated(
        padded,
        kernel,
        (1, 1, 1),
        "VALID",
        dimension_numbers=("NCDHW", "OIDHW", "NCDHW"),
        preferred_element_type=F32,
    )


def kernel_grad(padded, grad):
    result = lax.conv_general_dilated(
        padded,
        grad,
        (1, 1, 1),
        "VALID",
        dimension_numbers=("CNDHW", "IODHW", "NCDHW"),
        preferred_element_type=F32,
    )
    return result.transpose(1, 0, 2, 3, 4)


def average_pool(values):
    bat, chan, xs, ys, zs = values.shape
    return values.reshape(bat, chan, xs // 2, 2, ys // 2, 2, zs // 2, 2).mean(axis=(3, 5, 7))


def spread_back(values):
    bat, chan, xs, ys, zs = values.shape
    grown = jnp.broadcast_to(
        values[:, :, :, None, :, None, :, None], (bat, chan, xs, 2, ys, 2, zs, 2)
    )
    return grown.reshape(bat, chan, 2 * xs, 2 * ys, 2 * zs) * 0.125


def unflatten(values, factor):
    return values[:, :, 0, 0].reshape(
        values.shape[0], values.shape[1], CX // factor, CY // factor, CZ // factor
    )


def flatten(values):
    return values.reshape(values.shape[0], values.shape[1], 1, 1, -1)


def extend_along(values, dim, axis, routes):
    size = values.shape[dim]
    first = lax.slice_in_dim(values, 0, 1, axis=dim)
    last = lax.slice_in_dim(values, size - 1, size, axis=dim)
    before = lax.ppermute(last, axis, routes)
    after = lax.ppermute(first, axis, [(b, a) for a, b in routes])
    return jnp.concatenate([before, values, after], axis=dim)


def extend(values, rows_y, rows_z):
    planes = lax.axis_size("gx")
    count = rows_y * rows_z
    values = extend_along(values, 2, "gx", [(i, i + 1) for i in range(planes - 1)])
    values = extend_along(values, 3, "yz", [(i, i + rows_z) for i in range(count - rows_z)])
    return extend_along(
        values, 4, "yz", [(i, i + 1) for i in range(count - 1) if (i + 1) % rows_z]
    )


def on_device_plain(rows_y, rows_z, volumes, first_kernel, second_kernel, cotangent):
    upstream = unflatten(cotangent, 4)
    padded_in = extend(unflatten(volumes, 1), rows_y, rows_z)
    pre_first = convolve_valid(padded_in, first_kernel)
    act_first = average_pool(leaky(pre_first)).astype(BF16)
    padded_mid = extend(act_first, rows_y, rows_z)
    pre_second = convolve_valid(padded_mid, second_kernel)
    features = average_pool(leaky(pre_second)).astype(BF16)
    grad_second = (spread_back(upstream.astype(F32)) * leaky_slope(pre_second)).astype(BF16)
    flipped = jnp.flip(second_kernel, (2, 3, 4)).transpose(1, 0, 2, 3, 4)
    act_grad = convolve_valid(extend(grad_second, rows_y, rows_z), flipped)
    grad_first = (spread_back(act_grad) * leaky_slope(pre_first)).astype(BF16)
    first_grad, second_grad = lax.psum(
        (kernel_grad(padded_in, grad_first), kernel_grad(padded_mid, grad_second)),
        ("dp", "gx", "yz"),
    )
    return (flatten(features), flatten(act_grad), first_grad, second_grad)


FINE = 48 * CZ
KEPT = 40 * CZ
OWN = CY * CZ
COARSE = 256
MID = (CY // 2) * (CZ // 2)
NF = 18
NS = 17


def grid(shape):
    return [lax.broadcasted_iota(jnp.int32, shape, dim) for dim in range(2)]


def one_where(condition, value=1.0):
    return jnp.where(condition, value, 0.0).astype(BF16)


def fine_to_mid(lane):
    return (lane >> 5) * 8 + ((lane & 15) >> 1) + jnp.where(lane >= OWN + 64, 96, 0)


def rim_table():
    row, lane = grid((256, 256))
    edge = jnp.where(lane < 128, 0, 7)
    place = (row >> 5) * 4 + (row & 3)
    return one_where(jnp.logical_and(((row >> 2) & 7) == edge, place == (lane & 127)))


def pool_first_table():
    row, lane = grid((KEPT, COARSE))
    place = jnp.where((row & 17) == 0, fine_to_mid(row), -1)
    return one_where(place == lane, 0.125)


def spread_first_table():
    row, lane = grid((MID, OWN))
    return one_where(fine_to_mid(lane) == row, 0.125)


def pool_second_table():
    row, lane = grid((MID, 128))
    place = jnp.where((row & 9) == 0, (row >> 4) * 4 + ((row & 7) >> 1), -1)
    return one_where(place == lane, 0.125)


def spread_second_table():
    row, lane = grid((128, COARSE))
    place = jnp.where(lane < MID, (lane >> 4) * 4, jnp.where(lane < 192, 32, 36))
    place = place + ((lane & 7) >> 1)
    used = jnp.logical_or(lane < MID + 8, lane >= COARSE - 8)
    return one_where(jnp.logical_and(used, place == row), 0.125)


def fold_rows(values):
    lane = grid((16, 128))[1]
    kept = [
        jnp.where(lane < 32, values[16 * q : 16 * q + 16], jnp.zeros((16, 128), F32))
        for q in range(4)
    ]
    return kept[0] + sum(pltpu.roll(kept[q], 32 * q, 1) for q in range(1, 4))


def unfold_rows(values):
    parts = [values] + [pltpu.roll(values, 128 - 32 * q, 1) for q in range(1, 4)]
    return jnp.concatenate(parts, axis=0)


def dot(a, b):
    return jnp.dot(a, b, preferred_element_type=F32)


def dot_lanes(a, b):
    return lax.dot_general(a, b, (((1,), (1,)), ((), ())), preferred_element_type=F32)


def pack_kernel(vol_ref, cot_ref, own_ref, x_ref, near_ref, far_ref, xnear_ref, xfar_ref):
    gx = lax.axis_index("gx")
    odd = lax.axis_index("yz") % 2
    own_ref[0:8, :] = jnp.zeros((8, OWN), F32)
    own_ref[128:136, :] = jnp.zeros((8, OWN), F32)
    for x in range(CX):
        own_ref[4 + 4 * x : 8 + 4 * x, :] = vol_ref[:, x * OWN : (x + 1) * OWN].astype(F32)
    start = pl.multiple_of(112 * (1 - gx), 8)
    blank = jnp.zeros((8, OWN), F32)
    face = jnp.concatenate([own_ref[pl.ds(start, 24), :], blank])
    x_ref[0:32, :] = face.astype(BF16)
    cot = cot_ref[...]
    wide = cot.astype(F32)
    first = gx == 0
    end = jnp.where(first, pltpu.roll(wide[:, 128:256], 32, 1), wide[:, 0:128])
    x_ref[32:48, 0:128] = fold_rows(end).astype(BF16)
    x_ref[32:48, 128:OWN] = jnp.zeros((16, OWN - 128), BF16)
    rims = dot(cot, rim_table())
    for low, side_ref, xside_ref in ((odd, near_ref, xnear_ref), (1 - odd, far_ref, xfar_ref)):
        lanes = pl.ds(pl.multiple_of((OWN - 128) * (1 - low), 128), 128)
        tail = jnp.concatenate([own_ref[128:136, lanes], blank[:, 0:128]])
        side_ref[0:128, :] = own_ref[0:128, lanes].astype(BF16)
        side_ref[128:144, :] = tail.astype(BF16)
        edge = jnp.concatenate([own_ref[pl.ds(start, 24), lanes], blank[:, 0:128]])
        xside_ref[0:32, :] = edge.astype(BF16)
        rim = jnp.where(low == 1, rims[:, 0:128], rims[:, 128:256])
        side_ref[144:160, :] = fold_rows(rim).astype(BF16)
        corner = jnp.where(first, pltpu.roll(rim, 100, 1), rim)
        xside_ref[32:48, :] = fold_rows(corner).astype(BF16)


def prepare_kernel(
    after_ref,
    k1_ref,
    k2_ref,
    w1_ref,
    w2_ref,
    w3_ref,
    pool_first_ref,
    spread_first_ref,
    pool_second_ref,
    spread_second_ref,
    w1_rows,
):
    del after_ref
    pool_first_ref[...] = pool_first_table()
    spread_first_ref[...] = spread_first_table()
    pool_second_ref[...] = pool_second_table()
    spread_second_ref[...] = spread_second_table()
    w1_rows[...] = jnp.zeros_like(w1_rows)
    for dx in range(3):
        for at in range(9):
            block = k1_ref[dx * 9 + at].astype(F32)
            for k in range(2):
                row = at * 16 + 4 * (dx + k)
                w1_rows[row : row + 4, 32 * k : 32 * k + 32] = block
    w1_ref[...] = w1_rows[...].T.astype(BF16)
    k2 = k2_ref[...].astype(F32)
    flipped = jnp.concatenate([k2[32 * n : 32 * n + 32] for n in range(26, -1, -1)], axis=1)
    for out_ref, one in ((w2_ref, k2.T), (w3_ref, flipped)):
        high, wide = one.shape
        for r in range(4):
            parts = [jnp.zeros((high, wide // 3 * r), F32)] if r else []
            parts.append(one)
            if r < 3:
                parts.append(jnp.zeros((high, wide // 3 * (3 - r)), F32))
            row = jnp.concatenate(parts, axis=1)
            out_ref[high * r : high * r + high, :] = row.astype(BF16)


def shifted(tile, period, lane):
    size = tile.shape[1]
    z = lane % period
    blank = jnp.zeros_like(tile)
    along = (
        jnp.where(z == 0, blank, pltpu.roll(tile, 1, 1)),
        tile,
        jnp.where(z == period - 1, blank, pltpu.roll(tile, size - 1, 1)),
    )
    for shift in (period, 0, size - period):
        for moved in along:
            yield pltpu.roll(moved, shift, 1) if shift else moved


def pooled(values, period):
    blocks = []
    for at in range(0, values.shape[1], 128):
        block = values[:, at : at + 128]
        block = block + pltpu.roll(block, 127, 1)
        blocks.append(block + pltpu.roll(block, 128 - period, 1))
    return jnp.concatenate(blocks, axis=1).astype(BF16)


def split(values):
    top = values.astype(BF16)
    return jnp.concatenate([top, (values - top.astype(F32)).astype(BF16)], axis=0)


def main_kernel(
    rows_y,
    own_ref,
    cot_ref,
    rx_ref,
    rnear_ref,
    rfar_ref,
    rxnear_ref,
    rxfar_ref,
    w1_ref,
    w2_ref,
    w3_ref,
    pool_first_ref,
    spread_first_ref,
    spread_second_ref,
    act_second,
    act_grad_ref,
    kept_ref,
    sent_ref,
    vol,
    cols_first,
    pre_first,
    pooled_first,
    cols_second,
    spread_up,
    grad_own,
    cols_grad,
    half_grad,
    grads_ref,
    sums_ref,
):
    gx = lax.axis_index("gx")
    block_y = lax.axis_index("yz")

    odd = block_y % 2 == 1
    inner = jnp.logical_and(block_y > 0, block_y < rows_y - 1)

    def above_below(near, far):
        near, far = near.astype(F32), far.astype(F32)
        far = jnp.where(inner, far, jnp.zeros_like(far))
        return jnp.where(odd, far, near), jnp.where(odd, near, far)

    vol[...] = jnp.zeros_like(vol)
    up, down = above_below(rnear_ref[0:144, :], rfar_ref[0:144, :])
    vol[pl.ds(2 * gx, 17), :, OWN : OWN + 128] = up[0:136].reshape(17, 8, 128)
    vol[pl.ds(2 * gx, 17), :, OWN + 128 : FINE] = down[0:136].reshape(17, 8, 128)
    vol[pl.ds(2 * gx, 17), :, 0:OWN] = own_ref[...]
    end = pl.ds(16 * (1 - gx), 3)
    vol[end, :, 0:OWN] += rx_ref[0:32, :].astype(F32)[0:24].reshape(3, 8, OWN)
    up, down = above_below(rxnear_ref[0:32, :], rxfar_ref[0:32, :])
    vol[end, :, OWN : OWN + 128] += up[0:24].reshape(3, 8, 128)
    vol[end, :, OWN + 128 : FINE] += down[0:24].reshape(3, 8, 128)

    slot = grid((64, 128))[1]

    def upstream(plane, up, down):
        return jnp.where(slot < 32, plane, jnp.where(slot < 36, up, down)).astype(BF16)

    def moved_to(values, lane_from, lane_to):
        shift = (lane_to - lane_from) % 128
        return pltpu.roll(values, shift, 1) if shift else values

    cot = cot_ref[...].astype(F32)
    up, down = above_below(rnear_ref[144:160, :], rfar_ref[144:160, :])
    up, down = unfold_rows(up), unfold_rows(down)
    planes = [
        upstream(
            moved_to(cot[:, p // 4 * 128 : p // 4 * 128 + 128], p % 4 * 32, 0),
            moved_to(up, 4 * p, 32),
            moved_to(down, 4 * p, 36),
        )
        for p in range(8)
    ]
    up, down = above_below(rxnear_ref[32:48, :], rxfar_ref[32:48, :])
    planes.append(
        upstream(
            unfold_rows(rx_ref[32:48, 0:128].astype(F32)),
            moved_to(unfold_rows(up), 0, 32),
            moved_to(unfold_rows(down), 0, 36),
        )
    )
    spread = dot(jnp.concatenate(planes, axis=0), spread_second_ref[...])
    for p in range(8):
        spread_up[p + gx] = spread[64 * p : 64 * p + 64]
    spread_up[8 * (1 - gx)] = spread[512:576]

    lane_fine = lax.broadcasted_iota(jnp.int32, (16, FINE), 1)
    near = lax.broadcasted_iota(jnp.int32, (16, 128), 1) < 64

    def first_layer(j):
        tile = jnp.concatenate([vol[j], vol[j + 1]], axis=0).astype(BF16)
        for n, moved in enumerate(shifted(tile, CZ, lane_fine)):
            edge = jnp.where(near, moved[:, OWN : OWN + 128], moved[:, OWN + 128 : FINE])
            cols_first[j, 16 * n : 16 * n + 16, 0:OWN] = moved[:, 0:OWN]
            cols_first[j, 16 * n : 16 * n + 16, OWN:KEPT] = edge
        pre = dot(w1_ref[...], cols_first[j])
        pre_first[j] = pre[:, 0:OWN]
        sloped = leaky(pre)
        pooled_first[j] = pooled(sloped[0:32] + sloped[32:64], CZ)

    lane = lax.broadcasted_iota(jnp.int32, (32, COARSE), 1)
    valid = jnp.logical_or(
        lane < MID,
        jnp.logical_or(
            jnp.logical_and(lane < 192, block_y < rows_y - 1),
            jnp.logical_and(lane >= 192, block_y > 0),
        ),
    )

    def columns_second(step):
        six = pooled_first[6 * step : 6 * step + 6].reshape(192, KEPT)
        picked = dot(six, pool_first_ref[...])
        for k in range(6):
            plane = jnp.where(valid, picked[k * 32 : k * 32 + 32], 0.0).astype(BF16)
            for n, moved in enumerate(shifted(plane, CZ // 2, lane)):
                cols_second[6 * step + k + 1, 32 * n : 32 * n + 32, :] = moved

    lane_grad = lax.broadcasted_iota(jnp.int32, (64, COARSE), 1)

    def second_layer(k, pre):
        act_second[k] = leaky(pre[:, 0:MID])
        given = spread_up[(k + gx) // 2]
        rounded = jnp.where(pre > 0, given, SLOPE * given).astype(BF16)
        for n, moved in enumerate(shifted(rounded, CZ // 2, lane_grad)):
            cols_grad[k + 1, 64 * n : 64 * n + 64, :] = moved[:, 0:MID]
        kept = rounded[:, 0:MID]
        if k == 0:
            kept = jnp.where(gx == 0, kept, jnp.zeros_like(kept))
        if k == NS - 1:
            kept = jnp.where(gx == 1, kept, jnp.zeros_like(kept))
        grad_own[k + 2 - gx] = kept

    def four_second(k):
        four = dot(w2_ref[...], cols_second[pl.ds(k + gx, 6)].reshape(1728, COARSE))
        for r in range(4):
            second_layer(k + r, four[64 * r : 64 * r + 64])

    def eight_back(base):
        cols = jnp.concatenate(
            [
                cols_grad[pl.ds(base + gx, 6)].reshape(3456, MID),
                cols_grad[pl.ds(base + 4 + gx, 6)].reshape(3456, MID),
            ],
            axis=1,
        )
        back = dot(w3_ref[...], cols)
        for m in range(8):
            row, lanes = 32 * (m % 4), MID * (m // 4)
            plane = back[row : row + 32, lanes : lanes + MID]
            act_grad_ref[:, base + m, :] = plane
            half_grad[base + m] = split(plane)

    def four_first(step):
        backs = []
        for k in range(4):
            if k % 2 == 0:
                two = half_grad[4 * step + k : 4 * step + k + 2].reshape(128, MID)
                spread = dot(two, spread_first_ref[...])
            row = k % 2 * 64
            whole = spread[row : row + 32] + spread[row + 32 : row + 64]
            less = SLOPE * whole
            pre = pre_first[4 * step + k + 2 * gx]
            parts = [jnp.where(pre[r : r + 32] > 0, whole, less) for r in (0, 32)]
            backs.append(jnp.concatenate(parts, axis=0).astype(BF16))
        cols = [cols_first[4 * step + k + 2 * gx][:, 0:OWN] for k in range(4)]
        return dot_lanes(jnp.concatenate(cols, axis=1), jnp.concatenate(backs, axis=1))

    cols_second[0] = jnp.zeros((288, COARSE), BF16)
    cols_second[NF + 1] = jnp.zeros((288, COARSE), BF16)
    cols_grad[0] = jnp.zeros((576, MID), BF16)
    cols_grad[NS + 1] = jnp.zeros((576, MID), BF16)
    for k in (0, 1, 18, 19):
        grad_own[k] = jnp.zeros((64, MID), BF16)

    for step in range(3):
        for j in range(6 * step, 6 * step + 6):
            first_layer(j)
        columns_second(step)
        four_second(4 * step)
    eight_back(0)
    four_second(12)
    last = cols_second[pl.ds(NS - 1 + gx, 3)].reshape(864, COARSE)
    second_layer(NS - 1, dot(w2_ref[0:64, 0:864], last))
    first = four_first(0) + four_first(1)
    eight_back(8)
    left = jnp.concatenate([cols_second[q + 2 * gx][:, 0:MID] for q in range(18)], axis=1)
    right = jnp.concatenate([grad_own[q : q + 3].reshape(192, MID) for q in range(18)], axis=1)
    grads_ref[:, 0:192] = dot_lanes(left, right)
    first = first + four_first(2) + four_first(3)
    grads_ref[0:144, 192:256] = first

    both = pltpu.roll(grads_ref[0:144, 128:256], 64, 1)
    sums_ref[...] = both + pltpu.roll(pltpu.roll(both, 96, 1), 140, 0)
    slot = grid((72, 128))[1]
    place = grid((24, 128))[1] // 32

    def folded(half):
        rows = pl.multiple_of(144 * half, 8)
        right = grads_ref[pl.ds(rows, 72), 128:256]
        right_next = pltpu.roll(grads_ref[pl.ds(rows + 72, 72), 128:256], 64, 1)
        parts = [
            sums_ref[pl.ds(pl.multiple_of(72 * half + 24 * q, 8), 24), :] for q in range(3)
        ]
        last = jnp.where(place == 2, pltpu.roll(parts[2], 64, 1), jnp.zeros((24, 128), F32))
        last = jnp.where(place == 1, pltpu.roll(parts[1], 32, 1), last)
        last = jnp.where(place == 0, parts[0], last)
        return [grads_ref[pl.ds(rows, 144), 0:128], jnp.where(slot < 64, right, right_next), last]

    for half_ref, half in ((kept_ref, gx), (sent_ref, 1 - gx)):
        row = 0
        for part in folded(half):
            half_ref[row : row + part.shape[0], :] = part.astype(half_ref.dtype)
            row += part.shape[0]


def features_kernel(act_second_ref, pool_second_ref, features_ref):
    gx = lax.axis_index("gx")
    sums = [
        pooled(act_second_ref[2 * p + gx] + act_second_ref[2 * p + 1 + gx], CZ // 2)
        for p in range(8)
    ]
    picked = dot(jnp.concatenate(sums, axis=0), pool_second_ref[...])
    for half in range(2):
        whole = picked[256 * half : 256 * half + 64]
        for k in range(1, 4):
            block = picked[256 * half + 64 * k : 256 * half + 64 * k + 64]
            whole = whole + pltpu.roll(block, 32 * k, 1)
        features_ref[:, 128 * half : 128 * half + 128] = whole.astype(BF16)


def unpack_kernel(mine_ref, other_ref, second_ref, first_ref):
    first = lax.axis_index("gx") == 0
    mine, other = mine_ref[...].astype(F32), other_ref[...].astype(F32)
    halves = jnp.where(first, mine, other), jnp.where(first, other, mine)
    for h, half in enumerate(halves):
        row = 144 * h
        second_ref[2, row : row + 144] = half[0:144, 0:64]
        second_ref[1, row : row + 144] = half[0:144, 64:128]
        second_ref[0, row : row + 72] = half[144:216, 0:64]
        second_ref[0, row + 72 : row + 144] = half[144:216, 64:128]
    for at in range(9):
        for dx in range(3):
            h, row = divmod(at * 16 + 4 * dx, 72)
            q, row = divmod(row, 24)
            first_ref[dx * 9 + at] = halves[h][216 + row : 220 + row, 32 * q : 32 * q + 32]


def call(kernel, outs, limit, scratch=(), cost=None, in_vmem=False):
    return pl.pallas_call(
        kernel,
        out_shape=[
            pltpu.VMEM(shape, dtype) if in_vmem else jax.ShapeDtypeStruct(shape, dtype)
            for shape, dtype in outs
        ],
        cost_estimate=cost,
        scratch_shapes=[pltpu.VMEM(shape, dtype) for shape, dtype in scratch],
        compiler_params=pltpu.CompilerParams(vmem_limit_bytes=limit * 1024 * 1024),
    )


def in_hbm(values):
    return pltpu.with_memory_space_constraint(values, pltpu.HBM)


def swap_cores(values):
    return lax.ppermute(values, "gx", [(0, 1), (1, 0)])


def sum_of_four(part, axis):
    came = [lax.ppermute(part, axis, [(i, i ^ k) for i in range(4)]) for k in range(1, 4)]
    terms = [term.astype(F32) for term in [part] + came]
    return ((terms[0] + terms[1]) + (terms[2] + terms[3])).astype(BF16)


def on_device_kernels(rows_y, volumes, first_kernel, second_kernel, cotangent):
    cot = cotangent.reshape(64, 256)
    k1 = first_kernel.transpose(2, 3, 4, 1, 0).reshape(27, 4, 32)
    k2 = second_kernel.transpose(2, 3, 4, 1, 0).reshape(864, 64)
    own, x_face, near, far, x_near, x_far = call(
        pack_kernel,
        [
            ((136, OWN), F32),
            ((48, OWN), BF16),
            ((160, 128), BF16),
            ((160, 128), BF16),
            ((48, 128), BF16),
            ((48, 128), BF16),
        ],
        16,
    )(in_hbm(volumes.reshape(4, CX * OWN)), in_hbm(cot))
    *weights, pool_first, spread_first, pool_second, spread_second = call(
        prepare_kernel,
        [
            ((64, 144), BF16),
            ((256, 1728), BF16),
            ((128, 3456), BF16),
            ((KEPT, COARSE), BF16),
            ((MID, OWN), BF16),
            ((MID, 128), BF16),
            ((128, COARSE), BF16),
        ],
        16,
        [((144, 64), F32)],
        pl.CostEstimate(flops=10**8, bytes_accessed=2 * 10**6, transcendentals=0),
    )(x_far, in_hbm(k1), in_hbm(k2))

    def paired(values, partner):
        routes = [
            (g * rows_y + i, partner(g, i)) for g in range(2) for i in range(rows_y)
        ]
        return lax.ppermute(values, ("gx", "yz"), routes)

    def other_side(g, i, across):
        j = i + (1 if i % 2 else -1)
        if 0 <= j < rows_y:
            return (g ^ across) * rows_y + j
        return (1 - g) * rows_y + i

    got_near = lax.ppermute(near, "yz", [(i, i ^ 1) for i in range(rows_y)])
    got_far = paired(far, lambda g, i: other_side(g, i, 0))
    got_x = lax.ppermute(x_face, "gx", [(0, 1), (1, 0)])
    got_x_near = paired(x_near, lambda g, i: (1 - g) * rows_y + (i ^ 1))
    got_x_far = paired(x_far, lambda g, i: other_side(g, i, 1))

    act_second, act_grad, kept, sent = call(
        functools.partial(main_kernel, rows_y),
        [
            ((NS, 64, MID), F32),
            ((32, 16, MID), F32),
            ((240, 128), F32),
            ((240, 128), BF16),
        ],
        32,
        [
            ((19, 8, FINE), F32),
            ((NF, 144, KEPT), BF16),
            ((NF, 64, OWN), F32),
            ((NF, 32, KEPT), BF16),
            ((NF + 2, 288, COARSE), BF16),
            ((9, 64, COARSE), F32),
            ((20, 64, MID), BF16),
            ((NS + 2, 576, MID), BF16),
            ((16, 64, MID), BF16),
            ((288, 256), F32),
            ((144, 128), F32),
        ],
        in_vmem=True,
    )(
        own.reshape(17, 8, OWN),
        cot,
        got_x,
        got_near,
        got_far,
        got_x_near,
        got_x_far,
        *weights,
        pool_first,
        spread_first,
        spread_second,
    )
    [features] = call(features_kernel, [((64, 256), BF16)], 8)(act_second, pool_second)
    part = (kept + swap_cores(sent).astype(F32)).astype(BF16)
    part = sum_of_four(part, "dp")
    part, features = lax.optimization_barrier((part, features))
    mine = sum_of_four(part, "yz")
    second, first = call(unpack_kernel, [((3, 288, 64), F32), ((27, 4, 32), F32)], 8)(
        mine, swap_cores(mine)
    )
    return (
        features.reshape(1, 64, 1, 1, 256),
        act_grad.reshape(1, 32, 1, 1, 2048),
        first.reshape(3, 3, 3, 4, 32).transpose(4, 3, 0, 1, 2),
        second.reshape(3, 3, 3, 32, 64).transpose(4, 3, 0, 1, 2),
    )


def solution(mesh):
    placed = (P("dp", None, "gx", "yz", None), P(), P(), P("dp", None, "gx", "yz", None))
    rows_y = min(4, mesh.shape["yz"])
    rows_z = mesh.shape["yz"] // rows_y
    if rows_z == 1 and rows_y == 4 and mesh.shape["gx"] == 2 and mesh.shape["dp"] == 4:
        body = functools.partial(on_device_kernels, rows_y)
    else:
        body = functools.partial(on_device_plain, rows_y, rows_z)
    return jax.shard_map(
        body,
        mesh=mesh,
        in_specs=placed,
        out_specs=(P("dp", None, "gx", "yz", None), P("dp", None, "gx", "yz", None), P(), P()),
        check_vma=False,
    )
```
